32 devices in a mesh: expert: 8 (over z, y), shard: 4 (over x, core).
Axes of the slice: x: 2, y: 2, z: 4, core: 2. Of those that a mesh axis runs over, the one named last changes fastest.
Arguments:
- tokens: bfloat16 [4096, 768], P(('expert', 'shard')), may hold values from -6 to 6
- lengths: int32 [8, 3], P('expert'), may hold values from 1 to 448, 512 in all within a row
- routes: int32 [4096, 1], P(('expert', 'shard')), may hold values from 0 to 7; in each aligned block of 128 rows (0 to 127, 128 to 255, ...) at most 19 rows name the same one
- attention_in: bfloat16 [768, 2304], P('shard'), may hold values from -0.109375 to 0.109375
- attention_out: bfloat16 [768, 768], P('shard'), may hold values from -1.75 to 1.75
- position_bias: bfloat16 [12, 32], P('shard'), may hold values from -4 to 4
- first_gain: bfloat16 [768], P('shard'), may hold values from 0.5 to 1.5
- second_gain: bfloat16 [768], P('shard'), may hold values from 0.5 to 1.5
- router: float32 [768, 8], replicated, may hold values from -0.109375 to 0.109375
- expert_in: bfloat16 [8, 768, 3072], P('expert', None, 'shard'), may hold values from -0.21875 to 0.21875
- expert_out: bfloat16 [8, 3072, 768], P('expert', 'shard'), may hold values from -1.296875 to 1.296875
- cotangent: bfloat16 [4096, 768], P(('expert', 'shard')), may hold values from -6 to 6
Outputs:
- layer_out: bfloat16 [4096, 768], P(('expert', 'shard'))
- grad_tokens: bfloat16 [4096, 768], P(('expert', 'shard'))
- grad_attention_in: float32 [768, 2304], P('shard')
- grad_attention_out: float32 [768, 768], P('shard')
- grad_position_bias: float32 [12, 32], P('shard')
- grad_first_gain: float32 [768], P('shard')
- grad_second_gain: float32 [768], P('shard')
- grad_router: float32 [768, 8], P('shard')
- grad_expert_in: float32 [8, 768, 3072], P('expert', None, 'shard')
- grad_expert_out: float32 [8, 3072, 768], P('expert', 'shard')
The draws below stay inside these ranges and needn't reach their ends.
Inputs may be any that keep to these rules, and one draw needn't show every extreme that they name: Each row holds the lengths of the 3 sequences that fill one group, and its largest is exactly 448. `routes`: among the tokens of one device no expert is named more than 19 times; in some device some expert is named exactly 19 times.
All inputs are finite; a program needn't handle non-finite values.
Results may differ from the reference program's by a relative error of at most 0.019.
Values may be sent and summed in bfloat16 or wider, within the bound.
No kernel may reach another device: no remote copies, remote signals or barrier semaphores. Data moves between devices by JAX's collectives and lax.ppermute only.
A program may use at most 128 MiB of HBM per device.

```python
import math
import jax
import jax.numpy as jnp
import numpy as np
from jax import lax

D = 768
HEADS = 12
HEAD_DIM = 64
FF = 3072
BUCKETS = 32
SEQS = 3
TOK_DEV = 128
GROUPS = 8
EXPERTS = 8
GROUP_TOK = 512
LONGEST = 448
CAP = 19
TOKENS = 4096
N_EXPERT = 8
N_SHARD = 4


def block_levels(rng, shape, split, least, largest):
    def one(axis_at, blocks):
        heights = jax.random.uniform(jax.random.fold_in(jax.random.fold_in(rng, 6), axis_at), (blocks,), jnp.float32, least / len(split), largest / len(split))
        return jnp.repeat(jnp.exp(heights), shape[axis_at] // blocks).reshape((-1,) + (1,) * (len(shape) - axis_at - 1))

    factor_of = one(*split[0])
    for cut in split[1:]:
        factor_of = factor_of * one(*cut)
    return factor_of


def split_up(number_of, total, limit, skew):
    loads = [(1 << 20) // math.isqrt(rank ** skew) + 1 for rank in range(2, number_of + 1)]
    spare, counts = total - limit - (number_of - 1), [1] * (number_of - 1)
    while spare > 0:
        free = [i for i in range(number_of - 1) if counts[i] < limit]
        pool, remaining = sum([loads[i] for i in free]), spare
        for i in free:
            addition = min(limit - counts[i], max(1, remaining * loads[i] // pool), spare)
            counts[i] = counts[i] + addition
            spare = spare - addition
    return np.array([limit] + counts)


def ragged_sizes(stream_key, count, total, reach, skew):
    if count == 2:
        one = jax.random.randint(stream_key, (), max(1, total - reach), min(reach, total - 1) + 1)
        return jnp.stack([one, total - one])
    tallies = jnp.asarray(split_up(count, total, reach, skew), jnp.int32)
    twos = (count - 1) // 2
    source_of, sink = tallies[1:1 + 2 * twos:2], tallies[2:2 + 2 * twos:2]
    margin = jnp.minimum(source_of - 1, reach - sink)
    passed = jax.random.randint(jax.random.fold_in(stream_key, 1), (twos,), 0, 1 << 20) % (margin + 1)
    tallies = tallies.at[1:1 + 2 * twos:2].set(source_of - passed).at[2:2 + 2 * twos:2].set(sink + passed)
    return tallies[jax.random.permutation(jax.random.fold_in(stream_key, 2), count)]


def shared_out(rng, own, number, rows, amount, top, limit, slope):
    ranking = jax.random.permutation(rng, amount)
    crowded, usual = shares(amount, rows * top, limit, slope, True), shares(amount, rows * top, limit, slope, False)
    places = jnp.arange(amount)

    def named(sizes, turn):
        used = int((sizes > 0).sum())
        fixed = max(1, used // 4)
        passed = fixed + (places - fixed + turn * (used - fixed)) % max(1, amount - fixed)
        return jnp.zeros((amount,), jnp.int32).at[ranking[jnp.where(places < fixed, places, passed)]].set(jnp.asarray(sizes, jnp.int32))

    sizes = jnp.where(number % 4 == 0, named(crowded, number // 4), named(usual, number - number // 4 - 1))
    mixed = jax.random.permutation(jax.random.fold_in(own, 3), amount)
    giver, receiver = mixed[0:amount // 2 * 2:2], mixed[1:amount // 2 * 2:2]
    slack = jnp.minimum(sizes[giver] - 1, limit - sizes[receiver]) // 2
    slack = jnp.where((giver == ranking[0]) | (receiver == ranking[0]) | (sizes[receiver] == 0), 0, jnp.maximum(slack, 0))
    passed = jax.random.randint(jax.random.fold_in(own, 4), (amount // 2,), 0, 1 << 20) % (slack + 1)
    sizes = sizes.at[giver].add(-passed).at[receiver].add(passed)
    members = jnp.searchsorted(jnp.cumsum(sizes), jnp.arange(rows * top), side="right").astype(jnp.int32)
    table = members.reshape(top, rows).T
    table = table[jax.random.permutation(jax.random.fold_in(own, 1), rows)]
    turn = jax.random.randint(jax.random.fold_in(own, 2), (rows, 1), 0, top)
    return jnp.take_along_axis(table, (jnp.arange(top)[None, :] + turn) % top, axis=1)


def shares(number_of, total, reach, slope, full):
    weights = [(1 << 20) // math.isqrt(rank ** slope) + 1 for rank in range(1, number_of + 1)]
    largest = reach if full else min(reach, max(-(-total // number_of), total * weights[0] // sum(weights)))
    least = 1 if total - largest >= number_of - 1 else 0
    holding, spare = [largest] + [least] * (number_of - 1), total - largest - least * (number_of - 1)
    while spare > 0:
        movable = [i for i in range(1, number_of) if holding[i] < largest] or [i for i in range(1, number_of) if holding[i] < reach]
        pool, budget = sum([weights[i] for i in movable]), spare
        for i in movable:
            extra = min(reach - holding[i], max(1, budget * weights[i] // pool), spare)
            holding[i] = holding[i] + extra
            spare = spare - extra
    return np.array(holding)


def scatter_about(key, extent, scale, bound, cuts=(), kind=jnp.bfloat16):
    factor_of = block_levels(key, extent, cuts, -0.22, 0.18) if cuts else 1.0
    array = jax.random.normal(key, extent, jnp.float32) * scale * factor_of
    return jnp.minimum(jnp.maximum(array, -bound), bound).astype(kind)


def setup_inputs(seed: int = 0) -> dict:
    streams_of = jax.random.split(jax.random.key(seed), 13)
    tokens = scatter_about(streams_of[0], (TOKENS, D), 1.0, 6.0, ((0, 32),))
    lengths = jax.vmap(lambda own: ragged_sizes(own, SEQS, GROUP_TOK, LONGEST, 2))(jax.random.split(streams_of[1], GROUPS)).reshape((GROUPS, SEQS)).astype(jnp.int32)
    routes_keys = jax.random.split(jax.random.fold_in(streams_of[2], 1), TOKENS // TOK_DEV)
    routes_turns = jax.random.permutation(jax.random.fold_in(streams_of[2], 3), TOKENS // TOK_DEV)
    routes = jax.vmap(lambda own, number: shared_out(jax.random.fold_in(streams_of[2], 2), own, number, TOK_DEV, EXPERTS, 1, CAP, 1))(routes_keys, routes_turns).reshape((TOKENS, 1))
    attention_in = scatter_about(streams_of[3], (D, 3 * D), (4 * D) ** -0.5, 0.109375, ((0, 4),))
    attention_out = scatter_about(streams_of[4], (D, D), (D // 64) ** -0.5, 1.75, ((0, 4),))
    position_bias = scatter_about(streams_of[5], (HEADS, BUCKETS), 1.0, 4.0, ((0, 4),))
    first_gain = jnp.clip(1.0 + 0.1 * jax.random.normal(streams_of[6], (D,), jnp.float32), 0.5, 1.5).astype(jnp.bfloat16)
    second_gain = jnp.clip(1.0 + 0.1 * jax.random.normal(streams_of[7], (D,), jnp.float32), 0.5, 1.5).astype(jnp.bfloat16)
    router = scatter_about(streams_of[8], (D, EXPERTS), (4 * D) ** -0.5, 0.109375, (), jnp.float32)
    expert_in = scatter_about(streams_of[9], (EXPERTS, D, FF), D ** -0.5, 0.21875, ((0, 8), (2, 4)))
    expert_out = scatter_about(streams_of[10], (EXPERTS, FF, D), (1.5 * EXPERTS * FF ** -0.5), 1.296875, ((0, 8), (1, 4)))
    cotangent = scatter_about(streams_of[11], (TOKENS, D), 1.0, 6.0, ((0, 32),))
    return {"tokens": tokens, "lengths": lengths, "routes": routes, "attention_in": attention_in, "attention_out": attention_out, "position_bias": position_bias, "first_gain": first_gain, "second_gain": second_gain, "router": router, "expert_in": expert_in, "expert_out": expert_out, "cotangent": cotangent}


norm_eps = 1e-06
gelu_scale = 0.7978845608028654
gelu_cubic = 0.044715
big_negative = -1e+30
far_steps = (12, 16, 23, 32, 46, 64, 91)

@jax.custom_vjp
def low(v):
    return lax.optimization_barrier(v.astype(jnp.bfloat16)).astype(jnp.float32)

@jax.custom_vjp
def low_back(v):
    return v

def low_keep(v):
    return (low(v), None)

def low_pass(kept, grad):
    return (grad,)

def back_keep(v):
    return (v, None)

def back_low(kept, grad):
    return (low(grad),)
low.defvjp(low_keep, low_pass)
low_back.defvjp(back_keep, back_low)

def both_ways(value):
    return low(low_back(value))

def exact_dot(left, right):
    return jnp.dot(left, right, precision=lax.Precision.HIGHEST)

def bucket_index(offset):
    distance = jnp.abs(offset)
    far_level = jnp.full_like(distance, 8)
    for step_edge in far_steps:
        far_level = far_level + (distance >= step_edge).astype(jnp.int32)
    near = jnp.where(distance < 8, distance, far_level)
    return near + 16 * (offset > 0).astype(jnp.int32)

def gelu_tanh(value):
    inner = gelu_scale * (value + gelu_cubic * value * value * value)
    return 0.5 * value * (1.0 + jnp.tanh(inner))

def rms_scale(value, gain):
    return value * lax.rsqrt(lax.optimization_barrier(jnp.mean(value * value, axis=-1, keepdims=True)) + norm_eps) * gain

def grouped_attention_apply(projected, segment, table, bucket):
    queries = projected[:, :D].reshape(GROUP_TOK, HEADS, HEAD_DIM)
    keys_h = projected[:, D:2 * D].reshape(GROUP_TOK, HEADS, HEAD_DIM)
    values_h = projected[:, 2 * D:].reshape(GROUP_TOK, HEADS, HEAD_DIM)
    scores = jnp.einsum('qhd,khd->hqk', queries, keys_h, precision=lax.Precision.HIGHEST)
    scores = low_back(scores + jnp.take(table, bucket, axis=1))
    same_seq = segment[:, None] == segment[None, :]
    scores = jnp.where(same_seq[None], scores, big_negative)
    top_score = lax.optimization_barrier(jnp.max(scores, axis=-1, keepdims=True))
    raised = jnp.exp(scores - top_score)
    attention = raised / lax.optimization_barrier(jnp.sum(raised, axis=-1, keepdims=True))
    mixed = jnp.einsum('hqk,khd->qhd', low(attention), values_h, precision=lax.Precision.HIGHEST)
    return mixed.reshape(GROUP_TOK, D)

def expert_apply(rows, weight_up, weight_down):
    before = low_back(exact_dot(rows, weight_up))
    hidden = low(gelu_tanh(before))
    return both_ways(exact_dot(hidden, weight_down))

def reference(tokens, lengths, routes, attention_in, attention_out, position_bias, first_gain, second_gain, router, expert_in, expert_out, cotangent):
    ends = jnp.cumsum(lengths, axis=1)
    place = lax.iota(jnp.int32, GROUP_TOK)
    segment = lax.optimization_barrier(jnp.sum((place[None, :, None] >= ends[:, None, :]).astype(jnp.int32), axis=2))
    bucket = bucket_index(place[None, :] - place[:, None])
    route = routes[:, 0]
    sources = N_EXPERT * N_SHARD
    chosen = (route[:, None] == lax.iota(jnp.int32, EXPERTS)[None, :]).astype(jnp.int32)
    running = jnp.cumsum(chosen.reshape(sources, TOK_DEV, EXPERTS), axis=1).reshape(TOKENS, EXPERTS)
    slot = lax.optimization_barrier(jnp.sum((running - 1) * chosen, axis=1))
    source = lax.iota(jnp.int32, TOKENS) // TOK_DEV
    position = route * (sources * CAP) + source * CAP + slot

    def forward(inputs, w_attn_in, w_attn_out, table, gain_one, gain_two, w_router, w_up, w_down):
        normed = low(rms_scale(inputs, gain_one))
        projected = both_ways(exact_dot(normed, w_attn_in))
        group_fn = jax.checkpoint(lambda pair: grouped_attention_apply(pair[0], pair[1], table, bucket))
        mixed = lax.map(group_fn, (projected.reshape(N_EXPERT, GROUP_TOK, 3 * D), segment))
        mixed = both_ways(mixed.reshape(TOKENS, D))
        first_hidden_state = inputs + low_back(exact_dot(mixed, w_attn_out))
        normed_two = rms_scale(first_hidden_state, gain_two)
        logits = exact_dot(normed_two, w_router)
        shifted = jnp.exp(logits - lax.optimization_barrier(jnp.max(logits, axis=-1, keepdims=True)))
        probs = shifted / lax.optimization_barrier(jnp.sum(shifted, axis=-1, keepdims=True))
        gate = lax.optimization_barrier(jnp.sum(probs * chosen.astype(jnp.float32), axis=1))
        sent = both_ways(normed_two)
        buffer = jnp.zeros((EXPERTS * sources * CAP, D), jnp.float32).at[position].set(sent)
        expert_fn = jax.checkpoint(lambda trio: expert_apply(trio[0], trio[1], trio[2]))
        result = lax.map(expert_fn, (buffer.reshape(EXPERTS, sources * CAP, D), w_up, w_down))
        returned = result.reshape(EXPERTS * sources * CAP, D)[position]
        return first_hidden_state + gate[:, None] * returned
    arguments = (tokens.astype(jnp.float32), attention_in.astype(jnp.float32), attention_out.astype(jnp.float32), position_bias.astype(jnp.float32), first_gain.astype(jnp.float32), second_gain.astype(jnp.float32), router.astype(jnp.float32), expert_in.astype(jnp.float32), expert_out.astype(jnp.float32))
    layer_output, pullback = jax.vjp(forward, *arguments)
    grads = pullback(cotangent.astype(jnp.float32))
    return (layer_output.astype(jnp.bfloat16), grads[0].astype(jnp.bfloat16), grads[1], grads[2], grads[3], grads[4], grads[5], grads[6], grads[7], grads[8])
```

```python
import jax
import jax.numpy as jnp
from jax import lax
from jax.experimental import pallas as pl
from jax.experimental.pallas import tpu as pltpu
from jax.sharding import PartitionSpec as P

norm_eps = 1e-06
gelu_scale = 0.7978845608028654
gelu_cubic = 0.044715
big_negative = -1e30
near_steps = 8
far_steps = (12, 16, 23, 32, 46, 64, 91)
bf16 = jnp.bfloat16
f32 = jnp.float32
row_tile = 8
gain_rows = 16


def bucket_index(offset):
    distance = jnp.abs(offset)
    far_level = jnp.full_like(distance, near_steps)
    for step_edge in far_steps:
        far_level = far_level + (distance >= step_edge).astype(jnp.int32)
    near = jnp.where(distance < near_steps, distance, far_level)
    return near + 16 * (offset > 0).astype(jnp.int32)


def dot(left, right):
    return jnp.dot(left, right, preferred_element_type=f32)


def dot_nt(left, right):
    return lax.dot_general(left, right, (((1,), (1,)), ((), ())), preferred_element_type=f32)


def dot_tn(left, right):
    return lax.dot_general(left, right, (((0,), (0,)), ((), ())), preferred_element_type=f32)


def swap(value, axis, bit):
    size = lax.axis_size(axis)
    return lax.ppermute(value, axis, [(i, i ^ bit) for i in range(size)])


def gather_relative(value, axis):
    blocks = [value]
    bit = lax.axis_size(axis) // 2
    parts = {0: value}
    while bit:
        for p in list(parts):
            parts[p ^ bit] = swap(parts[p], axis, bit)
        bit //= 2
    return [parts[p] for p in range(lax.axis_size(axis))]


def exchange_relative(blocks, axis):
    return [blocks[0]] + [swap(block, axis, p) for p, block in enumerate(blocks) if p]


def call(kernel, out_shape, operands, spaces=None, scratch=(), flops=0, size=0):
    vmem = pl.BlockSpec(memory_space=pltpu.VMEM)
    smem = pl.BlockSpec(memory_space=pltpu.SMEM)
    spaces = spaces or ""
    in_specs = [smem if i < len(spaces) and spaces[i] == "s" else vmem for i in range(len(operands))]
    return pl.pallas_call(
        kernel,
        out_shape=out_shape,
        in_specs=in_specs,
        out_specs=jax.tree.map(lambda _: vmem, out_shape),
        scratch_shapes=list(scratch),
        compiler_params=pltpu.CompilerParams(vmem_limit_bytes=56 * 2**20),
        cost_estimate=pl.CostEstimate(flops=flops, bytes_accessed=size, transcendentals=0),
    )(*operands)


def shape(dims, dtype=bf16):
    return jax.ShapeDtypeStruct(tuple(dims), dtype)


def attention_forward(n, rows, width, heads, seqs, buckets, *refs):
    index, lengths, table = refs[:3]
    token_refs = refs[3 : 3 + n]
    weight_refs = refs[3 + n : 3 + 2 * n]
    normed_out, weight_out, projected_out, weights_out = refs[3 + 2 * n : 7 + 2 * n]
    mixed_out = refs[7 + 2 * n : 7 + 3 * n]
    tokens_scr, mixed_scr = refs[7 + 3 * n :]
    s = index[0]
    part = width // n
    head_dim = part // heads
    gain = jnp.zeros((1, width), f32)
    for p in range(n):
        place = s ^ p
        tokens_scr[place] = token_refs[p][:rows, :]
        gain = gain + token_refs[p][rows : rows + gain_rows, :].astype(f32)[0:1, :]
        weight_out[pl.ds(pl.multiple_of(place * part, part & -part), part), :] = weight_refs[p][...]
    for j in range(n):
        value = tokens_scr[j].astype(f32)
        factor = lax.rsqrt(jnp.mean(value * value, axis=-1, keepdims=True) + norm_eps)
        normed_out[j * rows : (j + 1) * rows, :] = (value * factor * gain).astype(bf16)
    projected_out[...] = dot(normed_out[...], weight_out[...]).astype(bf16)
    total_rows = n * rows
    key_place = lax.broadcasted_iota(jnp.int32, (1, total_rows), 1)
    key_segment = jnp.zeros((1, total_rows), jnp.int32)
    end = jnp.int32(0)
    ends = []
    for j in range(seqs):
        end = end + lengths[0, j]
        ends.append(end)
        key_segment = key_segment + (key_place >= end).astype(jnp.int32)
    base = lax.broadcasted_iota(jnp.int32, (rows, rows), 1) - lax.broadcasted_iota(
        jnp.int32, (rows, rows), 0
    )
    steps = {diff: bucket_index(base + diff * rows) for diff in (-1, 0, 1)}
    for h in range(heads):
        query = projected_out[:, h * head_dim : (h + 1) * head_dim]
        key = projected_out[:, part + h * head_dim : part + (h + 1) * head_dim]
        value = projected_out[:, 2 * part + h * head_dim : 2 * part + (h + 1) * head_dim]
        bias = {}
        for diff in (-1, 0, 1):
            block = jnp.zeros((rows, rows), f32)
            for b in range(buckets):
                block = jnp.where(steps[diff] == b, table[h, b], block)
            bias[diff] = block
        low_side = jnp.full((rows, rows), table[h, buckets // 2 - 1], f32)
        high_side = jnp.full((rows, rows), table[h, buckets - 1], f32)
        for i in range(n):
            scores = dot_nt(query[i * rows : (i + 1) * rows, :], key)
            side = [
                bias[j - i] if abs(j - i) <= 1 else (high_side if j > i else low_side)
                for j in range(n)
            ]
            scores = scores + jnp.concatenate(side, axis=1)
            query_place = i * rows + lax.broadcasted_iota(jnp.int32, (rows, 1), 0)
            query_segment = jnp.zeros((rows, 1), jnp.int32)
            for j in range(seqs):
                query_segment = query_segment + (query_place >= ends[j]).astype(jnp.int32)
            scores = jnp.where(query_segment == key_segment, scores, big_negative)
            top = jnp.max(scores, axis=-1, keepdims=True)
            raised = jnp.exp(scores - top)
            total = jnp.sum(raised, axis=-1, keepdims=True)
            weights = (raised * (1.0 / total)).astype(bf16)
            weights_out[h, i * rows : (i + 1) * rows, :] = weights
            mixed_scr[i, :, h * head_dim : (h + 1) * head_dim] = dot(weights, value).astype(bf16)
    for p in range(n):
        mixed_out[p][...] = mixed_scr[s ^ p]


def attention_backward(n, m, rows, width, heads, buckets, *refs):
    index, projected, normed, weight, weights = refs[:5]
    grad_refs = refs[5 : 5 + n]
    at = 5 + n
    share_out = refs[at : at + m]
    normed_grad_out = refs[at + m : at + m + n]
    table_out = refs[at + m + n]
    grad_scr, scores_scr, projected_scr, total_scr, normed_scr = refs[at + m + n + 1 :]
    s = index[0]
    e = index[1]
    part = width // n
    head_dim = part // heads
    for p in range(n):
        grad_scr[s ^ p] = grad_refs[p][...]
    base = lax.broadcasted_iota(jnp.int32, (rows, rows), 1) - lax.broadcasted_iota(
        jnp.int32, (rows, rows), 0
    )
    steps = {diff: bucket_index(base + diff * rows) for diff in (-1, 0, 1)}
    lane = lax.broadcasted_iota(jnp.int32, (row_tile, 128), 1)
    line = lax.broadcasted_iota(jnp.int32, (row_tile, 128), 0)
    table_total = jnp.zeros((row_tile, 128), f32)
    for h in range(heads):
        query = projected[:, h * head_dim : (h + 1) * head_dim]
        key = projected[:, part + h * head_dim : part + (h + 1) * head_dim]
        value = projected[:, 2 * part + h * head_dim : 2 * part + (h + 1) * head_dim]
        near = {diff: jnp.zeros((rows, rows), f32) for diff in (-1, 0, 1)}
        low_side = jnp.zeros((rows, rows), f32)
        high_side = jnp.zeros((rows, rows), f32)
        upstream = jnp.concatenate(
            [grad_scr[i, :, h * head_dim : (h + 1) * head_dim] for i in range(n)], axis=0
        )
        for i in range(n):
            weights_i = weights[h, i * rows : (i + 1) * rows, :].astype(f32)
            grad_weights = dot_nt(upstream[i * rows : (i + 1) * rows, :], value)
            inner = jnp.sum(weights_i * grad_weights, axis=-1, keepdims=True)
            grad_scores = weights_i * (grad_weights - inner)
            scores_scr[i * rows : (i + 1) * rows, :] = grad_scores.astype(bf16)
            for j in range(n):
                block = grad_scores[:, j * rows : (j + 1) * rows]
                if abs(j - i) <= 1:
                    near[j - i] = near[j - i] + block
                elif j > i:
                    high_side = high_side + block
                else:
                    low_side = low_side + block
        for b in range(buckets):
            amount = jnp.zeros((1, rows), f32)
            for diff in (-1, 0, 1):
                if diff < 0 and b >= buckets // 2 or diff > 0 and b < buckets // 2:
                    continue
                amount = amount + jnp.sum(
                    jnp.where(steps[diff] == b, near[diff], 0.0), axis=0, keepdims=True
                )
            if b == buckets - 1:
                amount = amount + jnp.sum(high_side, axis=0, keepdims=True)
            if b == buckets // 2 - 1:
                amount = amount + jnp.sum(low_side, axis=0, keepdims=True)
            amount = jnp.sum(amount, axis=1, keepdims=True)
            table_total = jnp.where((line == h) & (lane == b), amount, table_total)
        grad_scores_all = scores_scr[...]
        projected_scr[:, h * head_dim : (h + 1) * head_dim] = dot(grad_scores_all, key).astype(bf16)
        projected_scr[:, part + h * head_dim : part + (h + 1) * head_dim] = dot_tn(
            grad_scores_all, query
        ).astype(bf16)
        projected_scr[:, 2 * part + h * head_dim : 2 * part + (h + 1) * head_dim] = dot_tn(
            weights[h], upstream
        ).astype(bf16)
    table_out[...] = table_total
    grad_projected = projected_scr[...]
    total_scr[...] = dot_tn(normed[...], grad_projected)
    for d in range(m):
        piece = part // m
        for t in range(n):
            start = pl.multiple_of(t * part + (e ^ d) * piece if m > 1 else t * part, row_tile)
            share_out[d][t] = total_scr[pl.ds(start, piece), :].astype(bf16)
    normed_scr[...] = dot_nt(grad_projected, weight[...]).astype(bf16).reshape(n, rows, width)
    for p in range(n):
        normed_grad_out[p][...] = normed_scr[s ^ p]


def expert_forward(n, rows, *refs):
    row_refs = refs[:n]
    up, down, hidden_out, slope_out = refs[n : n + 4]
    keep_out, send_out = refs[n + 4 :]
    for p in range(n):
        before = dot(row_refs[p][...], up[0])
        square = before * before
        tanh_value = jnp.tanh(gelu_scale * before * (1.0 + gelu_cubic * square))
        half = 0.5 * (1.0 + tanh_value)
        hidden = (before * half).astype(bf16)
        slope = half + 0.5 * before * (1.0 - tanh_value * tanh_value) * gelu_scale * (
            1.0 + 3.0 * gelu_cubic * square
        )
        hidden_out[p * rows : (p + 1) * rows, :] = hidden
        slope_out[p * rows : (p + 1) * rows, :] = slope.astype(bf16)
        result = dot(hidden, down[0]).astype(bf16)
        target = send_out if p & 1 else keep_out
        at = (p >> 1) * rows
        target[at : at + rows, :] = result


def expert_backward(n, rows, *refs):
    grad_refs = refs[:n]
    up, down, slope, before_out = refs[n : n + 4]
    keep_out, send_out = refs[n + 4 :]
    for p in range(n):
        grad_hidden = dot_nt(grad_refs[p][...], down[0])
        grad_before = (grad_hidden * slope[p * rows : (p + 1) * rows, :].astype(f32)).astype(bf16)
        before_out[p * rows : (p + 1) * rows, :] = grad_before
        result = dot_nt(grad_before, up[0]).astype(bf16)
        target = send_out if p & 1 else keep_out
        at = (p >> 1) * rows
        target[at : at + rows, :] = result


def expert_weights(n, *refs):
    row_refs = refs[:n]
    grad_refs = refs[n : 2 * n]
    hidden, grad_before, up_out, down_out = refs[2 * n :]
    grads = jnp.concatenate([r[...] for r in grad_refs], axis=0)
    rows = jnp.concatenate([r[...] for r in row_refs], axis=0)
    down_out[0] = dot_tn(hidden[...], grads)
    up_out[0] = dot_tn(rows, grad_before[...])


def reduce_shard(keep, send, rows):
    came = swap(send, "shard", 1)
    forward = (keep[rows:].astype(f32) + came[rows:].astype(f32)).astype(bf16)
    own = keep[:rows].astype(f32) + came[:rows].astype(f32)
    return (own + swap(forward, "shard", 2).astype(f32)).astype(bf16)


def rms_factor(value):
    return lax.rsqrt(jnp.mean(value * value, axis=-1, keepdims=True) + norm_eps)


def rms_backward(value, factor, gain, upstream):
    scaled = upstream * gain
    grad_value = factor * scaled - value * factor * factor * factor * jnp.mean(
        scaled * value, axis=-1, keepdims=True
    )
    grad_gain = jnp.sum(upstream * value * factor, axis=0)
    return (grad_value, grad_gain)


def local(
    tokens,
    lengths,
    routes,
    attention_in,
    attention_out,
    position_bias,
    first_gain,
    second_gain,
    router,
    expert_in,
    expert_out,
    cotangent,
):
    n = lax.axis_size("shard")
    m = lax.axis_size("expert")
    s = lax.axis_index("shard")
    e = lax.axis_index("expert")
    index = jnp.stack([s, e]).astype(jnp.int32)
    rows, width = tokens.shape
    heads, buckets = position_bias.shape
    part = width // n
    seqs = lengths.shape[1]
    experts = router.shape[1]
    direct = m <= 8

    gains = jnp.zeros((gain_rows, width), bf16)
    gains = lax.dynamic_update_slice(gains, jnp.stack([first_gain, second_gain]), (0, s * part))
    token_blocks = gather_relative(jnp.concatenate([tokens, gains], axis=0), "shard")
    by_target = attention_in.reshape(part, 3, n, part).transpose(2, 0, 1, 3).reshape(n, part, 3 * part)
    weight_blocks = exchange_relative(
        [lax.dynamic_index_in_dim(by_target, s ^ p, 0, keepdims=False) for p in range(n)], "shard"
    )
    out_blocks = gather_relative(attention_out, "shard")
    gain_one, gain_two = (
        sum(block[rows + i : rows + i + 1].astype(f32) for block in token_blocks) for i in range(2)
    )

    group = n * rows
    head_flops = 2 * heads * group * group * (part // heads)
    answers = call(
        lambda *refs: attention_forward(n, rows, width, heads, seqs, buckets, *refs),
        (
            shape((group, width)),
            shape((width, 3 * part)),
            shape((group, 3 * part)),
            shape((heads, group, group)),
            *[shape((rows, part))] * n,
        ),
        (index, lengths, position_bias.astype(f32), *token_blocks, *weight_blocks),
        "sss",
        [pltpu.VMEM((n, rows, width), bf16), pltpu.VMEM((n, rows, part), bf16)],
        flops=2 * group * width * 3 * part + 8 * head_flops,
        size=8 * 2**20,
    )
    normed, weight, projected, weights = answers[:4]
    mixed_mine = answers[4:]
    mixed_blocks = exchange_relative(list(mixed_mine), "shard")

    inputs = tokens.astype(f32)
    hidden_one = inputs + sum(dot(mixed_blocks[p], out_blocks[p]) for p in range(n))
    factor_two = rms_factor(hidden_one)
    normed_two = hidden_one * factor_two * gain_two
    logits = jnp.dot(
        normed_two, router, precision=lax.Precision.HIGHEST, preferred_element_type=f32
    )
    shifted = jnp.exp(logits - jnp.max(logits, axis=-1, keepdims=True))
    probs = shifted / jnp.sum(shifted, axis=-1, keepdims=True)
    route = routes[:, 0]
    chosen = (route[:, None] == lax.iota(jnp.int32, experts)[None, :]).astype(f32)
    gate = jnp.sum(probs * chosen, axis=1)
    lower = (lax.iota(jnp.int32, rows)[:, None] >= lax.iota(jnp.int32, rows)[None, :]).astype(bf16)
    running = dot(lower, chosen.astype(bf16))
    slot = jnp.sum((running - 1.0) * chosen, axis=1).astype(jnp.int32)
    capacity = max(2, 9 * rows // (8 * experts) + 1)
    capacity = -(-capacity // row_tile) * row_tile
    holder = route ^ e if direct else route
    target = holder * capacity + slot
    places = experts * capacity
    collect = (target[:, None] == lax.iota(jnp.int32, places)[None, :]).astype(bf16)
    upstream = cotangent.astype(f32)
    grad_result = (gate[:, None] * upstream).astype(bf16)

    def send(value):
        if not direct:
            return lax.all_to_all(
                value.reshape(experts, capacity, width), "expert", 0, 0, tiled=True
            ).reshape(places, width)
        return jnp.concatenate(
            exchange_relative(
                [value[d * capacity : (d + 1) * capacity] for d in range(experts)], "expert"
            ),
            axis=0,
        )

    arrived = send(dot_tn(collect, normed_two.astype(bf16)).astype(bf16))
    row_blocks = gather_relative(arrived, "shard")
    arrived_grad = send(dot_tn(collect, grad_result).astype(bf16))
    grad_blocks = gather_relative(arrived_grad, "shard")

    units = expert_in.shape[2]
    all_rows = n * places
    expert_flops = 2 * all_rows * width * units
    hidden, slope, keep, out = call(
        lambda *refs: expert_forward(n, places, *refs),
        (
            shape((all_rows, units)),
            shape((all_rows, units)),
            shape((all_rows // 2, width)),
            shape((all_rows // 2, width)),
        ),
        (*row_blocks, expert_in, expert_out),
        flops=2 * expert_flops,
        size=6 * 2**20,
    )
    returned = send(reduce_shard(keep, out, places))
    grad_before, keep_grad, out_grad = call(
        lambda *refs: expert_backward(n, places, *refs),
        (
            shape((all_rows, units)),
            shape((all_rows // 2, width)),
            shape((all_rows // 2, width)),
        ),
        (*grad_blocks, expert_in, expert_out, slope),
        flops=2 * expert_flops,
        size=6 * 2**20,
    )
    returned_grad = send(reduce_shard(keep_grad, out_grad, places))
    grad_up, grad_down = call(
        lambda *refs: expert_weights(n, *refs),
        (shape(expert_in.shape, f32), shape(expert_out.shape, f32)),
        (*row_blocks, *grad_blocks, hidden, grad_before),
        flops=2 * expert_flops,
        size=9 * 2**20,
    )

    expert_result = dot(collect, returned)
    layer_out = (hidden_one + gate[:, None] * expert_result).astype(bf16)
    grad_gate = jnp.sum(upstream * expert_result, axis=1)
    grad_logits = (grad_gate * gate)[:, None] * (chosen - probs)
    grad_router = lax.dot_general(
        normed_two,
        grad_logits,
        (((0,), (0,)), ((), ())),
        precision=lax.Precision.HIGHEST,
        preferred_element_type=f32,
    )
    grad_normed_two = dot(collect, returned_grad) + lax.dot_general(
        grad_logits,
        router,
        (((1,), (1,)), ((), ())),
        precision=lax.Precision.HIGHEST,
        preferred_element_type=f32,
    )
    grad_middle, grad_gain_two = rms_backward(hidden_one, factor_two, gain_two, grad_normed_two)
    grad_hidden = upstream + grad_middle
    grad_branch = grad_hidden.astype(bf16)
    grad_mixed_blocks = exchange_relative(
        [dot_nt(grad_branch, out_blocks[p]).astype(bf16) for p in range(n)], "shard"
    )
    branch_blocks = gather_relative(grad_branch, "shard")
    holders = m if direct else 1

    answers = call(
        lambda *refs: attention_backward(n, holders, rows, width, heads, buckets, *refs),
        (
            *[shape((n, part // holders, 3 * part))] * holders,
            *[shape((rows, width))] * n,
            shape((row_tile, 128), f32),
        ),
        (index, projected, normed, weight, weights, *grad_mixed_blocks),
        "s",
        [
            pltpu.VMEM((n, rows, part), bf16),
            pltpu.VMEM((group, group), bf16),
            pltpu.VMEM((group, 3 * part), bf16),
            pltpu.VMEM((width, 3 * part), f32),
            pltpu.VMEM((n, rows, width), bf16),
        ],
        flops=8 * head_flops,
        size=8 * 2**20,
    )
    piece = part // m
    grad_weight_out = sum(dot_tn(mixed_mine[p], branch_blocks[p]) for p in range(n))

    shares = list(answers[:holders])
    normed_grads = answers[holders : holders + n]
    grad_table = answers[holders + n][:heads, :buckets]

    def spread(blocks):
        if direct:
            return exchange_relative(blocks, "expert")
        return list(lax.all_to_all(blocks, "expert", 0, 0, tiled=True))

    def gather(value):
        if direct:
            stacked = jnp.stack(gather_relative(value, "expert"))
            return stacked[lax.iota(jnp.int32, m) ^ e]
        return lax.all_gather(value, "expert", axis=0, tiled=False)

    if direct:
        out_shares = [
            lax.dynamic_slice_in_dim(grad_weight_out, (e ^ d) * piece, piece, 0).astype(bf16)
            for d in range(m)
        ]
    else:
        out_shares = grad_weight_out.astype(bf16).reshape(m, piece, width)
        shares = shares[0].reshape(n, m, piece, 3 * part).swapaxes(0, 1)
    total_out = sum(x.astype(f32) for x in spread(out_shares)).astype(bf16)
    grad_attention_out = gather(total_out).astype(f32).reshape(part, width)

    summed = sum(x.astype(f32) for x in spread(shares)).astype(bf16)
    mine = exchange_relative(
        [lax.dynamic_index_in_dim(summed, s ^ p, 0, keepdims=False) for p in range(n)], "shard"
    )
    mine = jnp.stack(mine)[lax.iota(jnp.int32, n) ^ s]
    mine = mine.reshape(n, piece, 3, part).transpose(1, 2, 0, 3).reshape(piece, 3 * width)
    grad_attention_in = gather(mine).astype(f32).reshape(part, 3 * width)

    grad_normed = sum(x.astype(f32) for x in exchange_relative(list(normed_grads), "shard"))
    grad_input_norm, grad_gain_one = rms_backward(inputs, rms_factor(inputs), gain_one, grad_normed)
    grad_tokens = (grad_hidden + grad_input_norm).astype(bf16)

    small = jnp.concatenate([grad_gain_one[:, None], grad_gain_two[:, None], grad_router], axis=1)
    small_total = lax.psum(small, ("expert", "shard"))
    small_mine = lax.dynamic_slice_in_dim(small_total, s * part, part, 0)
    table_total = lax.psum(grad_table, "expert")
    return (
        layer_out,
        grad_tokens,
        grad_attention_in,
        grad_attention_out,
        table_total,
        small_mine[:, 0],
        small_mine[:, 1],
        small_mine[:, 2:],
        grad_up,
        grad_down,
    )


def solution(mesh):
    in_specs = (
        P(("expert", "shard"), None),
        P("expert", None),
        P(("expert", "shard"), None),
        P("shard", None),
        P("shard", None),
        P("shard", None),
        P("shard"),
        P("shard"),
        P(),
        P("expert", None, "shard"),
        P("expert", "shard", None),
        P(("expert", "shard"), None),
    )
    out_specs = (
        P(("expert", "shard"), None),
        P(("expert", "shard"), None),
        P("shard", None),
        P("shard", None),
        P("shard", None),
        P("shard"),
        P("shard"),
        P("shard", None),
        P("expert", None, "shard"),
        P("expert", "shard", None),
    )
    return jax.shard_map(local, mesh=mesh, in_specs=in_specs, out_specs=out_specs, check_vma=False)
```

```python
import jax
import jax.numpy as jnp
from jax import lax
from jax.experimental import pallas as pl
from jax.experimental.pallas import tpu as pltpu
from jax.sharding import PartitionSpec as P

norm_eps = 1e-06
gelu_scale = 0.7978845608028654
gelu_cubic = 0.044715
big_negative = -1e30
near_steps = 8
far_steps = (12, 16, 23, 32, 46, 64, 91)
bf16 = jnp.bfloat16
f32 = jnp.float32
row_tile = 8
gain_rows = 16
slot_tile = 4


def bucket_index(offset):
    distance = jnp.abs(offset)
    far_level = jnp.full_like(distance, near_steps)
    for step_edge in far_steps:
        far_level = far_level + (distance >= step_edge).astype(jnp.int32)
    near = jnp.where(distance < near_steps, distance, far_level)
    return near + 16 * (offset > 0).astype(jnp.int32)


def dot(left, right):
    return jnp.dot(left, right, preferred_element_type=f32)


def dot_nt(left, right):
    return lax.dot_general(left, right, (((1,), (1,)), ((), ())), preferred_element_type=f32)


def dot_tn(left, right):
    return lax.dot_general(left, right, (((0,), (0,)), ((), ())), preferred_element_type=f32)


def swap(value, axis, bit):
    size = lax.axis_size(axis)
    return lax.ppermute(value, axis, [(i, i ^ bit) for i in range(size)])


def gather_relative(value, axis):
    blocks = [value]
    bit = lax.axis_size(axis) // 2
    parts = {0: value}
    while bit:
        for p in list(parts):
            parts[p ^ bit] = swap(parts[p], axis, bit)
        bit //= 2
    return [parts[p] for p in range(lax.axis_size(axis))]


def exchange_relative(blocks, axis):
    return [blocks[0]] + [swap(block, axis, p) for p, block in enumerate(blocks) if p]


def call(kernel, out_shape, operands, spaces=None, scratch=(), flops=0, size=0):
    vmem = pl.BlockSpec(memory_space=pltpu.VMEM)
    smem = pl.BlockSpec(memory_space=pltpu.SMEM)
    spaces = spaces or ""
    in_specs = [smem if i < len(spaces) and spaces[i] == "s" else vmem for i in range(len(operands))]
    return pl.pallas_call(
        kernel,
        out_shape=out_shape,
        in_specs=in_specs,
        out_specs=jax.tree.map(lambda _: vmem, out_shape),
        scratch_shapes=list(scratch),
        compiler_params=pltpu.CompilerParams(vmem_limit_bytes=56 * 2**20),
        cost_estimate=pl.CostEstimate(flops=flops, bytes_accessed=size, transcendentals=0),
    )(*operands)


def shape(dims, dtype=bf16):
    return jax.ShapeDtypeStruct(tuple(dims), dtype)


def prepare_tokens(n, rows, part, index, tokens, gains, out):
    out[:rows, :] = tokens[...]
    out[rows:, :] = jnp.zeros((gain_rows, n * part), bf16)
    for k in range(n):

        @pl.when(index[0] == k)
        def _():
            out[rows:, k * part : (k + 1) * part] = gains[...]


def prepare_weight(n, part, index, weight, *outs):
    for k in range(n):

        @pl.when(index[0] == k)
        def _():
            for p in range(n):
                for kind in range(3):
                    at = (kind * n + (k ^ p)) * part
                    outs[p][:, kind * part : (kind + 1) * part] = weight[:, at : at + part]


def attention_forward(n, rows, width, heads, seqs, buckets, *refs):
    index, lengths, table = refs[:3]
    token_refs = refs[3 : 3 + n]
    weight_refs = refs[3 + n : 3 + 2 * n]
    normed_out, weight_out, projected_out, weights_out, unit_out = refs[3 + 2 * n : 8 + 2 * n]
    mixed_out = refs[8 + 2 * n : 8 + 3 * n]
    tokens_scr, mixed_scr = refs[8 + 3 * n :]
    s = index[0]
    part = width // n
    head_dim = part // heads
    gain = jnp.zeros((1, width), f32)
    for p in range(n):
        place = s ^ p
        tokens_scr[place] = token_refs[p][:rows, :]
        gain = gain + token_refs[p][rows : rows + gain_rows, :].astype(f32)[0:1, :]
        weight_out[pl.ds(pl.multiple_of(place * part, part & -part), part), :] = weight_refs[p][...]
    for j in range(n):
        value = tokens_scr[j].astype(f32)
        factor = lax.rsqrt(jnp.mean(value * value, axis=-1, keepdims=True) + norm_eps)
        unit = value * factor
        unit_out[j * rows : (j + 1) * rows, :] = unit
        normed_out[j * rows : (j + 1) * rows, :] = (unit * gain).astype(bf16)
    projected_out[...] = dot(normed_out[...], weight_out[...]).astype(bf16)
    total_rows = n * rows
    key_place = lax.broadcasted_iota(jnp.int32, (1, total_rows), 1)
    key_segment = jnp.zeros((1, total_rows), jnp.int32)
    end = jnp.int32(0)
    ends = []
    for j in range(seqs):
        end = end + lengths[0, j]
        ends.append(end)
        key_segment = key_segment + (key_place >= end).astype(jnp.int32)
    base = lax.broadcasted_iota(jnp.int32, (rows, rows), 1) - lax.broadcasted_iota(
        jnp.int32, (rows, rows), 0
    )
    steps = {diff: bucket_index(base + diff * rows) for diff in (-1, 0, 1)}
    for h in range(heads):
        query = projected_out[:, h * head_dim : (h + 1) * head_dim]
        key = projected_out[:, part + h * head_dim : part + (h + 1) * head_dim]
        value = projected_out[:, 2 * part + h * head_dim : 2 * part + (h + 1) * head_dim]
        bias = {}
        for diff in (-1, 0, 1):
            block = jnp.zeros((rows, rows), f32)
            for b in range(buckets):
                block = jnp.where(steps[diff] == b, table[h, b], block)
            bias[diff] = block
        low_side = jnp.full((rows, rows), table[h, buckets // 2 - 1], f32)
        high_side = jnp.full((rows, rows), table[h, buckets - 1], f32)
        for i in range(n):
            scores = dot_nt(query[i * rows : (i + 1) * rows, :], key)
            side = [
                bias[j - i] if abs(j - i) <= 1 else (high_side if j > i else low_side)
                for j in range(n)
            ]
            scores = scores + jnp.concatenate(side, axis=1)
            query_place = i * rows + lax.broadcasted_iota(jnp.int32, (rows, 1), 0)
            query_segment = jnp.zeros((rows, 1), jnp.int32)
            for j in range(seqs):
                query_segment = query_segment + (query_place >= ends[j]).astype(jnp.int32)
            scores = jnp.where(query_segment == key_segment, scores, big_negative)
            top = jnp.max(scores, axis=-1, keepdims=True)
            raised = jnp.exp(scores - top)
            total = jnp.sum(raised, axis=-1, keepdims=True)
            weights = (raised * (1.0 / total)).astype(bf16)
            weights_out[h, i * rows : (i + 1) * rows, :] = weights
            mixed_scr[i, :, h * head_dim : (h + 1) * head_dim] = dot(weights, value).astype(bf16)
    for p in range(n):
        mixed_out[p][...] = mixed_scr[s ^ p]


def attention_backward(n, m, rows, width, heads, buckets, *refs):
    index, projected, normed, weight, weights, unit, small = refs[:7]
    grad_refs = refs[7 : 7 + n]
    at = 7 + n
    share_out = refs[at : at + m]
    normed_grad_out = refs[at + m : at + m + n]
    gain_out, table_out = refs[at + m + n : at + m + n + 2]
    grad_scr, scores_scr, projected_scr, total_scr, normed_scr = refs[at + m + n + 2 :]
    s = index[0]
    e = index[1]
    part = width // n
    head_dim = part // heads
    for p in range(n):
        grad_scr[s ^ p] = grad_refs[p][...]
    base = lax.broadcasted_iota(jnp.int32, (rows, rows), 1) - lax.broadcasted_iota(
        jnp.int32, (rows, rows), 0
    )
    steps = {diff: bucket_index(base + diff * rows) for diff in (-1, 0, 1)}
    lane = lax.broadcasted_iota(jnp.int32, (row_tile, 128), 1)
    line = lax.broadcasted_iota(jnp.int32, (row_tile, 128), 0)
    table_total = jnp.zeros((row_tile, 128), f32)
    for h in range(heads):
        query = projected[:, h * head_dim : (h + 1) * head_dim]
        key = projected[:, part + h * head_dim : part + (h + 1) * head_dim]
        value = projected[:, 2 * part + h * head_dim : 2 * part + (h + 1) * head_dim]
        near = {diff: jnp.zeros((rows, rows), f32) for diff in (-1, 0, 1)}
        low_side = jnp.zeros((rows, rows), f32)
        high_side = jnp.zeros((rows, rows), f32)
        upstream = jnp.concatenate(
            [grad_scr[i, :, h * head_dim : (h + 1) * head_dim] for i in range(n)], axis=0
        )
        for i in range(n):
            weights_i = weights[h, i * rows : (i + 1) * rows, :].astype(f32)
            grad_weights = dot_nt(upstream[i * rows : (i + 1) * rows, :], value)
            inner = jnp.sum(weights_i * grad_weights, axis=-1, keepdims=True)
            grad_scores = weights_i * (grad_weights - inner)
            scores_scr[i * rows : (i + 1) * rows, :] = grad_scores.astype(bf16)
            for j in range(n):
                block = grad_scores[:, j * rows : (j + 1) * rows]
                if abs(j - i) <= 1:
                    near[j - i] = near[j - i] + block
                elif j > i:
                    high_side = high_side + block
                else:
                    low_side = low_side + block
        for b in range(buckets):
            amount = jnp.zeros((1, rows), f32)
            for diff in (-1, 0, 1):
                if diff < 0 and b >= buckets // 2 or diff > 0 and b < buckets // 2:
                    continue
                amount = amount + jnp.sum(
                    jnp.where(steps[diff] == b, near[diff], 0.0), axis=0, keepdims=True
                )
            if b == buckets - 1:
                amount = amount + jnp.sum(high_side, axis=0, keepdims=True)
            if b == buckets // 2 - 1:
                amount = amount + jnp.sum(low_side, axis=0, keepdims=True)
            amount = jnp.sum(amount, axis=1, keepdims=True)
            table_total = jnp.where((line == h) & (lane == b), amount, table_total)
        grad_scores_all = scores_scr[...]
        projected_scr[:, h * head_dim : (h + 1) * head_dim] = dot(grad_scores_all, key).astype(bf16)
        projected_scr[:, part + h * head_dim : part + (h + 1) * head_dim] = dot_tn(
            grad_scores_all, query
        ).astype(bf16)
        projected_scr[:, 2 * part + h * head_dim : 2 * part + (h + 1) * head_dim] = dot_tn(
            weights[h], upstream
        ).astype(bf16)
    table_out[...] = table_total
    grad_projected = projected_scr[...]
    normed_grad = dot_nt(grad_projected, weight[...])
    normed_scr[...] = normed_grad.astype(bf16).reshape(n, rows, width)
    for p in range(n):
        normed_grad_out[p][...] = normed_scr[s ^ p]
    grad_gain = jnp.sum(normed_grad * unit[...], axis=0, keepdims=True)
    gain_out[...] = jnp.broadcast_to(grad_gain, gain_out.shape)
    wide = 3 * part
    total_scr[:, :wide] = dot_tn(normed[...], grad_projected)
    piece = part // m
    if m > 1:
        extra = small.shape[1]
        eye = lax.broadcasted_iota(jnp.int32, (128, 128), 0) == lax.broadcasted_iota(
            jnp.int32, (128, 128), 1
        )
        first = lax.broadcasted_iota(jnp.int32, (128, extra), 1) == 0
        for c in range(width // 128):
            row = jnp.broadcast_to(grad_gain[:, c * 128 : (c + 1) * 128], (128, 128))
            column = jnp.sum(jnp.where(eye, row, 0.0), axis=1, keepdims=True)
            block = jnp.where(first, column, small[c * 128 : (c + 1) * 128, :])
            total_scr[c * 128 : (c + 1) * 128, wide : wide + extra] = block
        for d in range(m):
            total_scr[d * piece : d * piece + row_tile, wide + extra - buckets : wide + extra] = (
                table_total[:, :buckets]
            )
    for d in range(m):
        for t in range(n):
            start = pl.multiple_of(t * part + (e ^ d) * piece if m > 1 else t * part, row_tile)
            share_out[d][t] = total_scr[pl.ds(start, piece), :].astype(bf16)


def assemble(m, piece, wide, narrow, index, *refs):
    total_out, out_out, small_out = refs[m:]
    for d in range(m):
        start = pl.multiple_of((index[1] ^ d) * piece, row_tile)
        total_out[pl.ds(start, piece), :] = refs[d][:, :wide].astype(f32)
        out_out[pl.ds(start, piece), :] = refs[d][:, wide : wide + narrow].astype(f32)
        small_out[pl.ds(start, piece), :] = refs[d][:, wide + narrow :].astype(f32)


def expert_forward(n, rows, *refs):
    row_refs = refs[:n]
    up, down, hidden_out, slope_out = refs[n : n + 4]
    keep_out, send_out = refs[n + 4 :]
    for p in range(n):
        before = dot(row_refs[p][...], up[0])
        square = before * before
        tanh_value = jnp.tanh(gelu_scale * before * (1.0 + gelu_cubic * square))
        half = 0.5 * (1.0 + tanh_value)
        hidden = (before * half).astype(bf16)
        slope = half + 0.5 * before * (1.0 - tanh_value * tanh_value) * gelu_scale * (
            1.0 + 3.0 * gelu_cubic * square
        )
        hidden_out[p * rows : (p + 1) * rows, :] = hidden
        slope_out[p * rows : (p + 1) * rows, :] = slope.astype(bf16)
        result = dot(hidden, down[0]).astype(bf16)
        target = send_out if p & 1 else keep_out
        at = (p >> 1) * rows
        target[at : at + rows, :] = result


def expert_backward(n, rows, *refs):
    grad_refs = refs[:n]
    up, down, slope, before_out = refs[n : n + 4]
    keep_out, send_out = refs[n + 4 :]
    for p in range(n):
        grad_hidden = dot_nt(grad_refs[p][...], down[0])
        grad_before = (grad_hidden * slope[p * rows : (p + 1) * rows, :].astype(f32)).astype(bf16)
        before_out[p * rows : (p + 1) * rows, :] = grad_before
        result = dot_nt(grad_before, up[0]).astype(bf16)
        target = send_out if p & 1 else keep_out
        at = (p >> 1) * rows
        target[at : at + rows, :] = result


def expert_weights(n, *refs):
    row_refs = refs[:n]
    grad_refs = refs[n : 2 * n]
    hidden, grad_before, up_out, down_out = refs[2 * n :]
    grads = jnp.concatenate([r[...] for r in grad_refs], axis=0)
    rows = jnp.concatenate([r[...] for r in row_refs], axis=0)
    down_out[0] = dot_tn(hidden[...], grads)
    up_out[0] = dot_tn(rows, grad_before[...])


def reduce_shard(keep, send, rows):
    came = swap(send, "shard", 1)
    forward = (keep[rows:].astype(f32) + came[rows:].astype(f32)).astype(bf16)
    own = keep[:rows].astype(f32) + came[:rows].astype(f32)
    return (own + swap(forward, "shard", 2).astype(f32)).astype(bf16)


def rms_factor(value):
    return lax.rsqrt(jnp.mean(value * value, axis=-1, keepdims=True) + norm_eps)


def rms_backward(value, factor, gain, upstream):
    scaled = upstream * gain
    grad_value = factor * scaled - value * factor * factor * factor * jnp.mean(
        scaled * value, axis=-1, keepdims=True
    )
    grad_gain = jnp.sum(upstream * value * factor, axis=0)
    return (grad_value, grad_gain)


def local(
    tokens,
    lengths,
    routes,
    attention_in,
    attention_out,
    position_bias,
    first_gain,
    second_gain,
    router,
    expert_in,
    expert_out,
    cotangent,
):
    n = lax.axis_size("shard")
    m = lax.axis_size("expert")
    s = lax.axis_index("shard")
    e = lax.axis_index("expert")
    index = jnp.stack([s, e]).astype(jnp.int32)
    rows, width = tokens.shape
    heads, buckets = position_bias.shape
    part = width // n
    seqs = lengths.shape[1]
    experts = router.shape[1]
    direct = m <= 8

    gains = jnp.pad(jnp.stack([first_gain, second_gain]), ((0, gain_rows - 2), (0, 0)))
    own_tokens = call(
        lambda *refs: prepare_tokens(n, rows, part, *refs),
        shape((rows + gain_rows, width)),
        (index, tokens, gains),
        "s",
    )
    token_blocks = gather_relative(own_tokens, "shard")
    own_weight, own_tokens = lax.optimization_barrier((attention_in, own_tokens))
    weight_blocks = exchange_relative(
        call(
            lambda *refs: prepare_weight(n, part, *refs),
            [shape((part, 3 * part))] * n,
            (index, own_weight),
            "s",
        ),
        "shard",
    )
    own_out, token_blocks, weight_blocks = lax.optimization_barrier(
        (attention_out, token_blocks, weight_blocks)
    )
    out_blocks = gather_relative(own_out, "shard")
    gain_one, gain_two = (
        sum(block[rows + i : rows + i + 1].astype(f32) for block in token_blocks) for i in range(2)
    )

    group = n * rows
    head_flops = 2 * heads * group * group * (part // heads)
    answers = call(
        lambda *refs: attention_forward(n, rows, width, heads, seqs, buckets, *refs),
        (
            shape((group, width)),
            shape((width, 3 * part)),
            shape((group, 3 * part)),
            shape((heads, group, group)),
            shape((group, width), f32),
            *[shape((rows, part))] * n,
        ),
        (index, lengths, position_bias.astype(f32), *token_blocks, *weight_blocks),
        "sss",
        [pltpu.VMEM((n, rows, width), bf16), pltpu.VMEM((n, rows, part), bf16)],
        flops=2 * group * width * 3 * part + 8 * head_flops,
        size=8 * 2**20,
    )
    normed, weight, projected, weights, unit = answers[:5]
    mixed_mine = answers[5:]
    mixed_blocks = exchange_relative(list(mixed_mine), "shard")

    inputs = tokens.astype(f32)
    hidden_one = inputs + sum(dot(mixed_blocks[p], out_blocks[p]) for p in range(n))
    factor_two = rms_factor(hidden_one)
    normed_two = hidden_one * factor_two * gain_two
    logits = jnp.dot(
        normed_two, router, precision=lax.Precision.HIGHEST, preferred_element_type=f32
    )
    shifted = jnp.exp(logits - jnp.max(logits, axis=-1, keepdims=True))
    probs = shifted / jnp.sum(shifted, axis=-1, keepdims=True)
    route = routes[:, 0]
    chosen = (route[:, None] == lax.iota(jnp.int32, experts)[None, :]).astype(f32)
    gate = jnp.sum(probs * chosen, axis=1)
    lower = (lax.iota(jnp.int32, rows)[:, None] >= lax.iota(jnp.int32, rows)[None, :]).astype(bf16)
    running = dot(lower, chosen.astype(bf16))
    slot = jnp.sum((running - 1.0) * chosen, axis=1).astype(jnp.int32)
    capacity = max(2, 9 * rows // (8 * experts) + 1)
    capacity = -(-capacity // slot_tile) * slot_tile
    places = experts * capacity
    half = places // 2
    if direct:
        holder = route ^ e
        target = (holder & 1) * half + (holder >> 1) * capacity + slot
    else:
        target = route * capacity + slot
    collect = (target[:, None] == lax.iota(jnp.int32, places)[None, :]).astype(bf16)
    upstream = cotangent.astype(f32)
    grad_result = (gate[:, None] * upstream).astype(bf16)

    def plain(value):
        return lax.all_to_all(
            value.reshape(experts, capacity, width), "expert", 0, 0, tiled=True
        ).reshape(places, width)

    def send(value):
        if not direct:
            return plain(value)
        came = swap(value[half:], "expert", 1).reshape(m // 2, capacity, width)
        own = value[:half].reshape(m // 2, capacity, width)
        both = jnp.concatenate([own, came], axis=1)
        blocks = [both[d] if d == 0 else swap(both[d], "expert", 2 * d) for d in range(m // 2)]
        return jnp.concatenate(blocks, axis=0)

    def give_back(value):
        if not direct:
            return plain(value)
        both = value.reshape(m // 2, 2 * capacity, width)
        blocks = [both[d] if d == 0 else swap(both[d], "expert", 2 * d) for d in range(m // 2)]
        own = [block[:capacity] for block in blocks]
        other = swap(jnp.concatenate([block[capacity:] for block in blocks]), "expert", 1)
        return jnp.concatenate([*own, other])

    arrived = send(dot_tn(collect, normed_two.astype(bf16)).astype(bf16))
    row_blocks = gather_relative(arrived, "shard")
    arrived_grad = send(dot_tn(collect, grad_result).astype(bf16))
    grad_blocks = gather_relative(arrived_grad, "shard")

    units = expert_in.shape[2]
    all_rows = n * places
    expert_flops = 2 * all_rows * width * units
    hidden, slope, keep, out = call(
        lambda *refs: expert_forward(n, places, *refs),
        (
            shape((all_rows, units)),
            shape((all_rows, units)),
            shape((all_rows // 2, width)),
            shape((all_rows // 2, width)),
        ),
        (*row_blocks, expert_in, expert_out),
        flops=2 * expert_flops,
        size=6 * 2**20,
    )
    returned = give_back(reduce_shard(keep, out, places))
    grad_before, keep_grad, out_grad = call(
        lambda *refs: expert_backward(n, places, *refs),
        (
            shape((all_rows, units)),
            shape((all_rows // 2, width)),
            shape((all_rows // 2, width)),
        ),
        (*grad_blocks, expert_in, expert_out, slope),
        flops=2 * expert_flops,
        size=6 * 2**20,
    )
    returned_grad = give_back(reduce_shard(keep_grad, out_grad, places))
    grad_up, grad_down = call(
        lambda *refs: expert_weights(n, *refs),
        (shape(expert_in.shape, f32), shape(expert_out.shape, f32)),
        (*row_blocks, *grad_blocks, hidden, grad_before),
        flops=2 * expert_flops,
        size=9 * 2**20,
    )

    expert_result = dot(collect, returned)
    layer_out = (hidden_one + gate[:, None] * expert_result).astype(bf16)
    grad_gate = jnp.sum(upstream * expert_result, axis=1)
    grad_logits = (grad_gate * gate)[:, None] * (chosen - probs)
    grad_router = lax.dot_general(
        normed_two,
        grad_logits,
        (((0,), (0,)), ((), ())),
        precision=lax.Precision.HIGHEST,
        preferred_element_type=f32,
    )
    grad_normed_two = dot(collect, returned_grad) + lax.dot_general(
        grad_logits,
        router,
        (((1,), (1,)), ((), ())),
        precision=lax.Precision.HIGHEST,
        preferred_element_type=f32,
    )
    grad_middle, grad_gain_two = rms_backward(hidden_one, factor_two, gain_two, grad_normed_two)
    grad_hidden = upstream + grad_middle
    grad_branch = grad_hidden.astype(bf16)
    grad_mixed_blocks = exchange_relative(
        [dot_nt(grad_branch, out_blocks[p]).astype(bf16) for p in range(n)], "shard"
    )
    own_branch, grad_mixed_blocks = lax.optimization_barrier((grad_branch, grad_mixed_blocks))
    branch_blocks = gather_relative(own_branch, "shard")
    grad_weight_out = sum(dot_tn(mixed_mine[p], branch_blocks[p]) for p in range(n)).astype(bf16)
    total_out = lax.psum_scatter(grad_weight_out, "expert", scatter_dimension=0, tiled=True)

    holders = m if direct else 1
    wide = 3 * part
    extra = -wide % 128
    while direct and extra < 2 + experts + buckets:
        extra = extra + 128
    small = jnp.concatenate([grad_gain_two[:, None], grad_router], axis=1)
    answers = call(
        lambda *refs: attention_backward(n, holders, rows, width, heads, buckets, *refs),
        (
            *[shape((n, part // holders, wide + extra))] * holders,
            *[shape((rows, width))] * n,
            shape((row_tile, width), f32),
            shape((row_tile, 128), f32),
        ),
        (
            index,
            projected,
            normed,
            weight,
            weights,
            unit,
            jnp.pad(small, ((0, 0), (1, extra - experts - 2))) if direct else small,
            *grad_mixed_blocks,
        ),
        "s",
        [
            pltpu.VMEM((n, rows, part), bf16),
            pltpu.VMEM((group, group), bf16),
            pltpu.VMEM((group, wide), bf16),
            pltpu.VMEM((width, wide + extra), f32),
            pltpu.VMEM((n, rows, width), bf16),
        ],
        flops=8 * head_flops,
        size=8 * 2**20,
    )
    shares = list(answers[:holders])
    normed_grads = answers[holders : holders + n]
    gain_row, table = answers[holders + n :]

    piece = part // m
    if direct:
        came = exchange_relative(shares, "expert")
    else:
        came = lax.all_to_all(
            shares[0].reshape(n, m, piece, wide + extra).swapaxes(0, 1), "expert", 0, 0, tiled=True
        )
    summed = sum(x.astype(f32) for x in came)
    table_total = summed[0, :heads, wide + extra - buckets :]
    summed = summed.astype(bf16)
    mine = exchange_relative(
        [lax.dynamic_index_in_dim(summed, s ^ p, 0, keepdims=False) for p in range(n)], "shard"
    )
    small_mine = sum(block[:, wide:].astype(f32) for block in mine).astype(bf16)
    mine = jnp.stack(mine)[lax.iota(jnp.int32, n) ^ s][:, :, :wide]
    mine = mine.reshape(n, piece, 3, part).transpose(1, 2, 0, 3).reshape(piece, 3 * width)
    if direct:
        mine = jnp.concatenate([mine, total_out, small_mine], axis=1)
        mine = jnp.pad(mine, ((0, 0), (0, -extra % 128)))
        blocks = gather_relative(mine, "expert")
        grad_attention_in, grad_attention_out, small_total = call(
            lambda *refs: assemble(m, piece, 3 * width, width, *refs),
            (
                shape((part, 3 * width), f32),
                shape((part, width), f32),
                shape((part, mine.shape[1] - 4 * width), f32),
            ),
            (index, *blocks),
            "s",
        )
    else:
        grad_attention_in = lax.all_gather(mine, "expert", axis=0, tiled=True).astype(f32)
        grad_attention_out = lax.all_gather(total_out, "expert", axis=0, tiled=True).astype(f32)
        small = jnp.concatenate([gain_row[0][:, None], small], axis=1)
        small_total = lax.psum_scatter(small, "shard", scatter_dimension=0, tiled=True)
        small_total, table_total = lax.psum((small_total, table[:heads, :buckets]), "expert")

    grad_normed = sum(x.astype(f32) for x in exchange_relative(list(normed_grads), "shard"))
    grad_input_norm, _ = rms_backward(inputs, rms_factor(inputs), gain_one, grad_normed)
    grad_tokens = (grad_hidden + grad_input_norm).astype(bf16)
    return (
        layer_out,
        grad_tokens,
        grad_attention_in,
        grad_attention_out,
        table_total,
        small_total[:, 0],
        small_total[:, 1],
        small_total[:, 2 : 2 + experts],
        grad_up,
        grad_down,
    )


def solution(mesh):
    in_specs = (
        P(("expert", "shard"), None),
        P("expert", None),
        P(("expert", "shard"), None),
        P("shard", None),
        P("shard", None),
        P("shard", None),
        P("shard"),
        P("shard"),
        P(),
        P("expert", None, "shard"),
        P("expert", "shard", None),
        P(("expert", "shard"), None),
    )
    out_specs = (
        P(("expert", "shard"), None),
        P(("expert", "shard"), None),
        P("shard", None),
        P("shard", None),
        P("shard", None),
        P("shard"),
        P("shard"),
        P("shard", None),
        P("expert", None, "shard"),
        P("expert", "shard", None),
    )
    return jax.shard_map(local, mesh=mesh, in_specs=in_specs, out_specs=out_specs, check_vma=False)
```

```python
import jax
import jax.numpy as jnp
from jax import lax
from jax.experimental import pallas as pl
from jax.experimental.pallas import tpu as pltpu
from jax.sharding import PartitionSpec as P

norm_eps = 1e-06
gelu_scale = 0.7978845608028654
gelu_cubic = 0.044715
big_negative = -1e30
near_steps = 8
far_steps = (12, 16, 23, 32, 46, 64, 91)
bf16 = jnp.bfloat16
f32 = jnp.float32
row_tile = 8
pair = 1
slot_tile = 4


def bucket_index(offset):
    distance = jnp.abs(offset)
    far_level = jnp.full_like(distance, near_steps)
    for step_edge in far_steps:
        far_level = far_level + (distance >= step_edge).astype(jnp.int32)
    near = jnp.where(distance < near_steps, distance, far_level)
    return near + 16 * (offset > 0).astype(jnp.int32)


def dot(left, right):
    return jnp.dot(left, right, preferred_element_type=f32)


def dot_nt(left, right):
    return lax.dot_general(left, right, (((1,), (1,)), ((), ())), preferred_element_type=f32)


def dot_tn(left, right):
    return lax.dot_general(left, right, (((0,), (0,)), ((), ())), preferred_element_type=f32)


def swap(value, axis, bit):
    size = lax.axis_size(axis)
    return lax.ppermute(value, axis, [(i, i ^ bit) for i in range(size)])


def gather_relative(value, axis):
    blocks = [value]
    bit = lax.axis_size(axis) // 2
    parts = {0: value}
    while bit:
        for p in list(parts):
            parts[p ^ bit] = swap(parts[p], axis, bit)
        bit //= 2
    return [parts[p] for p in range(lax.axis_size(axis))]


def exchange_relative(blocks, axis):
    return [blocks[0]] + [swap(block, axis, p) for p, block in enumerate(blocks) if p]


def call(kernel, out_shape, operands, spaces="", scratch=(), work=0):
    vmem = pl.BlockSpec(memory_space=pltpu.VMEM)
    smem = pl.BlockSpec(memory_space=pltpu.SMEM)
    in_specs = [smem if spaces[i : i + 1] == "s" else vmem for i in range(len(operands))]
    return pl.pallas_call(
        kernel,
        out_shape=out_shape,
        in_specs=in_specs,
        out_specs=jax.tree.map(lambda _: vmem, out_shape),
        scratch_shapes=list(scratch),
        compiler_params=pltpu.CompilerParams(vmem_limit_bytes=56 * 2**20),
        cost_estimate=pl.CostEstimate(flops=work, bytes_accessed=0, transcendentals=0),
    )(*operands)


def shape(dims, dtype=bf16):
    return jax.ShapeDtypeStruct(tuple(dims), dtype)


def diagonal(size):
    return lax.broadcasted_iota(jnp.int32, (size, size), 0) == lax.broadcasted_iota(
        jnp.int32, (size, size), 1
    )


def to_column(row, size):
    return jnp.sum(jnp.where(diagonal(size), row, 0.0), axis=1, keepdims=True)


def to_row(column, size):
    return jnp.sum(jnp.where(diagonal(size), column, 0.0), axis=0, keepdims=True)


def prepare_weight(n, part, weight, gain_one, gain_two, *outs):
    wide = 3 * part
    s = lax.axis_index("shard")
    extra = outs[0].shape[1] - wide
    one, two = (to_column(gain[...].astype(f32), part) for gain in (gain_one, gain_two))
    lane = lax.broadcasted_iota(jnp.int32, (part, extra), 1)
    beside = jnp.where(lane == 0, one, jnp.where(lane == 1, two, 0.0)).astype(bf16)
    for p in range(n):
        outs[p][:, wide:] = beside
    for k in range(n):

        @pl.when(s == k)
        def _():
            for p in range(n):
                for kind in range(3):
                    at = (kind * n + (k ^ p)) * part
                    outs[p][:, kind * part : (kind + 1) * part] = weight[:, at : at + part]


def offsets(rows):
    return lax.broadcasted_iota(jnp.int32, (rows, rows), 1) - lax.broadcasted_iota(
        jnp.int32, (rows, rows), 0
    )


def near_buckets(diff, buckets):
    if diff == 0:
        return range(buckets)
    return range(buckets // 2, buckets) if diff > 0 else range(buckets // 2)


def attention_forward(n, rows, width, heads, seqs, buckets, *refs):
    lengths, table = refs[:2]
    token_refs = refs[2 : 2 + n]
    weight_refs = refs[2 + n : 2 + 2 * n]
    tokens_out, weight_out, projected_out, weights_out, gains_out, mixed_all = refs[
        2 + 2 * n : 8 + 2 * n
    ]
    mixed_out = refs[8 + 2 * n : 8 + 3 * n]
    (normed_scr,) = refs[8 + 3 * n :]
    s = lax.axis_index("shard")
    part = width // n
    wide = 3 * part
    head_dim = part // heads
    for p in range(n):
        tokens_out[s ^ p] = token_refs[p][...]
        weight_out[pl.ds(pl.multiple_of((s ^ p) * part, part & -part), part), :] = weight_refs[p][...]
    size = 128
    for c in range(width // size):
        beside = weight_out[c * size : (c + 1) * size, wide:].astype(f32)
        for i in range(2):
            gains_out[i : i + 1, c * size : (c + 1) * size] = to_row(beside[:, i : i + 1], size)
    gain = gains_out[0:1, :]
    for j in range(n):
        value = tokens_out[j].astype(f32)
        factor = lax.rsqrt(jnp.mean(value * value, axis=-1, keepdims=True) + norm_eps)
        normed_scr[j * rows : (j + 1) * rows, :] = (value * factor * gain).astype(bf16)
    projected_out[...] = dot(normed_scr[...], weight_out[:, :wide]).astype(bf16)
    total_rows = n * rows
    key_place = lax.broadcasted_iota(jnp.int32, (1, total_rows), 1)
    key_segment = jnp.zeros((1, total_rows), jnp.int32)
    end = jnp.int32(0)
    ends = []
    for j in range(seqs):
        end = end + lengths[0, j]
        ends.append(end)
        key_segment = key_segment + (key_place >= end).astype(jnp.int32)
    base = offsets(rows)
    steps = {diff: bucket_index(base + diff * rows) for diff in (-1, 0, 1)}
    for h in range(heads):
        query = projected_out[:, h * head_dim : (h + 1) * head_dim]
        key = projected_out[:, part + h * head_dim : part + (h + 1) * head_dim]
        value = projected_out[:, 2 * part + h * head_dim : 2 * part + (h + 1) * head_dim]
        bias = {}
        for diff in (-1, 0, 1):
            block = jnp.zeros((rows, rows), f32)
            for b in near_buckets(diff, buckets):
                block = jnp.where(steps[diff] == b, table[h, b], block)
            bias[diff] = block
        low_side = jnp.full((rows, rows), table[h, buckets // 2 - 1], f32)
        high_side = jnp.full((rows, rows), table[h, buckets - 1], f32)
        for i in range(n):
            scores = dot_nt(query[i * rows : (i + 1) * rows, :], key)
            side = [
                bias[j - i] if abs(j - i) <= 1 else (high_side if j > i else low_side)
                for j in range(n)
            ]
            scores = scores + jnp.concatenate(side, axis=1)
            query_place = i * rows + lax.broadcasted_iota(jnp.int32, (rows, 1), 0)
            query_segment = jnp.zeros((rows, 1), jnp.int32)
            for j in range(seqs):
                query_segment = query_segment + (query_place >= ends[j]).astype(jnp.int32)
            scores = jnp.where(query_segment == key_segment, scores, big_negative)
            top = jnp.max(scores, axis=-1, keepdims=True)
            raised = jnp.exp(scores - top)
            total = jnp.sum(raised, axis=-1, keepdims=True)
            weights = (raised * (1.0 / total)).astype(bf16)
            weights_out[h, i * rows : (i + 1) * rows, :] = weights
            mixed_all[i, :, h * head_dim : (h + 1) * head_dim] = dot(weights, value).astype(bf16)
    for p in range(n):
        mixed_out[p][...] = mixed_all[s ^ p]


def attention_backward(n, m, rows, width, heads, buckets, experts, *refs):
    projected, tokens, gains, weight, weights, mixed, weight_out, gain_two, router = refs[:9]
    branch_refs = refs[9 : 9 + n]
    at = 9 + n
    shares = 4 if m > 1 else 2
    share_out = refs[at : at + shares]
    normed_grad_out = refs[at + shares : at + shares + n]
    gain_out, table_out = refs[at + shares + n : at + shares + n + 2]
    branch_scr, scores_scr, projected_scr, total_scr, out_scr, normed_scr, send_scr = refs[
        at + shares + n + 2 :
    ]
    s = lax.axis_index("shard")
    e = lax.axis_index("expert")
    part = width // n
    wide = 3 * part
    group = n * rows
    head_dim = part // heads
    for p in range(n):
        branch_scr[s ^ p] = branch_refs[p][...]
    branch = branch_scr[...].reshape(group, width)
    grad_mixed = dot_nt(branch, weight_out[...]).astype(bf16)
    out_scr[...] = dot_tn(mixed[...].reshape(group, part), branch)
    base = offsets(rows)
    steps = {diff: bucket_index(base + diff * rows) for diff in (-1, 0, 1)}
    lane = lax.broadcasted_iota(jnp.int32, (row_tile, 128), 1)
    line = lax.broadcasted_iota(jnp.int32, (row_tile, 128), 0)
    table_total = jnp.zeros((row_tile, 128), f32)
    per_line = buckets // row_tile
    for h in range(heads):
        query = projected[:, h * head_dim : (h + 1) * head_dim]
        key = projected[:, part + h * head_dim : part + (h + 1) * head_dim]
        value = projected[:, 2 * part + h * head_dim : 2 * part + (h + 1) * head_dim]
        near = {diff: jnp.zeros((rows, rows), f32) for diff in (-1, 0, 1)}
        low_side = jnp.zeros((1, rows), f32)
        high_side = jnp.zeros((1, rows), f32)
        upstream = grad_mixed[:, h * head_dim : (h + 1) * head_dim]
        for i in range(n):
            weights_i = weights[h, i * rows : (i + 1) * rows, :].astype(f32)
            grad_weights = dot_nt(upstream[i * rows : (i + 1) * rows, :], value)
            inner = jnp.sum(weights_i * grad_weights, axis=-1, keepdims=True)
            grad_scores = weights_i * (grad_weights - inner)
            scores_scr[i * rows : (i + 1) * rows, :] = grad_scores.astype(bf16)
            for j in range(n):
                block = grad_scores[:, j * rows : (j + 1) * rows]
                if abs(j - i) <= 1:
                    near[j - i] = near[j - i] + block
                elif j > i:
                    high_side = high_side + jnp.sum(block, axis=0, keepdims=True)
                else:
                    low_side = low_side + jnp.sum(block, axis=0, keepdims=True)
        for b in range(buckets):
            amount = jnp.zeros((1, rows), f32)
            for diff in (-1, 0, 1):
                if b in near_buckets(diff, buckets):
                    amount = amount + jnp.sum(
                        jnp.where(steps[diff] == b, near[diff], 0.0), axis=0, keepdims=True
                    )
            if b == buckets - 1:
                amount = amount + high_side
            if b == buckets // 2 - 1:
                amount = amount + low_side
            amount = jnp.sum(amount, axis=1, keepdims=True)
            spot = (line == b // per_line) & (lane == h * per_line + b % per_line)
            table_total = jnp.where(spot, amount, table_total)
        grad_scores_all = scores_scr[...]
        projected_scr[:, h * head_dim : (h + 1) * head_dim] = dot(grad_scores_all, key).astype(bf16)
        projected_scr[:, part + h * head_dim : part + (h + 1) * head_dim] = (
            dot_tn(query, grad_scores_all).T.astype(bf16)
        )
        projected_scr[:, 2 * part + h * head_dim : 2 * part + (h + 1) * head_dim] = (
            dot_tn(upstream, weights[h]).T.astype(bf16)
        )
    table_out[...] = table_total
    grad_projected = projected_scr[...]
    normed_grad = dot_nt(grad_projected, weight[:, :wide])
    send_scr[...] = normed_grad.astype(bf16).reshape(n, rows, width)
    for p in range(n):
        normed_grad_out[p][...] = send_scr[s ^ p]
    gain = gains[0:1, :]
    grad_gain = jnp.zeros((1, width), f32)
    for j in range(n):
        value = tokens[j].astype(f32)
        unit = value * lax.rsqrt(jnp.mean(value * value, axis=-1, keepdims=True) + norm_eps)
        normed_scr[j * rows : (j + 1) * rows, :] = (unit * gain).astype(bf16)
        grad_gain = grad_gain + jnp.sum(
            normed_grad[j * rows : (j + 1) * rows, :] * unit, axis=0, keepdims=True
        )
    gain_out[...] = jnp.broadcast_to(grad_gain, gain_out.shape)
    total_scr[:, :wide] = dot_tn(normed_scr[...], grad_projected)
    full = total_scr.shape[1]
    if m == 1:
        for t in range(n):
            share_out[0][t] = total_scr[t * part : (t + 1) * part, :wide].astype(bf16)
        share_out[1][...] = out_scr[...].astype(bf16)
        return
    piece = part // m
    total_scr[:, wide:] = jnp.zeros((width, full - wide), f32)
    size = 128
    for c in range(width // size):
        here = slice(c * size, (c + 1) * size)
        total_scr[here, wide : wide + 1] = to_column(grad_gain[:, here], size)
        total_scr[here, wide + 1 : wide + 2] = to_column(gain_two[0:1, here], size)
    total_scr[:, wide + 2 : wide + 2 + experts] = router[...]
    at = wide + 2 + experts
    rest = (width - full) // n
    for t in range(n):
        total_scr[t * part : (t + 1) * part, at : at + rest] = out_scr[
            :, full + t * rest : full + (t + 1) * rest
        ]
    at = at + rest
    for d in range(m):
        total_scr[d * piece : d * piece + row_tile, at : at + heads * per_line] = table_total[
            :, : heads * per_line
        ]
    for d in range(m):
        target = share_out[(d & 1) + 2 * (d < m // 2)]
        place = (d >> 1) % (m // 4)
        start = (e ^ d) * piece
        for t in range(n):
            rows_at = pl.multiple_of(t * part + start, row_tile)
            target[place, t] = total_scr[pl.ds(rows_at, piece), :].astype(bf16)
        rows_at = pl.multiple_of(start, row_tile)
        target[place, n] = out_scr[pl.ds(rows_at, piece), :full].astype(bf16)


def assemble(n, m, part, piece, experts, *refs):
    total_out, out_out, small_out = refs[m:]
    s = lax.axis_index("shard")
    e = lax.axis_index("expert")
    wide = 3 * part
    full = refs[0].shape[2]
    at = wide + 2 + experts
    rest = (n * part - full) // n
    for d in range(m):
        start = pl.multiple_of((e ^ d) * piece, row_tile)
        own = pl.ds(start, piece)
        small = jnp.zeros((piece, full - wide), f32)
        for p in range(n):
            small = small + refs[d][p, :, wide:].astype(f32)
            out_out[own, full + p * rest : full + (p + 1) * rest] = refs[d][p, :, at : at + rest].astype(
                f32
            )
        out_out[own, :full] = refs[d][n].astype(f32)
        small_out[own, :] = small
    for k in range(n):

        @pl.when(s == k)
        def _():
            for d in range(m):
                own = pl.ds(pl.multiple_of((e ^ d) * piece, row_tile), piece)
                for p in range(n):
                    for kind in range(3):
                        to = (kind * n + (k ^ p)) * part
                        total_out[own, to : to + part] = refs[d][
                            p, :, kind * part : (kind + 1) * part
                        ].astype(f32)


def expert_forward(rows, own, came, up_own, up_pair, down_own, down_pair, *outs):
    hidden_out, slope_out, keep_out, send_out = outs
    for i, source in enumerate((own, came)):
        result = 0.0
        for k, (up, down) in enumerate(((up_own, down_own), (up_pair, down_pair))):
            before = dot(source[...], up[0])
            square = before * before
            tanh_value = jnp.tanh(gelu_scale * before * (1.0 + gelu_cubic * square))
            half = 0.5 * (1.0 + tanh_value)
            hidden = (before * half).astype(bf16)
            slope = half + 0.5 * before * (1.0 - tanh_value * tanh_value) * gelu_scale * (
                1.0 + 3.0 * gelu_cubic * square
            )
            hidden_out[k, i * rows : (i + 1) * rows, :] = hidden
            slope_out[k, i * rows : (i + 1) * rows, :] = slope.astype(bf16)
            result = result + dot(hidden, down[0])
        if i:
            send_out[...] = result.astype(bf16)
        else:
            keep_out[...] = result


def expert_backward(rows, own, came, up_own, up_pair, down_own, down_pair, slope, *outs):
    before_out, keep_out, send_out = outs
    grads = jnp.concatenate([own[...], came[...]], axis=0)
    result = 0.0
    for k, (up, down) in enumerate(((up_own, down_own), (up_pair, down_pair))):
        grad_before = (dot_nt(grads, down[0]) * slope[k].astype(f32)).astype(bf16)
        before_out[k] = grad_before
        result = result + dot_nt(grad_before, up[0])
    keep_out[...] = result[:rows]
    send_out[...] = result[rows:].astype(bf16)


def expert_weights(own, came, own_grad, came_grad, hidden, grad_before, *outs):
    up_out, down_out, up_send, down_send = outs
    grads = jnp.concatenate([own_grad[...], came_grad[...]], axis=0)
    rows = jnp.concatenate([own[...], came[...]], axis=0)
    up_send[0] = dot_tn(rows, grad_before[1]).astype(bf16)
    down_send[0] = dot_tn(hidden[1], grads).astype(bf16)
    up_out[0] = dot_tn(rows, grad_before[0])
    down_out[0] = dot_tn(hidden[0], grads)


def rms_factor(value):
    return lax.rsqrt(jnp.mean(value * value, axis=-1, keepdims=True) + norm_eps)


def rms_backward(value, factor, gain, upstream):
    scaled = upstream * gain
    grad_value = factor * scaled - value * factor * factor * factor * jnp.mean(
        scaled * value, axis=-1, keepdims=True
    )
    grad_gain = jnp.sum(upstream * value * factor, axis=0)
    return (grad_value, grad_gain)


def local(
    tokens,
    lengths,
    routes,
    attention_in,
    attention_out,
    position_bias,
    first_gain,
    second_gain,
    router,
    expert_in,
    expert_out,
    cotangent,
):
    n = lax.axis_size("shard")
    m = lax.axis_size("expert")
    s = lax.axis_index("shard")
    e = lax.axis_index("expert")
    rows, width = tokens.shape
    heads, buckets = position_bias.shape
    part = width // n
    wide = 3 * part
    group = n * rows
    seqs = lengths.shape[1]
    experts = router.shape[1]
    direct = m == 8
    full = wide + -wide % 128
    micro = 10**9

    token_blocks = gather_relative(tokens, "shard")
    weight_blocks = exchange_relative(
        call(
            lambda *refs: prepare_weight(n, part, *refs),
            [shape((part, full))] * n,
            (attention_in, first_gain.reshape(1, part), second_gain.reshape(1, part)),
        ),
        "shard",
    )
    own_out, own_up, own_down, token_blocks, weight_blocks = lax.optimization_barrier(
        (attention_out, expert_in, expert_out, token_blocks, weight_blocks)
    )
    out_blocks = gather_relative(own_out, "shard")
    pair_up = swap(own_up, "shard", pair)
    pair_down = swap(own_down, "shard", pair)

    answers = call(
        lambda *refs: attention_forward(n, rows, width, heads, seqs, buckets, *refs),
        (
            shape((n, rows, width)),
            shape((width, full)),
            shape((group, wide)),
            shape((heads, group, group)),
            shape((row_tile, width), f32),
            shape((n, rows, part)),
            *[shape((rows, part))] * n,
        ),
        (lengths, position_bias.astype(f32), *token_blocks, *weight_blocks),
        "ss",
        [pltpu.VMEM((group, width), bf16)],
        work=10 * micro,
    )
    tokens_all, weight, projected, weights, gains, mixed = answers[:6]
    mixed_blocks = exchange_relative(list(answers[6:]), "shard")
    gain_one, gain_two = gains[0:1], gains[1:2]

    inputs = tokens.astype(f32)
    hidden_one = inputs + sum(dot(mixed_blocks[p], out_blocks[p]) for p in range(n))
    factor_two = rms_factor(hidden_one)
    normed_two = hidden_one * factor_two * gain_two
    logits = jnp.dot(
        normed_two, router, precision=lax.Precision.HIGHEST, preferred_element_type=f32
    )
    shifted = jnp.exp(logits - jnp.max(logits, axis=-1, keepdims=True))
    probs = shifted / jnp.sum(shifted, axis=-1, keepdims=True)
    route = routes[:, 0]
    chosen = (route[:, None] == lax.iota(jnp.int32, experts)[None, :]).astype(f32)
    gate = jnp.sum(probs * chosen, axis=1)
    lower = (lax.iota(jnp.int32, rows)[:, None] >= lax.iota(jnp.int32, rows)[None, :]).astype(bf16)
    running = dot(lower, chosen.astype(bf16))
    slot = jnp.sum((running - 1.0) * chosen, axis=1).astype(jnp.int32)
    capacity = max(2, 9 * rows // (8 * experts) + 1)
    capacity = -(-capacity // slot_tile) * slot_tile
    places = experts * capacity
    half = places // 2
    if direct:
        holder = route ^ e
        target = (holder & 1) * half + (holder >> 1) * capacity + slot
    else:
        target = route * capacity + slot
    collect = (target[:, None] == lax.iota(jnp.int32, places)[None, :]).astype(bf16)
    upstream = cotangent.astype(f32)
    grad_result = (gate[:, None] * upstream).astype(bf16)

    def plain(value):
        return lax.all_to_all(
            value.reshape(experts, capacity, width), "expert", 0, 0, tiled=True
        ).reshape(places, width)

    def send(value):
        if not direct:
            return plain(dot_tn(collect, value).astype(bf16))
        came = swap(dot_tn(collect[:, half:], value).astype(bf16), "expert", 1)
        own = dot_tn(collect[:, :half], value).astype(bf16).reshape(m // 2, capacity, width)
        both = jnp.concatenate([own, came.reshape(m // 2, capacity, width)], axis=1)
        blocks = [both[d] if d == 0 else swap(both[d], "expert", 2 * d) for d in range(m // 2)]
        return jnp.concatenate(blocks, axis=0)

    def give_back(value):
        if not direct:
            return dot(collect, plain(value))
        both = value.reshape(m // 2, 2 * capacity, width)
        blocks = [both[d] if d == 0 else swap(both[d], "expert", 2 * d) for d in range(m // 2)]
        own = jnp.concatenate([block[:capacity] for block in blocks])
        other = swap(jnp.concatenate([block[capacity:] for block in blocks]), "expert", 1)
        return dot(collect[:, :half], own) + dot(collect[:, half:], other)

    def reduce_shard(keep, out):
        return (keep + swap(out, "shard", 2 * pair).astype(f32)).astype(bf16)

    arrived = send(normed_two.astype(bf16))
    row_blocks = (arrived, swap(arrived, "shard", 2 * pair))
    arrived_grad = send(grad_result)
    grad_blocks = (arrived_grad, swap(arrived_grad, "shard", 2 * pair))

    units = expert_in.shape[2]
    both_rows = 2 * places
    expert_weight = (own_up, pair_up, own_down, pair_down)
    hidden, slope, keep, out = call(
        lambda *refs: expert_forward(places, *refs),
        (
            shape((2, both_rows, units)),
            shape((2, both_rows, units)),
            shape((places, width), f32),
            shape((places, width)),
        ),
        (*row_blocks, *expert_weight),
        work=6 * micro,
    )
    expert_result = give_back(reduce_shard(keep, out))
    grad_before, keep_grad, out_grad = call(
        lambda *refs: expert_backward(places, *refs),
        (
            shape((2, both_rows, units)),
            shape((places, width), f32),
            shape((places, width)),
        ),
        (*grad_blocks, *expert_weight, slope),
        work=6 * micro,
    )
    grad_sent = give_back(reduce_shard(keep_grad, out_grad))
    grad_up, grad_down, up_send, down_send = call(
        expert_weights,
        (
            shape(expert_in.shape, f32),
            shape(expert_out.shape, f32),
            shape(expert_in.shape),
            shape(expert_out.shape),
        ),
        (*row_blocks, *grad_blocks, hidden, grad_before),
        work=6 * micro,
    )
    grad_up = grad_up + swap(up_send, "shard", pair).astype(f32)
    grad_down = grad_down + swap(down_send, "shard", pair).astype(f32)

    layer_out = (hidden_one + gate[:, None] * expert_result).astype(bf16)
    grad_gate = jnp.sum(upstream * expert_result, axis=1)
    grad_logits = (grad_gate * gate)[:, None] * (chosen - probs)
    grad_router = lax.dot_general(
        normed_two,
        grad_logits,
        (((0,), (0,)), ((), ())),
        precision=lax.Precision.HIGHEST,
        preferred_element_type=f32,
    )
    grad_normed_two = grad_sent + lax.dot_general(
        grad_logits,
        router,
        (((1,), (1,)), ((), ())),
        precision=lax.Precision.HIGHEST,
        preferred_element_type=f32,
    )
    grad_middle, grad_gain_two = rms_backward(hidden_one, factor_two, gain_two, grad_normed_two)
    grad_hidden = upstream + grad_middle
    branch_blocks = gather_relative(grad_hidden.astype(bf16), "shard")

    holders = m if direct else 1
    piece = part // m
    if direct:
        share_shapes = [shape((m // 4, n + 1, piece, full))] * 4
    else:
        share_shapes = [shape((n, part, wide)), shape((part, width))]
    answers = call(
        lambda *refs: attention_backward(n, holders, rows, width, heads, buckets, experts, *refs),
        (
            *share_shapes,
            *[shape((rows, width))] * n,
            shape((row_tile, width), f32),
            shape((row_tile, 128), f32),
        ),
        (
            projected,
            tokens_all,
            gains,
            weight,
            weights,
            mixed,
            own_out,
            grad_gain_two[None],
            grad_router,
            *branch_blocks,
        ),
        "",
        [
            pltpu.VMEM((n, rows, width), bf16),
            pltpu.VMEM((group, group), bf16),
            pltpu.VMEM((group, wide), bf16),
            pltpu.VMEM((width, full), f32),
            pltpu.VMEM((part, width), f32),
            pltpu.VMEM((group, width), bf16),
            pltpu.VMEM((n, rows, width), bf16),
        ],
        work=8 * micro,
    )
    shares = answers[: len(share_shapes)]
    normed_grads = answers[len(share_shapes) : len(share_shapes) + n]
    gain_row, table = answers[len(share_shapes) + n :]

    per_line = buckets // row_tile

    def biases(block):
        return block.reshape(row_tile, heads, per_line).swapaxes(0, 1).reshape(heads, buckets)

    grad_normed = sum(x.astype(f32) for x in exchange_relative(list(normed_grads), "shard"))
    grad_input_norm, _ = rms_backward(inputs, rms_factor(inputs), gain_one, grad_normed)
    grad_tokens = (grad_hidden + grad_input_norm).astype(bf16)
    if direct:
        far_keep, far_send, near_keep, near_send = shares
        far = far_keep.astype(f32) + swap(far_send, "expert", 1).astype(f32)
        near = near_keep.astype(f32) + swap(near_send, "expert", 1).astype(f32)
        came = [swap(far[d].astype(bf16), "expert", m // 2 + 2 * d) for d in range(m // 4)]
        came += [swap(near[d].astype(bf16), "expert", 2 * d) for d in range(1, m // 4)]
        summed = near[0] + sum(x.astype(f32) for x in came)
        at = wide + 2 + experts
        rest = (width - full) // n
        table_total = biases(
            summed[0, :row_tile, at + rest : at + rest + heads * per_line]
        )
        low = summed.astype(bf16)
        mine = exchange_relative(
            [lax.dynamic_index_in_dim(low, s ^ p, 0, keepdims=False) for p in range(n)], "shard"
        )
        lane = lax.iota(jnp.int32, full)[None, :]
        own_lane = (lane >= at) & (lane < at + rest)
        mine = jnp.stack(
            [jnp.where(own_lane, low[p], mine[p]) for p in range(n)] + [low[n]], axis=0
        )
        blocks = gather_relative(mine, "expert")
        grad_attention_in, grad_attention_out, small_total = call(
            lambda *refs: assemble(n, m, part, piece, experts, *refs),
            (shape((part, 3 * width), f32), shape((part, width), f32), shape((part, full - wide), f32)),
            (*blocks,),
        )
    else:
        came = lax.all_to_all(
            shares[0].reshape(n, m, piece, wide).swapaxes(0, 1), "expert", 0, 0, tiled=True
        )
        summed = sum(x.astype(f32) for x in came).astype(bf16)
        mine = lax.all_to_all(summed, "shard", 0, 0, tiled=True)
        mine = mine.reshape(n, piece, 3, part).transpose(1, 2, 0, 3).reshape(piece, 3 * width)
        came = lax.all_to_all(shares[1].reshape(m, piece, width), "expert", 0, 0, tiled=True)
        out_mine = sum(x.astype(f32) for x in came).astype(bf16)
        grad_attention_in = lax.all_gather(mine, "expert", axis=0, tiled=True).astype(f32)
        grad_attention_out = lax.all_gather(out_mine, "expert", axis=0, tiled=True).astype(f32)
        small = jnp.concatenate([gain_row[0][:, None], grad_gain_two[:, None], grad_router], axis=1)
        small_total = lax.psum_scatter(small, "shard", scatter_dimension=0, tiled=True)
        small_total, table_total = lax.psum(
            (small_total, biases(table[:, : heads * per_line])), "expert"
        )
    return (
        layer_out,
        grad_tokens,
        grad_attention_in,
        grad_attention_out,
        table_total,
        small_total[:, 0],
        small_total[:, 1],
        small_total[:, 2 : 2 + experts],
        grad_up,
        grad_down,
    )


def solution(mesh):
    in_specs = (
        P(("expert", "shard"), None),
        P("expert", None),
        P(("expert", "shard"), None),
        P("shard", None),
        P("shard", None),
        P("shard", None),
        P("shard"),
        P("shard"),
        P(),
        P("expert", None, "shard"),
        P("expert", "shard", None),
        P(("expert", "shard"), None),
    )
    out_specs = (
        P(("expert", "shard"), None),
        P(("expert", "shard"), None),
        P("shard", None),
        P("shard", None),
        P("shard", None),
        P("shard"),
        P("shard"),
        P("shard", None),
        P("expert", None, "shard"),
        P("expert", "shard", None),
    )
    return jax.shard_map(local, mesh=mesh, in_specs=in_specs, out_specs=out_specs, check_vma=False)
```

```python
import jax
import jax.numpy as jnp
from jax import lax
from jax.experimental import pallas as pl
from jax.experimental.pallas import tpu as pltpu
from jax.sharding import PartitionSpec as P

norm_eps = 1e-06
gelu_scale = 0.7978845608028654
gelu_cubic = 0.044715
big_negative = -1e30
near_steps = 8
far_steps = (12, 16, 23, 32, 46, 64, 91)
bf16 = jnp.bfloat16
f32 = jnp.float32
row_tile = 8
pair = 1
slot_tile = 4


def bucket_index(offset):
    distance = jnp.abs(offset)
    far_level = jnp.full_like(distance, near_steps)
    for step_edge in far_steps:
        far_level = far_level + (distance >= step_edge).astype(jnp.int32)
    near = jnp.where(distance < near_steps, distance, far_level)
    return near + 16 * (offset > 0).astype(jnp.int32)


def dot(left, right):
    return jnp.dot(left, right, preferred_element_type=f32)


def dot_nt(left, right):
    return lax.dot_general(left, right, (((1,), (1,)), ((), ())), preferred_element_type=f32)


def dot_tn(left, right):
    return lax.dot_general(left, right, (((0,), (0,)), ((), ())), preferred_element_type=f32)


def swap(value, axis, bit):
    size = lax.axis_size(axis)
    return lax.ppermute(value, axis, [(i, i ^ bit) for i in range(size)])


def gather_relative(value, axis):
    blocks = [value]
    bit = lax.axis_size(axis) // 2
    parts = {0: value}
    while bit:
        for p in list(parts):
            parts[p ^ bit] = swap(parts[p], axis, bit)
        bit //= 2
    return [parts[p] for p in range(lax.axis_size(axis))]


def exchange_relative(blocks, axis):
    return [blocks[0]] + [swap(block, axis, p) for p, block in enumerate(blocks) if p]


def call(kernel, out_shape, operands, spaces="", scratch=(), work=0):
    vmem = pl.BlockSpec(memory_space=pltpu.VMEM)
    smem = pl.BlockSpec(memory_space=pltpu.SMEM)
    in_specs = [smem if spaces[i : i + 1] == "s" else vmem for i in range(len(operands))]
    return pl.pallas_call(
        kernel,
        out_shape=out_shape,
        in_specs=in_specs,
        out_specs=jax.tree.map(lambda _: vmem, out_shape),
        scratch_shapes=list(scratch),
        compiler_params=pltpu.CompilerParams(vmem_limit_bytes=56 * 2**20),
        cost_estimate=pl.CostEstimate(flops=work, bytes_accessed=0, transcendentals=0),
    )(*operands)


def shape(dims, dtype=bf16):
    return jax.ShapeDtypeStruct(tuple(dims), dtype)


def diagonal(size):
    return lax.broadcasted_iota(jnp.int32, (size, size), 0) == lax.broadcasted_iota(
        jnp.int32, (size, size), 1
    )


def to_column(row, size):
    return jnp.sum(jnp.where(diagonal(size), row, 0.0), axis=1, keepdims=True)


def to_row(column, size):
    return jnp.sum(jnp.where(diagonal(size), column, 0.0), axis=0, keepdims=True)


def prepare_weight(n, part, weight, gains, *outs):
    wide = 3 * part
    s = lax.axis_index("shard")
    extra = outs[0].shape[1] - wide
    one, two = (to_column(gains[i : i + 1, :].astype(f32), part) for i in range(2))
    lane = lax.broadcasted_iota(jnp.int32, (part, extra), 1)
    beside = jnp.where(lane == 0, one, jnp.where(lane == 1, two, 0.0)).astype(bf16)
    for p in range(n):
        outs[p][:, wide:] = beside
    for k in range(n):

        @pl.when(s == k)
        def _():
            for p in range(n):
                for kind in range(3):
                    at = (kind * n + (k ^ p)) * part
                    outs[p][:, kind * part : (kind + 1) * part] = weight[:, at : at + part]


def offsets(rows):
    return lax.broadcasted_iota(jnp.int32, (rows, rows), 1) - lax.broadcasted_iota(
        jnp.int32, (rows, rows), 0
    )


def near_buckets(diff, buckets):
    if diff == 0:
        return range(buckets)
    return range(buckets // 2, buckets) if diff > 0 else range(buckets // 2)


def attention_forward(n, rows, width, heads, seqs, buckets, *refs):
    lengths, table = refs[:2]
    token_refs = refs[2 : 2 + n]
    weight_refs = refs[2 + n : 2 + 2 * n]
    tokens_out, weight_out, projected_out, weights_out, gains_out, mixed_all = refs[
        2 + 2 * n : 8 + 2 * n
    ]
    mixed_out = refs[8 + 2 * n : 8 + 3 * n]
    (normed_scr,) = refs[8 + 3 * n :]
    s = lax.axis_index("shard")
    part = width // n
    wide = 3 * part
    head_dim = part // heads
    for p in range(n):
        tokens_out[s ^ p] = token_refs[p][...]
        weight_out[pl.ds(pl.multiple_of((s ^ p) * part, part & -part), part), :] = weight_refs[p][...]
    size = 128
    for c in range(width // size):
        beside = weight_out[c * size : (c + 1) * size, wide:].astype(f32)
        for i in range(2):
            gains_out[i : i + 1, c * size : (c + 1) * size] = to_row(beside[:, i : i + 1], size)
    gain = gains_out[0:1, :]
    for j in range(n):
        value = tokens_out[j].astype(f32)
        factor = lax.rsqrt(jnp.mean(value * value, axis=-1, keepdims=True) + norm_eps)
        normed_scr[j * rows : (j + 1) * rows, :] = (value * factor * gain).astype(bf16)
    projected_out[...] = dot(normed_scr[...], weight_out[:, :wide]).astype(bf16)
    total_rows = n * rows
    key_place = lax.broadcasted_iota(jnp.int32, (1, total_rows), 1)
    key_segment = jnp.zeros((1, total_rows), jnp.int32)
    end = jnp.int32(0)
    ends = []
    for j in range(seqs):
        end = end + lengths[0, j]
        ends.append(end)
        key_segment = key_segment + (key_place >= end).astype(jnp.int32)
    base = offsets(rows)
    steps = {diff: bucket_index(base + diff * rows) for diff in (-1, 0, 1)}
    for h in range(heads):
        query = projected_out[:, h * head_dim : (h + 1) * head_dim]
        key = projected_out[:, part + h * head_dim : part + (h + 1) * head_dim]
        value = projected_out[:, 2 * part + h * head_dim : 2 * part + (h + 1) * head_dim]
        bias = {}
        for diff in (-1, 0, 1):
            block = jnp.zeros((rows, rows), f32)
            for b in near_buckets(diff, buckets):
                block = jnp.where(steps[diff] == b, table[h, b], block)
            bias[diff] = block
        low_side = jnp.full((rows, rows), table[h, buckets // 2 - 1], f32)
        high_side = jnp.full((rows, rows), table[h, buckets - 1], f32)
        for i in range(n):
            scores = dot_nt(query[i * rows : (i + 1) * rows, :], key)
            side = [
                bias[j - i] if abs(j - i) <= 1 else (high_side if j > i else low_side)
                for j in range(n)
            ]
            scores = scores + jnp.concatenate(side, axis=1)
            query_place = i * rows + lax.broadcasted_iota(jnp.int32, (rows, 1), 0)
            query_segment = jnp.zeros((rows, 1), jnp.int32)
            for j in range(seqs):
                query_segment = query_segment + (query_place >= ends[j]).astype(jnp.int32)
            scores = jnp.where(query_segment == key_segment, scores, big_negative)
            top = jnp.max(scores, axis=-1, keepdims=True)
            raised = jnp.exp(scores - top)
            total = jnp.sum(raised, axis=-1, keepdims=True)
            weights = (raised * (1.0 / total)).astype(bf16)
            weights_out[h, i * rows : (i + 1) * rows, :] = weights
            mixed_all[i, :, h * head_dim : (h + 1) * head_dim] = dot(weights, value).astype(bf16)
    for p in range(n):
        mixed_out[p][...] = mixed_all[s ^ p]


def attention_backward(n, m, rows, width, heads, buckets, experts, *refs):
    projected, tokens, gains, weight, weights, mixed, weight_out, gain_two, router = refs[:9]
    branch_refs = refs[9 : 9 + n]
    at = 9 + n
    shares = 4 if m > 1 else 2
    share_out = refs[at : at + shares]
    normed_grad_out = refs[at + shares : at + shares + n]
    gain_out, table_out = refs[at + shares + n : at + shares + n + 2]
    branch_scr, scores_scr, projected_scr, total_scr, out_scr, normed_scr, send_scr = refs[
        at + shares + n + 2 :
    ]
    s = lax.axis_index("shard")
    e = lax.axis_index("expert")
    part = width // n
    wide = 3 * part
    group = n * rows
    head_dim = part // heads
    for p in range(n):
        branch_scr[s ^ p] = branch_refs[p][...]
    branch = branch_scr[...].reshape(group, width)
    grad_mixed = dot_nt(branch, weight_out[...]).astype(bf16)
    out_scr[...] = dot_tn(mixed[...].reshape(group, part), branch)
    base = offsets(rows)
    steps = {diff: bucket_index(base + diff * rows) for diff in (-1, 0, 1)}
    lane = lax.broadcasted_iota(jnp.int32, (row_tile, 128), 1)
    line = lax.broadcasted_iota(jnp.int32, (row_tile, 128), 0)
    table_total = jnp.zeros((row_tile, 128), f32)
    per_line = buckets // row_tile
    for h in range(heads):
        query = projected[:, h * head_dim : (h + 1) * head_dim]
        key = projected[:, part + h * head_dim : part + (h + 1) * head_dim]
        value = projected[:, 2 * part + h * head_dim : 2 * part + (h + 1) * head_dim]
        near = {diff: jnp.zeros((rows, rows), f32) for diff in (-1, 0, 1)}
        low_side = jnp.zeros((1, rows), f32)
        high_side = jnp.zeros((1, rows), f32)
        upstream = grad_mixed[:, h * head_dim : (h + 1) * head_dim]
        for i in range(n):
            weights_i = weights[h, i * rows : (i + 1) * rows, :].astype(f32)
            grad_weights = dot_nt(upstream[i * rows : (i + 1) * rows, :], value)
            inner = jnp.sum(weights_i * grad_weights, axis=-1, keepdims=True)
            grad_scores = weights_i * (grad_weights - inner)
            scores_scr[i * rows : (i + 1) * rows, :] = grad_scores.astype(bf16)
            for j in range(n):
                block = grad_scores[:, j * rows : (j + 1) * rows]
                if abs(j - i) <= 1:
                    near[j - i] = near[j - i] + block
                elif j > i:
                    high_side = high_side + jnp.sum(block, axis=0, keepdims=True)
                else:
                    low_side = low_side + jnp.sum(block, axis=0, keepdims=True)
        for b in range(buckets):
            amount = jnp.zeros((1, rows), f32)
            for diff in (-1, 0, 1):
                if b in near_buckets(diff, buckets):
                    amount = amount + jnp.sum(
                        jnp.where(steps[diff] == b, near[diff], 0.0), axis=0, keepdims=True
                    )
            if b == buckets - 1:
                amount = amount + high_side
            if b == buckets // 2 - 1:
                amount = amount + low_side
            amount = jnp.sum(amount, axis=1, keepdims=True)
            spot = (line == b // per_line) & (lane == h * per_line + b % per_line)
            table_total = jnp.where(spot, amount, table_total)
        grad_scores_all = scores_scr[...]
        projected_scr[:, h * head_dim : (h + 1) * head_dim] = dot(grad_scores_all, key).astype(bf16)
        projected_scr[:, part + h * head_dim : part + (h + 1) * head_dim] = (
            dot_tn(query, grad_scores_all).T.astype(bf16)
        )
        projected_scr[:, 2 * part + h * head_dim : 2 * part + (h + 1) * head_dim] = (
            dot_tn(upstream, weights[h]).T.astype(bf16)
        )
    table_out[...] = table_total
    grad_projected = projected_scr[...]
    normed_grad = dot_nt(grad_projected, weight[:, :wide])
    send_scr[...] = normed_grad.astype(bf16).reshape(n, rows, width)
    for p in range(n):
        normed_grad_out[p][...] = send_scr[s ^ p]
    gain = gains[0:1, :]
    grad_gain = jnp.zeros((1, width), f32)
    for j in range(n):
        value = tokens[j].astype(f32)
        unit = value * lax.rsqrt(jnp.mean(value * value, axis=-1, keepdims=True) + norm_eps)
        normed_scr[j * rows : (j + 1) * rows, :] = (unit * gain).astype(bf16)
        grad_gain = grad_gain + jnp.sum(
            normed_grad[j * rows : (j + 1) * rows, :] * unit, axis=0, keepdims=True
        )
    gain_out[...] = jnp.broadcast_to(grad_gain, gain_out.shape)
    total_scr[:, :wide] = dot_tn(normed_scr[...], grad_projected)
    full = total_scr.shape[1]
    if m == 1:
        for t in range(n):
            share_out[0][t] = total_scr[t * part : (t + 1) * part, :wide].astype(bf16)
        share_out[1][...] = out_scr[...].astype(bf16)
        return
    piece = part // m
    total_scr[:, wide:] = jnp.zeros((width, full - wide), f32)
    size = 128
    for c in range(width // size):
        here = slice(c * size, (c + 1) * size)
        total_scr[here, wide : wide + 1] = to_column(grad_gain[:, here], size)
        total_scr[here, wide + 1 : wide + 2] = to_column(gain_two[0:1, here], size)
    total_scr[:, wide + 2 : wide + 2 + experts] = router[...]
    at = wide + 2 + experts
    rest = (width - full) // n
    for t in range(n):
        total_scr[t * part : (t + 1) * part, at : at + rest] = out_scr[
            :, full + t * rest : full + (t + 1) * rest
        ]
    at = at + rest
    for d in range(m):
        total_scr[d * piece : d * piece + row_tile, at : at + heads * per_line] = table_total[
            :, : heads * per_line
        ]
    for d in range(m):
        target = share_out[(d & 1) + 2 * (d < m // 2)]
        place = (d >> 1) % (m // 4)
        start = (e ^ d) * piece
        for t in range(n):
            rows_at = pl.multiple_of(t * part + start, row_tile)
            target[place, t] = total_scr[pl.ds(rows_at, piece), :].astype(bf16)
        rows_at = pl.multiple_of(start, row_tile)
        target[place, n] = out_scr[pl.ds(rows_at, piece), :full].astype(bf16)


def assemble(n, m, part, piece, experts, *refs):
    total_out, out_out, small_out = refs[m:]
    s = lax.axis_index("shard")
    e = lax.axis_index("expert")
    wide = 3 * part
    full = refs[0].shape[2]
    at = wide + 2 + experts
    rest = (n * part - full) // n
    for d in range(m):
        start = pl.multiple_of((e ^ d) * piece, row_tile)
        own = pl.ds(start, piece)
        small = jnp.zeros((piece, full - wide), f32)
        for p in range(n):
            small = small + refs[d][p, :, wide:].astype(f32)
            out_out[own, full + p * rest : full + (p + 1) * rest] = refs[d][p, :, at : at + rest].astype(
                f32
            )
        out_out[own, :full] = refs[d][n].astype(f32)
        small_out[own, :] = small
    for k in range(n):

        @pl.when(s == k)
        def _():
            for d in range(m):
                own = pl.ds(pl.multiple_of((e ^ d) * piece, row_tile), piece)
                for p in range(n):
                    for kind in range(3):
                        to = (kind * n + (k ^ p)) * part
                        total_out[own, to : to + part] = refs[d][
                            p, :, kind * part : (kind + 1) * part
                        ].astype(f32)


def expert_forward(source, up_own, up_pair, down_own, down_pair, *outs):
    hidden_out, slope_out, result_out = outs
    result = 0.0
    for k, (up, down) in enumerate(((up_own, down_own), (up_pair, down_pair))):
        before = dot(source[...], up[0])
        square = before * before
        tanh_value = jnp.tanh(gelu_scale * before * (1.0 + gelu_cubic * square))
        half = 0.5 * (1.0 + tanh_value)
        hidden = (before * half).astype(bf16)
        slope = half + 0.5 * before * (1.0 - tanh_value * tanh_value) * gelu_scale * (
            1.0 + 3.0 * gelu_cubic * square
        )
        hidden_out[k] = hidden
        slope_out[k] = slope.astype(bf16)
        result = result + dot(hidden, down[0])
    result_out[...] = result.astype(result_out.dtype)


def expert_backward(grads, up_own, up_pair, down_own, down_pair, slope, *outs):
    before_out, result_out = outs
    result = 0.0
    for k, (up, down) in enumerate(((up_own, down_own), (up_pair, down_pair))):
        grad_before = (dot_nt(grads[...], down[0]) * slope[k].astype(f32)).astype(bf16)
        before_out[k] = grad_before
        result = result + dot_nt(grad_before, up[0])
    result_out[...] = result.astype(result_out.dtype)


def expert_weights(*refs):
    rows, grads, hidden, grad_before = (
        jnp.concatenate([own[...], came[...]], axis=-2)
        for own, came in zip(refs[0:8:2], refs[1:8:2])
    )
    up_out, down_out, up_send, down_send = refs[8:]
    up_send[0] = dot_tn(rows, grad_before[1]).astype(bf16)
    down_send[0] = dot_tn(hidden[1], grads).astype(bf16)
    up_out[0] = dot_tn(rows, grad_before[0])
    down_out[0] = dot_tn(hidden[0], grads)


def rms_factor(value):
    return lax.rsqrt(jnp.mean(value * value, axis=-1, keepdims=True) + norm_eps)


def rms_backward(value, factor, gain, upstream):
    scaled = upstream * gain
    grad_value = factor * scaled - value * factor * factor * factor * jnp.mean(
        scaled * value, axis=-1, keepdims=True
    )
    grad_gain = jnp.sum(upstream * value * factor, axis=0)
    return (grad_value, grad_gain)


def local(
    tokens,
    lengths,
    routes,
    attention_in,
    attention_out,
    position_bias,
    first_gain,
    second_gain,
    router,
    expert_in,
    expert_out,
    cotangent,
):
    n = lax.axis_size("shard")
    m = lax.axis_size("expert")
    s = lax.axis_index("shard")
    e = lax.axis_index("expert")
    rows, width = tokens.shape
    heads, buckets = position_bias.shape
    part = width // n
    wide = 3 * part
    group = n * rows
    seqs = lengths.shape[1]
    experts = router.shape[1]
    direct = m == 8
    full = wide + -wide % 128
    micro = 10**9

    far_tokens, pair_tokens = swap(tokens, "shard", 2 * pair), swap(tokens, "shard", pair)
    weight_blocks = exchange_relative(
        call(
            lambda *refs: prepare_weight(n, part, *refs),
            [shape((part, full))] * n,
            (attention_in, jnp.stack([first_gain, second_gain])),
        ),
        "shard",
    )
    far_tokens, own_up, own_down, table_scalars = lax.optimization_barrier(
        (far_tokens, expert_in, expert_out, position_bias.astype(f32))
    )
    token_blocks = [tokens, pair_tokens, far_tokens, swap(far_tokens, "shard", pair)]
    pair_up = swap(own_up, "shard", pair)
    pair_down = swap(own_down, "shard", pair)
    own_out, token_blocks, weight_blocks = lax.optimization_barrier(
        (attention_out, token_blocks, weight_blocks)
    )
    far_out, pair_out = swap(own_out, "shard", 2 * pair), swap(own_out, "shard", pair)

    answers = call(
        lambda *refs: attention_forward(n, rows, width, heads, seqs, buckets, *refs),
        (
            shape((n, rows, width)),
            shape((width, full)),
            shape((group, wide)),
            shape((heads, group, group)),
            shape((row_tile, width), f32),
            shape((n, rows, part)),
            *[shape((rows, part))] * n,
        ),
        (lengths, table_scalars, *token_blocks, *weight_blocks),
        "ss",
        [pltpu.VMEM((group, width), bf16)],
        work=10 * micro,
    )
    tokens_all, weight, projected, weights, gains, mixed = answers[:6]
    mixed_mine, pair_up, pair_down, far_out, pair_out = lax.optimization_barrier(
        (list(answers[6:]), pair_up, pair_down, far_out, pair_out)
    )
    mixed_blocks = exchange_relative(mixed_mine, "shard")
    out_blocks = [own_out, pair_out, far_out, swap(far_out, "shard", pair)]
    gain_one, gain_two = gains[0:1], gains[1:2]

    inputs = tokens.astype(f32)
    hidden_one = inputs + sum(dot(mixed_blocks[p], out_blocks[p]) for p in range(n))
    factor_two = rms_factor(hidden_one)
    normed_two = hidden_one * factor_two * gain_two
    logits = jnp.dot(
        normed_two, router, precision=lax.Precision.HIGHEST, preferred_element_type=f32
    )
    shifted = jnp.exp(logits - jnp.max(logits, axis=-1, keepdims=True))
    probs = shifted / jnp.sum(shifted, axis=-1, keepdims=True)
    route = routes[:, 0]
    chosen = (route[:, None] == lax.iota(jnp.int32, experts)[None, :]).astype(f32)
    gate = jnp.sum(probs * chosen, axis=1)
    lower = (lax.iota(jnp.int32, rows)[:, None] >= lax.iota(jnp.int32, rows)[None, :]).astype(bf16)
    running = dot(lower, chosen.astype(bf16))
    slot = jnp.sum((running - 1.0) * chosen, axis=1).astype(jnp.int32)
    capacity = max(2, 9 * rows // (8 * experts) + 1)
    capacity = -(-capacity // slot_tile) * slot_tile
    places = experts * capacity
    half = places // 2
    if direct:
        holder = route ^ e
        target = (holder & 1) * half + (holder >> 1) * capacity + slot
    else:
        target = route * capacity + slot
    collect = (target[:, None] == lax.iota(jnp.int32, places)[None, :]).astype(bf16)
    upstream = cotangent.astype(f32)
    grad_result = (gate[:, None] * upstream).astype(bf16)

    def plain(value):
        return lax.all_to_all(
            value.reshape(experts, capacity, width), "expert", 0, 0, tiled=True
        ).reshape(places, width)

    def send(value):
        if not direct:
            return plain(dot_tn(collect, value).astype(bf16))
        came = swap(dot_tn(collect[:, half:], value).astype(bf16), "expert", 1)
        own = dot_tn(collect[:, :half], value).astype(bf16).reshape(m // 2, capacity, width)
        both = jnp.concatenate([own, came.reshape(m // 2, capacity, width)], axis=1)
        blocks = [both[d] if d == 0 else swap(both[d], "expert", 2 * d) for d in range(m // 2)]
        return jnp.concatenate(blocks, axis=0)

    def give_back(value):
        if not direct:
            return dot(collect, plain(value))
        both = value.reshape(m // 2, 2 * capacity, width)
        blocks = [both[d] if d == 0 else swap(both[d], "expert", 2 * d) for d in range(m // 2)]
        own = jnp.concatenate([block[:capacity] for block in blocks])
        other = jnp.concatenate([block[capacity:] for block in blocks])
        other = swap(other, "expert", 1)
        return dot(collect[:, :half], own) + dot(collect[:, half:], other)

    def reduce_shard(keep, out):
        return (keep + swap(out, "shard", 2 * pair).astype(f32)).astype(bf16)

    arrived = send(normed_two.astype(bf16))
    row_blocks = (arrived, swap(arrived, "shard", 2 * pair))
    arrived_grad = send(grad_result)
    grad_blocks = (arrived_grad, swap(arrived_grad, "shard", 2 * pair))

    units = expert_in.shape[2]
    expert_weight = (own_up, pair_up, own_down, pair_down)
    middle = shape((2, places, units))
    kept, sent = shape((places, width), f32), shape((places, width))
    forward = [
        call(expert_forward, (middle, middle, end), (block, *expert_weight), work=3 * micro)
        for block, end in zip(row_blocks, (kept, sent))
    ]
    backward = [
        call(
            expert_backward, (middle, end), (block, *expert_weight, ahead[1]), work=3 * micro
        )
        for block, end, ahead in zip(grad_blocks, (kept, sent), forward)
    ]
    expert_result = give_back(reduce_shard(*[half[2] for half in forward]))
    grad_sent = give_back(reduce_shard(*[half[1] for half in backward]))

    layer_out = (hidden_one + gate[:, None] * expert_result).astype(bf16)
    grad_gate = jnp.sum(upstream * expert_result, axis=1)
    grad_logits = (grad_gate * gate)[:, None] * (chosen - probs)
    grad_router = lax.dot_general(
        normed_two,
        grad_logits,
        (((0,), (0,)), ((), ())),
        precision=lax.Precision.HIGHEST,
        preferred_element_type=f32,
    )
    grad_normed_two = grad_sent + lax.dot_general(
        grad_logits,
        router,
        (((1,), (1,)), ((), ())),
        precision=lax.Precision.HIGHEST,
        preferred_element_type=f32,
    )
    grad_middle, grad_gain_two = rms_backward(hidden_one, factor_two, gain_two, grad_normed_two)
    grad_hidden = upstream + grad_middle
    branch, late_rows = lax.optimization_barrier((grad_hidden.astype(bf16), row_blocks))
    grad_up, grad_down, up_send, down_send = call(
        expert_weights,
        (
            shape(expert_in.shape, f32),
            shape(expert_out.shape, f32),
            shape(expert_in.shape),
            shape(expert_out.shape),
        ),
        (
            *late_rows,
            *grad_blocks,
            *[half[0] for half in forward],
            *[half[0] for half in backward],
        ),
        work=6 * micro,
    )
    far_branch, pair_branch = swap(branch, "shard", 2 * pair), swap(branch, "shard", pair)
    far_branch, grad_router, gain_two_row, up_send, down_send = lax.optimization_barrier(
        (far_branch, grad_router, grad_gain_two[None], up_send, down_send)
    )
    branch_blocks = [branch, pair_branch, far_branch, swap(far_branch, "shard", pair)]
    holders = m if direct else 1
    piece = part // m
    if direct:
        share_shapes = [shape((m // 4, n + 1, piece, full))] * 4
    else:
        share_shapes = [shape((n, part, wide)), shape((part, width))]
    answers = call(
        lambda *refs: attention_backward(n, holders, rows, width, heads, buckets, experts, *refs),
        (
            *share_shapes,
            *[shape((rows, width))] * n,
            shape((row_tile, width), f32),
            shape((row_tile, 128), f32),
        ),
        (
            projected,
            tokens_all,
            gains,
            weight,
            weights,
            mixed,
            own_out,
            gain_two_row,
            grad_router,
            *branch_blocks,
        ),
        "",
        [
            pltpu.VMEM((n, rows, width), bf16),
            pltpu.VMEM((group, group), bf16),
            pltpu.VMEM((group, wide), bf16),
            pltpu.VMEM((width, full), f32),
            pltpu.VMEM((part, width), f32),
            pltpu.VMEM((group, width), bf16),
            pltpu.VMEM((n, rows, width), bf16),
        ],
        work=8 * micro,
    )
    shares = answers[: len(share_shapes)]
    normed_grads = answers[len(share_shapes) : len(share_shapes) + n]
    gain_row, table = answers[len(share_shapes) + n :]

    per_line = buckets // row_tile

    def biases(block):
        return block.reshape(row_tile, heads, per_line).swapaxes(0, 1).reshape(heads, buckets)

    def finish_tokens(blocks):
        grad_normed = sum(x.astype(f32) for x in exchange_relative(list(blocks), "shard"))
        grad_input_norm, _ = rms_backward(inputs, rms_factor(inputs), gain_one, grad_normed)
        return (grad_hidden + grad_input_norm).astype(bf16)

    if direct:
        far_keep, far_send, near_keep, near_send = shares
        far_came = swap(far_send, "expert", 1)
        far = far_keep.astype(f32) + far_came.astype(f32)
        normed_grads, far_came = lax.optimization_barrier((normed_grads, far_came))
        grad_tokens = finish_tokens(normed_grads)
        near = near_keep.astype(f32) + swap(near_send, "expert", 1).astype(f32)
        came = [swap(far[d].astype(bf16), "expert", m // 2 + 2 * d) for d in range(m // 4)]
        came += [swap(near[d].astype(bf16), "expert", 2 * d) for d in range(1, m // 4)]
        summed = near[0] + sum(x.astype(f32) for x in came)
        at = wide + 2 + experts
        rest = (width - full) // n
        table_total = biases(
            summed[0, :row_tile, at + rest : at + rest + heads * per_line]
        )
        low, up_send, down_send = lax.optimization_barrier((summed.astype(bf16), up_send, down_send))
        mine = exchange_relative(
            [lax.dynamic_index_in_dim(low, s ^ p, 0, keepdims=False) for p in range(n)], "shard"
        )
        lane = lax.iota(jnp.int32, full)[None, :]
        own_lane = (lane >= at) & (lane < at + rest)
        mine = jnp.stack(
            [jnp.where(own_lane, low[p], mine[p]) for p in range(n)] + [low[n]], axis=0
        )
        blocks = {0: mine, 1: swap(mine, "expert", 1), 4: swap(mine, "expert", 4)}
        blocks[2] = swap(mine, "expert", 2)
        blocks[4], blocks[1], grad_tokens = lax.optimization_barrier(
            (blocks[4], blocks[1], grad_tokens)
        )
        blocks[6] = swap(blocks[4], "expert", 2)
        blocks[5] = swap(blocks[4], "expert", 1)
        blocks[3] = swap(blocks[2], "expert", 1)
        blocks[6], grad_up, grad_down = lax.optimization_barrier(
            (
                blocks[6],
                grad_up + swap(up_send, "shard", pair).astype(f32),
                grad_down + swap(down_send, "shard", pair).astype(f32),
            )
        )
        blocks[7] = swap(blocks[6], "expert", 1)
        blocks = [blocks[d] for d in range(m)]
        grad_attention_in, grad_attention_out, small_total = call(
            lambda *refs: assemble(n, m, part, piece, experts, *refs),
            (shape((part, 3 * width), f32), shape((part, width), f32), shape((part, full - wide), f32)),
            (*blocks,),
        )
    else:
        grad_tokens = finish_tokens(normed_grads)
        grad_up = grad_up + swap(up_send, "shard", pair).astype(f32)
        grad_down = grad_down + swap(down_send, "shard", pair).astype(f32)
        came = lax.all_to_all(
            shares[0].reshape(n, m, piece, wide).swapaxes(0, 1), "expert", 0, 0, tiled=True
        )
        summed = sum(x.astype(f32) for x in came).astype(bf16)
        mine = lax.all_to_all(summed, "shard", 0, 0, tiled=True)
        mine = mine.reshape(n, piece, 3, part).transpose(1, 2, 0, 3).reshape(piece, 3 * width)
        came = lax.all_to_all(shares[1].reshape(m, piece, width), "expert", 0, 0, tiled=True)
        out_mine = sum(x.astype(f32) for x in came).astype(bf16)
        grad_attention_in = lax.all_gather(mine, "expert", axis=0, tiled=True).astype(f32)
        grad_attention_out = lax.all_gather(out_mine, "expert", axis=0, tiled=True).astype(f32)
        small = jnp.concatenate([gain_row[0][:, None], grad_gain_two[:, None], grad_router], axis=1)
        small_total = lax.psum_scatter(small, "shard", scatter_dimension=0, tiled=True)
        small_total, table_total = lax.psum(
            (small_total, biases(table[:, : heads * per_line])), "expert"
        )
    return (
        layer_out,
        grad_tokens,
        grad_attention_in,
        grad_attention_out,
        table_total,
        small_total[:, 0],
        small_total[:, 1],
        small_total[:, 2 : 2 + experts],
        grad_up,
        grad_down,
    )


def solution(mesh):
    in_specs = (
        P(("expert", "shard"), None),
        P("expert", None),
        P(("expert", "shard"), None),
        P("shard", None),
        P("shard", None),
        P("shard", None),
        P("shard"),
        P("shard"),
        P(),
        P("expert", None, "shard"),
        P("expert", "shard", None),
        P(("expert", "shard"), None),
    )
    out_specs = (
        P(("expert", "shard"), None),
        P(("expert", "shard"), None),
        P("shard", None),
        P("shard", None),
        P("shard", None),
        P("shard"),
        P("shard"),
        P("shard", None),
        P("expert", None, "shard"),
        P("expert", "shard", None),
    )
    return jax.shard_map(local, mesh=mesh, in_specs=in_specs, out_specs=out_specs, check_vma=False)
```

```python
import jax
import jax.numpy as jnp
from jax import lax
from jax.experimental import pallas as pl
from jax.experimental.pallas import tpu as pltpu
from jax.sharding import PartitionSpec as P

norm_eps = 1e-06
gelu_scale = 0.7978845608028654
gelu_cubic = 0.044715
big_negative = -1e30
near_steps = 8
far_steps = (12, 16, 23, 32, 46, 64, 91)
bf16 = jnp.bfloat16
f32 = jnp.float32
row_tile = 8
pair = 1
slot_tile = 4


def bucket_index(offset):
    distance = jnp.abs(offset)
    far_level = jnp.full_like(distance, near_steps)
    for step_edge in far_steps:
        far_level = far_level + (distance >= step_edge).astype(jnp.int32)
    near = jnp.where(distance < near_steps, distance, far_level)
    return near + 16 * (offset > 0).astype(jnp.int32)


def dot(left, right):
    return jnp.dot(left, right, preferred_element_type=f32)


def dot_nt(left, right):
    return lax.dot_general(left, right, (((1,), (1,)), ((), ())), preferred_element_type=f32)


def dot_tn(left, right):
    return lax.dot_general(left, right, (((0,), (0,)), ((), ())), preferred_element_type=f32)


def swap(value, axis, bit):
    size = lax.axis_size(axis)
    return lax.ppermute(value, axis, [(i, i ^ bit) for i in range(size)])


def gather_relative(value, axis):
    blocks = [value]
    bit = lax.axis_size(axis) // 2
    parts = {0: value}
    while bit:
        for p in list(parts):
            parts[p ^ bit] = swap(parts[p], axis, bit)
        bit //= 2
    return [parts[p] for p in range(lax.axis_size(axis))]


def exchange_relative(blocks, axis):
    return [blocks[0]] + [swap(block, axis, p) for p, block in enumerate(blocks) if p]


def call(kernel, out_shape, operands, spaces="", scratch=(), work=0):
    vmem = pl.BlockSpec(memory_space=pltpu.VMEM)
    smem = pl.BlockSpec(memory_space=pltpu.SMEM)
    in_specs = [smem if spaces[i : i + 1] == "s" else vmem for i in range(len(operands))]
    return pl.pallas_call(
        kernel,
        out_shape=out_shape,
        in_specs=in_specs,
        out_specs=jax.tree.map(lambda _: vmem, out_shape),
        scratch_shapes=list(scratch),
        compiler_params=pltpu.CompilerParams(vmem_limit_bytes=56 * 2**20),
        cost_estimate=pl.CostEstimate(flops=work, bytes_accessed=0, transcendentals=0),
    )(*operands)


def shape(dims, dtype=bf16):
    return jax.ShapeDtypeStruct(tuple(dims), dtype)


def diagonal(size):
    return lax.broadcasted_iota(jnp.int32, (size, size), 0) == lax.broadcasted_iota(
        jnp.int32, (size, size), 1
    )


def to_column(row, size):
    return jnp.sum(jnp.where(diagonal(size), row, 0.0), axis=1, keepdims=True)


def to_row(column, size):
    return jnp.sum(jnp.where(diagonal(size), column, 0.0), axis=0, keepdims=True)


def prepare_weight(n, part, weight, gains, *outs):
    wide = 3 * part
    s = lax.axis_index("shard")
    extra = outs[0].shape[1] - wide
    one, two = (to_column(gains[i : i + 1, :].astype(f32), part) for i in range(2))
    lane = lax.broadcasted_iota(jnp.int32, (part, extra), 1)
    beside = jnp.where(lane == 0, one, jnp.where(lane == 1, two, 0.0)).astype(bf16)
    for p in range(n):
        outs[p][:, wide:] = beside
    for k in range(n):

        @pl.when(s == k)
        def _():
            for p in range(n):
                for kind in range(3):
                    at = (kind * n + (k ^ p)) * part
                    outs[p][:, kind * part : (kind + 1) * part] = weight[:, at : at + part]


def offsets(rows):
    return lax.broadcasted_iota(jnp.int32, (rows, rows), 1) - lax.broadcasted_iota(
        jnp.int32, (rows, rows), 0
    )


def near_buckets(diff, buckets):
    if diff == 0:
        return range(buckets)
    return range(buckets // 2, buckets) if diff > 0 else range(buckets // 2)


def attention_forward(n, rows, width, heads, seqs, buckets, *refs):
    lengths, table = refs[:2]
    token_refs = refs[2 : 2 + n]
    weight_refs = refs[2 + n : 2 + 2 * n]
    tokens_out, weight_out, projected_out, weights_out, gains_out, mixed_all = refs[
        2 + 2 * n : 8 + 2 * n
    ]
    mixed_out = refs[8 + 2 * n : 8 + 3 * n]
    normed_scr, scores_scr = refs[8 + 3 * n :]
    s = lax.axis_index("shard")
    part = width // n
    wide = 3 * part
    head_dim = part // heads
    for p in range(n):
        tokens_out[s ^ p] = token_refs[p][...]
        weight_out[pl.ds(pl.multiple_of((s ^ p) * part, part & -part), part), :] = weight_refs[p][...]
    size = 128
    for c in range(width // size):
        beside = weight_out[c * size : (c + 1) * size, wide:].astype(f32)
        for i in range(2):
            gains_out[i : i + 1, c * size : (c + 1) * size] = to_row(beside[:, i : i + 1], size)
    gain = gains_out[0:1, :]
    for j in range(n):
        value = tokens_out[j].astype(f32)
        factor = lax.rsqrt(jnp.mean(value * value, axis=-1, keepdims=True) + norm_eps)
        normed_scr[j * rows : (j + 1) * rows, :] = (value * factor * gain).astype(bf16)
    projected_out[...] = dot(normed_scr[...], weight_out[:, :wide]).astype(bf16)
    total_rows = n * rows
    key_place = lax.broadcasted_iota(jnp.int32, (1, total_rows), 1)
    key_segment = jnp.zeros((1, total_rows), jnp.int32)
    end = jnp.int32(0)
    ends = []
    for j in range(seqs):
        end = end + lengths[0, j]
        ends.append(end)
        key_segment = key_segment + (key_place >= end).astype(jnp.int32)
    base = offsets(rows)
    steps = {diff: bucket_index(base + diff * rows) for diff in (-1, 0, 1)}
    for h in range(heads):
        query = projected_out[:, h * head_dim : (h + 1) * head_dim]
        key = projected_out[:, part + h * head_dim : part + (h + 1) * head_dim]
        value = projected_out[:, 2 * part + h * head_dim : 2 * part + (h + 1) * head_dim]
        bias = {}
        for diff in (-1, 0, 1):
            block = jnp.zeros((rows, rows), f32)
            for b in near_buckets(diff, buckets):
                block = jnp.where(steps[diff] == b, table[h, b], block)
            bias[diff] = block
        low_side = jnp.full((rows, rows), table[h, buckets // 2 - 1], f32)
        high_side = jnp.full((rows, rows), table[h, buckets - 1], f32)
        scores_scr[...] = dot_nt(query, key)
        for i in range(n):
            scores = scores_scr[i * rows : (i + 1) * rows, :]
            side = [
                bias[j - i] if abs(j - i) <= 1 else (high_side if j > i else low_side)
                for j in range(n)
            ]
            scores = scores + jnp.concatenate(side, axis=1)
            query_place = i * rows + lax.broadcasted_iota(jnp.int32, (rows, 1), 0)
            query_segment = jnp.zeros((rows, 1), jnp.int32)
            for j in range(seqs):
                query_segment = query_segment + (query_place >= ends[j]).astype(jnp.int32)
            scores = jnp.where(query_segment == key_segment, scores, big_negative)
            top = jnp.max(scores, axis=-1, keepdims=True)
            raised = jnp.exp(scores - top)
            total = jnp.sum(raised, axis=-1, keepdims=True)
            weights = (raised * (1.0 / total)).astype(bf16)
            weights_out[h, i * rows : (i + 1) * rows, :] = weights
        mixed_all[:, :, h * head_dim : (h + 1) * head_dim] = (
            dot(weights_out[h], value).astype(bf16).reshape(n, rows, head_dim)
        )
    for p in range(n):
        mixed_out[p][...] = mixed_all[s ^ p]


def attention_backward(n, m, rows, width, heads, buckets, experts, *refs):
    projected, tokens, gains, weight, weights, mixed, weight_out, gain_two, router = refs[:9]
    branch_refs = refs[9 : 9 + n]
    at = 9 + n
    shares = 4 if m > 1 else 2
    share_out = refs[at : at + shares]
    normed_grad_out = refs[at + shares : at + shares + n]
    gain_out, table_out = refs[at + shares + n : at + shares + n + 2]
    branch_scr, scores_scr, projected_scr, total_scr, out_scr, normed_scr, send_scr, weights_scr = (
        refs[at + shares + n + 2 :]
    )
    s = lax.axis_index("shard")
    e = lax.axis_index("expert")
    part = width // n
    wide = 3 * part
    group = n * rows
    head_dim = part // heads
    for p in range(n):
        branch_scr[s ^ p] = branch_refs[p][...]
    branch = branch_scr[...].reshape(group, width)
    grad_mixed = dot_nt(branch, weight_out[...]).astype(bf16)
    out_scr[...] = dot_tn(mixed[...].reshape(group, part), branch)
    base = offsets(rows)
    steps = {diff: bucket_index(base + diff * rows) for diff in (-1, 0, 1)}
    lane = lax.broadcasted_iota(jnp.int32, (row_tile, 128), 1)
    line = lax.broadcasted_iota(jnp.int32, (row_tile, 128), 0)
    table_total = jnp.zeros((row_tile, 128), f32)
    per_line = buckets // row_tile
    for h in range(heads):
        query = projected[:, h * head_dim : (h + 1) * head_dim]
        key = projected[:, part + h * head_dim : part + (h + 1) * head_dim]
        value = projected[:, 2 * part + h * head_dim : 2 * part + (h + 1) * head_dim]
        near = {diff: jnp.zeros((rows, rows), f32) for diff in (-1, 0, 1)}
        low_side = jnp.zeros((1, rows), f32)
        high_side = jnp.zeros((1, rows), f32)
        upstream = grad_mixed[:, h * head_dim : (h + 1) * head_dim]
        weights_scr[...] = dot_nt(upstream, value)
        for i in range(n):
            weights_i = weights[h, i * rows : (i + 1) * rows, :].astype(f32)
            grad_weights = weights_scr[i * rows : (i + 1) * rows, :]
            inner = jnp.sum(weights_i * grad_weights, axis=-1, keepdims=True)
            grad_scores = weights_i * (grad_weights - inner)
            scores_scr[i * rows : (i + 1) * rows, :] = grad_scores.astype(bf16)
            for j in range(n):
                block = grad_scores[:, j * rows : (j + 1) * rows]
                if abs(j - i) <= 1:
                    near[j - i] = near[j - i] + block
                elif j > i:
                    high_side = high_side + jnp.sum(block, axis=0, keepdims=True)
                else:
                    low_side = low_side + jnp.sum(block, axis=0, keepdims=True)
        for b in range(buckets):
            amount = jnp.zeros((1, rows), f32)
            for diff in (-1, 0, 1):
                if b in near_buckets(diff, buckets):
                    amount = amount + jnp.sum(
                        jnp.where(steps[diff] == b, near[diff], 0.0), axis=0, keepdims=True
                    )
            if b == buckets - 1:
                amount = amount + high_side
            if b == buckets // 2 - 1:
                amount = amount + low_side
            amount = jnp.sum(amount, axis=1, keepdims=True)
            spot = (line == b // per_line) & (lane == h * per_line + b % per_line)
            table_total = jnp.where(spot, amount, table_total)
        grad_scores_all = scores_scr[...]
        projected_scr[:, h * head_dim : (h + 1) * head_dim] = dot(grad_scores_all, key).astype(bf16)
        projected_scr[:, part + h * head_dim : part + (h + 1) * head_dim] = (
            dot_tn(query, grad_scores_all).T.astype(bf16)
        )
        projected_scr[:, 2 * part + h * head_dim : 2 * part + (h + 1) * head_dim] = (
            dot_tn(upstream, weights[h]).T.astype(bf16)
        )
    table_out[...] = table_total
    grad_projected = projected_scr[...]
    normed_grad = dot_nt(grad_projected, weight[:, :wide])
    send_scr[...] = normed_grad.astype(bf16).reshape(n, rows, width)
    for p in range(n):
        normed_grad_out[p][...] = send_scr[s ^ p]
    gain = gains[0:1, :]
    grad_gain = jnp.zeros((1, width), f32)
    for j in range(n):
        value = tokens[j].astype(f32)
        unit = value * lax.rsqrt(jnp.mean(value * value, axis=-1, keepdims=True) + norm_eps)
        normed_scr[j * rows : (j + 1) * rows, :] = (unit * gain).astype(bf16)
        grad_gain = grad_gain + jnp.sum(
            normed_grad[j * rows : (j + 1) * rows, :] * unit, axis=0, keepdims=True
        )
    gain_out[...] = jnp.broadcast_to(grad_gain, gain_out.shape)
    total_scr[:, :wide] = dot_tn(normed_scr[...], grad_projected)
    full = total_scr.shape[1]
    if m == 1:
        for t in range(n):
            share_out[0][t] = total_scr[t * part : (t + 1) * part, :wide].astype(bf16)
        share_out[1][...] = out_scr[...].astype(bf16)
        return
    piece = part // m
    total_scr[:, wide:] = jnp.zeros((width, full - wide), f32)
    size = 128
    for c in range(width // size):
        here = slice(c * size, (c + 1) * size)
        total_scr[here, wide : wide + 1] = to_column(grad_gain[:, here], size)
        total_scr[here, wide + 1 : wide + 2] = to_column(gain_two[0:1, here], size)
        total_scr[here, wide + 2 : wide + 2 + experts] = router[:, here].T
    at = wide + 2 + experts
    rest = (width - full) // n
    for t in range(n):
        total_scr[t * part : (t + 1) * part, at : at + rest] = out_scr[
            :, full + t * rest : full + (t + 1) * rest
        ]
    at = at + rest
    for d in range(m):
        total_scr[d * piece : d * piece + row_tile, at : at + heads * per_line] = table_total[
            :, : heads * per_line
        ]
    for d in range(m):
        target = share_out[(d & 1) + 2 * (d < m // 2)]
        place = (d >> 1) % (m // 4)
        start = (e ^ d) * piece
        for t in range(n):
            rows_at = pl.multiple_of(t * part + start, row_tile)
            target[place, t] = total_scr[pl.ds(rows_at, piece), :].astype(bf16)
        rows_at = pl.multiple_of(start, row_tile)
        target[place, n] = out_scr[pl.ds(rows_at, piece), :full].astype(bf16)


def beside_columns(ref, p, wide):
    last = ref[p, :, ref.shape[2] - 128 :]
    skip = wide - (ref.shape[2] - 128)
    return jnp.concatenate([last[:, skip:], last[:, :skip]], axis=1)


def assemble(n, m, part, piece, experts, *refs):
    total_out, out_out, one_out, two_out, router_out, small_scr = refs[m:]
    s = lax.axis_index("shard")
    e = lax.axis_index("expert")
    wide = 3 * part
    full = refs[0].shape[2]
    at = wide + 2 + experts
    rest = (n * part - full) // n
    for d in range(m):
        start = pl.multiple_of((e ^ d) * piece, row_tile)
        own = pl.ds(start, piece)
        small = jnp.zeros((piece, 128), f32)
        for p in range(n):
            small = small + beside_columns(refs[d], p, wide).astype(f32)
            out_out[own, full + p * rest : full + (p + 1) * rest] = refs[d][p, :, at : at + rest].astype(
                f32
            )
        out_out[own, :full] = refs[d][n].astype(f32)
        small_scr[own, :] = small
    small = small_scr[...].T
    one_out[...] = small[0:1, :]
    two_out[...] = small[1:2, :]
    router_out[...] = small[2 : 2 + experts, :]
    for k in range(n):

        @pl.when(s == k)
        def _():
            for d in range(m):
                own = pl.ds(pl.multiple_of((e ^ d) * piece, row_tile), piece)
                for p in range(n):
                    for kind in range(3):
                        to = (kind * n + (k ^ p)) * part
                        total_out[own, to : to + part] = refs[d][
                            p, :, kind * part : (kind + 1) * part
                        ].astype(f32)


def expert_forward(rows, own, came, up_own, up_pair, down_own, down_pair, *outs):
    hidden_out, slope_out, keep_out, send_out = outs
    source = jnp.concatenate([own[...], came[...]], axis=0)
    result = 0.0
    for k, (up, down) in enumerate(((up_own, down_own), (up_pair, down_pair))):
        before = dot(source, up[0])
        square = before * before
        tanh_value = jnp.tanh(gelu_scale * before * (1.0 + gelu_cubic * square))
        half = 0.5 * (1.0 + tanh_value)
        hidden = (before * half).astype(bf16)
        slope = half + 0.5 * before * (1.0 - tanh_value * tanh_value) * gelu_scale * (
            1.0 + 3.0 * gelu_cubic * square
        )
        hidden_out[k] = hidden
        slope_out[k] = slope.astype(bf16)
        result = result + dot(hidden, down[0])
    keep_out[...] = result[:rows]
    send_out[...] = result[rows:].astype(bf16)


def expert_backward(rows, own, came, up_own, up_pair, down_own, down_pair, slope, *outs):
    before_out, keep_out, send_out = outs
    grads = jnp.concatenate([own[...], came[...]], axis=0)
    result = 0.0
    for k, (up, down) in enumerate(((up_own, down_own), (up_pair, down_pair))):
        grad_before = (dot_nt(grads, down[0]) * slope[k].astype(f32)).astype(bf16)
        before_out[k] = grad_before
        result = result + dot_nt(grad_before, up[0])
    keep_out[...] = result[:rows]
    send_out[...] = result[rows:].astype(bf16)


def expert_weights(own, came, own_grad, came_grad, hidden, grad_before, *outs):
    up_out, down_out, up_send, down_send = outs
    grads = jnp.concatenate([own_grad[...], came_grad[...]], axis=0)
    rows = jnp.concatenate([own[...], came[...]], axis=0)
    up_send[0] = dot_tn(rows, grad_before[1]).astype(bf16)
    down_send[0] = dot_tn(hidden[1], grads).astype(bf16)
    up_out[0] = dot_tn(rows, grad_before[0])
    down_out[0] = dot_tn(hidden[0], grads)


def rms_factor(value):
    return lax.rsqrt(jnp.mean(value * value, axis=-1, keepdims=True) + norm_eps)


def rms_backward(value, factor, gain, upstream):
    scaled = upstream * gain
    grad_value = factor * scaled - value * factor * factor * factor * jnp.mean(
        scaled * value, axis=-1, keepdims=True
    )
    grad_gain = jnp.sum(upstream * value * factor, axis=0, keepdims=True)
    return (grad_value, grad_gain)


def local(
    tokens,
    lengths,
    routes,
    attention_in,
    attention_out,
    position_bias,
    first_gain,
    second_gain,
    router,
    expert_in,
    expert_out,
    cotangent,
):
    n = lax.axis_size("shard")
    m = lax.axis_size("expert")
    s = lax.axis_index("shard")
    e = lax.axis_index("expert")
    rows, width = tokens.shape
    heads, buckets = position_bias.shape
    part = width // n
    wide = 3 * part
    group = n * rows
    seqs = lengths.shape[1]
    experts = router.shape[1]
    direct = m == 8
    full = wide + -wide % 128
    micro = 10**9

    far_tokens, pair_tokens = swap(tokens, "shard", 2 * pair), swap(tokens, "shard", pair)
    weight_blocks = exchange_relative(
        call(
            lambda *refs: prepare_weight(n, part, *refs),
            [shape((part, full))] * n,
            (attention_in, jnp.stack([first_gain, second_gain])),
        ),
        "shard",
    )
    far_tokens, own_up, own_down, table_scalars = lax.optimization_barrier(
        (far_tokens, expert_in, expert_out, position_bias.astype(f32))
    )
    token_blocks = [tokens, pair_tokens, far_tokens, swap(far_tokens, "shard", pair)]
    pair_up = swap(own_up, "shard", pair)
    pair_down = swap(own_down, "shard", pair)
    own_out, token_blocks, weight_blocks = lax.optimization_barrier(
        (attention_out, token_blocks, weight_blocks)
    )
    far_out, pair_out = swap(own_out, "shard", 2 * pair), swap(own_out, "shard", pair)

    answers = call(
        lambda *refs: attention_forward(n, rows, width, heads, seqs, buckets, *refs),
        (
            shape((n, rows, width)),
            shape((width, full)),
            shape((group, wide)),
            shape((heads, group, group)),
            shape((row_tile, width), f32),
            shape((n, rows, part)),
            *[shape((rows, part))] * n,
        ),
        (lengths, table_scalars, *token_blocks, *weight_blocks),
        "ss",
        [pltpu.VMEM((group, width), bf16), pltpu.VMEM((group, group), f32)],
        work=10 * micro,
    )
    tokens_all, weight, projected, weights, gains, mixed = answers[:6]
    mixed_mine, pair_up, pair_down, far_out, pair_out = lax.optimization_barrier(
        (list(answers[6:]), pair_up, pair_down, far_out, pair_out)
    )
    mixed_blocks = exchange_relative(mixed_mine, "shard")
    out_blocks = [own_out, pair_out, far_out, swap(far_out, "shard", pair)]
    gain_one, gain_two = gains[0:1], gains[1:2]

    inputs = tokens.astype(f32)
    hidden_one = inputs + sum(dot(mixed_blocks[p], out_blocks[p]) for p in range(n))
    factor_two = rms_factor(hidden_one)
    normed_two = hidden_one * factor_two * gain_two
    logits = jnp.dot(
        normed_two, router, precision=lax.Precision.HIGHEST, preferred_element_type=f32
    )
    shifted = jnp.exp(logits - jnp.max(logits, axis=-1, keepdims=True))
    probs = shifted / jnp.sum(shifted, axis=-1, keepdims=True)
    route = routes[:, 0]
    chosen = (route[:, None] == lax.iota(jnp.int32, experts)[None, :]).astype(f32)
    gate = jnp.sum(probs * chosen, axis=1)
    lower = (lax.iota(jnp.int32, rows)[:, None] >= lax.iota(jnp.int32, rows)[None, :]).astype(bf16)
    running = dot(lower, chosen.astype(bf16))
    slot = jnp.sum((running - 1.0) * chosen, axis=1).astype(jnp.int32)
    capacity = max(2, 9 * rows // (8 * experts) + 1)
    capacity = -(-capacity // slot_tile) * slot_tile
    places = experts * capacity
    half = places // 2
    if direct:
        holder = route ^ e
        target = (holder & 1) * half + (holder >> 1) * capacity + slot
    else:
        target = route * capacity + slot
    collect = (target[:, None] == lax.iota(jnp.int32, places)[None, :]).astype(bf16)
    upstream = cotangent.astype(f32)
    grad_result = (gate[:, None] * upstream).astype(bf16)

    def plain(value):
        return lax.all_to_all(
            value.reshape(experts, capacity, width), "expert", 0, 0, tiled=True
        ).reshape(places, width)

    def send(value, after=None):
        if not direct:
            return plain(dot_tn(collect, value).astype(bf16))
        came = swap(dot_tn(collect[:, half:], value).astype(bf16), "expert", 1)
        own = dot_tn(collect[:, :half], value).astype(bf16).reshape(m // 2, capacity, width)
        both = jnp.concatenate([own, came.reshape(m // 2, capacity, width)], axis=1)
        if after is not None:
            both, _ = lax.optimization_barrier((both, after))
        blocks = [both[d] if d == 0 else swap(both[d], "expert", 2 * d) for d in range(m // 2)]
        return jnp.concatenate(blocks, axis=0)

    def give_back(value):
        if not direct:
            return dot(collect, plain(value)), value
        both = value.reshape(m // 2, 2 * capacity, width)
        blocks = [both[d] if d == 0 else swap(both[d], "expert", 2 * d) for d in range(m // 2)]
        own = jnp.concatenate([block[:capacity] for block in blocks])
        other = jnp.concatenate([block[capacity:] for block in blocks])
        other = swap(other, "expert", 1)
        return dot(collect[:, :half], own) + dot(collect[:, half:], other), own

    def reduce_shard(keep, out):
        return (keep + swap(out, "shard", 2 * pair).astype(f32)).astype(bf16)

    arrived = send(normed_two.astype(bf16))
    row_blocks = (arrived, swap(arrived, "shard", 2 * pair))
    arrived_grad = send(grad_result, arrived)
    grad_blocks = (arrived_grad, swap(arrived_grad, "shard", 2 * pair))

    units = expert_in.shape[2]
    expert_weight = (own_up, pair_up, own_down, pair_down)
    middle = shape((2, 2 * places, units))
    kept, sent = shape((places, width), f32), shape((places, width))
    hidden, slope, *forward = call(
        lambda *refs: expert_forward(places, *refs),
        (middle, middle, kept, sent),
        (*row_blocks, *expert_weight),
        work=6 * micro,
    )
    grad_before, *backward = call(
        lambda *refs: expert_backward(places, *refs),
        (middle, kept, sent),
        (*grad_blocks, *expert_weight, slope),
        work=6 * micro,
    )
    expert_result, first_back = give_back(reduce_shard(*forward))
    keep_grad, came_grad = backward[0], swap(backward[1], "shard", 2 * pair)
    came_grad, _ = lax.optimization_barrier((came_grad, first_back))
    grad_sent, _ = give_back((keep_grad + came_grad.astype(f32)).astype(bf16))

    layer_out = (hidden_one + gate[:, None] * expert_result).astype(bf16)
    grad_gate = jnp.sum(upstream * expert_result, axis=1)
    grad_logits = (grad_gate * gate)[:, None] * (chosen - probs)
    grad_router = lax.dot_general(
        grad_logits,
        normed_two,
        (((0,), (0,)), ((), ())),
        precision=lax.Precision.HIGHEST,
        preferred_element_type=f32,
    )
    grad_normed_two = grad_sent + lax.dot_general(
        grad_logits,
        router,
        (((1,), (1,)), ((), ())),
        precision=lax.Precision.HIGHEST,
        preferred_element_type=f32,
    )
    grad_middle, grad_gain_two = rms_backward(hidden_one, factor_two, gain_two, grad_normed_two)
    grad_hidden = upstream + grad_middle
    branch, late_rows = lax.optimization_barrier((grad_hidden.astype(bf16), row_blocks))
    grad_up, grad_down, up_send, down_send = call(
        expert_weights,
        (
            shape(expert_in.shape, f32),
            shape(expert_out.shape, f32),
            shape(expert_in.shape),
            shape(expert_out.shape),
        ),
        (
            *late_rows,
            *grad_blocks,
            hidden,
            grad_before,
        ),
        work=6 * micro,
    )
    far_branch, pair_branch = swap(branch, "shard", 2 * pair), swap(branch, "shard", pair)
    far_branch, grad_router, gain_two_row, up_send, down_send = lax.optimization_barrier(
        (far_branch, grad_router, grad_gain_two, up_send, down_send)
    )
    branch_blocks = [branch, pair_branch, far_branch, swap(far_branch, "shard", pair)]
    holders = m if direct else 1
    piece = part // m
    if direct:
        share_shapes = [shape((m // 4, n + 1, piece, full))] * 4
    else:
        share_shapes = [shape((n, part, wide)), shape((part, width))]
    answers = call(
        lambda *refs: attention_backward(n, holders, rows, width, heads, buckets, experts, *refs),
        (
            *share_shapes,
            *[shape((rows, width))] * n,
            shape((row_tile, width), f32),
            shape((row_tile, 128), f32),
        ),
        (
            projected,
            tokens_all,
            gains,
            weight,
            weights,
            mixed,
            own_out,
            gain_two_row,
            grad_router,
            *branch_blocks,
        ),
        "",
        [
            pltpu.VMEM((n, rows, width), bf16),
            pltpu.VMEM((group, group), bf16),
            pltpu.VMEM((group, wide), bf16),
            pltpu.VMEM((width, full), f32),
            pltpu.VMEM((part, width), f32),
            pltpu.VMEM((group, width), bf16),
            pltpu.VMEM((n, rows, width), bf16),
            pltpu.VMEM((group, group), f32),
        ],
        work=8 * micro,
    )
    shares = answers[: len(share_shapes)]
    normed_grads = answers[len(share_shapes) : len(share_shapes) + n]
    gain_row, table = answers[len(share_shapes) + n :]

    per_line = buckets // row_tile

    def biases(block):
        return block.reshape(row_tile, heads, per_line).swapaxes(0, 1).reshape(heads, buckets)

    def finish_tokens(blocks):
        grad_normed = sum(x.astype(f32) for x in exchange_relative(list(blocks), "shard"))
        grad_input_norm, _ = rms_backward(inputs, rms_factor(inputs), gain_one, grad_normed)
        return (grad_hidden + grad_input_norm).astype(bf16)

    if direct:
        far_keep, far_send, near_keep, near_send = shares
        far_came = swap(far_send, "expert", 1)
        far = far_keep.astype(f32) + far_came.astype(f32)
        normed_grads, far_came = lax.optimization_barrier((normed_grads, far_came))
        grad_tokens = finish_tokens(normed_grads)
        near = near_keep.astype(f32) + swap(near_send, "expert", 1).astype(f32)
        came = [swap(far[d].astype(bf16), "expert", m // 2 + 2 * d) for d in range(m // 4)]
        came += [swap(near[d].astype(bf16), "expert", 2 * d) for d in range(1, m // 4)]
        summed = near[0] + sum(x.astype(f32) for x in came)
        at = wide + 2 + experts
        rest = (width - full) // n
        table_total = biases(
            summed[0, :row_tile, at + rest : at + rest + heads * per_line]
        )
        low, grad_tokens = lax.optimization_barrier((summed.astype(bf16), grad_tokens))
        mine = exchange_relative(
            [lax.dynamic_index_in_dim(low, s ^ p, 0, keepdims=False) for p in range(n)], "shard"
        )
        lane = lax.iota(jnp.int32, full)[None, :]
        own_lane = (lane >= at) & (lane < at + rest)
        mine = jnp.stack(
            [jnp.where(own_lane, low[p], mine[p]) for p in range(n)] + [low[n]], axis=0
        )
        mine, up_send, down_send = lax.optimization_barrier((mine, up_send, down_send))
        blocks = {0: mine, 1: swap(mine, "expert", 1), 4: swap(mine, "expert", 4)}
        blocks[2] = swap(mine, "expert", 2)
        blocks[4], blocks[1] = lax.optimization_barrier((blocks[4], blocks[1]))
        blocks[6] = swap(blocks[4], "expert", 2)
        blocks[5] = swap(blocks[4], "expert", 1)
        blocks[3] = swap(blocks[2], "expert", 1)
        blocks[6], grad_up, grad_down = lax.optimization_barrier(
            (
                blocks[6],
                grad_up + swap(up_send, "shard", pair).astype(f32),
                grad_down + swap(down_send, "shard", pair).astype(f32),
            )
        )
        blocks[7] = swap(blocks[6], "expert", 1)
        blocks = [blocks[d] for d in range(m)]
        grad_attention_in, grad_attention_out, total_one, total_two, total_router = call(
            lambda *refs: assemble(n, m, part, piece, experts, *refs),
            (
                shape((part, 3 * width), f32),
                shape((part, width), f32),
                shape((1, part), f32),
                shape((1, part), f32),
                shape((experts, part), f32),
            ),
            (*blocks,),
            "",
            [pltpu.VMEM((part, 128), f32)],
        )
    else:
        grad_tokens = finish_tokens(normed_grads)
        grad_up = grad_up + swap(up_send, "shard", pair).astype(f32)
        grad_down = grad_down + swap(down_send, "shard", pair).astype(f32)
        came = lax.all_to_all(
            shares[0].reshape(n, m, piece, wide).swapaxes(0, 1), "expert", 0, 0, tiled=True
        )
        summed = sum(x.astype(f32) for x in came).astype(bf16)
        mine = lax.all_to_all(summed, "shard", 0, 0, tiled=True)
        mine = mine.reshape(n, piece, 3, part).transpose(1, 2, 0, 3).reshape(piece, 3 * width)
        came = lax.all_to_all(shares[1].reshape(m, piece, width), "expert", 0, 0, tiled=True)
        out_mine = sum(x.astype(f32) for x in came).astype(bf16)
        grad_attention_in = lax.all_gather(mine, "expert", axis=0, tiled=True).astype(f32)
        grad_attention_out = lax.all_gather(out_mine, "expert", axis=0, tiled=True).astype(f32)
        small = jnp.concatenate([gain_row[0:1], grad_gain_two, grad_router], axis=0)
        small_total = lax.psum_scatter(small, "shard", scatter_dimension=1, tiled=True)
        small_total, table_total = lax.psum(
            (small_total, biases(table[:, : heads * per_line])), "expert"
        )
        total_one, total_two, total_router = small_total[0:1], small_total[1:2], small_total[2:]
    return (
        layer_out,
        grad_tokens,
        grad_attention_in,
        grad_attention_out,
        table_total,
        total_one[0],
        total_two[0],
        total_router.T,
        grad_up,
        grad_down,
    )


def solution(mesh):
    in_specs = (
        P(("expert", "shard"), None),
        P("expert", None),
        P(("expert", "shard"), None),
        P("shard", None),
        P("shard", None),
        P("shard", None),
        P("shard"),
        P("shard"),
        P(),
        P("expert", None, "shard"),
        P("expert", "shard", None),
        P(("expert", "shard"), None),
    )
    out_specs = (
        P(("expert", "shard"), None),
        P(("expert", "shard"), None),
        P("shard", None),
        P("shard", None),
        P("shard", None),
        P("shard"),
        P("shard"),
        P("shard", None),
        P("expert", None, "shard"),
        P("expert", "shard", None),
    )
    return jax.shard_map(local, mesh=mesh, in_specs=in_specs, out_specs=out_specs, check_vma=False)
```

```python
import jax
import jax.numpy as jnp
from jax import lax
from jax.experimental import pallas as pl
from jax.experimental.pallas import tpu as pltpu
from jax.sharding import PartitionSpec as P

norm_eps = 1e-06
gelu_scale = 0.7978845608028654
gelu_cubic = 0.044715
big_negative = -1e30
near_steps = 8
far_steps = (12, 16, 23, 32, 46, 64, 91)
bf16 = jnp.bfloat16
f32 = jnp.float32
row_tile = 8
pair = 1
slot_tile = 4


def bucket_index(offset):
    distance = jnp.abs(offset)
    far_level = jnp.full_like(distance, near_steps)
    for step_edge in far_steps:
        far_level = far_level + (distance >= step_edge).astype(jnp.int32)
    near = jnp.where(distance < near_steps, distance, far_level)
    return near + 16 * (offset > 0).astype(jnp.int32)


def dot(left, right):
    return jnp.dot(left, right, preferred_element_type=f32)


def dot_nt(left, right):
    return lax.dot_general(left, right, (((1,), (1,)), ((), ())), preferred_element_type=f32)


def dot_tn(left, right):
    return lax.dot_general(left, right, (((0,), (0,)), ((), ())), preferred_element_type=f32)


def swap(value, axis, bit):
    size = lax.axis_size(axis)
    return lax.ppermute(value, axis, [(i, i ^ bit) for i in range(size)])


def gather_relative(value, axis):
    blocks = [value]
    bit = lax.axis_size(axis) // 2
    parts = {0: value}
    while bit:
        for p in list(parts):
            parts[p ^ bit] = swap(parts[p], axis, bit)
        bit //= 2
    return [parts[p] for p in range(lax.axis_size(axis))]


def exchange_relative(blocks, axis):
    return [blocks[0]] + [swap(block, axis, p) for p, block in enumerate(blocks) if p]


def call(kernel, out_shape, operands, spaces="", scratch=(), work=0):
    vmem = pl.BlockSpec(memory_space=pltpu.VMEM)
    smem = pl.BlockSpec(memory_space=pltpu.SMEM)
    in_specs = [smem if spaces[i : i + 1] == "s" else vmem for i in range(len(operands))]
    return pl.pallas_call(
        kernel,
        out_shape=out_shape,
        in_specs=in_specs,
        out_specs=jax.tree.map(lambda _: vmem, out_shape),
        scratch_shapes=list(scratch),
        compiler_params=pltpu.CompilerParams(vmem_limit_bytes=56 * 2**20),
        cost_estimate=pl.CostEstimate(flops=work, bytes_accessed=0, transcendentals=0),
    )(*operands)


def shape(dims, dtype=bf16):
    return jax.ShapeDtypeStruct(tuple(dims), dtype)


def diagonal(size):
    return lax.broadcasted_iota(jnp.int32, (size, size), 0) == lax.broadcasted_iota(
        jnp.int32, (size, size), 1
    )


def to_column(row, size):
    return jnp.sum(jnp.where(diagonal(size), row, 0.0), axis=1, keepdims=True)


def to_row(column, size):
    return jnp.sum(jnp.where(diagonal(size), column, 0.0), axis=0, keepdims=True)


def prepare_weight(n, part, weight, gains, *outs):
    wide = 3 * part
    s = lax.axis_index("shard")
    extra = outs[0].shape[1] - wide
    one, two = (to_column(gains[i : i + 1, :].astype(f32), part) for i in range(2))
    lane = lax.broadcasted_iota(jnp.int32, (part, extra), 1)
    beside = jnp.where(lane == 0, one, jnp.where(lane == 1, two, 0.0)).astype(bf16)
    for p in range(n):
        outs[p][:, wide:] = beside
    for k in range(n):

        @pl.when(s == k)
        def _():
            for p in range(n):
                for kind in range(3):
                    at = (kind * n + (k ^ p)) * part
                    outs[p][:, kind * part : (kind + 1) * part] = weight[:, at : at + part]


def offsets(rows):
    return lax.broadcasted_iota(jnp.int32, (rows, rows), 1) - lax.broadcasted_iota(
        jnp.int32, (rows, rows), 0
    )


def near_buckets(diff, buckets):
    if diff == 0:
        return range(buckets)
    return range(buckets // 2, buckets) if diff > 0 else range(buckets // 2)


def attention_forward(n, rows, width, heads, seqs, buckets, *refs):
    lengths, table = refs[:2]
    token_refs = refs[2 : 2 + n]
    weight_refs = refs[2 + n : 2 + 2 * n]
    tokens_out, weight_out, projected_out, weights_out, *gains_out, mixed_all = refs[
        2 + 2 * n : 9 + 2 * n
    ]
    mixed_out = refs[9 + 2 * n : 9 + 3 * n]
    normed_scr, scores_scr = refs[9 + 3 * n :]
    s = lax.axis_index("shard")
    part = width // n
    wide = 3 * part
    head_dim = part // heads
    for p in range(n):
        tokens_out[s ^ p] = token_refs[p][...]
        weight_out[pl.ds(pl.multiple_of((s ^ p) * part, part & -part), part), :] = weight_refs[p][...]
    size = 128
    for c in range(width // size):
        beside = weight_out[c * size : (c + 1) * size, wide:].astype(f32)
        for i in range(2):
            gains_out[i][:, c * size : (c + 1) * size] = to_row(beside[:, i : i + 1], size)
    gain = gains_out[0][...]
    for j in range(n):
        value = tokens_out[j].astype(f32)
        factor = lax.rsqrt(jnp.mean(value * value, axis=-1, keepdims=True) + norm_eps)
        normed_scr[j * rows : (j + 1) * rows, :] = (value * factor * gain).astype(bf16)
    projected_out[...] = dot(normed_scr[...], weight_out[:, :wide]).astype(bf16)
    total_rows = n * rows
    key_place = lax.broadcasted_iota(jnp.int32, (1, total_rows), 1)
    key_segment = jnp.zeros((1, total_rows), jnp.int32)
    end = jnp.int32(0)
    ends = []
    for j in range(seqs):
        end = end + lengths[0, j]
        ends.append(end)
        key_segment = key_segment + (key_place >= end).astype(jnp.int32)
    base = offsets(rows)
    steps = {diff: bucket_index(base + diff * rows) for diff in (-1, 0, 1)}
    for h in range(heads):
        query = projected_out[:, h * head_dim : (h + 1) * head_dim]
        key = projected_out[:, part + h * head_dim : part + (h + 1) * head_dim]
        value = projected_out[:, 2 * part + h * head_dim : 2 * part + (h + 1) * head_dim]
        bias = {}
        for diff in (-1, 0, 1):
            block = jnp.zeros((rows, rows), f32)
            for b in near_buckets(diff, buckets):
                block = jnp.where(steps[diff] == b, table[h, b], block)
            bias[diff] = block
        low_side = jnp.full((rows, rows), table[h, buckets // 2 - 1], f32)
        high_side = jnp.full((rows, rows), table[h, buckets - 1], f32)
        scores_scr[...] = dot_nt(query, key)
        for i in range(n):
            scores = scores_scr[i * rows : (i + 1) * rows, :]
            side = [
                bias[j - i] if abs(j - i) <= 1 else (high_side if j > i else low_side)
                for j in range(n)
            ]
            scores = scores + jnp.concatenate(side, axis=1)
            query_place = i * rows + lax.broadcasted_iota(jnp.int32, (rows, 1), 0)
            query_segment = jnp.zeros((rows, 1), jnp.int32)
            for j in range(seqs):
                query_segment = query_segment + (query_place >= ends[j]).astype(jnp.int32)
            scores = jnp.where(query_segment == key_segment, scores, big_negative)
            top = jnp.max(scores, axis=-1, keepdims=True)
            raised = jnp.exp(scores - top)
            total = jnp.sum(raised, axis=-1, keepdims=True)
            weights = (raised * (1.0 / total)).astype(bf16)
            weights_out[h, i * rows : (i + 1) * rows, :] = weights
        mixed_all[:, :, h * head_dim : (h + 1) * head_dim] = (
            dot(weights_out[h], value).astype(bf16).reshape(n, rows, head_dim)
        )
    for p in range(n):
        mixed_out[p][...] = mixed_all[s ^ p]


def attention_backward(n, m, rows, width, heads, buckets, experts, *refs):
    projected, tokens, gains, weight, weights, mixed, weight_out, gain_two, router = refs[:9]
    branch_refs = refs[9 : 9 + n]
    at = 9 + n
    shares = 4 if m > 1 else 2
    share_out = refs[at : at + shares]
    normed_grad_out = refs[at + shares : at + shares + n]
    gain_out, table_out = refs[at + shares + n : at + shares + n + 2]
    branch_scr, scores_scr, projected_scr, total_scr, out_scr, normed_scr, send_scr, weights_scr = (
        refs[at + shares + n + 2 :]
    )
    s = lax.axis_index("shard")
    e = lax.axis_index("expert")
    part = width // n
    wide = 3 * part
    group = n * rows
    head_dim = part // heads
    for p in range(n):
        branch_scr[s ^ p] = branch_refs[p][...]
    branch = branch_scr[...].reshape(group, width)
    grad_mixed = dot_nt(branch, weight_out[...]).astype(bf16)
    out_scr[...] = dot_tn(mixed[...].reshape(group, part), branch)
    base = offsets(rows)
    steps = {diff: bucket_index(base + diff * rows) for diff in (-1, 0, 1)}
    lane = lax.broadcasted_iota(jnp.int32, (row_tile, 128), 1)
    line = lax.broadcasted_iota(jnp.int32, (row_tile, 128), 0)
    table_total = jnp.zeros((row_tile, 128), f32)
    per_line = buckets // row_tile
    for h in range(heads):
        query = projected[:, h * head_dim : (h + 1) * head_dim]
        key = projected[:, part + h * head_dim : part + (h + 1) * head_dim]
        value = projected[:, 2 * part + h * head_dim : 2 * part + (h + 1) * head_dim]
        near = {diff: jnp.zeros((rows, rows), f32) for diff in (-1, 0, 1)}
        low_side = jnp.zeros((1, rows), f32)
        high_side = jnp.zeros((1, rows), f32)
        upstream = grad_mixed[:, h * head_dim : (h + 1) * head_dim]
        weights_scr[...] = dot_nt(upstream, value)
        for i in range(n):
            weights_i = weights[h, i * rows : (i + 1) * rows, :].astype(f32)
            grad_weights = weights_scr[i * rows : (i + 1) * rows, :]
            inner = jnp.sum(weights_i * grad_weights, axis=-1, keepdims=True)
            grad_scores = weights_i * (grad_weights - inner)
            scores_scr[i * rows : (i + 1) * rows, :] = grad_scores.astype(bf16)
            for j in range(n):
                block = grad_scores[:, j * rows : (j + 1) * rows]
                if abs(j - i) <= 1:
                    near[j - i] = near[j - i] + block
                elif j > i:
                    high_side = high_side + jnp.sum(block, axis=0, keepdims=True)
                else:
                    low_side = low_side + jnp.sum(block, axis=0, keepdims=True)
        for b in range(buckets):
            amount = jnp.zeros((1, rows), f32)
            for diff in (-1, 0, 1):
                if b in near_buckets(diff, buckets):
                    amount = amount + jnp.sum(
                        jnp.where(steps[diff] == b, near[diff], 0.0), axis=0, keepdims=True
                    )
            if b == buckets - 1:
                amount = amount + high_side
            if b == buckets // 2 - 1:
                amount = amount + low_side
            amount = jnp.sum(amount, axis=1, keepdims=True)
            spot = (line == b // per_line) & (lane == h * per_line + b % per_line)
            table_total = jnp.where(spot, amount, table_total)
        grad_scores_all = scores_scr[...]
        projected_scr[:, h * head_dim : (h + 1) * head_dim] = dot(grad_scores_all, key).astype(bf16)
        projected_scr[:, part + h * head_dim : part + (h + 1) * head_dim] = (
            dot_tn(query, grad_scores_all).T.astype(bf16)
        )
        projected_scr[:, 2 * part + h * head_dim : 2 * part + (h + 1) * head_dim] = (
            dot_tn(upstream, weights[h]).T.astype(bf16)
        )
    table_out[...] = table_total
    grad_projected = projected_scr[...]
    normed_grad = dot_nt(grad_projected, weight[:, :wide])
    send_scr[...] = normed_grad.astype(bf16).reshape(n, rows, width)
    for p in range(n):
        normed_grad_out[p][...] = send_scr[s ^ p]
    gain = gains[...]
    grad_gain = jnp.zeros((1, width), f32)
    for j in range(n):
        value = tokens[j].astype(f32)
        unit = value * lax.rsqrt(jnp.mean(value * value, axis=-1, keepdims=True) + norm_eps)
        normed_scr[j * rows : (j + 1) * rows, :] = (unit * gain).astype(bf16)
        grad_gain = grad_gain + jnp.sum(
            normed_grad[j * rows : (j + 1) * rows, :] * unit, axis=0, keepdims=True
        )
    gain_out[...] = jnp.broadcast_to(grad_gain, gain_out.shape)
    total_scr[:, :wide] = dot_tn(normed_scr[...], grad_projected)
    full = total_scr.shape[1]
    if m == 1:
        for t in range(n):
            share_out[0][t] = total_scr[t * part : (t + 1) * part, :wide].astype(bf16)
        share_out[1][...] = out_scr[...].astype(bf16)
        return
    piece = part // m
    total_scr[:, wide:] = jnp.zeros((width, full - wide), f32)
    size = 128
    for c in range(width // size):
        here = slice(c * size, (c + 1) * size)
        total_scr[here, wide : wide + 1] = to_column(grad_gain[:, here], size)
        total_scr[here, wide + 1 : wide + 2] = to_column(gain_two[0:1, here], size)
        total_scr[here, wide + 2 : wide + 2 + experts] = router[:, here].T
    at = wide + 2 + experts
    rest = (width - full) // n
    for t in range(n):
        total_scr[t * part : (t + 1) * part, at : at + rest] = out_scr[
            :, full + t * rest : full + (t + 1) * rest
        ]
    at = at + rest
    for d in range(m):
        total_scr[d * piece : d * piece + row_tile, at : at + heads * per_line] = table_total[
            :, : heads * per_line
        ]
    for d in range(m):
        target = share_out[(d & 1) + 2 * (d < m // 2)]
        place = (d >> 1) % (m // 4)
        start = (e ^ d) * piece
        for t in range(n):
            rows_at = pl.multiple_of(t * part + start, row_tile)
            target[place, t] = total_scr[pl.ds(rows_at, piece), :].astype(bf16)
        rows_at = pl.multiple_of(start, row_tile)
        target[place, n] = out_scr[pl.ds(rows_at, piece), :full].astype(bf16)


def beside_columns(ref, p, wide):
    last = ref[p, :, ref.shape[2] - 128 :]
    skip = wide - (ref.shape[2] - 128)
    return jnp.concatenate([last[:, skip:], last[:, :skip]], axis=1)


def assemble(n, m, part, piece, experts, *refs):
    total_out, out_out, one_out, two_out, router_out, small_scr = refs[m:]
    s = lax.axis_index("shard")
    e = lax.axis_index("expert")
    wide = 3 * part
    full = refs[0].shape[2]
    at = wide + 2 + experts
    rest = (n * part - full) // n
    for d in range(m):
        start = pl.multiple_of((e ^ d) * piece, row_tile)
        own = pl.ds(start, piece)
        small = jnp.zeros((piece, 128), f32)
        for p in range(n):
            small = small + beside_columns(refs[d], p, wide).astype(f32)
            out_out[own, full + p * rest : full + (p + 1) * rest] = refs[d][p, :, at : at + rest].astype(
                f32
            )
        out_out[own, :full] = refs[d][n].astype(f32)
        small_scr[own, :] = small
    small = small_scr[...].T
    one_out[...] = small[0:1, :]
    two_out[...] = small[1:2, :]
    router_out[...] = small[2 : 2 + experts, :]
    for k in range(n):

        @pl.when(s == k)
        def _():
            for d in range(m):
                own = pl.ds(pl.multiple_of((e ^ d) * piece, row_tile), piece)
                for p in range(n):
                    for kind in range(3):
                        to = (kind * n + (k ^ p)) * part
                        total_out[own, to : to + part] = refs[d][
                            p, :, kind * part : (kind + 1) * part
                        ].astype(f32)


def expert_forward(rows, own, came, up_own, up_pair, down_own, down_pair, *outs):
    hidden_out, slope_out, keep_out, send_out = outs
    source = jnp.concatenate([own[...], came[...]], axis=0)
    result = 0.0
    for k, (up, down) in enumerate(((up_own, down_own), (up_pair, down_pair))):
        before = dot(source, up[0])
        square = before * before
        tanh_value = jnp.tanh(gelu_scale * before * (1.0 + gelu_cubic * square))
        half = 0.5 * (1.0 + tanh_value)
        hidden = (before * half).astype(bf16)
        slope = half + 0.5 * before * (1.0 - tanh_value * tanh_value) * gelu_scale * (
            1.0 + 3.0 * gelu_cubic * square
        )
        hidden_out[k] = hidden
        slope_out[k] = slope.astype(bf16)
        result = result + dot(hidden, down[0])
    keep_out[...] = result[:rows]
    send_out[...] = result[rows:].astype(bf16)


def expert_backward(rows, own, came, up_own, up_pair, down_own, down_pair, slope, *outs):
    before_out, keep_out, send_out = outs
    grads = jnp.concatenate([own[...], came[...]], axis=0)
    result = 0.0
    for k, (up, down) in enumerate(((up_own, down_own), (up_pair, down_pair))):
        grad_before = (dot_nt(grads, down[0]) * slope[k].astype(f32)).astype(bf16)
        before_out[k] = grad_before
        result = result + dot_nt(grad_before, up[0])
    keep_out[...] = result[:rows]
    send_out[...] = result[rows:].astype(bf16)


def weights_to_send(own, came, own_grad, came_grad, hidden, grad_before, up_send, down_send):
    grads = jnp.concatenate([own_grad[...], came_grad[...]], axis=0)
    rows = jnp.concatenate([own[...], came[...]], axis=0)
    up_send[0] = dot_tn(rows, grad_before[1]).astype(bf16)
    down_send[0] = dot_tn(hidden[1], grads).astype(bf16)


def weights_to_keep(
    own, came, own_grad, came_grad, hidden, grad_before, up_came, down_came, up_out, down_out
):
    grads = jnp.concatenate([own_grad[...], came_grad[...]], axis=0)
    rows = jnp.concatenate([own[...], came[...]], axis=0)
    up_out[0] = dot_tn(rows, grad_before[0]) + up_came[0].astype(f32)
    down_out[0] = dot_tn(hidden[0], grads) + down_came[0].astype(f32)


def rms_factor(value):
    return lax.rsqrt(jnp.mean(value * value, axis=-1, keepdims=True) + norm_eps)


def rms_backward(value, factor, gain, upstream):
    scaled = upstream * gain
    grad_value = factor * scaled - value * factor * factor * factor * jnp.mean(
        scaled * value, axis=-1, keepdims=True
    )
    grad_gain = jnp.sum(upstream * value * factor, axis=0, keepdims=True)
    return (grad_value, grad_gain)


def local(
    tokens,
    lengths,
    routes,
    attention_in,
    attention_out,
    position_bias,
    first_gain,
    second_gain,
    router,
    expert_in,
    expert_out,
    cotangent,
):
    n = lax.axis_size("shard")
    m = lax.axis_size("expert")
    s = lax.axis_index("shard")
    e = lax.axis_index("expert")
    rows, width = tokens.shape
    heads, buckets = position_bias.shape
    part = width // n
    wide = 3 * part
    group = n * rows
    seqs = lengths.shape[1]
    experts = router.shape[1]
    direct = m == 8
    full = wide + -wide % 128
    micro = 10**9

    far_tokens, pair_tokens = swap(tokens, "shard", 2 * pair), swap(tokens, "shard", pair)
    weight_blocks = exchange_relative(
        call(
            lambda *refs: prepare_weight(n, part, *refs),
            [shape((part, full))] * n,
            (attention_in, jnp.stack([first_gain, second_gain])),
        ),
        "shard",
    )
    far_tokens, own_up, own_down, table_scalars = lax.optimization_barrier(
        (far_tokens, expert_in, expert_out, position_bias.astype(f32))
    )
    token_blocks = [tokens, pair_tokens, far_tokens, swap(far_tokens, "shard", pair)]
    pair_up = swap(own_up, "shard", pair)
    pair_down = swap(own_down, "shard", pair)
    own_out, token_blocks, weight_blocks = lax.optimization_barrier(
        (attention_out, token_blocks, weight_blocks)
    )
    far_out, pair_out = swap(own_out, "shard", 2 * pair), swap(own_out, "shard", pair)

    answers = call(
        lambda *refs: attention_forward(n, rows, width, heads, seqs, buckets, *refs),
        (
            shape((n, rows, width)),
            shape((width, full)),
            shape((group, wide)),
            shape((heads, group, group)),
            shape((1, width), f32),
            shape((1, width), f32),
            shape((n, rows, part)),
            *[shape((rows, part))] * n,
        ),
        (lengths, table_scalars, *token_blocks, *weight_blocks),
        "ss",
        [pltpu.VMEM((group, width), bf16), pltpu.VMEM((group, group), f32)],
        work=10 * micro,
    )
    tokens_all, weight, projected, weights, gain_one, gain_two, mixed = answers[:7]
    mixed_mine, pair_up, pair_down, far_out, pair_out = lax.optimization_barrier(
        (list(answers[7:]), pair_up, pair_down, far_out, pair_out)
    )
    mixed_blocks = exchange_relative(mixed_mine, "shard")
    out_blocks = [own_out, pair_out, far_out, swap(far_out, "shard", pair)]

    inputs = tokens.astype(f32)
    hidden_one = inputs + sum(dot(mixed_blocks[p], out_blocks[p]) for p in range(n))
    factor_two = rms_factor(hidden_one)
    normed_two = hidden_one * factor_two * gain_two
    logits = jnp.dot(
        normed_two, router, precision=lax.Precision.HIGHEST, preferred_element_type=f32
    )
    shifted = jnp.exp(logits - jnp.max(logits, axis=-1, keepdims=True))
    probs = shifted / jnp.sum(shifted, axis=-1, keepdims=True)
    route = routes[:, 0]
    chosen = (route[:, None] == lax.iota(jnp.int32, experts)[None, :]).astype(f32)
    gate = jnp.sum(probs * chosen, axis=1)
    lower = (lax.iota(jnp.int32, rows)[:, None] >= lax.iota(jnp.int32, rows)[None, :]).astype(bf16)
    running = dot(lower, chosen.astype(bf16))
    slot = jnp.sum((running - 1.0) * chosen, axis=1).astype(jnp.int32)
    capacity = max(2, 9 * rows // (8 * experts) + 1)
    capacity = -(-capacity // slot_tile) * slot_tile
    places = experts * capacity
    half = places // 2
    if direct:
        holder = route ^ e
        target = (holder & 1) * half + (holder >> 1) * capacity + slot
    else:
        target = route * capacity + slot
    collect = (target[:, None] == lax.iota(jnp.int32, places)[None, :]).astype(bf16)
    upstream = cotangent.astype(f32)
    grad_result = (gate[:, None] * upstream).astype(bf16)

    def plain(value):
        return lax.all_to_all(
            value.reshape(experts, capacity, width), "expert", 0, 0, tiled=True
        ).reshape(places, width)

    def dispatch(forward, backward):
        if not direct:
            return [plain(dot_tn(collect, x).astype(bf16)) for x in (forward, backward)]
        value = jnp.concatenate([forward, backward], axis=1)
        came = swap(dot_tn(collect[:, half:], value).astype(bf16), "expert", 1)
        own = dot_tn(collect[:, :half], value).astype(bf16).reshape(m // 2, capacity, 2 * width)
        both = jnp.concatenate([own, came.reshape(m // 2, capacity, 2 * width)], axis=1)
        blocks = [both[d] if d == 0 else swap(both[d], "expert", 2 * d) for d in range(m // 2)]
        return [
            jnp.concatenate([block[:, i * width : (i + 1) * width] for block in blocks], axis=0)
            for i in range(2)
        ]

    def among_pairs(value):
        both = value.reshape(m // 2, 2 * capacity, width)
        return [both[d] if d == 0 else swap(both[d], "expert", 2 * d) for d in range(m // 2)]

    def give_back(forward, backward):
        if not direct:
            return [dot(collect, plain(x)) for x in (forward, backward)]
        blocks = [among_pairs(forward)]
        backward, _ = lax.optimization_barrier((backward, blocks[0]))
        blocks.append(among_pairs(backward))
        own, other = (
            jnp.concatenate(
                [jnp.concatenate([x[at : at + capacity] for x in side]) for side in blocks], axis=1
            )
            for at in (0, capacity)
        )
        total = dot(collect[:, :half], own) + dot(collect[:, half:], swap(other, "expert", 1))
        return total[:, :width], total[:, width:]

    def reduce_shard(keep, out, after=None):
        came = swap(out, "shard", 2 * pair)
        if after is not None:
            came, _ = lax.optimization_barrier((came, after))
        return (keep + came.astype(f32)).astype(bf16)

    arrived, arrived_grad = dispatch(normed_two.astype(bf16), grad_result)
    came = swap(arrived, "shard", 2 * pair)
    came, arrived_grad = lax.optimization_barrier((came, arrived_grad))
    row_blocks = (arrived, came)
    grad_blocks = (arrived_grad, swap(arrived_grad, "shard", 2 * pair))

    units = expert_in.shape[2]
    expert_weight = (own_up, pair_up, own_down, pair_down)
    middle = shape((2, 2 * places, units))
    kept, sent = shape((places, width), f32), shape((places, width))
    hidden, slope, *forward = call(
        lambda *refs: expert_forward(places, *refs),
        (middle, middle, kept, sent),
        (*row_blocks, *expert_weight),
        work=6 * micro,
    )
    grad_before, *backward = call(
        lambda *refs: expert_backward(places, *refs),
        (middle, kept, sent),
        (*grad_blocks, *expert_weight, slope),
        work=6 * micro,
    )
    expert_result, grad_sent = give_back(
        reduce_shard(*forward, backward[1]), reduce_shard(*backward)
    )

    layer_out = (hidden_one + gate[:, None] * expert_result).astype(bf16)
    grad_gate = jnp.sum(upstream * expert_result, axis=1)
    grad_logits = (grad_gate * gate)[:, None] * (chosen - probs)
    grad_router = lax.dot_general(
        grad_logits,
        normed_two,
        (((0,), (0,)), ((), ())),
        precision=lax.Precision.HIGHEST,
        preferred_element_type=f32,
    )
    grad_normed_two = grad_sent + lax.dot_general(
        grad_logits,
        router,
        (((1,), (1,)), ((), ())),
        precision=lax.Precision.HIGHEST,
        preferred_element_type=f32,
    )
    grad_middle, grad_gain_two = rms_backward(hidden_one, factor_two, gain_two, grad_normed_two)
    grad_hidden = upstream + grad_middle
    branch, late_rows = lax.optimization_barrier((grad_hidden.astype(bf16), row_blocks))
    sources = (*grad_blocks, hidden, grad_before)
    up_send, down_send = call(
        weights_to_send,
        (shape(expert_in.shape), shape(expert_out.shape)),
        (*late_rows, *sources),
        work=4 * micro,
    )
    far_branch, pair_branch = swap(branch, "shard", 2 * pair), swap(branch, "shard", pair)
    far_branch, grad_router, gain_two_row, up_send, down_send = lax.optimization_barrier(
        (far_branch, grad_router, grad_gain_two, up_send, down_send)
    )
    branch_blocks = [branch, pair_branch, far_branch, swap(far_branch, "shard", pair)]
    branch_blocks, up_send, down_send = lax.optimization_barrier(
        (branch_blocks, up_send, down_send)
    )
    up_came, down_came = swap(up_send, "shard", pair), swap(down_send, "shard", pair)
    holders = m if direct else 1
    piece = part // m
    if direct:
        share_shapes = [shape((m // 4, n + 1, piece, full))] * 4
    else:
        share_shapes = [shape((n, part, wide)), shape((part, width))]
    answers = call(
        lambda *refs: attention_backward(n, holders, rows, width, heads, buckets, experts, *refs),
        (
            *share_shapes,
            *[shape((rows, width))] * n,
            shape((row_tile, width), f32),
            shape((row_tile, 128), f32),
        ),
        (
            projected,
            tokens_all,
            gain_one,
            weight,
            weights,
            mixed,
            own_out,
            gain_two_row,
            grad_router,
            *branch_blocks,
        ),
        "",
        [
            pltpu.VMEM((n, rows, width), bf16),
            pltpu.VMEM((group, group), bf16),
            pltpu.VMEM((group, wide), bf16),
            pltpu.VMEM((width, full), f32),
            pltpu.VMEM((part, width), f32),
            pltpu.VMEM((group, width), bf16),
            pltpu.VMEM((n, rows, width), bf16),
            pltpu.VMEM((group, group), f32),
        ],
        work=8 * micro,
    )
    shares = answers[: len(share_shapes)]
    normed_grads = answers[len(share_shapes) : len(share_shapes) + n]
    gain_row, table = answers[len(share_shapes) + n :]
    late_rows, normed_grads = lax.optimization_barrier((row_blocks, list(normed_grads)))
    grad_up, grad_down = call(
        weights_to_keep,
        (shape(expert_in.shape, f32), shape(expert_out.shape, f32)),
        (*late_rows, *sources, up_came, down_came),
        work=4 * micro,
    )
    per_line = buckets // row_tile

    def biases(block):
        return block.reshape(row_tile, heads, per_line).swapaxes(0, 1).reshape(heads, buckets)

    def finish_tokens(blocks):
        grad_normed = sum(x.astype(f32) for x in exchange_relative(list(blocks), "shard"))
        grad_input_norm, _ = rms_backward(inputs, rms_factor(inputs), gain_one, grad_normed)
        return (grad_hidden + grad_input_norm).astype(bf16)

    if direct:
        far_keep, far_send, near_keep, near_send = shares
        far_came = swap(far_send, "expert", 1)
        far_came, near_send, grad_up, grad_down = lax.optimization_barrier(
            (far_came, near_send, grad_up, grad_down)
        )
        far = far_keep.astype(f32) + far_came.astype(f32)
        near_came, normed_grads = lax.optimization_barrier(
            (swap(near_send, "expert", 1), normed_grads)
        )
        near = near_keep.astype(f32) + near_came.astype(f32)
        grad_tokens = finish_tokens(normed_grads)
        came = [swap(far[d].astype(bf16), "expert", m // 2 + 2 * d) for d in range(m // 4)]
        came += [swap(near[d].astype(bf16), "expert", 2 * d) for d in range(1, m // 4)]
        summed = near[0] + sum(x.astype(f32) for x in came)
        at = wide + 2 + experts
        rest = (width - full) // n
        table_total = biases(
            summed[0, :row_tile, at + rest : at + rest + heads * per_line]
        )
        low, grad_tokens = lax.optimization_barrier((summed.astype(bf16), grad_tokens))
        mine = exchange_relative(
            [lax.dynamic_index_in_dim(low, s ^ p, 0, keepdims=False) for p in range(n)], "shard"
        )
        lane = lax.iota(jnp.int32, full)[None, :]
        own_lane = (lane >= at) & (lane < at + rest)
        mine = jnp.stack(
            [jnp.where(own_lane, low[p], mine[p]) for p in range(n)] + [low[n]], axis=0
        )
        blocks = {0: mine, 1: swap(mine, "expert", 1), 4: swap(mine, "expert", 4)}
        blocks[2] = swap(mine, "expert", 2)
        blocks[2], blocks[1] = lax.optimization_barrier((blocks[2], blocks[1]))
        blocks[3] = swap(blocks[2], "expert", 1)
        blocks[4], blocks[3] = lax.optimization_barrier((blocks[4], blocks[3]))
        blocks[6] = swap(blocks[4], "expert", 2)
        blocks[5] = swap(blocks[4], "expert", 1)
        blocks[7] = swap(blocks[6], "expert", 1)
        blocks = [blocks[d] for d in range(m)]
        grad_attention_in, grad_attention_out, total_one, total_two, total_router = call(
            lambda *refs: assemble(n, m, part, piece, experts, *refs),
            (
                shape((part, 3 * width), f32),
                shape((part, width), f32),
                shape((1, part), f32),
                shape((1, part), f32),
                shape((experts, part), f32),
            ),
            (*blocks,),
            "",
            [pltpu.VMEM((part, 128), f32)],
        )
    else:
        grad_tokens = finish_tokens(normed_grads)
        came = lax.all_to_all(
            shares[0].reshape(n, m, piece, wide).swapaxes(0, 1), "expert", 0, 0, tiled=True
        )
        summed = sum(x.astype(f32) for x in came).astype(bf16)
        mine = lax.all_to_all(summed, "shard", 0, 0, tiled=True)
        mine = mine.reshape(n, piece, 3, part).transpose(1, 2, 0, 3).reshape(piece, 3 * width)
        came = lax.all_to_all(shares[1].reshape(m, piece, width), "expert", 0, 0, tiled=True)
        out_mine = sum(x.astype(f32) for x in came).astype(bf16)
        grad_attention_in = lax.all_gather(mine, "expert", axis=0, tiled=True).astype(f32)
        grad_attention_out = lax.all_gather(out_mine, "expert", axis=0, tiled=True).astype(f32)
        small = jnp.concatenate([gain_row[0:1], grad_gain_two, grad_router], axis=0)
        small_total = lax.psum_scatter(small, "shard", scatter_dimension=1, tiled=True)
        small_total, table_total = lax.psum(
            (small_total, biases(table[:, : heads * per_line])), "expert"
        )
        total_one, total_two, total_router = small_total[0:1], small_total[1:2], small_total[2:]
    return (
        layer_out,
        grad_tokens,
        grad_attention_in,
        grad_attention_out,
        table_total,
        total_one[0],
        total_two[0],
        total_router.T,
        grad_up,
        grad_down,
    )


def solution(mesh):
    in_specs = (
        P(("expert", "shard"), None),
        P("expert", None),
        P(("expert", "shard"), None),
        P("shard", None),
        P("shard", None),
        P("shard", None),
        P("shard"),
        P("shard"),
        P(),
        P("expert", None, "shard"),
        P("expert", "shard", None),
        P(("expert", "shard"), None),
    )
    out_specs = (
        P(("expert", "shard"), None),
        P(("expert", "shard"), None),
        P("shard", None),
        P("shard", None),
        P("shard", None),
        P("shard"),
        P("shard"),
        P("shard", None),
        P("expert", None, "shard"),
        P("expert", "shard", None),
    )
    return jax.shard_map(local, mesh=mesh, in_specs=in_specs, out_specs=out_specs, check_vma=False)
```

```python
import jax
import jax.numpy as jnp
from jax import lax
from jax.experimental import pallas as pl
from jax.experimental.pallas import tpu as pltpu
from jax.sharding import PartitionSpec as P

norm_eps = 1e-06
gelu_scale = 0.7978845608028654
gelu_cubic = 0.044715
big_negative = -1e30
near_steps = 8
far_steps = (12, 16, 23, 32, 46, 64, 91)
bf16 = jnp.bfloat16
f32 = jnp.float32
row_tile = 8
pair = 1
slot_tile = 4


def bucket_index(offset):
    distance = jnp.abs(offset)
    far_level = jnp.full_like(distance, near_steps)
    for step_edge in far_steps:
        far_level = far_level + (distance >= step_edge).astype(jnp.int32)
    near = jnp.where(distance < near_steps, distance, far_level)
    return near + 16 * (offset > 0).astype(jnp.int32)


def dot(left, right):
    return jnp.dot(left, right, preferred_element_type=f32)


def dot_nt(left, right):
    return lax.dot_general(left, right, (((1,), (1,)), ((), ())), preferred_element_type=f32)


def dot_tn(left, right):
    return lax.dot_general(left, right, (((0,), (0,)), ((), ())), preferred_element_type=f32)


def swap(value, axis, bit):
    size = lax.axis_size(axis)
    return lax.ppermute(value, axis, [(i, i ^ bit) for i in range(size)])


def gather_relative(value, axis):
    blocks = [value]
    bit = lax.axis_size(axis) // 2
    parts = {0: value}
    while bit:
        for p in list(parts):
            parts[p ^ bit] = swap(parts[p], axis, bit)
        bit //= 2
    return [parts[p] for p in range(lax.axis_size(axis))]


def exchange_relative(blocks, axis):
    return [blocks[0]] + [swap(block, axis, p) for p, block in enumerate(blocks) if p]


def call(kernel, out_shape, operands, spaces="", scratch=(), work=0):
    vmem = pl.BlockSpec(memory_space=pltpu.VMEM)
    smem = pl.BlockSpec(memory_space=pltpu.SMEM)
    in_specs = [smem if spaces[i : i + 1] == "s" else vmem for i in range(len(operands))]
    return pl.pallas_call(
        kernel,
        out_shape=out_shape,
        in_specs=in_specs,
        out_specs=jax.tree.map(lambda _: vmem, out_shape),
        scratch_shapes=list(scratch),
        compiler_params=pltpu.CompilerParams(vmem_limit_bytes=56 * 2**20),
        cost_estimate=pl.CostEstimate(flops=work, bytes_accessed=0, transcendentals=0),
    )(*operands)


def shape(dims, dtype=bf16):
    return jax.ShapeDtypeStruct(tuple(dims), dtype)


def diagonal(size):
    return lax.broadcasted_iota(jnp.int32, (size, size), 0) == lax.broadcasted_iota(
        jnp.int32, (size, size), 1
    )


def to_column(row, size):
    return jnp.sum(jnp.where(diagonal(size), row, 0.0), axis=1, keepdims=True)


def to_row(column, size):
    return jnp.sum(jnp.where(diagonal(size), column, 0.0), axis=0, keepdims=True)


def prepare_weight(n, part, weight, gain_one, gain_two, *outs):
    wide = 3 * part
    s = lax.axis_index("shard")
    extra = outs[0].shape[1] - wide
    one, two = (
        to_column(gain[...].astype(f32).reshape(1, part), part) for gain in (gain_one, gain_two)
    )
    lane = lax.broadcasted_iota(jnp.int32, (part, extra), 1)
    beside = jnp.where(lane == 0, one, jnp.where(lane == 1, two, 0.0)).astype(bf16)
    for p in range(n):
        outs[p][:, wide:] = beside
    for k in range(n):

        @pl.when(s == k)
        def _():
            for p in range(n):
                for kind in range(3):
                    at = (kind * n + (k ^ p)) * part
                    outs[p][:, kind * part : (kind + 1) * part] = weight[:, at : at + part]


def offsets(rows):
    return lax.broadcasted_iota(jnp.int32, (rows, rows), 1) - lax.broadcasted_iota(
        jnp.int32, (rows, rows), 0
    )


def near_buckets(diff, buckets):
    if diff == 0:
        return range(buckets)
    return range(buckets // 2, buckets) if diff > 0 else range(buckets // 2)


def attention_forward(n, rows, width, heads, seqs, buckets, *refs):
    lengths, table = refs[:2]
    token_refs = refs[2 : 2 + n]
    weight_refs = refs[2 + n : 2 + 2 * n]
    tokens_out, weight_out, projected_out, weights_out, *gains_out, mixed_all = refs[
        2 + 2 * n : 9 + 2 * n
    ]
    mixed_out = refs[9 + 2 * n : 9 + 3 * n]
    normed_scr, scores_scr = refs[9 + 3 * n :]
    s = lax.axis_index("shard")
    part = width // n
    wide = 3 * part
    head_dim = part // heads
    for p in range(n):
        tokens_out[s ^ p] = token_refs[p][...]
        weight_out[pl.ds(pl.multiple_of((s ^ p) * part, part & -part), part), :] = weight_refs[p][...]
    size = 128
    for c in range(width // size):
        beside = weight_out[c * size : (c + 1) * size, wide:].astype(f32)
        for i in range(2):
            gains_out[i][:, c * size : (c + 1) * size] = to_row(beside[:, i : i + 1], size)
    gain = gains_out[0][...]
    for j in range(n):
        value = tokens_out[j].astype(f32)
        factor = lax.rsqrt(jnp.mean(value * value, axis=-1, keepdims=True) + norm_eps)
        normed_scr[j * rows : (j + 1) * rows, :] = (value * factor * gain).astype(bf16)
    projected_out[...] = dot(normed_scr[...], weight_out[:, :wide]).astype(bf16)
    total_rows = n * rows
    key_place = lax.broadcasted_iota(jnp.int32, (1, total_rows), 1)
    key_segment = jnp.zeros((1, total_rows), jnp.int32)
    end = jnp.int32(0)
    ends = []
    for j in range(seqs):
        end = end + lengths[0, j]
        ends.append(end)
        key_segment = key_segment + (key_place >= end).astype(jnp.int32)
    base = offsets(rows)
    steps = {diff: bucket_index(base + diff * rows) for diff in (-1, 0, 1)}
    for h in range(heads):
        query = projected_out[:, h * head_dim : (h + 1) * head_dim]
        key = projected_out[:, part + h * head_dim : part + (h + 1) * head_dim]
        value = projected_out[:, 2 * part + h * head_dim : 2 * part + (h + 1) * head_dim]
        bias = {}
        for diff in (-1, 0, 1):
            block = jnp.zeros((rows, rows), f32)
            for b in near_buckets(diff, buckets):
                block = jnp.where(steps[diff] == b, table[h, b], block)
            bias[diff] = block
        low_side = jnp.full((rows, rows), table[h, buckets // 2 - 1], f32)
        high_side = jnp.full((rows, rows), table[h, buckets - 1], f32)
        scores_scr[...] = dot_nt(query, key)
        for i in range(n):
            scores = scores_scr[i * rows : (i + 1) * rows, :]
            side = [
                bias[j - i] if abs(j - i) <= 1 else (high_side if j > i else low_side)
                for j in range(n)
            ]
            scores = scores + jnp.concatenate(side, axis=1)
            query_place = i * rows + lax.broadcasted_iota(jnp.int32, (rows, 1), 0)
            query_segment = jnp.zeros((rows, 1), jnp.int32)
            for j in range(seqs):
                query_segment = query_segment + (query_place >= ends[j]).astype(jnp.int32)
            scores = jnp.where(query_segment == key_segment, scores, big_negative)
            top = jnp.max(scores, axis=-1, keepdims=True)
            raised = jnp.exp(scores - top)
            total = jnp.sum(raised, axis=-1, keepdims=True)
            weights = (raised * (1.0 / total)).astype(bf16)
            weights_out[h, i * rows : (i + 1) * rows, :] = weights
        mixed_all[:, :, h * head_dim : (h + 1) * head_dim] = (
            dot(weights_out[h], value).astype(bf16).reshape(n, rows, head_dim)
        )
    for p in range(n):
        mixed_out[p][...] = mixed_all[s ^ p]


def attention_backward(n, m, rows, width, heads, buckets, experts, *refs):
    projected, tokens, gains, weight, weights, mixed, weight_out, gain_two, router = refs[:9]
    branch_refs = refs[9 : 9 + n]
    at = 9 + n
    shares = 4 if m > 1 else 2
    share_out = refs[at : at + shares]
    normed_grad_out = refs[at + shares : at + shares + 2]
    gain_out, table_out = refs[at + shares + 2 : at + shares + 4]
    branch_scr, scores_scr, projected_scr, total_scr, out_scr, normed_scr, send_scr, weights_scr = (
        refs[at + shares + 4 :]
    )
    s = lax.axis_index("shard")
    e = lax.axis_index("expert")
    part = width // n
    wide = 3 * part
    group = n * rows
    head_dim = part // heads
    for p in range(n):
        branch_scr[s ^ p] = branch_refs[p][...]
    branch = branch_scr[...].reshape(group, width)
    grad_mixed = dot_nt(branch, weight_out[...]).astype(bf16)
    out_scr[...] = dot_tn(mixed[...].reshape(group, part), branch)
    base = offsets(rows)
    steps = {diff: bucket_index(base + diff * rows) for diff in (-1, 0, 1)}
    lane = lax.broadcasted_iota(jnp.int32, (row_tile, 128), 1)
    line = lax.broadcasted_iota(jnp.int32, (row_tile, 128), 0)
    table_total = jnp.zeros((row_tile, 128), f32)
    per_line = buckets // row_tile
    for h in range(heads):
        query = projected[:, h * head_dim : (h + 1) * head_dim]
        key = projected[:, part + h * head_dim : part + (h + 1) * head_dim]
        value = projected[:, 2 * part + h * head_dim : 2 * part + (h + 1) * head_dim]
        near = {diff: jnp.zeros((rows, rows), f32) for diff in (-1, 0, 1)}
        low_side = jnp.zeros((1, rows), f32)
        high_side = jnp.zeros((1, rows), f32)
        upstream = grad_mixed[:, h * head_dim : (h + 1) * head_dim]
        weights_scr[...] = dot_nt(upstream, value)
        for i in range(n):
            weights_i = weights[h, i * rows : (i + 1) * rows, :].astype(f32)
            grad_weights = weights_scr[i * rows : (i + 1) * rows, :]
            inner = jnp.sum(weights_i * grad_weights, axis=-1, keepdims=True)
            grad_scores = weights_i * (grad_weights - inner)
            scores_scr[i * rows : (i + 1) * rows, :] = grad_scores.astype(bf16)
            for j in range(n):
                block = grad_scores[:, j * rows : (j + 1) * rows]
                if abs(j - i) <= 1:
                    near[j - i] = near[j - i] + block
                elif j > i:
                    high_side = high_side + jnp.sum(block, axis=0, keepdims=True)
                else:
                    low_side = low_side + jnp.sum(block, axis=0, keepdims=True)
        for b in range(buckets):
            amount = jnp.zeros((1, rows), f32)
            for diff in (-1, 0, 1):
                if b in near_buckets(diff, buckets):
                    amount = amount + jnp.sum(
                        jnp.where(steps[diff] == b, near[diff], 0.0), axis=0, keepdims=True
                    )
            if b == buckets - 1:
                amount = amount + high_side
            if b == buckets // 2 - 1:
                amount = amount + low_side
            amount = jnp.sum(amount, axis=1, keepdims=True)
            spot = (line == b // per_line) & (lane == h * per_line + b % per_line)
            table_total = jnp.where(spot, amount, table_total)
        grad_scores_all = scores_scr[...]
        projected_scr[:, h * head_dim : (h + 1) * head_dim] = dot(grad_scores_all, key).astype(bf16)
        projected_scr[:, part + h * head_dim : part + (h + 1) * head_dim] = (
            dot_tn(query, grad_scores_all).T.astype(bf16)
        )
        projected_scr[:, 2 * part + h * head_dim : 2 * part + (h + 1) * head_dim] = (
            dot_tn(upstream, weights[h]).T.astype(bf16)
        )
    table_out[...] = table_total
    grad_projected = projected_scr[...]
    normed_grad = dot_nt(grad_projected, weight[:, :wide])
    send_scr[...] = normed_grad.astype(bf16).reshape(n, rows, width)
    for p in range(n):
        normed_grad_out[p & 1][p >> 1] = send_scr[s ^ p]
    gain = gains[...]
    grad_gain = jnp.zeros((1, width), f32)
    for j in range(n):
        value = tokens[j].astype(f32)
        unit = value * lax.rsqrt(jnp.mean(value * value, axis=-1, keepdims=True) + norm_eps)
        normed_scr[j * rows : (j + 1) * rows, :] = (unit * gain).astype(bf16)
        grad_gain = grad_gain + jnp.sum(
            normed_grad[j * rows : (j + 1) * rows, :] * unit, axis=0, keepdims=True
        )
    gain_out[...] = jnp.broadcast_to(grad_gain, gain_out.shape)
    total_scr[:, :wide] = dot_tn(normed_scr[...], grad_projected)
    full = total_scr.shape[1]
    if m == 1:
        for t in range(n):
            share_out[0][t] = total_scr[t * part : (t + 1) * part, :wide].astype(bf16)
        share_out[1][...] = out_scr[...].astype(bf16)
        return
    piece = part // m
    total_scr[:, wide:] = jnp.zeros((width, full - wide), f32)
    size = 128
    for c in range(width // size):
        here = slice(c * size, (c + 1) * size)
        total_scr[here, wide : wide + 1] = to_column(grad_gain[:, here], size)
        total_scr[here, wide + 1 : wide + 2] = to_column(gain_two[0:1, here], size)
        total_scr[here, wide + 2 : wide + 2 + experts] = router[:, here].T
    at = wide + 2 + experts
    rest = (width - full) // n
    for t in range(n):
        total_scr[t * part : (t + 1) * part, at : at + rest] = out_scr[
            :, full + t * rest : full + (t + 1) * rest
        ]
    at = at + rest
    for d in range(m):
        total_scr[d * piece : d * piece + row_tile, at : at + heads * per_line] = table_total[
            :, : heads * per_line
        ]
    for d in range(m):
        target = share_out[(d & 1) + 2 * (d < m // 2)]
        place = (d >> 1) % (m // 4)
        start = (e ^ d) * piece
        for t in range(n):
            rows_at = pl.multiple_of(t * part + start, row_tile)
            target[place, t] = total_scr[pl.ds(rows_at, piece), :].astype(bf16)
        rows_at = pl.multiple_of(start, row_tile)
        target[place, n] = out_scr[pl.ds(rows_at, piece), :full].astype(bf16)


def beside_columns(ref, p, wide):
    last = ref[p, :, ref.shape[2] - 128 :]
    skip = wide - (ref.shape[2] - 128)
    return jnp.concatenate([last[:, skip:], last[:, :skip]], axis=1)


def assemble(n, m, part, piece, experts, *refs):
    total_out, out_out, one_out, two_out, router_out, small_scr = refs[m:]
    s = lax.axis_index("shard")
    e = lax.axis_index("expert")
    wide = 3 * part
    full = refs[0].shape[2]
    at = wide + 2 + experts
    rest = (n * part - full) // n
    for d in range(m):
        start = pl.multiple_of((e ^ d) * piece, row_tile)
        own = pl.ds(start, piece)
        small = jnp.zeros((piece, 128), f32)
        for p in range(n):
            small = small + beside_columns(refs[d], p, wide).astype(f32)
            out_out[own, full + p * rest : full + (p + 1) * rest] = refs[d][p, :, at : at + rest].astype(
                f32
            )
        out_out[own, :full] = refs[d][n].astype(f32)
        small_scr[own, :] = small
    small = small_scr[...].T
    one_out[...] = small[0:1, :]
    two_out[...] = small[1:2, :]
    router_out[...] = small[2 : 2 + experts, :]
    for k in range(n):

        @pl.when(s == k)
        def _():
            for d in range(m):
                own = pl.ds(pl.multiple_of((e ^ d) * piece, row_tile), piece)
                for p in range(n):
                    for kind in range(3):
                        to = (kind * n + (k ^ p)) * part
                        total_out[own, to : to + part] = refs[d][
                            p, :, kind * part : (kind + 1) * part
                        ].astype(f32)


def expert_forward(rows, own, came, up_own, up_pair, down_own, down_pair, *outs):
    hidden_out, slope_out, keep_out, send_out = outs
    source = jnp.concatenate([own[...], came[...]], axis=0)
    result = 0.0
    for k, (up, down) in enumerate(((up_own, down_own), (up_pair, down_pair))):
        before = dot(source, up[0])
        square = before * before
        tanh_value = jnp.tanh(gelu_scale * before * (1.0 + gelu_cubic * square))
        half = 0.5 * (1.0 + tanh_value)
        hidden = (before * half).astype(bf16)
        slope = half + 0.5 * before * (1.0 - tanh_value * tanh_value) * gelu_scale * (
            1.0 + 3.0 * gelu_cubic * square
        )
        hidden_out[k] = hidden
        slope_out[k] = slope.astype(bf16)
        result = result + dot(hidden, down[0])
    keep_out[...] = result[:rows]
    send_out[...] = result[rows:].astype(bf16)


def expert_backward(rows, own, came, up_own, up_pair, down_own, down_pair, slope, *outs):
    before_out, keep_out, send_out = outs
    grads = jnp.concatenate([own[...], came[...]], axis=0)
    result = 0.0
    for k, (up, down) in enumerate(((up_own, down_own), (up_pair, down_pair))):
        grad_before = (dot_nt(grads, down[0]) * slope[k].astype(f32)).astype(bf16)
        before_out[k] = grad_before
        result = result + dot_nt(grad_before, up[0])
    keep_out[...] = result[:rows]
    send_out[...] = result[rows:].astype(bf16)


def weights_to_send(own, came, own_grad, came_grad, hidden, grad_before, up_send, down_send):
    grads = jnp.concatenate([own_grad[...], came_grad[...]], axis=0)
    rows = jnp.concatenate([own[...], came[...]], axis=0)
    up_send[0] = dot_tn(rows, grad_before[1]).astype(bf16)
    down_send[0] = dot_tn(hidden[1], grads).astype(bf16)


def weights_to_keep(
    own, came, own_grad, came_grad, hidden, grad_before, up_came, down_came, up_out, down_out
):
    grads = jnp.concatenate([own_grad[...], came_grad[...]], axis=0)
    rows = jnp.concatenate([own[...], came[...]], axis=0)
    up_out[0] = dot_tn(rows, grad_before[0]) + up_came[0].astype(f32)
    down_out[0] = dot_tn(hidden[0], grads) + down_came[0].astype(f32)


def rms_factor(value):
    return lax.rsqrt(jnp.mean(value * value, axis=-1, keepdims=True) + norm_eps)


def rms_backward(value, factor, gain, upstream):
    scaled = upstream * gain
    grad_value = factor * scaled - value * factor * factor * factor * jnp.mean(
        scaled * value, axis=-1, keepdims=True
    )
    grad_gain = jnp.sum(upstream * value * factor, axis=0, keepdims=True)
    return (grad_value, grad_gain)


def local(
    tokens,
    lengths,
    routes,
    attention_in,
    attention_out,
    position_bias,
    first_gain,
    second_gain,
    router,
    expert_in,
    expert_out,
    cotangent,
):
    n = lax.axis_size("shard")
    m = lax.axis_size("expert")
    s = lax.axis_index("shard")
    e = lax.axis_index("expert")
    rows, width = tokens.shape
    heads, buckets = position_bias.shape
    part = width // n
    wide = 3 * part
    group = n * rows
    seqs = lengths.shape[1]
    experts = router.shape[1]
    direct = m == 8
    full = wide + -wide % 128
    micro = 10**9

    far_tokens, pair_tokens = swap(tokens, "shard", 2 * pair), swap(tokens, "shard", pair)
    weight_blocks = exchange_relative(
        call(
            lambda *refs: prepare_weight(n, part, *refs),
            [shape((part, full))] * n,
            (attention_in, first_gain, second_gain),
        ),
        "shard",
    )
    far_tokens, own_up, own_down, table_scalars = lax.optimization_barrier(
        (far_tokens, expert_in, expert_out, position_bias.astype(f32))
    )
    token_blocks = [tokens, pair_tokens, far_tokens, swap(far_tokens, "shard", pair)]
    pair_up = swap(own_up, "shard", pair)
    pair_down = swap(own_down, "shard", pair)
    own_out, token_blocks, weight_blocks = lax.optimization_barrier(
        (attention_out, token_blocks, weight_blocks)
    )
    far_out, pair_out = swap(own_out, "shard", 2 * pair), swap(own_out, "shard", pair)

    answers = call(
        lambda *refs: attention_forward(n, rows, width, heads, seqs, buckets, *refs),
        (
            shape((n, rows, width)),
            shape((width, full)),
            shape((group, wide)),
            shape((heads, group, group)),
            shape((1, width), f32),
            shape((1, width), f32),
            shape((n, rows, part)),
            *[shape((rows, part))] * n,
        ),
        (lengths, table_scalars, *token_blocks, *weight_blocks),
        "ss",
        [pltpu.VMEM((group, width), bf16), pltpu.VMEM((group, group), f32)],
        work=10 * micro,
    )
    tokens_all, weight, projected, weights, gain_one, gain_two, mixed = answers[:7]
    mixed_mine, pair_up, pair_down, pair_out = lax.optimization_barrier(
        (list(answers[7:]), pair_up, pair_down, pair_out)
    )
    mixed_blocks = exchange_relative(mixed_mine, "shard")
    out_blocks = [own_out, pair_out, far_out, swap(far_out, "shard", pair)]

    inputs = tokens.astype(f32)
    hidden_one = inputs + sum(dot(mixed_blocks[p], out_blocks[p]) for p in range(n))
    factor_two = rms_factor(hidden_one)
    normed_two = hidden_one * factor_two * gain_two
    logits = jnp.dot(
        normed_two, router, precision=lax.Precision.HIGHEST, preferred_element_type=f32
    )
    shifted = jnp.exp(logits - jnp.max(logits, axis=-1, keepdims=True))
    probs = shifted / jnp.sum(shifted, axis=-1, keepdims=True)
    route = routes[:, 0]
    chosen = (route[:, None] == lax.iota(jnp.int32, experts)[None, :]).astype(f32)
    gate = jnp.sum(probs * chosen, axis=1)
    lower = (lax.iota(jnp.int32, rows)[:, None] >= lax.iota(jnp.int32, rows)[None, :]).astype(bf16)
    running = dot(lower, chosen.astype(bf16))
    slot = jnp.sum((running - 1.0) * chosen, axis=1).astype(jnp.int32)
    capacity = max(2, 9 * rows // (8 * experts) + 1)
    capacity = -(-capacity // slot_tile) * slot_tile
    places = experts * capacity
    half = places // 2
    if direct:
        holder = route ^ e
        target = (holder & 1) * half + (holder >> 1) * capacity + slot
    else:
        target = route * capacity + slot
    collect = (target[:, None] == lax.iota(jnp.int32, places)[None, :]).astype(bf16)
    upstream = cotangent.astype(f32)
    grad_result = (gate[:, None] * upstream).astype(bf16)

    def plain(value):
        return lax.all_to_all(
            value.reshape(experts, capacity, width), "expert", 0, 0, tiled=True
        ).reshape(places, width)

    def dispatch(forward, backward):
        if not direct:
            return [plain(dot_tn(collect, x).astype(bf16)) for x in (forward, backward)]
        value = jnp.concatenate([forward, backward], axis=1)
        came = swap(dot_tn(collect[:, half:], value).astype(bf16), "expert", 1)
        own = dot_tn(collect[:, :half], value).astype(bf16).reshape(m // 2, capacity, 2 * width)
        both = jnp.concatenate([own, came.reshape(m // 2, capacity, 2 * width)], axis=1)
        first = among_pairs(both[:, :, :width])
        second, first[-1] = lax.optimization_barrier((both[:, :, width:], first[-1]))
        return [jnp.concatenate(x, axis=0) for x in (first, among_pairs(second))]

    def among_pairs(both):
        return [both[d] if d == 0 else swap(both[d], "expert", 2 * d) for d in range(m // 2)]

    def give_back(forward, backward, late, work):
        if not direct:
            return [dot(collect, plain(x)) for x in (forward, backward)] + [work(late)]
        forward, backward = (
            x.reshape(m // 2, 2 * capacity, width) for x in (forward, backward)
        )
        blocks = [among_pairs(forward)]
        backward, blocks[0][-1] = lax.optimization_barrier((backward, blocks[0][-1]))
        blocks.append(among_pairs(backward))
        late, blocks = lax.optimization_barrier((late, blocks))
        own, other = (
            jnp.concatenate(
                [jnp.concatenate([x[at : at + capacity] for x in side]) for side in blocks], axis=1
            )
            for at in (0, capacity)
        )
        beside = work(late)
        other, beside = lax.optimization_barrier((swap(other, "expert", 1), beside))
        total = dot(collect[:, :half], own) + dot(collect[:, half:], other)
        return total[:, :width], total[:, width:], beside

    def reduce_shard(keep, out, after=None):
        came = swap(out, "shard", 2 * pair)
        if after is not None:
            came, _ = lax.optimization_barrier((came, after))
        return (keep + came.astype(f32)).astype(bf16)

    arrived, arrived_grad = dispatch(normed_two.astype(bf16), grad_result)
    came = swap(arrived, "shard", 2 * pair)
    row_blocks = (arrived, came)
    grad_blocks = (arrived_grad, swap(arrived_grad, "shard", 2 * pair))

    units = expert_in.shape[2]
    expert_weight = (own_up, pair_up, own_down, pair_down)
    middle = shape((2, 2 * places, units))
    kept, sent = shape((places, width), f32), shape((places, width))
    hidden, slope, *forward = call(
        lambda *refs: expert_forward(places, *refs),
        (middle, middle, kept, sent),
        (*row_blocks, *expert_weight),
        work=6 * micro,
    )
    grad_before, *backward = call(
        lambda *refs: expert_backward(places, *refs),
        (middle, kept, sent),
        (*grad_blocks, *expert_weight, slope),
        work=6 * micro,
    )
    sources = (*grad_blocks, hidden, grad_before)
    expert_result, grad_sent, (up_send, down_send) = give_back(
        reduce_shard(*forward, backward[1]),
        reduce_shard(*backward),
        row_blocks,
        lambda rows_late: call(
            weights_to_send,
            (shape(expert_in.shape), shape(expert_out.shape)),
            (*rows_late, *sources),
            work=4 * micro,
        ),
    )

    layer_out = (hidden_one + gate[:, None] * expert_result).astype(bf16)
    grad_gate = jnp.sum(upstream * expert_result, axis=1)
    grad_logits = (grad_gate * gate)[:, None] * (chosen - probs)
    grad_router = lax.dot_general(
        grad_logits,
        normed_two,
        (((0,), (0,)), ((), ())),
        precision=lax.Precision.HIGHEST,
        preferred_element_type=f32,
    )
    grad_normed_two = grad_sent + lax.dot_general(
        grad_logits,
        router,
        (((1,), (1,)), ((), ())),
        precision=lax.Precision.HIGHEST,
        preferred_element_type=f32,
    )
    grad_middle, grad_gain_two = rms_backward(hidden_one, factor_two, gain_two, grad_normed_two)
    grad_hidden = upstream + grad_middle
    branch = grad_hidden.astype(bf16)
    far_branch, pair_branch = swap(branch, "shard", 2 * pair), swap(branch, "shard", pair)
    far_branch, grad_router, gain_two_row = lax.optimization_barrier(
        (far_branch, grad_router, grad_gain_two)
    )
    branch_blocks = [branch, pair_branch, far_branch, swap(far_branch, "shard", pair)]
    branch_blocks, up_send, down_send = lax.optimization_barrier(
        (branch_blocks, up_send, down_send)
    )
    up_came, down_came = swap(up_send, "shard", pair), swap(down_send, "shard", pair)
    holders = m if direct else 1
    piece = part // m
    if direct:
        share_shapes = [shape((m // 4, n + 1, piece, full))] * 4
    else:
        share_shapes = [shape((n, part, wide)), shape((part, width))]
    answers = call(
        lambda *refs: attention_backward(n, holders, rows, width, heads, buckets, experts, *refs),
        (
            *share_shapes,
            *[shape((n // 2, rows, width))] * 2,
            shape((row_tile, width), f32),
            shape((row_tile, 128), f32),
        ),
        (
            projected,
            tokens_all,
            gain_one,
            weight,
            weights,
            mixed,
            own_out,
            gain_two_row,
            grad_router,
            *branch_blocks,
        ),
        "",
        [
            pltpu.VMEM((n, rows, width), bf16),
            pltpu.VMEM((group, group), bf16),
            pltpu.VMEM((group, wide), bf16),
            pltpu.VMEM((width, full), f32),
            pltpu.VMEM((part, width), f32),
            pltpu.VMEM((group, width), bf16),
            pltpu.VMEM((n, rows, width), bf16),
            pltpu.VMEM((group, group), f32),
        ],
        work=8 * micro,
    )
    shares = answers[: len(share_shapes)]
    normed_keep, normed_send, gain_row, table = answers[len(share_shapes) :]

    def kept_weights(late_rows):
        return call(
            weights_to_keep,
            (shape(expert_in.shape, f32), shape(expert_out.shape, f32)),
            (*late_rows, *sources, up_came, down_came),
            work=4 * micro,
        )

    per_line = buckets // row_tile

    def biases(block):
        return block.reshape(row_tile, heads, per_line).swapaxes(0, 1).reshape(heads, buckets)

    normed_sum = normed_keep.astype(f32) + swap(normed_send, "shard", pair).astype(f32)
    far_sum = swap(normed_sum[1].astype(bf16), "shard", 2 * pair)
    late, far_sum = lax.optimization_barrier((tokens, far_sum))
    late = late.astype(f32)
    grad_input_norm, _ = rms_backward(
        late, rms_factor(late), gain_one, normed_sum[0] + far_sum.astype(f32)
    )
    grad_tokens = (grad_hidden + grad_input_norm).astype(bf16)
    if direct:
        far_keep, far_send, near_keep, near_send = shares
        far_came = swap(far_send, "expert", 1)
        far_came, near_send, late_rows = lax.optimization_barrier((far_came, near_send, row_blocks))
        far = far_keep.astype(f32) + far_came.astype(f32)
        near_came, (grad_up, grad_down) = lax.optimization_barrier(
            (swap(near_send, "expert", 1), kept_weights(late_rows))
        )
        near = near_keep.astype(f32) + near_came.astype(f32)
        came = [swap(far[d].astype(bf16), "expert", m // 2 + 2 * d) for d in range(m // 4)]
        came += [swap(near[d].astype(bf16), "expert", 2 * d) for d in range(1, m // 4)]
        summed = near[0] + sum(x.astype(f32) for x in came)
        at = wide + 2 + experts
        rest = (width - full) // n
        table_total = biases(
            summed[0, :row_tile, at + rest : at + rest + heads * per_line]
        )
        low = summed.astype(bf16)
        mine = exchange_relative(
            [lax.dynamic_index_in_dim(low, s ^ p, 0, keepdims=False) for p in range(n)], "shard"
        )
        lane = lax.iota(jnp.int32, full)[None, :]
        own_lane = (lane >= at) & (lane < at + rest)
        mine = jnp.stack(
            [jnp.where(own_lane, low[p], mine[p]) for p in range(n)] + [low[n]], axis=0
        )
        blocks = {0: mine, 1: swap(mine, "expert", 1), 4: swap(mine, "expert", 4)}
        blocks[2] = swap(mine, "expert", 2)
        blocks[2], blocks[1] = lax.optimization_barrier((blocks[2], blocks[1]))
        blocks[3] = swap(blocks[2], "expert", 1)
        blocks[4], blocks[3] = lax.optimization_barrier((blocks[4], blocks[3]))
        blocks[6] = swap(blocks[4], "expert", 2)
        blocks[5] = swap(blocks[4], "expert", 1)
        blocks[6], grad_tokens = lax.optimization_barrier((blocks[6], grad_tokens))
        blocks[7] = swap(blocks[6], "expert", 1)
        blocks = [blocks[d] for d in range(m)]
        grad_attention_in, grad_attention_out, total_one, total_two, total_router = call(
            lambda *refs: assemble(n, m, part, piece, experts, *refs),
            (
                shape((part, 3 * width), f32),
                shape((part, width), f32),
                shape((1, part), f32),
                shape((1, part), f32),
                shape((experts, part), f32),
            ),
            (*blocks,),
            "",
            [pltpu.VMEM((part, 128), f32)],
        )
    else:
        grad_up, grad_down = kept_weights(row_blocks)
        came = lax.all_to_all(
            shares[0].reshape(n, m, piece, wide).swapaxes(0, 1), "expert", 0, 0, tiled=True
        )
        summed = sum(x.astype(f32) for x in came).astype(bf16)
        mine = lax.all_to_all(summed, "shard", 0, 0, tiled=True)
        mine = mine.reshape(n, piece, 3, part).transpose(1, 2, 0, 3).reshape(piece, 3 * width)
        came = lax.all_to_all(shares[1].reshape(m, piece, width), "expert", 0, 0, tiled=True)
        out_mine = sum(x.astype(f32) for x in came).astype(bf16)
        grad_attention_in = lax.all_gather(mine, "expert", axis=0, tiled=True).astype(f32)
        grad_attention_out = lax.all_gather(out_mine, "expert", axis=0, tiled=True).astype(f32)
        small = jnp.concatenate([gain_row[0:1], grad_gain_two, grad_router], axis=0)
        small_total = lax.psum_scatter(small, "shard", scatter_dimension=1, tiled=True)
        small_total, table_total = lax.psum(
            (small_total, biases(table[:, : heads * per_line])), "expert"
        )
        total_one, total_two, total_router = small_total[0:1], small_total[1:2], small_total[2:]
    return (
        layer_out,
        grad_tokens,
        grad_attention_in,
        grad_attention_out,
        table_total,
        total_one[0],
        total_two[0],
        total_router.T,
        grad_up,
        grad_down,
    )


def solution(mesh):
    in_specs = (
        P(("expert", "shard"), None),
        P("expert", None),
        P(("expert", "shard"), None),
        P("shard", None),
        P("shard", None),
        P("shard", None),
        P("shard"),
        P("shard"),
        P(),
        P("expert", None, "shard"),
        P("expert", "shard", None),
        P(("expert", "shard"), None),
    )
    out_specs = (
        P(("expert", "shard"), None),
        P(("expert", "shard"), None),
        P("shard", None),
        P("shard", None),
        P("shard", None),
        P("shard"),
        P("shard"),
        P("shard", None),
        P("expert", None, "shard"),
        P("expert", "shard", None),
    )
    return jax.shard_map(local, mesh=mesh, in_specs=in_specs, out_specs=out_specs, check_vma=False)
```

```python
import jax
import jax.numpy as jnp
from jax import lax
from jax.experimental import pallas as pl
from jax.experimental.pallas import tpu as pltpu
from jax.sharding import PartitionSpec as P

norm_eps = 1e-06
gelu_scale = 0.7978845608028654
gelu_cubic = 0.044715
big_negative = -1e30
near_steps = 8
far_steps = (12, 16, 23, 32, 46, 64, 91)
bf16 = jnp.bfloat16
f32 = jnp.float32
row_tile = 8
pair = 1
slot_tile = 4


def bucket_index(offset):
    distance = jnp.abs(offset)
    far_level = jnp.full_like(distance, near_steps)
    for step_edge in far_steps:
        far_level = far_level + (distance >= step_edge).astype(jnp.int32)
    near = jnp.where(distance < near_steps, distance, far_level)
    return near + 16 * (offset > 0).astype(jnp.int32)


def dot(left, right):
    return jnp.dot(left, right, preferred_element_type=f32)


def dot_nt(left, right):
    return lax.dot_general(left, right, (((1,), (1,)), ((), ())), preferred_element_type=f32)


def dot_tn(left, right):
    return lax.dot_general(left, right, (((0,), (0,)), ((), ())), preferred_element_type=f32)


def swap(value, axis, bit):
    size = lax.axis_size(axis)
    return lax.ppermute(value, axis, [(i, i ^ bit) for i in range(size)])


def gather_relative(value, axis):
    blocks = [value]
    bit = lax.axis_size(axis) // 2
    parts = {0: value}
    while bit:
        for p in list(parts):
            parts[p ^ bit] = swap(parts[p], axis, bit)
        bit //= 2
    return [parts[p] for p in range(lax.axis_size(axis))]


def exchange_relative(blocks, axis):
    return [blocks[0]] + [swap(block, axis, p) for p, block in enumerate(blocks) if p]


def call(kernel, out_shape, operands, spaces="", scratch=(), work=0):
    vmem = pl.BlockSpec(memory_space=pltpu.VMEM)
    smem = pl.BlockSpec(memory_space=pltpu.SMEM)
    in_specs = [smem if spaces[i : i + 1] == "s" else vmem for i in range(len(operands))]
    return pl.pallas_call(
        kernel,
        out_shape=out_shape,
        in_specs=in_specs,
        out_specs=jax.tree.map(lambda _: vmem, out_shape),
        scratch_shapes=list(scratch),
        compiler_params=pltpu.CompilerParams(vmem_limit_bytes=56 * 2**20),
        cost_estimate=pl.CostEstimate(flops=work, bytes_accessed=0, transcendentals=0),
    )(*operands)


def shape(dims, dtype=bf16):
    return jax.ShapeDtypeStruct(tuple(dims), dtype)


def diagonal(size):
    return lax.broadcasted_iota(jnp.int32, (size, size), 0) == lax.broadcasted_iota(
        jnp.int32, (size, size), 1
    )


def to_column(row, size):
    return jnp.sum(jnp.where(diagonal(size), row, 0.0), axis=1, keepdims=True)


def to_row(column, size):
    return jnp.sum(jnp.where(diagonal(size), column, 0.0), axis=0, keepdims=True)


def prepare_weight(n, part, weight, gain_one, gain_two, *outs):
    wide = 3 * part
    s = lax.axis_index("shard")
    extra = outs[0].shape[1] - wide
    one, two = (
        to_column(gain[...].astype(f32).reshape(1, part), part) for gain in (gain_one, gain_two)
    )
    lane = lax.broadcasted_iota(jnp.int32, (part, extra), 1)
    beside = jnp.where(lane == 0, one, jnp.where(lane == 1, two, 0.0)).astype(bf16)
    for p in range(n):
        outs[p][:, wide:] = beside
    for k in range(n):

        @pl.when(s == k)
        def _():
            for p in range(n):
                for kind in range(3):
                    at = (kind * n + (k ^ p)) * part
                    outs[p][:, kind * part : (kind + 1) * part] = weight[:, at : at + part]


def offsets(rows):
    return lax.broadcasted_iota(jnp.int32, (rows, rows), 1) - lax.broadcasted_iota(
        jnp.int32, (rows, rows), 0
    )


def near_buckets(diff, buckets):
    if diff == 0:
        return range(buckets)
    return range(buckets // 2, buckets) if diff > 0 else range(buckets // 2)


def attention_forward(n, rows, width, heads, seqs, buckets, *refs):
    lengths, table = refs[:2]
    token_refs = refs[2 : 2 + n]
    weight_refs = refs[2 + n : 2 + 2 * n]
    tokens_out, weight_out, projected_out, weights_out, *gains_out, mixed_all = refs[
        2 + 2 * n : 9 + 2 * n
    ]
    mixed_out = refs[9 + 2 * n : 9 + 3 * n]
    normed_scr, scores_scr = refs[9 + 3 * n :]
    s = lax.axis_index("shard")
    part = width // n
    wide = 3 * part
    head_dim = part // heads
    for p in range(n):
        tokens_out[s ^ p] = token_refs[p][...]
        weight_out[pl.ds(pl.multiple_of((s ^ p) * part, part & -part), part), :] = weight_refs[p][...]
    size = 128
    for c in range(width // size):
        beside = weight_out[c * size : (c + 1) * size, wide:].astype(f32)
        for i in range(2):
            row = to_row(beside[:, i : i + 1], size)
            gains_out[i][:, c * size : (c + 1) * size] = jnp.broadcast_to(
                row, (gains_out[i].shape[0], size)
            )
    gain = gains_out[0][...]
    for j in range(n):
        value = tokens_out[j].astype(f32)
        factor = lax.rsqrt(jnp.mean(value * value, axis=-1, keepdims=True) + norm_eps)
        normed_scr[j * rows : (j + 1) * rows, :] = (value * factor * gain).astype(bf16)
    projected_out[...] = dot(normed_scr[...], weight_out[:, :wide]).astype(bf16)
    total_rows = n * rows
    key_place = lax.broadcasted_iota(jnp.int32, (1, total_rows), 1)
    key_segment = jnp.zeros((1, total_rows), jnp.int32)
    end = jnp.int32(0)
    ends = []
    for j in range(seqs):
        end = end + lengths[0, j]
        ends.append(end)
        key_segment = key_segment + (key_place >= end).astype(jnp.int32)
    base = offsets(rows)
    steps = {diff: bucket_index(base + diff * rows) for diff in (-1, 0, 1)}
    for h in range(heads):
        query = projected_out[:, h * head_dim : (h + 1) * head_dim]
        key = projected_out[:, part + h * head_dim : part + (h + 1) * head_dim]
        value = projected_out[:, 2 * part + h * head_dim : 2 * part + (h + 1) * head_dim]
        bias = {}
        for diff in (-1, 0, 1):
            block = jnp.zeros((rows, rows), f32)
            for b in near_buckets(diff, buckets):
                block = jnp.where(steps[diff] == b, table[h, b], block)
            bias[diff] = block
        low_side = jnp.full((rows, rows), table[h, buckets // 2 - 1], f32)
        high_side = jnp.full((rows, rows), table[h, buckets - 1], f32)
        scores_scr[...] = dot_nt(query, key)
        for i in range(n):
            scores = scores_scr[i * rows : (i + 1) * rows, :]
            side = [
                bias[j - i] if abs(j - i) <= 1 else (high_side if j > i else low_side)
                for j in range(n)
            ]
            scores = scores + jnp.concatenate(side, axis=1)
            query_place = i * rows + lax.broadcasted_iota(jnp.int32, (rows, 1), 0)
            query_segment = jnp.zeros((rows, 1), jnp.int32)
            for j in range(seqs):
                query_segment = query_segment + (query_place >= ends[j]).astype(jnp.int32)
            scores = jnp.where(query_segment == key_segment, scores, big_negative)
            top = jnp.max(scores, axis=-1, keepdims=True)
            raised = jnp.exp(scores - top)
            total = jnp.sum(raised, axis=-1, keepdims=True)
            weights = (raised * (1.0 / total)).astype(bf16)
            weights_out[h, i * rows : (i + 1) * rows, :] = weights
        mixed_all[:, :, h * head_dim : (h + 1) * head_dim] = (
            dot(weights_out[h], value).astype(bf16).reshape(n, rows, head_dim)
        )
    for p in range(n):
        mixed_out[p][...] = mixed_all[s ^ p]


def attention_backward(n, m, rows, width, heads, buckets, experts, *refs):
    projected, tokens, gains, weight, weights, mixed, weight_out, gain_two, router = refs[:9]
    branch_refs = refs[9 : 9 + n]
    at = 9 + n
    shares = 4 if m > 1 else 2
    share_out = refs[at : at + shares]
    normed_grad_out = refs[at + shares : at + shares + 2]
    gain_out, table_out = refs[at + shares + 2 : at + shares + 4]
    branch_scr, scores_scr, projected_scr, total_scr, out_scr, normed_scr, send_scr, weights_scr = (
        refs[at + shares + 4 :]
    )
    s = lax.axis_index("shard")
    e = lax.axis_index("expert")
    part = width // n
    wide = 3 * part
    group = n * rows
    head_dim = part // heads
    for p in range(n):
        branch_scr[s ^ p] = branch_refs[p][...]
    branch = branch_scr[...].reshape(group, width)
    grad_mixed = dot_nt(branch, weight_out[...]).astype(bf16)
    out_scr[...] = dot_tn(mixed[...].reshape(group, part), branch)
    base = offsets(rows)
    steps = {diff: bucket_index(base + diff * rows) for diff in (-1, 0, 1)}
    lane = lax.broadcasted_iota(jnp.int32, (row_tile, 128), 1)
    line = lax.broadcasted_iota(jnp.int32, (row_tile, 128), 0)
    table_total = jnp.zeros((row_tile, 128), f32)
    per_line = buckets // row_tile
    for h in range(heads):
        query = projected[:, h * head_dim : (h + 1) * head_dim]
        key = projected[:, part + h * head_dim : part + (h + 1) * head_dim]
        value = projected[:, 2 * part + h * head_dim : 2 * part + (h + 1) * head_dim]
        near = {diff: jnp.zeros((rows, rows), f32) for diff in (-1, 0, 1)}
        low_side = jnp.zeros((1, rows), f32)
        high_side = jnp.zeros((1, rows), f32)
        upstream = grad_mixed[:, h * head_dim : (h + 1) * head_dim]
        weights_scr[...] = dot_nt(upstream, value)
        for i in range(n):
            weights_i = weights[h, i * rows : (i + 1) * rows, :].astype(f32)
            grad_weights = weights_scr[i * rows : (i + 1) * rows, :]
            inner = jnp.sum(weights_i * grad_weights, axis=-1, keepdims=True)
            grad_scores = weights_i * (grad_weights - inner)
            scores_scr[i * rows : (i + 1) * rows, :] = grad_scores.astype(bf16)
            for j in range(n):
                block = grad_scores[:, j * rows : (j + 1) * rows]
                if abs(j - i) <= 1:
                    near[j - i] = near[j - i] + block
                elif j > i:
                    high_side = high_side + jnp.sum(block, axis=0, keepdims=True)
                else:
                    low_side = low_side + jnp.sum(block, axis=0, keepdims=True)
        for b in range(buckets):
            amount = jnp.zeros((1, rows), f32)
            for diff in (-1, 0, 1):
                if b in near_buckets(diff, buckets):
                    amount = amount + jnp.sum(
                        jnp.where(steps[diff] == b, near[diff], 0.0), axis=0, keepdims=True
                    )
            if b == buckets - 1:
                amount = amount + high_side
            if b == buckets // 2 - 1:
                amount = amount + low_side
            amount = jnp.sum(amount, axis=1, keepdims=True)
            spot = (line == b // per_line) & (lane == h * per_line + b % per_line)
            table_total = jnp.where(spot, amount, table_total)
        grad_scores_all = scores_scr[...]
        projected_scr[:, h * head_dim : (h + 1) * head_dim] = dot(grad_scores_all, key).astype(bf16)
        projected_scr[:, part + h * head_dim : part + (h + 1) * head_dim] = (
            dot_tn(query, grad_scores_all).T.astype(bf16)
        )
        projected_scr[:, 2 * part + h * head_dim : 2 * part + (h + 1) * head_dim] = (
            dot_tn(upstream, weights[h]).T.astype(bf16)
        )
    table_out[...] = table_total
    grad_projected = projected_scr[...]
    normed_grad = dot_nt(grad_projected, weight[:, :wide])
    send_scr[...] = normed_grad.astype(bf16).reshape(n, rows, width)
    for p in range(n):
        normed_grad_out[p & 1][p >> 1] = send_scr[s ^ p]
    gain = gains[...]
    grad_gain = jnp.zeros((1, width), f32)
    for j in range(n):
        value = tokens[j].astype(f32)
        unit = value * lax.rsqrt(jnp.mean(value * value, axis=-1, keepdims=True) + norm_eps)
        normed_scr[j * rows : (j + 1) * rows, :] = (unit * gain).astype(bf16)
        grad_gain = grad_gain + jnp.sum(
            normed_grad[j * rows : (j + 1) * rows, :] * unit, axis=0, keepdims=True
        )
    gain_out[...] = jnp.broadcast_to(grad_gain, gain_out.shape)
    total_scr[:, :wide] = dot_tn(normed_scr[...], grad_projected)
    full = total_scr.shape[1]
    if m == 1:
        for t in range(n):
            share_out[0][t] = total_scr[t * part : (t + 1) * part, :wide].astype(bf16)
        share_out[1][...] = out_scr[...].astype(bf16)
        return
    piece = part // m
    total_scr[:, wide:] = jnp.zeros((width, full - wide), f32)
    grad_two = gain_two[...].reshape(1, width)
    size = 128
    for c in range(width // size):
        here = slice(c * size, (c + 1) * size)
        total_scr[here, wide : wide + 1] = to_column(grad_gain[:, here], size)
        total_scr[here, wide + 1 : wide + 2] = to_column(grad_two[:, here], size)
        total_scr[here, wide + 2 : wide + 2 + experts] = router[:, here].T
    at = wide + 2 + experts
    rest = (width - full) // n
    for t in range(n):
        total_scr[t * part : (t + 1) * part, at : at + rest] = out_scr[
            :, full + t * rest : full + (t + 1) * rest
        ]
    at = at + rest
    for d in range(m):
        total_scr[d * piece : d * piece + row_tile, at : at + heads * per_line] = table_total[
            :, : heads * per_line
        ]
    for d in range(m):
        target = share_out[(d & 1) + 2 * (d < m // 2)]
        place = (d >> 1) % (m // 4)
        start = (e ^ d) * piece
        for t in range(n):
            rows_at = pl.multiple_of(t * part + start, row_tile)
            target[place, t] = total_scr[pl.ds(rows_at, piece), :].astype(bf16)
        rows_at = pl.multiple_of(start, row_tile)
        target[place, n] = out_scr[pl.ds(rows_at, piece), :full].astype(bf16)


def beside_columns(ref, p, wide):
    last = ref[p, :, ref.shape[2] - 128 :]
    skip = wide - (ref.shape[2] - 128)
    return jnp.concatenate([last[:, skip:], last[:, :skip]], axis=1)


def assemble(n, m, part, piece, experts, *refs):
    total_out, out_out, one_out, two_out, router_out, small_scr = refs[m:]
    s = lax.axis_index("shard")
    e = lax.axis_index("expert")
    wide = 3 * part
    full = refs[0].shape[2]
    at = wide + 2 + experts
    rest = (n * part - full) // n
    for d in range(m):
        start = pl.multiple_of((e ^ d) * piece, row_tile)
        own = pl.ds(start, piece)
        small = jnp.zeros((piece, 128), f32)
        for p in range(n):
            small = small + beside_columns(refs[d], p, wide).astype(f32)
            out_out[own, full + p * rest : full + (p + 1) * rest] = refs[d][p, :, at : at + rest].astype(
                f32
            )
        out_out[own, :full] = refs[d][n].astype(f32)
        small_scr[own, :] = small
    small = small_scr[...].T
    one_out[...] = small[0:1, :]
    two_out[...] = small[1:2, :]
    router_out[...] = small[2 : 2 + experts, :]
    for k in range(n):

        @pl.when(s == k)
        def _():
            for d in range(m):
                own = pl.ds(pl.multiple_of((e ^ d) * piece, row_tile), piece)
                for p in range(n):
                    for kind in range(3):
                        to = (kind * n + (k ^ p)) * part
                        total_out[own, to : to + part] = refs[d][
                            p, :, kind * part : (kind + 1) * part
                        ].astype(f32)


def expert_forward(rows, own, came, up_own, up_pair, down_own, down_pair, *outs):
    hidden_out, slope_out, keep_out, send_out = outs
    source = jnp.concatenate([own[...], came[...]], axis=0)
    result = 0.0
    for k, (up, down) in enumerate(((up_own, down_own), (up_pair, down_pair))):
        before = dot(source, up[0])
        square = before * before
        tanh_value = jnp.tanh(gelu_scale * before * (1.0 + gelu_cubic * square))
        half = 0.5 * (1.0 + tanh_value)
        hidden = (before * half).astype(bf16)
        slope = half + 0.5 * before * (1.0 - tanh_value * tanh_value) * gelu_scale * (
            1.0 + 3.0 * gelu_cubic * square
        )
        hidden_out[k] = hidden
        slope_out[k] = slope.astype(bf16)
        result = result + dot(hidden, down[0])
    keep_out[...] = result[:rows]
    send_out[...] = result[rows:].astype(bf16)


def expert_backward(rows, own, came, up_own, up_pair, down_own, down_pair, slope, *outs):
    before_out, keep_out, send_out = outs
    grads = jnp.concatenate([own[...], came[...]], axis=0)
    result = 0.0
    for k, (up, down) in enumerate(((up_own, down_own), (up_pair, down_pair))):
        grad_before = (dot_nt(grads, down[0]) * slope[k].astype(f32)).astype(bf16)
        before_out[k] = grad_before
        result = result + dot_nt(grad_before, up[0])
    keep_out[...] = result[:rows]
    send_out[...] = result[rows:].astype(bf16)


def weights_to_send(own, came, own_grad, came_grad, hidden, grad_before, up_send, down_send):
    grads = jnp.concatenate([own_grad[...], came_grad[...]], axis=0)
    rows = jnp.concatenate([own[...], came[...]], axis=0)
    up_send[0] = dot_tn(rows, grad_before[1]).astype(bf16)
    down_send[0] = dot_tn(hidden[1], grads).astype(bf16)


def weights_to_keep(
    own, came, own_grad, came_grad, hidden, grad_before, up_came, down_came, up_out, down_out
):
    grads = jnp.concatenate([own_grad[...], came_grad[...]], axis=0)
    rows = jnp.concatenate([own[...], came[...]], axis=0)
    up_out[0] = dot_tn(rows, grad_before[0]) + up_came[0].astype(f32)
    down_out[0] = dot_tn(hidden[0], grads) + down_came[0].astype(f32)


def rms_factor(value):
    return lax.rsqrt(jnp.mean(value * value, axis=-1, keepdims=True) + norm_eps)


def rms_backward(value, factor, gain, upstream):
    scaled = upstream * gain
    grad_value = factor * scaled - value * factor * factor * factor * jnp.mean(
        scaled * value, axis=-1, keepdims=True
    )
    grad_gain = jnp.sum(upstream * value * factor, axis=0)
    return (grad_value, grad_gain)


def local(
    tokens,
    lengths,
    routes,
    attention_in,
    attention_out,
    position_bias,
    first_gain,
    second_gain,
    router,
    expert_in,
    expert_out,
    cotangent,
):
    n = lax.axis_size("shard")
    m = lax.axis_size("expert")
    s = lax.axis_index("shard")
    e = lax.axis_index("expert")
    rows, width = tokens.shape
    heads, buckets = position_bias.shape
    part = width // n
    wide = 3 * part
    group = n * rows
    seqs = lengths.shape[1]
    experts = router.shape[1]
    direct = m == 8
    full = wide + -wide % 128
    micro = 10**9

    far_tokens, pair_tokens = swap(tokens, "shard", 2 * pair), swap(tokens, "shard", pair)
    weight_blocks = exchange_relative(
        call(
            lambda *refs: prepare_weight(n, part, *refs),
            [shape((part, full))] * n,
            (attention_in, first_gain, second_gain),
        ),
        "shard",
    )
    far_tokens, own_up, own_down, table_scalars = lax.optimization_barrier(
        (far_tokens, expert_in, expert_out, position_bias.astype(f32))
    )
    token_blocks = [tokens, pair_tokens, far_tokens, swap(far_tokens, "shard", pair)]
    pair_up = swap(own_up, "shard", pair)
    pair_down = swap(own_down, "shard", pair)
    own_out, token_blocks, weight_blocks = lax.optimization_barrier(
        (attention_out, token_blocks, weight_blocks)
    )
    far_out, pair_out = swap(own_out, "shard", 2 * pair), swap(own_out, "shard", pair)

    answers = call(
        lambda *refs: attention_forward(n, rows, width, heads, seqs, buckets, *refs),
        (
            shape((n, rows, width)),
            shape((width, full)),
            shape((group, wide)),
            shape((heads, group, group)),
            shape((1, width), f32),
            shape((rows, width), f32),
            shape((n, rows, part)),
            *[shape((rows, part))] * n,
        ),
        (lengths, table_scalars, *token_blocks, *weight_blocks),
        "ss",
        [pltpu.VMEM((group, width), bf16), pltpu.VMEM((group, group), f32)],
        work=10 * micro,
    )
    tokens_all, weight, projected, weights, gain_one, gain_two, mixed = answers[:7]
    mixed_mine, pair_up, pair_down, pair_out = lax.optimization_barrier(
        (list(answers[7:]), pair_up, pair_down, pair_out)
    )
    mixed_blocks = exchange_relative(mixed_mine, "shard")
    out_blocks = [own_out, pair_out, far_out, swap(far_out, "shard", pair)]

    inputs = tokens.astype(f32)
    hidden_one = inputs + sum(dot(mixed_blocks[p], out_blocks[p]) for p in range(n))
    factor_two = rms_factor(hidden_one)
    normed_two = hidden_one * factor_two * gain_two
    logits = jnp.dot(
        normed_two, router, precision=lax.Precision.HIGHEST, preferred_element_type=f32
    )
    shifted = jnp.exp(logits - jnp.max(logits, axis=-1, keepdims=True))
    probs = shifted / jnp.sum(shifted, axis=-1, keepdims=True)
    route = routes[:, 0]
    chosen = (route[:, None] == lax.iota(jnp.int32, experts)[None, :]).astype(f32)
    gate = jnp.sum(probs * chosen, axis=1)
    lower = (lax.iota(jnp.int32, rows)[:, None] >= lax.iota(jnp.int32, rows)[None, :]).astype(bf16)
    running = dot(lower, chosen.astype(bf16))
    slot = jnp.sum((running - 1.0) * chosen, axis=1).astype(jnp.int32)
    capacity = max(2, 9 * rows // (8 * experts) + 1)
    capacity = -(-capacity // slot_tile) * slot_tile
    places = experts * capacity
    half = places // 2
    if direct:
        holder = route ^ e
        target = (holder & 1) * half + (holder >> 1) * capacity + slot
    else:
        target = route * capacity + slot
    collect = (target[:, None] == lax.iota(jnp.int32, places)[None, :]).astype(bf16)
    upstream = cotangent.astype(f32)
    grad_result = (gate[:, None] * upstream).astype(bf16)

    def plain(value):
        return lax.all_to_all(
            value.reshape(experts, capacity, width), "expert", 0, 0, tiled=True
        ).reshape(places, width)

    def dispatch(forward, backward):
        if not direct:
            return [plain(dot_tn(collect, x).astype(bf16)) for x in (forward, backward)]
        came = swap(dot_tn(collect[:, half:], forward).astype(bf16), "expert", 1)
        came, other = lax.optimization_barrier(
            (came, dot_tn(collect[:, half:], backward).astype(bf16))
        )

        def both(own, came):
            own = dot_tn(collect[:, :half], own).astype(bf16).reshape(m // 2, capacity, width)
            return jnp.concatenate([own, came.reshape(m // 2, capacity, width)], axis=1)

        first = among_pairs(both(forward, came))
        second, first[1] = lax.optimization_barrier(
            (both(backward, swap(other, "expert", 1)), first[1])
        )
        return [jnp.concatenate(x, axis=0) for x in (first, among_pairs(second))]

    def among_pairs(both):
        return [both[d] if d == 0 else swap(both[d], "expert", 2 * d) for d in range(m // 2)]

    def give_back(forward, backward, late, work):
        if not direct:
            return [dot(collect, plain(x)) for x in (forward, backward)] + [work(late)]
        forward, backward = (
            x.reshape(m // 2, 2 * capacity, width) for x in (forward, backward)
        )
        blocks = [among_pairs(forward)]
        backward, blocks[0][1] = lax.optimization_barrier((backward, blocks[0][1]))
        blocks.append(among_pairs(backward))
        late, blocks = lax.optimization_barrier((late, blocks))
        own, other = (
            jnp.concatenate(
                [jnp.concatenate([x[at : at + capacity] for x in side]) for side in blocks], axis=1
            )
            for at in (0, capacity)
        )
        beside = work(late)
        other, beside = lax.optimization_barrier((swap(other, "expert", 1), beside))
        total = dot(collect[:, :half], own) + dot(collect[:, half:], other)
        return total[:, :width], total[:, width:], beside

    def reduce_shard(keep, out, after=None):
        came = swap(out, "shard", 2 * pair)
        if after is not None:
            came, _ = lax.optimization_barrier((came, after))
        return (keep + came.astype(f32)).astype(bf16)

    arrived, arrived_grad = dispatch(normed_two.astype(bf16), grad_result)
    came = swap(arrived, "shard", 2 * pair)
    row_blocks = (arrived, came)
    grad_blocks = (arrived_grad, swap(arrived_grad, "shard", 2 * pair))

    units = expert_in.shape[2]
    expert_weight = (own_up, pair_up, own_down, pair_down)
    middle = shape((2, 2 * places, units))
    kept, sent = shape((places, width), f32), shape((places, width))
    hidden, slope, *forward = call(
        lambda *refs: expert_forward(places, *refs),
        (middle, middle, kept, sent),
        (*row_blocks, *expert_weight),
        work=6 * micro,
    )
    grad_before, *backward = call(
        lambda *refs: expert_backward(places, *refs),
        (middle, kept, sent),
        (*grad_blocks, *expert_weight, slope),
        work=6 * micro,
    )
    sources = (*grad_blocks, hidden, grad_before)
    expert_result, grad_sent, (up_send, down_send) = give_back(
        reduce_shard(*forward, backward[1]),
        reduce_shard(*backward),
        row_blocks,
        lambda rows_late: call(
            weights_to_send,
            (shape(expert_in.shape), shape(expert_out.shape)),
            (*rows_late, *sources),
            work=4 * micro,
        ),
    )

    layer_out = (hidden_one + gate[:, None] * expert_result).astype(bf16)
    grad_gate = jnp.sum(upstream * expert_result, axis=1)
    grad_logits = (grad_gate * gate)[:, None] * (chosen - probs)
    grad_router = lax.dot_general(
        grad_logits,
        normed_two,
        (((0,), (0,)), ((), ())),
        precision=lax.Precision.HIGHEST,
        preferred_element_type=f32,
    )
    grad_normed_two = grad_sent + lax.dot_general(
        grad_logits,
        router,
        (((1,), (1,)), ((), ())),
        precision=lax.Precision.HIGHEST,
        preferred_element_type=f32,
    )
    grad_middle, grad_gain_two = rms_backward(hidden_one, factor_two, gain_two, grad_normed_two)
    grad_hidden = upstream + grad_middle
    branch = grad_hidden.astype(bf16)
    far_branch, pair_branch = swap(branch, "shard", 2 * pair), swap(branch, "shard", pair)
    far_branch, grad_router, gain_two_row = lax.optimization_barrier(
        (far_branch, grad_router, grad_gain_two)
    )
    branch_blocks = [branch, pair_branch, far_branch, swap(far_branch, "shard", pair)]
    branch_blocks, up_send, down_send = lax.optimization_barrier(
        (branch_blocks, up_send, down_send)
    )
    up_came, down_came = swap(up_send, "shard", pair), swap(down_send, "shard", pair)
    holders = m if direct else 1
    piece = part // m
    if direct:
        share_shapes = [shape((m // 4, n + 1, piece, full))] * 4
    else:
        share_shapes = [shape((n, part, wide)), shape((part, width))]
    answers = call(
        lambda *refs: attention_backward(n, holders, rows, width, heads, buckets, experts, *refs),
        (
            *share_shapes,
            *[shape((n // 2, rows, width))] * 2,
            shape((row_tile, width), f32),
            shape((row_tile, 128), f32),
        ),
        (
            projected,
            tokens_all,
            gain_one,
            weight,
            weights,
            mixed,
            own_out,
            gain_two_row,
            grad_router,
            *branch_blocks,
        ),
        "",
        [
            pltpu.VMEM((n, rows, width), bf16),
            pltpu.VMEM((group, group), bf16),
            pltpu.VMEM((group, wide), bf16),
            pltpu.VMEM((width, full), f32),
            pltpu.VMEM((part, width), f32),
            pltpu.VMEM((group, width), bf16),
            pltpu.VMEM((n, rows, width), bf16),
            pltpu.VMEM((group, group), f32),
        ],
        work=8 * micro,
    )
    shares = answers[: len(share_shapes)]
    normed_keep, normed_send, gain_row, table = answers[len(share_shapes) :]

    def kept_weights(late_rows):
        return call(
            weights_to_keep,
            (shape(expert_in.shape, f32), shape(expert_out.shape, f32)),
            (*late_rows, *sources, up_came, down_came),
            work=4 * micro,
        )

    per_line = buckets // row_tile

    def biases(block):
        return block.reshape(row_tile, heads, per_line).swapaxes(0, 1).reshape(heads, buckets)

    normed_sum = normed_keep.astype(f32) + swap(normed_send, "shard", pair).astype(f32)
    far_sum = swap(normed_sum[1].astype(bf16), "shard", 2 * pair)
    late, far_sum = lax.optimization_barrier((tokens, far_sum))
    late = late.astype(f32)
    grad_input_norm, _ = rms_backward(
        late, rms_factor(late), gain_one, normed_sum[0] + far_sum.astype(f32)
    )
    grad_tokens = (grad_hidden + grad_input_norm).astype(bf16)
    if direct:
        far_keep, far_send, near_keep, near_send = shares
        far_came = swap(far_send, "expert", 1)
        far_came, near_send, up_came, down_came = lax.optimization_barrier(
            (far_came, near_send, up_came, down_came)
        )
        far = far_keep.astype(f32) + far_came.astype(f32)
        near_came, late_rows = lax.optimization_barrier((swap(near_send, "expert", 1), row_blocks))
        near = near_keep.astype(f32) + near_came.astype(f32)
        came = [swap(far[d].astype(bf16), "expert", m // 2 + 2 * d) for d in range(m // 4)]
        came += [swap(near[d].astype(bf16), "expert", 2 * d) for d in range(1, m // 4)]
        came, (grad_up, grad_down) = lax.optimization_barrier((came, kept_weights(late_rows)))
        summed = near[0] + sum(x.astype(f32) for x in came)
        at = wide + 2 + experts
        rest = (width - full) // n
        table_total = biases(
            summed[0, :row_tile, at + rest : at + rest + heads * per_line]
        )
        low = summed.astype(bf16)
        mine = exchange_relative(
            [lax.dynamic_index_in_dim(low, s ^ p, 0, keepdims=False) for p in range(n)], "shard"
        )
        lane = lax.iota(jnp.int32, full)[None, :]
        own_lane = (lane >= at) & (lane < at + rest)
        mine = jnp.stack(
            [jnp.where(own_lane, low[p], mine[p]) for p in range(n)] + [low[n]], axis=0
        )
        blocks = {0: mine, 1: swap(mine, "expert", 1), 4: swap(mine, "expert", 4)}
        blocks[2] = swap(mine, "expert", 2)
        blocks[2], blocks[1] = lax.optimization_barrier((blocks[2], blocks[1]))
        blocks[3] = swap(blocks[2], "expert", 1)
        blocks[4], blocks[3] = lax.optimization_barrier((blocks[4], blocks[3]))
        blocks[6] = swap(blocks[4], "expert", 2)
        blocks[5] = swap(blocks[4], "expert", 1)
        blocks[6], grad_tokens = lax.optimization_barrier((blocks[6], grad_tokens))
        blocks[7] = swap(blocks[6], "expert", 1)
        blocks = [blocks[d] for d in range(m)]
        grad_attention_in, grad_attention_out, total_one, total_two, total_router = call(
            lambda *refs: assemble(n, m, part, piece, experts, *refs),
            (
                shape((part, 3 * width), f32),
                shape((part, width), f32),
                shape((1, part), f32),
                shape((1, part), f32),
                shape((experts, part), f32),
            ),
            (*blocks,),
            "",
            [pltpu.VMEM((part, 128), f32)],
        )
    else:
        grad_up, grad_down = kept_weights(row_blocks)
        came = lax.all_to_all(
            shares[0].reshape(n, m, piece, wide).swapaxes(0, 1), "expert", 0, 0, tiled=True
        )
        summed = sum(x.astype(f32) for x in came).astype(bf16)
        mine = lax.all_to_all(summed, "shard", 0, 0, tiled=True)
        mine = mine.reshape(n, piece, 3, part).transpose(1, 2, 0, 3).reshape(piece, 3 * width)
        came = lax.all_to_all(shares[1].reshape(m, piece, width), "expert", 0, 0, tiled=True)
        out_mine = sum(x.astype(f32) for x in came).astype(bf16)
        grad_attention_in = lax.all_gather(mine, "expert", axis=0, tiled=True).astype(f32)
        grad_attention_out = lax.all_gather(out_mine, "expert", axis=0, tiled=True).astype(f32)
        small = jnp.concatenate([gain_row[0:1], grad_gain_two[None], grad_router], axis=0)
        small_total = lax.psum_scatter(small, "shard", scatter_dimension=1, tiled=True)
        small_total, table_total = lax.psum(
            (small_total, biases(table[:, : heads * per_line])), "expert"
        )
        total_one, total_two, total_router = small_total[0:1], small_total[1:2], small_total[2:]
    return (
        layer_out,
        grad_tokens,
        grad_attention_in,
        grad_attention_out,
        table_total,
        total_one[0],
        total_two[0],
        total_router.T,
        grad_up,
        grad_down,
    )


def solution(mesh):
    in_specs = (
        P(("expert", "shard"), None),
        P("expert", None),
        P(("expert", "shard"), None),
        P("shard", None),
        P("shard", None),
        P("shard", None),
        P("shard"),
        P("shard"),
        P(),
        P("expert", None, "shard"),
        P("expert", "shard", None),
        P(("expert", "shard"), None),
    )
    out_specs = (
        P(("expert", "shard"), None),
        P(("expert", "shard"), None),
        P("shard", None),
        P("shard", None),
        P("shard", None),
        P("shard"),
        P("shard"),
        P("shard", None),
        P("expert", None, "shard"),
        P("expert", "shard", None),
    )
    return jax.shard_map(local, mesh=mesh, in_specs=in_specs, out_specs=out_specs, check_vma=False)
```

```python
import jax
import jax.numpy as jnp
from jax import lax
from jax.experimental import pallas as pl
from jax.experimental.pallas import tpu as pltpu
from jax.sharding import PartitionSpec as P

norm_eps = 1e-06
gelu_scale = 0.7978845608028654
gelu_cubic = 0.044715
big_negative = -1e30
near_steps = 8
far_steps = (12, 16, 23, 32, 46, 64, 91)
bf16 = jnp.bfloat16
f32 = jnp.float32
row_tile = 8
pair = 1
slot_tile = 4


def bucket_index(offset):
    distance = jnp.abs(offset)
    far_level = jnp.full_like(distance, near_steps)
    for step_edge in far_steps:
        far_level = far_level + (distance >= step_edge).astype(jnp.int32)
    near = jnp.where(distance < near_steps, distance, far_level)
    return near + 16 * (offset > 0).astype(jnp.int32)


def dot(left, right):
    return jnp.dot(left, right, preferred_element_type=f32)


def dot_nt(left, right):
    return lax.dot_general(left, right, (((1,), (1,)), ((), ())), preferred_element_type=f32)


def dot_tn(left, right):
    return lax.dot_general(left, right, (((0,), (0,)), ((), ())), preferred_element_type=f32)


def swap(value, axis, bit):
    size = lax.axis_size(axis)
    return lax.ppermute(value, axis, [(i, i ^ bit) for i in range(size)])


def gather_relative(value, axis):
    blocks = [value]
    bit = lax.axis_size(axis) // 2
    parts = {0: value}
    while bit:
        for p in list(parts):
            parts[p ^ bit] = swap(parts[p], axis, bit)
        bit //= 2
    return [parts[p] for p in range(lax.axis_size(axis))]


def exchange_relative(blocks, axis):
    return [blocks[0]] + [swap(block, axis, p) for p, block in enumerate(blocks) if p]


def call(kernel, out_shape, operands, spaces="", scratch=(), work=0):
    vmem = pl.BlockSpec(memory_space=pltpu.VMEM)
    smem = pl.BlockSpec(memory_space=pltpu.SMEM)
    in_specs = [smem if spaces[i : i + 1] == "s" else vmem for i in range(len(operands))]
    return pl.pallas_call(
        kernel,
        out_shape=out_shape,
        in_specs=in_specs,
        out_specs=jax.tree.map(lambda _: vmem, out_shape),
        scratch_shapes=list(scratch),
        compiler_params=pltpu.CompilerParams(vmem_limit_bytes=56 * 2**20),
        cost_estimate=pl.CostEstimate(flops=work, bytes_accessed=0, transcendentals=0),
    )(*operands)


def shape(dims, dtype=bf16):
    return jax.ShapeDtypeStruct(tuple(dims), dtype)


def diagonal(size):
    return lax.broadcasted_iota(jnp.int32, (size, size), 0) == lax.broadcasted_iota(
        jnp.int32, (size, size), 1
    )


def to_column(row, size):
    return jnp.sum(jnp.where(diagonal(size), row, 0.0), axis=1, keepdims=True)


def to_row(column, size):
    return jnp.sum(jnp.where(diagonal(size), column, 0.0), axis=0, keepdims=True)


def prepare_weight(n, part, weight, gain_one, gain_two, *outs):
    wide = 3 * part
    s = lax.axis_index("shard")
    extra = outs[0].shape[1] - wide
    one, two = (
        to_column(gain[...].astype(f32).reshape(1, part), part) for gain in (gain_one, gain_two)
    )
    lane = lax.broadcasted_iota(jnp.int32, (part, extra), 1)
    beside = jnp.where(lane == 0, one, jnp.where(lane == 1, two, 0.0)).astype(bf16)
    for p in range(n):
        outs[p][:, wide:] = beside
    for k in range(n):

        @pl.when(s == k)
        def _():
            for p in range(n):
                for kind in range(3):
                    at = (kind * n + (k ^ p)) * part
                    outs[p][:, kind * part : (kind + 1) * part] = weight[:, at : at + part]


def offsets(rows):
    return lax.broadcasted_iota(jnp.int32, (rows, rows), 1) - lax.broadcasted_iota(
        jnp.int32, (rows, rows), 0
    )


def near_buckets(diff, buckets):
    if diff == 0:
        return range(buckets)
    return range(buckets // 2, buckets) if diff > 0 else range(buckets // 2)


def attention_forward(n, rows, width, heads, seqs, buckets, *refs):
    lengths, table = refs[:2]
    token_refs = refs[2 : 2 + n]
    weight_refs = refs[2 + n : 2 + 2 * n]
    tokens_out, weight_out, projected_out, weights_out, *gains_out, mixed_all = refs[
        2 + 2 * n : 9 + 2 * n
    ]
    mixed_out = refs[9 + 2 * n : 9 + 3 * n]
    normed_scr, scores_scr = refs[9 + 3 * n :]
    s = lax.axis_index("shard")
    part = width // n
    wide = 3 * part
    head_dim = part // heads
    for p in range(n):
        tokens_out[s ^ p] = token_refs[p][...]
        weight_out[pl.ds(pl.multiple_of((s ^ p) * part, part & -part), part), :] = weight_refs[p][...]
    size = 128
    for c in range(width // size):
        beside = weight_out[c * size : (c + 1) * size, wide:].astype(f32)
        for i in range(2):
            row = to_row(beside[:, i : i + 1], size)
            gains_out[i][:, c * size : (c + 1) * size] = jnp.broadcast_to(
                row, (gains_out[i].shape[0], size)
            )
    gain = gains_out[0][...]
    for j in range(n):
        value = tokens_out[j].astype(f32)
        factor = lax.rsqrt(jnp.mean(value * value, axis=-1, keepdims=True) + norm_eps)
        normed_scr[j * rows : (j + 1) * rows, :] = (value * factor * gain).astype(bf16)
    projected_out[...] = dot(normed_scr[...], weight_out[:, :wide]).astype(bf16)
    total_rows = n * rows
    key_place = lax.broadcasted_iota(jnp.int32, (1, total_rows), 1)
    key_segment = jnp.zeros((1, total_rows), jnp.int32)
    end = jnp.int32(0)
    ends = []
    for j in range(seqs):
        end = end + lengths[0, j]
        ends.append(end)
        key_segment = key_segment + (key_place >= end).astype(jnp.int32)
    base = offsets(rows)
    steps = {diff: bucket_index(base + diff * rows) for diff in (-1, 0, 1)}
    for h in range(heads):
        query = projected_out[:, h * head_dim : (h + 1) * head_dim]
        key = projected_out[:, part + h * head_dim : part + (h + 1) * head_dim]
        value = projected_out[:, 2 * part + h * head_dim : 2 * part + (h + 1) * head_dim]
        bias = {}
        for diff in (-1, 0, 1):
            block = jnp.zeros((rows, rows), f32)
            for b in near_buckets(diff, buckets):
                block = jnp.where(steps[diff] == b, table[h, b], block)
            bias[diff] = block
        low_side = jnp.full((rows, rows), table[h, buckets // 2 - 1], f32)
        high_side = jnp.full((rows, rows), table[h, buckets - 1], f32)
        scores_scr[...] = dot_nt(query, key)
        for i in range(n):
            scores = scores_scr[i * rows : (i + 1) * rows, :]
            side = [
                bias[j - i] if abs(j - i) <= 1 else (high_side if j > i else low_side)
                for j in range(n)
            ]
            scores = scores + jnp.concatenate(side, axis=1)
            query_place = i * rows + lax.broadcasted_iota(jnp.int32, (rows, 1), 0)
            query_segment = jnp.zeros((rows, 1), jnp.int32)
            for j in range(seqs):
                query_segment = query_segment + (query_place >= ends[j]).astype(jnp.int32)
            scores = jnp.where(query_segment == key_segment, scores, big_negative)
            top = jnp.max(scores, axis=-1, keepdims=True)
            raised = jnp.exp(scores - top)
            total = jnp.sum(raised, axis=-1, keepdims=True)
            weights = (raised * (1.0 / total)).astype(bf16)
            weights_out[h, i * rows : (i + 1) * rows, :] = weights
        mixed_all[:, :, h * head_dim : (h + 1) * head_dim] = (
            dot(weights_out[h], value).astype(bf16).reshape(n, rows, head_dim)
        )
    for p in range(n):
        mixed_out[p][...] = mixed_all[s ^ p]


def attention_backward(n, m, rows, width, heads, buckets, experts, *refs):
    projected, tokens, gains, weight, weights, mixed, weight_out, gain_two, router = refs[:9]
    branch_refs = refs[9 : 9 + n]
    at = 9 + n
    shares = 5 if m > 1 else 2
    share_out = refs[at : at + shares]
    projected_scr, gain_out, table_out = refs[at + shares : at + shares + 3]
    branch_scr, scores_scr, total_scr, out_scr, normed_scr, weights_scr = refs[at + shares + 3 :]
    s = lax.axis_index("shard")
    e = lax.axis_index("expert")
    part = width // n
    wide = 3 * part
    group = n * rows
    head_dim = part // heads
    for p in range(n):
        branch_scr[s ^ p] = branch_refs[p][...]
    branch = branch_scr[...].reshape(group, width)
    grad_mixed = dot_nt(branch, weight_out[...]).astype(bf16)
    out_scr[...] = dot_tn(mixed[...].reshape(group, part), branch)
    base = offsets(rows)
    steps = {diff: bucket_index(base + diff * rows) for diff in (-1, 0, 1)}
    lane = lax.broadcasted_iota(jnp.int32, (row_tile, 128), 1)
    line = lax.broadcasted_iota(jnp.int32, (row_tile, 128), 0)
    table_total = jnp.zeros((row_tile, 128), f32)
    per_line = buckets // row_tile
    for h in range(heads):
        query = projected[:, h * head_dim : (h + 1) * head_dim]
        key = projected[:, part + h * head_dim : part + (h + 1) * head_dim]
        value = projected[:, 2 * part + h * head_dim : 2 * part + (h + 1) * head_dim]
        near = {diff: jnp.zeros((rows, rows), f32) for diff in (-1, 0, 1)}
        low_side = jnp.zeros((1, rows), f32)
        high_side = jnp.zeros((1, rows), f32)
        upstream = grad_mixed[:, h * head_dim : (h + 1) * head_dim]
        weights_scr[...] = dot_nt(upstream, value)
        for i in range(n):
            weights_i = weights[h, i * rows : (i + 1) * rows, :].astype(f32)
            grad_weights = weights_scr[i * rows : (i + 1) * rows, :]
            inner = jnp.sum(weights_i * grad_weights, axis=-1, keepdims=True)
            grad_scores = weights_i * (grad_weights - inner)
            scores_scr[i * rows : (i + 1) * rows, :] = grad_scores.astype(bf16)
            for j in range(n):
                block = grad_scores[:, j * rows : (j + 1) * rows]
                if abs(j - i) <= 1:
                    near[j - i] = near[j - i] + block
                elif j > i:
                    high_side = high_side + jnp.sum(block, axis=0, keepdims=True)
                else:
                    low_side = low_side + jnp.sum(block, axis=0, keepdims=True)
        for b in range(buckets):
            amount = jnp.zeros((1, rows), f32)
            for diff in (-1, 0, 1):
                if b in near_buckets(diff, buckets):
                    amount = amount + jnp.sum(
                        jnp.where(steps[diff] == b, near[diff], 0.0), axis=0, keepdims=True
                    )
            if b == buckets - 1:
                amount = amount + high_side
            if b == buckets // 2 - 1:
                amount = amount + low_side
            amount = jnp.sum(amount, axis=1, keepdims=True)
            spot = (line == b // per_line) & (lane == h * per_line + b % per_line)
            table_total = jnp.where(spot, amount, table_total)
        grad_scores_all = scores_scr[...]
        projected_scr[:, h * head_dim : (h + 1) * head_dim] = dot(grad_scores_all, key).astype(bf16)
        projected_scr[:, part + h * head_dim : part + (h + 1) * head_dim] = (
            dot_tn(query, grad_scores_all).T.astype(bf16)
        )
        projected_scr[:, 2 * part + h * head_dim : 2 * part + (h + 1) * head_dim] = (
            dot_tn(upstream, weights[h]).T.astype(bf16)
        )
    table_out[...] = table_total
    grad_projected = projected_scr[...]
    gain = gains[...]
    for j in range(n):
        value = tokens[j].astype(f32)
        unit = value * lax.rsqrt(jnp.mean(value * value, axis=-1, keepdims=True) + norm_eps)
        normed_scr[j * rows : (j + 1) * rows, :] = (unit * gain).astype(bf16)
    grad_weight = dot_tn(normed_scr[...], grad_projected)
    total_scr[:, :wide] = grad_weight
    grad_gain = jnp.sum(grad_weight * weight[:, :wide].astype(f32), axis=1, keepdims=True)
    grad_gain = grad_gain / weight[:, wide : wide + 1].astype(f32)
    size = 128
    for c in range(width // size):
        here = slice(c * size, (c + 1) * size)
        gain_out[:, here] = to_row(grad_gain[here], size)
    full = total_scr.shape[1]
    if m == 1:
        for t in range(n):
            share_out[0][t] = total_scr[t * part : (t + 1) * part, :wide].astype(bf16)
        share_out[1][...] = out_scr[...].astype(bf16)
        return
    piece = part // m
    total_scr[:, wide:] = jnp.zeros((width, full - wide), f32)
    grad_two = gain_two[...].reshape(1, width)
    total_scr[:, wide : wide + 1] = grad_gain
    for c in range(width // size):
        here = slice(c * size, (c + 1) * size)
        total_scr[here, wide + 1 : wide + 2] = to_column(grad_two[:, here], size)
        total_scr[here, wide + 2 : wide + 2 + experts] = router[:, here].T
    at = wide + 2 + experts
    rest = (width - full) // n
    for t in range(n):
        total_scr[t * part : (t + 1) * part, at : at + rest] = out_scr[
            :, full + t * rest : full + (t + 1) * rest
        ]
    at = at + rest
    for d in range(m):
        total_scr[d * piece : d * piece + row_tile, at : at + heads * per_line] = table_total[
            :, : heads * per_line
        ]
    near_keep, far_keep, near_send, far_send, last_send = share_out
    for d in range(m):
        place = (d >> 1) % (m // 4)
        target = (far_send if d & 1 else far_keep) if d >= m // 2 else (near_send if d & 1 else near_keep)
        if d == m - 1:
            target, place = last_send, 0
        start = (e ^ d) * piece
        for t in range(n):
            rows_at = pl.multiple_of(t * part + start, row_tile)
            target[place, t] = total_scr[pl.ds(rows_at, piece), :].astype(bf16)
        rows_at = pl.multiple_of(start, row_tile)
        target[place, n] = out_scr[pl.ds(rows_at, piece), :full].astype(bf16)


def normed_backward(n, rows, projected, weight, keep_out, send_out, send_scr):
    s = lax.axis_index("shard")
    wide = projected.shape[1]
    grad = dot_nt(projected[...], weight[:, :wide])
    send_scr[...] = grad.astype(bf16).reshape(send_scr.shape)
    for p in range(n):
        (send_out if p & 1 else keep_out)[p >> 1] = send_scr[s ^ p]


def beside_columns(ref, p, wide):
    last = ref[p, :, ref.shape[2] - 128 :]
    skip = wide - (ref.shape[2] - 128)
    return jnp.concatenate([last[:, skip:], last[:, :skip]], axis=1)


def assemble(n, m, part, piece, experts, *refs):
    total_out, out_out, one_out, two_out, router_out, small_scr = refs[m:]
    s = lax.axis_index("shard")
    e = lax.axis_index("expert")
    wide = 3 * part
    full = refs[0].shape[2]
    at = wide + 2 + experts
    rest = (n * part - full) // n
    for d in range(m):
        start = pl.multiple_of((e ^ d) * piece, row_tile)
        own = pl.ds(start, piece)
        small = jnp.zeros((piece, 128), f32)
        for p in range(n):
            small = small + beside_columns(refs[d], p, wide).astype(f32)
            out_out[own, full + p * rest : full + (p + 1) * rest] = refs[d][p, :, at : at + rest].astype(
                f32
            )
        out_out[own, :full] = refs[d][n].astype(f32)
        small_scr[own, :] = small
    small = small_scr[...].T
    one_out[...] = small[0:1, :]
    two_out[...] = small[1:2, :]
    router_out[...] = small[2 : 2 + experts, :]
    for k in range(n):

        @pl.when(s == k)
        def _():
            for d in range(m):
                own = pl.ds(pl.multiple_of((e ^ d) * piece, row_tile), piece)
                for p in range(n):
                    for kind in range(3):
                        to = (kind * n + (k ^ p)) * part
                        total_out[own, to : to + part] = refs[d][
                            p, :, kind * part : (kind + 1) * part
                        ].astype(f32)


def expert_forward(rows, own, came, up_own, up_pair, down_own, down_pair, *outs):
    hidden_out, slope_out, keep_out, send_out = outs
    source = jnp.concatenate([own[...], came[...]], axis=0)
    result = 0.0
    for k, (up, down) in enumerate(((up_own, down_own), (up_pair, down_pair))):
        before = dot(source, up[0])
        square = before * before
        tanh_value = jnp.tanh(gelu_scale * before * (1.0 + gelu_cubic * square))
        half = 0.5 * (1.0 + tanh_value)
        hidden = (before * half).astype(bf16)
        slope = half + 0.5 * before * (1.0 - tanh_value * tanh_value) * gelu_scale * (
            1.0 + 3.0 * gelu_cubic * square
        )
        hidden_out[k] = hidden
        slope_out[k] = slope.astype(bf16)
        result = result + dot(hidden, down[0])
    keep_out[...] = result[:rows]
    send_out[...] = result[rows:].astype(bf16)


def expert_backward(rows, own, came, up_own, up_pair, down_own, down_pair, slope, *outs):
    before_out, keep_out, send_out = outs
    grads = jnp.concatenate([own[...], came[...]], axis=0)
    result = 0.0
    for k, (up, down) in enumerate(((up_own, down_own), (up_pair, down_pair))):
        grad_before = (dot_nt(grads, down[0]) * slope[k].astype(f32)).astype(bf16)
        before_out[k] = grad_before
        result = result + dot_nt(grad_before, up[0])
    keep_out[...] = result[:rows]
    send_out[...] = result[rows:].astype(bf16)


def weights_to_send(own, came, own_grad, came_grad, hidden, grad_before, up_send, down_send):
    grads = jnp.concatenate([own_grad[...], came_grad[...]], axis=0)
    rows = jnp.concatenate([own[...], came[...]], axis=0)
    up_send[0] = dot_tn(rows, grad_before[1]).astype(bf16)
    down_send[0] = dot_tn(hidden[1], grads).astype(bf16)


def weights_to_keep(
    own, came, own_grad, came_grad, hidden, grad_before, up_came, down_came, up_out, down_out
):
    grads = jnp.concatenate([own_grad[...], came_grad[...]], axis=0)
    rows = jnp.concatenate([own[...], came[...]], axis=0)
    up_out[0] = dot_tn(rows, grad_before[0]) + up_came[0].astype(f32)
    down_out[0] = dot_tn(hidden[0], grads) + down_came[0].astype(f32)


def rms_factor(value):
    return lax.rsqrt(jnp.mean(value * value, axis=-1, keepdims=True) + norm_eps)


def rms_backward(value, factor, gain, upstream):
    scaled = upstream * gain
    grad_value = factor * scaled - value * factor * factor * factor * jnp.mean(
        scaled * value, axis=-1, keepdims=True
    )
    grad_gain = jnp.sum(upstream * value * factor, axis=0)
    return (grad_value, grad_gain)


def local(
    tokens,
    lengths,
    routes,
    attention_in,
    attention_out,
    position_bias,
    first_gain,
    second_gain,
    router,
    expert_in,
    expert_out,
    cotangent,
):
    n = lax.axis_size("shard")
    m = lax.axis_size("expert")
    s = lax.axis_index("shard")
    e = lax.axis_index("expert")
    rows, width = tokens.shape
    heads, buckets = position_bias.shape
    part = width // n
    wide = 3 * part
    group = n * rows
    seqs = lengths.shape[1]
    experts = router.shape[1]
    direct = m == 8
    full = wide + -wide % 128
    micro = 10**9

    far_tokens, pair_tokens = swap(tokens, "shard", 2 * pair), swap(tokens, "shard", pair)
    weight_blocks = exchange_relative(
        call(
            lambda *refs: prepare_weight(n, part, *refs),
            [shape((part, full))] * n,
            (attention_in, first_gain, second_gain),
        ),
        "shard",
    )
    far_tokens, own_up, own_down, table_scalars = lax.optimization_barrier(
        (far_tokens, expert_in, expert_out, position_bias.astype(f32))
    )
    token_blocks = [tokens, pair_tokens, far_tokens, swap(far_tokens, "shard", pair)]
    pair_up = swap(own_up, "shard", pair)
    pair_down = swap(own_down, "shard", pair)
    own_out, token_blocks, weight_blocks = lax.optimization_barrier(
        (attention_out, token_blocks, weight_blocks)
    )
    far_out, pair_out = swap(own_out, "shard", 2 * pair), swap(own_out, "shard", pair)

    answers = call(
        lambda *refs: attention_forward(n, rows, width, heads, seqs, buckets, *refs),
        (
            shape((n, rows, width)),
            shape((width, full)),
            shape((group, wide)),
            shape((heads, group, group)),
            shape((1, width), f32),
            shape((rows, width), f32),
            shape((n, rows, part)),
            *[shape((rows, part))] * n,
        ),
        (lengths, table_scalars, *token_blocks, *weight_blocks),
        "ss",
        [pltpu.VMEM((group, width), bf16), pltpu.VMEM((group, group), f32)],
        work=10 * micro,
    )
    tokens_all, weight, projected, weights, gain_one, gain_two, mixed = answers[:7]
    mixed_mine, pair_up, pair_down, pair_out = lax.optimization_barrier(
        (list(answers[7:]), pair_up, pair_down, pair_out)
    )
    mixed_blocks = exchange_relative(mixed_mine, "shard")
    out_blocks = [own_out, pair_out, far_out, swap(far_out, "shard", pair)]

    inputs = tokens.astype(f32)
    hidden_one = inputs + sum(dot(mixed_blocks[p], out_blocks[p]) for p in range(n))
    factor_two = rms_factor(hidden_one)
    normed_two = hidden_one * factor_two * gain_two
    logits = jnp.dot(
        normed_two, router, precision=lax.Precision.HIGHEST, preferred_element_type=f32
    )
    shifted = jnp.exp(logits - jnp.max(logits, axis=-1, keepdims=True))
    probs = shifted / jnp.sum(shifted, axis=-1, keepdims=True)
    route = routes[:, 0]
    chosen = (route[:, None] == lax.iota(jnp.int32, experts)[None, :]).astype(f32)
    gate = jnp.sum(probs * chosen, axis=1)
    lower = (lax.iota(jnp.int32, rows)[:, None] >= lax.iota(jnp.int32, rows)[None, :]).astype(bf16)
    running = dot(lower, chosen.astype(bf16))
    slot = jnp.sum((running - 1.0) * chosen, axis=1).astype(jnp.int32)
    capacity = max(2, 9 * rows // (8 * experts) + 1)
    capacity = -(-capacity // slot_tile) * slot_tile
    places = experts * capacity
    half = places // 2
    if direct:
        holder = route ^ e
        target = (holder & 1) * half + (holder >> 1) * capacity + slot
    else:
        target = route * capacity + slot
    collect = (target[:, None] == lax.iota(jnp.int32, places)[None, :]).astype(bf16)
    upstream = cotangent.astype(f32)
    grad_result = (gate[:, None] * upstream).astype(bf16)

    def plain(value):
        return lax.all_to_all(
            value.reshape(experts, capacity, width), "expert", 0, 0, tiled=True
        ).reshape(places, width)

    def dispatch(forward, backward):
        if not direct:
            return [plain(dot_tn(collect, x).astype(bf16)) for x in (forward, backward)]
        came = swap(dot_tn(collect[:, half:], forward).astype(bf16), "expert", 1)
        came, other = lax.optimization_barrier(
            (came, dot_tn(collect[:, half:], backward).astype(bf16))
        )

        def both(own, came):
            own = dot_tn(collect[:, :half], own).astype(bf16).reshape(m // 2, capacity, width)
            return jnp.concatenate([own, came.reshape(m // 2, capacity, width)], axis=1)

        first = among_pairs(both(forward, came))
        second, first[1] = lax.optimization_barrier(
            (both(backward, swap(other, "expert", 1)), first[1])
        )
        return [jnp.concatenate(x, axis=0) for x in (first, among_pairs(second))]

    def among_pairs(both):
        return [both[d] if d == 0 else swap(both[d], "expert", 2 * d) for d in range(m // 2)]

    def give_back(forward, backward, late, work):
        if not direct:
            return [dot(collect, plain(x)) for x in (forward, backward)] + [work(late)]
        forward, backward = (
            x.reshape(m // 2, 2 * capacity, width) for x in (forward, backward)
        )
        blocks = [among_pairs(forward)]
        backward, blocks[0][1] = lax.optimization_barrier((backward, blocks[0][1]))
        blocks.append(among_pairs(backward))
        late, blocks = lax.optimization_barrier((late, blocks))
        own, other = (
            jnp.concatenate(
                [jnp.concatenate([x[at : at + capacity] for x in side]) for side in blocks], axis=1
            )
            for at in (0, capacity)
        )
        beside = work(late)
        other, beside = lax.optimization_barrier((swap(other, "expert", 1), beside))
        total = dot(collect[:, :half], own) + dot(collect[:, half:], other)
        return total[:, :width], total[:, width:], beside

    def reduce_shard(keep, out, after=None):
        came = swap(out, "shard", 2 * pair)
        if after is not None:
            came, _ = lax.optimization_barrier((came, after))
        return (keep + came.astype(f32)).astype(bf16)

    arrived, arrived_grad = dispatch(normed_two.astype(bf16), grad_result)
    came = swap(arrived, "shard", 2 * pair)
    row_blocks = (arrived, came)
    grad_blocks = (arrived_grad, swap(arrived_grad, "shard", 2 * pair))

    units = expert_in.shape[2]
    expert_weight = (own_up, pair_up, own_down, pair_down)
    middle = shape((2, 2 * places, units))
    kept, sent = shape((places, width), f32), shape((places, width))
    hidden, slope, *forward = call(
        lambda *refs: expert_forward(places, *refs),
        (middle, middle, kept, sent),
        (*row_blocks, *expert_weight),
        work=6 * micro,
    )
    grad_before, *backward = call(
        lambda *refs: expert_backward(places, *refs),
        (middle, kept, sent),
        (*grad_blocks, *expert_weight, slope),
        work=6 * micro,
    )
    sources = (*grad_blocks, hidden, grad_before)
    expert_result, grad_sent, (up_send, down_send) = give_back(
        reduce_shard(*forward, backward[1]),
        reduce_shard(*backward),
        row_blocks,
        lambda rows_late: call(
            weights_to_send,
            (shape(expert_in.shape), shape(expert_out.shape)),
            (*rows_late, *sources),
            work=4 * micro,
        ),
    )

    layer_out = (hidden_one + gate[:, None] * expert_result).astype(bf16)
    grad_gate = jnp.sum(upstream * expert_result, axis=1)
    grad_logits = (grad_gate * gate)[:, None] * (chosen - probs)
    grad_router = lax.dot_general(
        grad_logits,
        normed_two,
        (((0,), (0,)), ((), ())),
        precision=lax.Precision.HIGHEST,
        preferred_element_type=f32,
    )
    grad_normed_two = grad_sent + lax.dot_general(
        grad_logits,
        router,
        (((1,), (1,)), ((), ())),
        precision=lax.Precision.HIGHEST,
        preferred_element_type=f32,
    )
    grad_middle, grad_gain_two = rms_backward(hidden_one, factor_two, gain_two, grad_normed_two)
    grad_hidden = upstream + grad_middle
    branch = grad_hidden.astype(bf16)
    far_branch, pair_branch = swap(branch, "shard", 2 * pair), swap(branch, "shard", pair)
    far_branch, grad_router, gain_two_row = lax.optimization_barrier(
        (far_branch, grad_router, grad_gain_two)
    )
    branch_blocks = [branch, pair_branch, far_branch, swap(far_branch, "shard", pair)]
    branch_blocks, up_send, down_send = lax.optimization_barrier(
        (branch_blocks, up_send, down_send)
    )
    up_came, down_came = swap(up_send, "shard", pair), swap(down_send, "shard", pair)
    holders = m if direct else 1
    piece = part // m
    if direct:
        share_shapes = [
            shape((held, n + 1, piece, full)) for held in (m // 4, m // 4, m // 4, m // 4 - 1, 1)
        ]
    else:
        share_shapes = [shape((n, part, wide)), shape((part, width))]
    answers = call(
        lambda *refs: attention_backward(n, holders, rows, width, heads, buckets, experts, *refs),
        (
            *share_shapes,
            shape((group, wide)),
            shape((1, width), f32),
            shape((row_tile, 128), f32),
        ),
        (
            projected,
            tokens_all,
            gain_one,
            weight,
            weights,
            mixed,
            own_out,
            gain_two_row,
            grad_router,
            *branch_blocks,
        ),
        "",
        [
            pltpu.VMEM((n, rows, width), bf16),
            pltpu.VMEM((group, group), bf16),
            pltpu.VMEM((width, full), f32),
            pltpu.VMEM((part, width), f32),
            pltpu.VMEM((group, width), bf16),
            pltpu.VMEM((group, group), f32),
        ],
        work=8 * micro,
    )
    shares = answers[: len(share_shapes)]
    grad_projected, gain_row, table = answers[len(share_shapes) :]

    def kept_weights(late_rows):
        return call(
            weights_to_keep,
            (shape(expert_in.shape, f32), shape(expert_out.shape, f32)),
            (*late_rows, *sources, up_came, down_came),
            work=4 * micro,
        )

    per_line = buckets // row_tile

    def biases(block):
        return block.reshape(row_tile, heads, per_line).swapaxes(0, 1).reshape(heads, buckets)

    def normed_gradients(projected):
        return call(
            lambda *refs: normed_backward(n, rows, *refs),
            [shape((n // 2, rows, width))] * 2,
            (projected, weight),
            "",
            [pltpu.VMEM((n, rows, width), bf16)],
            work=2 * micro,
        )

    def finish_tokens(normed_keep, pair_came):
        normed_sum = normed_keep.astype(f32) + pair_came.astype(f32)
        far_sum = swap(normed_sum[1].astype(bf16), "shard", 2 * pair)
        late, far_sum = lax.optimization_barrier((tokens, far_sum))
        late = late.astype(f32)
        grad_input_norm, _ = rms_backward(
            late, rms_factor(late), gain_one, normed_sum[0] + far_sum.astype(f32)
        )
        return (grad_hidden + grad_input_norm).astype(bf16)

    if direct:
        near_keep, far_keep, near_send, far_send, last_send = shares
        last_came = swap(last_send, "expert", 1)[0]
        far_came = swap(far_send, "expert", 1)
        far_came, near_send, up_came, down_came = lax.optimization_barrier(
            (far_came, near_send, up_came, down_came)
        )
        last_came, late_rows = lax.optimization_barrier((last_came, row_blocks))
        came = [swap((far_keep[-1].astype(f32) + last_came.astype(f32)).astype(bf16), "expert", m - 2)]
        far = far_keep[:-1].astype(f32) + far_came.astype(f32)
        near_came, (grad_up, grad_down), grad_projected = lax.optimization_barrier(
            (swap(near_send, "expert", 1), kept_weights(late_rows), grad_projected)
        )
        normed_keep, normed_send = normed_gradients(grad_projected)
        normed_came = swap(normed_send, "shard", pair)
        near = near_keep.astype(f32) + near_came.astype(f32)
        came += [swap(far[d].astype(bf16), "expert", m // 2 + 2 * d) for d in range(m // 4 - 1)]
        came += [swap(near[d].astype(bf16), "expert", 2 * d) for d in range(1, m // 4)]
        came, normed_came = lax.optimization_barrier((came, normed_came))
        summed = near[0] + sum(x.astype(f32) for x in came)
        at = wide + 2 + experts
        rest = (width - full) // n
        table_total = biases(
            summed[0, :row_tile, at + rest : at + rest + heads * per_line]
        )
        low = summed.astype(bf16)
        mine = exchange_relative(
            [lax.dynamic_index_in_dim(low, s ^ p, 0, keepdims=False) for p in range(n)], "shard"
        )
        lane = lax.iota(jnp.int32, full)[None, :]
        own_lane = (lane >= at) & (lane < at + rest)
        mine = jnp.stack(
            [jnp.where(own_lane, low[p], mine[p]) for p in range(n)] + [low[n]], axis=0
        )
        blocks = {0: mine, 1: swap(mine, "expert", 1), 4: swap(mine, "expert", 4)}
        blocks[2] = swap(mine, "expert", 2)
        blocks[2], blocks[1], normed_came = lax.optimization_barrier(
            (blocks[2], blocks[1], normed_came)
        )
        grad_tokens = finish_tokens(normed_keep, normed_came)
        blocks[3] = swap(blocks[2], "expert", 1)
        blocks[4], blocks[3] = lax.optimization_barrier((blocks[4], blocks[3]))
        blocks[6] = swap(blocks[4], "expert", 2)
        blocks[5] = swap(blocks[4], "expert", 1)
        blocks[6], grad_tokens = lax.optimization_barrier((blocks[6], grad_tokens))
        blocks[7] = swap(blocks[6], "expert", 1)
        blocks = [blocks[d] for d in range(m)]
        grad_attention_in, grad_attention_out, total_one, total_two, total_router = call(
            lambda *refs: assemble(n, m, part, piece, experts, *refs),
            (
                shape((part, 3 * width), f32),
                shape((part, width), f32),
                shape((1, part), f32),
                shape((1, part), f32),
                shape((experts, part), f32),
            ),
            (*blocks,),
            "",
            [pltpu.VMEM((part, 128), f32)],
        )
    else:
        grad_up, grad_down = kept_weights(row_blocks)
        normed_keep, normed_send = normed_gradients(grad_projected)
        grad_tokens = finish_tokens(normed_keep, swap(normed_send, "shard", pair))
        came = lax.all_to_all(
            shares[0].reshape(n, m, piece, wide).swapaxes(0, 1), "expert", 0, 0, tiled=True
        )
        summed = sum(x.astype(f32) for x in came).astype(bf16)
        mine = lax.all_to_all(summed, "shard", 0, 0, tiled=True)
        mine = mine.reshape(n, piece, 3, part).transpose(1, 2, 0, 3).reshape(piece, 3 * width)
        came = lax.all_to_all(shares[1].reshape(m, piece, width), "expert", 0, 0, tiled=True)
        out_mine = sum(x.astype(f32) for x in came).astype(bf16)
        grad_attention_in = lax.all_gather(mine, "expert", axis=0, tiled=True).astype(f32)
        grad_attention_out = lax.all_gather(out_mine, "expert", axis=0, tiled=True).astype(f32)
        small = jnp.concatenate([gain_row[0:1], grad_gain_two[None], grad_router], axis=0)
        small_total = lax.psum_scatter(small, "shard", scatter_dimension=1, tiled=True)
        small_total, table_total = lax.psum(
            (small_total, biases(table[:, : heads * per_line])), "expert"
        )
        total_one, total_two, total_router = small_total[0:1], small_total[1:2], small_total[2:]
    return (
        layer_out,
        grad_tokens,
        grad_attention_in,
        grad_attention_out,
        table_total,
        total_one[0],
        total_two[0],
        total_router.T,
        grad_up,
        grad_down,
    )


def solution(mesh):
    in_specs = (
        P(("expert", "shard"), None),
        P("expert", None),
        P(("expert", "shard"), None),
        P("shard", None),
        P("shard", None),
        P("shard", None),
        P("shard"),
        P("shard"),
        P(),
        P("expert", None, "shard"),
        P("expert", "shard", None),
        P(("expert", "shard"), None),
    )
    out_specs = (
        P(("expert", "shard"), None),
        P(("expert", "shard"), None),
        P("shard", None),
        P("shard", None),
        P("shard", None),
        P("shard"),
        P("shard"),
        P("shard", None),
        P("expert", None, "shard"),
        P("expert", "shard", None),
    )
    return jax.shard_map(local, mesh=mesh, in_specs=in_specs, out_specs=out_specs, check_vma=False)
```

```python
import jax
import jax.numpy as jnp
from jax import lax
from jax.experimental import pallas as pl
from jax.experimental.pallas import tpu as pltpu
from jax.sharding import PartitionSpec as P

norm_eps = 1e-06
gelu_scale = 0.7978845608028654
gelu_cubic = 0.044715
big_negative = -1e30
near_steps = 8
far_steps = (12, 16, 23, 32, 46, 64, 91)
bf16 = jnp.bfloat16
f32 = jnp.float32
row_tile = 8
pair = 1
slot_tile = 4


def bucket_index(offset):
    distance = jnp.abs(offset)
    far_level = jnp.full_like(distance, near_steps)
    for step_edge in far_steps:
        far_level = far_level + (distance >= step_edge).astype(jnp.int32)
    near = jnp.where(distance < near_steps, distance, far_level)
    return near + 16 * (offset > 0).astype(jnp.int32)


def dot(left, right):
    return jnp.dot(left, right, preferred_element_type=f32)


def dot_nt(left, right):
    return lax.dot_general(left, right, (((1,), (1,)), ((), ())), preferred_element_type=f32)


def dot_tn(left, right):
    return lax.dot_general(left, right, (((0,), (0,)), ((), ())), preferred_element_type=f32)


def swap(value, axis, bit):
    size = lax.axis_size(axis)
    return lax.ppermute(value, axis, [(i, i ^ bit) for i in range(size)])


def gather_relative(value, axis):
    blocks = [value]
    bit = lax.axis_size(axis) // 2
    parts = {0: value}
    while bit:
        for p in list(parts):
            parts[p ^ bit] = swap(parts[p], axis, bit)
        bit //= 2
    return [parts[p] for p in range(lax.axis_size(axis))]


def exchange_relative(blocks, axis):
    return [blocks[0]] + [swap(block, axis, p) for p, block in enumerate(blocks) if p]


def call(kernel, out_shape, operands, spaces="", scratch=(), work=0):
    vmem = pl.BlockSpec(memory_space=pltpu.VMEM)
    smem = pl.BlockSpec(memory_space=pltpu.SMEM)
    in_specs = [smem if spaces[i : i + 1] == "s" else vmem for i in range(len(operands))]
    return pl.pallas_call(
        kernel,
        out_shape=out_shape,
        in_specs=in_specs,
        out_specs=jax.tree.map(lambda _: vmem, out_shape),
        scratch_shapes=list(scratch),
        compiler_params=pltpu.CompilerParams(vmem_limit_bytes=56 * 2**20),
        cost_estimate=pl.CostEstimate(flops=work, bytes_accessed=0, transcendentals=0),
    )(*operands)


def shape(dims, dtype=bf16):
    return jax.ShapeDtypeStruct(tuple(dims), dtype)


def diagonal(size):
    return lax.broadcasted_iota(jnp.int32, (size, size), 0) == lax.broadcasted_iota(
        jnp.int32, (size, size), 1
    )


def to_column(row, size):
    return jnp.sum(jnp.where(diagonal(size), row, 0.0), axis=1, keepdims=True)


def to_row(column, size):
    return jnp.sum(jnp.where(diagonal(size), column, 0.0), axis=0, keepdims=True)


def prepare_weight(n, part, weight, gain_one, gain_two, *outs):
    wide = 3 * part
    s = lax.axis_index("shard")
    extra = outs[0].shape[1] - wide
    one, two = (
        to_column(gain[...].astype(f32).reshape(1, part), part) for gain in (gain_one, gain_two)
    )
    lane = lax.broadcasted_iota(jnp.int32, (part, extra), 1)
    beside = jnp.where(lane == 0, one, jnp.where(lane == 1, two, 0.0)).astype(bf16)
    for p in range(n):
        outs[p][:, wide:] = beside
    for k in range(n):

        @pl.when(s == k)
        def _():
            for p in range(n):
                for kind in range(3):
                    at = (kind * n + (k ^ p)) * part
                    outs[p][:, kind * part : (kind + 1) * part] = weight[:, at : at + part]


def offsets(rows):
    return lax.broadcasted_iota(jnp.int32, (rows, rows), 1) - lax.broadcasted_iota(
        jnp.int32, (rows, rows), 0
    )


def near_buckets(diff, buckets):
    if diff == 0:
        return range(buckets)
    return range(buckets // 2, buckets) if diff > 0 else range(buckets // 2)


def attention_forward(n, rows, width, heads, seqs, buckets, *refs):
    lengths, table = refs[:2]
    token_refs = refs[2 : 2 + n]
    weight_refs = refs[2 + n : 2 + 2 * n]
    tokens_out, weight_out, projected_out, weights_out, *gains_out, mixed_all = refs[
        2 + 2 * n : 9 + 2 * n
    ]
    mixed_out = refs[9 + 2 * n : 9 + 3 * n]
    normed_scr, scores_scr = refs[9 + 3 * n :]
    s = lax.axis_index("shard")
    part = width // n
    wide = 3 * part
    head_dim = part // heads
    for p in range(n):
        tokens_out[s ^ p] = token_refs[p][...]
        weight_out[pl.ds(pl.multiple_of((s ^ p) * part, part & -part), part), :] = weight_refs[p][...]
    size = 128
    for c in range(width // size):
        beside = weight_out[c * size : (c + 1) * size, wide:].astype(f32)
        for i in range(2):
            row = to_row(beside[:, i : i + 1], size)
            gains_out[i][:, c * size : (c + 1) * size] = jnp.broadcast_to(
                row, (gains_out[i].shape[0], size)
            )
    gain = gains_out[0][...]
    for j in range(n):
        value = tokens_out[j].astype(f32)
        factor = lax.rsqrt(jnp.mean(value * value, axis=-1, keepdims=True) + norm_eps)
        normed_scr[j * rows : (j + 1) * rows, :] = (value * factor * gain).astype(bf16)
    projected_out[...] = dot(normed_scr[...], weight_out[:, :wide]).astype(bf16)
    total_rows = n * rows
    key_place = lax.broadcasted_iota(jnp.int32, (1, total_rows), 1)
    key_segment = jnp.zeros((1, total_rows), jnp.int32)
    end = jnp.int32(0)
    ends = []
    for j in range(seqs):
        end = end + lengths[0, j]
        ends.append(end)
        key_segment = key_segment + (key_place >= end).astype(jnp.int32)
    base = offsets(rows)
    steps = {diff: bucket_index(base + diff * rows) for diff in (-1, 0, 1)}
    for h in range(heads):
        query = projected_out[:, h * head_dim : (h + 1) * head_dim]
        key = projected_out[:, part + h * head_dim : part + (h + 1) * head_dim]
        value = projected_out[:, 2 * part + h * head_dim : 2 * part + (h + 1) * head_dim]
        bias = {}
        for diff in (-1, 0, 1):
            block = jnp.zeros((rows, rows), f32)
            for b in near_buckets(diff, buckets):
                block = jnp.where(steps[diff] == b, table[h, b], block)
            bias[diff] = block
        low_side = jnp.full((rows, rows), table[h, buckets // 2 - 1], f32)
        high_side = jnp.full((rows, rows), table[h, buckets - 1], f32)
        scores_scr[...] = dot_nt(query, key)
        for i in range(n):
            scores = scores_scr[i * rows : (i + 1) * rows, :]
            side = [
                bias[j - i] if abs(j - i) <= 1 else (high_side if j > i else low_side)
                for j in range(n)
            ]
            scores = scores + jnp.concatenate(side, axis=1)
            query_place = i * rows + lax.broadcasted_iota(jnp.int32, (rows, 1), 0)
            query_segment = jnp.zeros((rows, 1), jnp.int32)
            for j in range(seqs):
                query_segment = query_segment + (query_place >= ends[j]).astype(jnp.int32)
            scores = jnp.where(query_segment == key_segment, scores, big_negative)
            top = jnp.max(scores, axis=-1, keepdims=True)
            raised = jnp.exp(scores - top)
            total = jnp.sum(raised, axis=-1, keepdims=True)
            weights = (raised * (1.0 / total)).astype(bf16)
            weights_out[h, i * rows : (i + 1) * rows, :] = weights
        mixed_all[:, :, h * head_dim : (h + 1) * head_dim] = (
            dot(weights_out[h], value).astype(bf16).reshape(n, rows, head_dim)
        )
    for p in range(n):
        mixed_out[p][...] = mixed_all[s ^ p]


def attention_backward(n, m, rows, width, heads, buckets, experts, *refs):
    projected, tokens, gains, weight, weights, mixed, weight_out, gain_two, router = refs[:9]
    branch_refs = refs[9 : 9 + n]
    at = 9 + n
    shares = 5 if m > 1 else 2
    share_out = refs[at : at + shares]
    normed_grad_out = refs[at + shares : at + shares + 2]
    gain_out, table_out = refs[at + shares + 2 : at + shares + 4]
    branch_scr, scores_scr, projected_scr, total_scr, out_scr, normed_scr, send_scr, weights_scr = (
        refs[at + shares + 4 :]
    )
    s = lax.axis_index("shard")
    e = lax.axis_index("expert")
    part = width // n
    wide = 3 * part
    group = n * rows
    head_dim = part // heads
    for p in range(n):
        branch_scr[s ^ p] = branch_refs[p][...]
    branch = branch_scr[...].reshape(group, width)
    grad_mixed = dot_nt(branch, weight_out[...]).astype(bf16)
    out_scr[...] = dot_tn(mixed[...].reshape(group, part), branch)
    base = offsets(rows)
    steps = {diff: bucket_index(base + diff * rows) for diff in (-1, 0, 1)}
    lane = lax.broadcasted_iota(jnp.int32, (row_tile, 128), 1)
    line = lax.broadcasted_iota(jnp.int32, (row_tile, 128), 0)
    table_total = jnp.zeros((row_tile, 128), f32)
    per_line = buckets // row_tile
    for h in range(heads):
        query = projected[:, h * head_dim : (h + 1) * head_dim]
        key = projected[:, part + h * head_dim : part + (h + 1) * head_dim]
        value = projected[:, 2 * part + h * head_dim : 2 * part + (h + 1) * head_dim]
        near = {diff: jnp.zeros((rows, rows), f32) for diff in (-1, 0, 1)}
        low_side = jnp.zeros((1, rows), f32)
        high_side = jnp.zeros((1, rows), f32)
        upstream = grad_mixed[:, h * head_dim : (h + 1) * head_dim]
        weights_scr[...] = dot_nt(upstream, value)
        for i in range(n):
            weights_i = weights[h, i * rows : (i + 1) * rows, :].astype(f32)
            grad_weights = weights_scr[i * rows : (i + 1) * rows, :]
            inner = jnp.sum(weights_i * grad_weights, axis=-1, keepdims=True)
            grad_scores = weights_i * (grad_weights - inner)
            scores_scr[i * rows : (i + 1) * rows, :] = grad_scores.astype(bf16)
            for j in range(n):
                block = grad_scores[:, j * rows : (j + 1) * rows]
                if abs(j - i) <= 1:
                    near[j - i] = near[j - i] + block
                elif j > i:
                    high_side = high_side + jnp.sum(block, axis=0, keepdims=True)
                else:
                    low_side = low_side + jnp.sum(block, axis=0, keepdims=True)
        for b in range(buckets):
            amount = jnp.zeros((1, rows), f32)
            for diff in (-1, 0, 1):
                if b in near_buckets(diff, buckets):
                    amount = amount + jnp.sum(
                        jnp.where(steps[diff] == b, near[diff], 0.0), axis=0, keepdims=True
                    )
            if b == buckets - 1:
                amount = amount + high_side
            if b == buckets // 2 - 1:
                amount = amount + low_side
            amount = jnp.sum(amount, axis=1, keepdims=True)
            spot = (line == b // per_line) & (lane == h * per_line + b % per_line)
            table_total = jnp.where(spot, amount, table_total)
        grad_scores_all = scores_scr[...]
        projected_scr[:, h * head_dim : (h + 1) * head_dim] = dot(grad_scores_all, key).astype(bf16)
        projected_scr[:, part + h * head_dim : part + (h + 1) * head_dim] = (
            dot_tn(query, grad_scores_all).T.astype(bf16)
        )
        projected_scr[:, 2 * part + h * head_dim : 2 * part + (h + 1) * head_dim] = (
            dot_tn(upstream, weights[h]).T.astype(bf16)
        )
    table_out[...] = table_total
    grad_projected = projected_scr[...]
    normed_grad = dot_nt(grad_projected, weight[:, :wide])
    send_scr[...] = normed_grad.astype(bf16).reshape(n, rows, width)
    for p in range(n):
        normed_grad_out[p & 1][p >> 1] = send_scr[s ^ p]
    gain = gains[...]
    grad_gain = jnp.zeros((1, width), f32)
    for j in range(n):
        value = tokens[j].astype(f32)
        unit = value * lax.rsqrt(jnp.mean(value * value, axis=-1, keepdims=True) + norm_eps)
        normed_scr[j * rows : (j + 1) * rows, :] = (unit * gain).astype(bf16)
        grad_gain = grad_gain + jnp.sum(
            normed_grad[j * rows : (j + 1) * rows, :] * unit, axis=0, keepdims=True
        )
    gain_out[...] = jnp.broadcast_to(grad_gain, gain_out.shape)
    total_scr[:, :wide] = dot_tn(normed_scr[...], grad_projected)
    full = total_scr.shape[1]
    if m == 1:
        for t in range(n):
            share_out[0][t] = total_scr[t * part : (t + 1) * part, :wide].astype(bf16)
        share_out[1][...] = out_scr[...].astype(bf16)
        return
    piece = part // m
    total_scr[:, wide:] = jnp.zeros((width, full - wide), f32)
    grad_two = gain_two[...].reshape(1, width)
    size = 128
    for c in range(width // size):
        here = slice(c * size, (c + 1) * size)
        total_scr[here, wide : wide + 1] = to_column(grad_gain[:, here], size)
        total_scr[here, wide + 1 : wide + 2] = to_column(grad_two[:, here], size)
        total_scr[here, wide + 2 : wide + 2 + experts] = router[:, here].T
    at = wide + 2 + experts
    rest = (width - full) // n
    for t in range(n):
        total_scr[t * part : (t + 1) * part, at : at + rest] = out_scr[
            :, full + t * rest : full + (t + 1) * rest
        ]
    at = at + rest
    for d in range(m):
        total_scr[d * piece : d * piece + row_tile, at : at + heads * per_line] = table_total[
            :, : heads * per_line
        ]
    near_keep, far_keep, near_send, far_send, last_send = share_out
    for d in range(m):
        place = (d >> 1) % (m // 4)
        target = (far_send if d & 1 else far_keep) if d >= m // 2 else (near_send if d & 1 else near_keep)
        if d == m - 1:
            target, place = last_send, 0
        start = (e ^ d) * piece
        for t in range(n):
            rows_at = pl.multiple_of(t * part + start, row_tile)
            target[place, t] = total_scr[pl.ds(rows_at, piece), :].astype(bf16)
        rows_at = pl.multiple_of(start, row_tile)
        target[place, n] = out_scr[pl.ds(rows_at, piece), :full].astype(bf16)


def beside_columns(ref, p, wide):
    last = ref[p, :, ref.shape[2] - 128 :]
    skip = wide - (ref.shape[2] - 128)
    return jnp.concatenate([last[:, skip:], last[:, :skip]], axis=1)


def assemble(n, m, part, piece, experts, *refs):
    total_out, out_out, one_out, two_out, router_out, small_scr = refs[m:]
    s = lax.axis_index("shard")
    e = lax.axis_index("expert")
    wide = 3 * part
    full = refs[0].shape[2]
    at = wide + 2 + experts
    rest = (n * part - full) // n
    for d in range(m):
        start = pl.multiple_of((e ^ d) * piece, row_tile)
        own = pl.ds(start, piece)
        small = jnp.zeros((piece, 128), f32)
        for p in range(n):
            small = small + beside_columns(refs[d], p, wide).astype(f32)
            out_out[own, full + p * rest : full + (p + 1) * rest] = refs[d][p, :, at : at + rest].astype(
                f32
            )
        out_out[own, :full] = refs[d][n].astype(f32)
        small_scr[own, :] = small
    small = small_scr[...].T
    one_out[...] = small[0:1, :]
    two_out[...] = small[1:2, :]
    router_out[...] = small[2 : 2 + experts, :]
    for k in range(n):

        @pl.when(s == k)
        def _():
            for d in range(m):
                own = pl.ds(pl.multiple_of((e ^ d) * piece, row_tile), piece)
                for p in range(n):
                    for kind in range(3):
                        to = (kind * n + (k ^ p)) * part
                        total_out[own, to : to + part] = refs[d][
                            p, :, kind * part : (kind + 1) * part
                        ].astype(f32)


def expert_forward(rows, own, came, up_own, up_pair, down_own, down_pair, *outs):
    hidden_out, slope_out, keep_out, send_out = outs
    source = jnp.concatenate([own[...], came[...]], axis=0)
    result = 0.0
    for k, (up, down) in enumerate(((up_own, down_own), (up_pair, down_pair))):
        before = dot(source, up[0])
        square = before * before
        tanh_value = jnp.tanh(gelu_scale * before * (1.0 + gelu_cubic * square))
        half = 0.5 * (1.0 + tanh_value)
        hidden = (before * half).astype(bf16)
        slope = half + 0.5 * before * (1.0 - tanh_value * tanh_value) * gelu_scale * (
            1.0 + 3.0 * gelu_cubic * square
        )
        hidden_out[k] = hidden
        slope_out[k] = slope.astype(bf16)
        result = result + dot(hidden, down[0])
    keep_out[...] = result[:rows]
    send_out[...] = result[rows:].astype(bf16)


def expert_backward(rows, own, came, up_own, up_pair, down_own, down_pair, slope, *outs):
    before_out, keep_out, send_out = outs
    grads = jnp.concatenate([own[...], came[...]], axis=0)
    result = 0.0
    for k, (up, down) in enumerate(((up_own, down_own), (up_pair, down_pair))):
        grad_before = (dot_nt(grads, down[0]) * slope[k].astype(f32)).astype(bf16)
        before_out[k] = grad_before
        result = result + dot_nt(grad_before, up[0])
    keep_out[...] = result[:rows]
    send_out[...] = result[rows:].astype(bf16)


def weights_to_send(own, came, own_grad, came_grad, hidden, grad_before, up_send, down_send):
    grads = jnp.concatenate([own_grad[...], came_grad[...]], axis=0)
    rows = jnp.concatenate([own[...], came[...]], axis=0)
    up_send[0] = dot_tn(rows, grad_before[1]).astype(bf16)
    down_send[0] = dot_tn(hidden[1], grads).astype(bf16)


def weights_to_keep(
    own, came, own_grad, came_grad, hidden, grad_before, up_came, down_came, up_out, down_out
):
    grads = jnp.concatenate([own_grad[...], came_grad[...]], axis=0)
    rows = jnp.concatenate([own[...], came[...]], axis=0)
    up_out[0] = dot_tn(rows, grad_before[0]) + up_came[0].astype(f32)
    down_out[0] = dot_tn(hidden[0], grads) + down_came[0].astype(f32)


def rms_factor(value):
    return lax.rsqrt(jnp.mean(value * value, axis=-1, keepdims=True) + norm_eps)


def rms_backward(value, factor, gain, upstream):
    scaled = upstream * gain
    grad_value = factor * scaled - value * factor * factor * factor * jnp.mean(
        scaled * value, axis=-1, keepdims=True
    )
    grad_gain = jnp.sum(upstream * value * factor, axis=0)
    return (grad_value, grad_gain)


def local(
    tokens,
    lengths,
    routes,
    attention_in,
    attention_out,
    position_bias,
    first_gain,
    second_gain,
    router,
    expert_in,
    expert_out,
    cotangent,
):
    n = lax.axis_size("shard")
    m = lax.axis_size("expert")
    s = lax.axis_index("shard")
    e = lax.axis_index("expert")
    rows, width = tokens.shape
    heads, buckets = position_bias.shape
    part = width // n
    wide = 3 * part
    group = n * rows
    seqs = lengths.shape[1]
    experts = router.shape[1]
    direct = m == 8
    full = wide + -wide % 128
    micro = 10**9

    far_tokens, pair_tokens = swap(tokens, "shard", 2 * pair), swap(tokens, "shard", pair)
    weight_blocks = exchange_relative(
        call(
            lambda *refs: prepare_weight(n, part, *refs),
            [shape((part, full))] * n,
            (attention_in, first_gain, second_gain),
        ),
        "shard",
    )
    far_tokens, own_up, own_down, table_scalars = lax.optimization_barrier(
        (far_tokens, expert_in, expert_out, position_bias.astype(f32))
    )
    token_blocks = [tokens, pair_tokens, far_tokens, swap(far_tokens, "shard", pair)]
    pair_up = swap(own_up, "shard", pair)
    pair_down = swap(own_down, "shard", pair)
    own_out, token_blocks, weight_blocks = lax.optimization_barrier(
        (attention_out, token_blocks, weight_blocks)
    )
    far_out, pair_out = swap(own_out, "shard", 2 * pair), swap(own_out, "shard", pair)

    answers = call(
        lambda *refs: attention_forward(n, rows, width, heads, seqs, buckets, *refs),
        (
            shape((n, rows, width)),
            shape((width, full)),
            shape((group, wide)),
            shape((heads, group, group)),
            shape((1, width), f32),
            shape((rows, width), f32),
            shape((n, rows, part)),
            *[shape((rows, part))] * n,
        ),
        (lengths, table_scalars, *token_blocks, *weight_blocks),
        "ss",
        [pltpu.VMEM((group, width), bf16), pltpu.VMEM((group, group), f32)],
        work=10 * micro,
    )
    tokens_all, weight, projected, weights, gain_one, gain_two, mixed = answers[:7]
    mixed_mine, pair_up, pair_down, pair_out = lax.optimization_barrier(
        (list(answers[7:]), pair_up, pair_down, pair_out)
    )
    mixed_blocks = exchange_relative(mixed_mine, "shard")
    out_blocks = [own_out, pair_out, far_out, swap(far_out, "shard", pair)]

    inputs = tokens.astype(f32)
    hidden_one = inputs + sum(dot(mixed_blocks[p], out_blocks[p]) for p in range(n))
    factor_two = rms_factor(hidden_one)
    normed_two = hidden_one * factor_two * gain_two
    logits = jnp.dot(
        normed_two, router, precision=lax.Precision.HIGHEST, preferred_element_type=f32
    )
    shifted = jnp.exp(logits - jnp.max(logits, axis=-1, keepdims=True))
    probs = shifted / jnp.sum(shifted, axis=-1, keepdims=True)
    route = routes[:, 0]
    chosen = (route[:, None] == lax.iota(jnp.int32, experts)[None, :]).astype(f32)
    gate = jnp.sum(probs * chosen, axis=1)
    lower = (lax.iota(jnp.int32, rows)[:, None] >= lax.iota(jnp.int32, rows)[None, :]).astype(bf16)
    running = dot(lower, chosen.astype(bf16))
    slot = jnp.sum((running - 1.0) * chosen, axis=1).astype(jnp.int32)
    capacity = max(2, 9 * rows // (8 * experts) + 1)
    capacity = -(-capacity // slot_tile) * slot_tile
    places = experts * capacity
    half = places // 2
    if direct:
        holder = route ^ e
        target = (holder & 1) * half + (holder >> 1) * capacity + slot
    else:
        target = route * capacity + slot
    collect = (target[:, None] == lax.iota(jnp.int32, places)[None, :]).astype(bf16)
    upstream = cotangent.astype(f32)
    grad_result = (gate[:, None] * upstream).astype(bf16)

    def plain(value):
        return lax.all_to_all(
            value.reshape(experts, capacity, width), "expert", 0, 0, tiled=True
        ).reshape(places, width)

    def dispatch(forward, backward):
        if not direct:
            return [plain(dot_tn(collect, x).astype(bf16)) for x in (forward, backward)]
        came = swap(dot_tn(collect[:, half:], forward).astype(bf16), "expert", 1)
        came, other = lax.optimization_barrier(
            (came, dot_tn(collect[:, half:], backward).astype(bf16))
        )

        def both(own, came):
            own = dot_tn(collect[:, :half], own).astype(bf16).reshape(m // 2, capacity, width)
            return jnp.concatenate([own, came.reshape(m // 2, capacity, width)], axis=1)

        first = among_pairs(both(forward, came))
        second, first[1] = lax.optimization_barrier(
            (both(backward, swap(other, "expert", 1)), first[1])
        )
        return [jnp.concatenate(x, axis=0) for x in (first, among_pairs(second))]

    def among_pairs(both):
        return [both[d] if d == 0 else swap(both[d], "expert", 2 * d) for d in range(m // 2)]

    def give_back(forward, backward, late, work):
        if not direct:
            return [dot(collect, plain(x)) for x in (forward, backward)] + [work(late)]
        forward, backward = (
            x.reshape(m // 2, 2 * capacity, width) for x in (forward, backward)
        )
        blocks = [among_pairs(forward)]
        backward, blocks[0][1] = lax.optimization_barrier((backward, blocks[0][1]))
        blocks.append(among_pairs(backward))
        late, blocks = lax.optimization_barrier((late, blocks))
        own, other = (
            jnp.concatenate(
                [jnp.concatenate([x[at : at + capacity] for x in side]) for side in blocks], axis=1
            )
            for at in (0, capacity)
        )
        beside = work(late)
        other, beside = lax.optimization_barrier((swap(other, "expert", 1), beside))
        total = dot(collect[:, :half], own) + dot(collect[:, half:], other)
        return total[:, :width], total[:, width:], beside

    def reduce_shard(keep, out, after=None):
        came = swap(out, "shard", 2 * pair)
        if after is not None:
            came, _ = lax.optimization_barrier((came, after))
        return (keep + came.astype(f32)).astype(bf16)

    arrived, arrived_grad = dispatch(normed_two.astype(bf16), grad_result)
    came = swap(arrived, "shard", 2 * pair)
    row_blocks = (arrived, came)
    grad_blocks = (arrived_grad, swap(arrived_grad, "shard", 2 * pair))

    units = expert_in.shape[2]
    expert_weight = (own_up, pair_up, own_down, pair_down)
    middle = shape((2, 2 * places, units))
    kept, sent = shape((places, width), f32), shape((places, width))
    hidden, slope, *forward = call(
        lambda *refs: expert_forward(places, *refs),
        (middle, middle, kept, sent),
        (*row_blocks, *expert_weight),
        work=6 * micro,
    )
    grad_before, *backward = call(
        lambda *refs: expert_backward(places, *refs),
        (middle, kept, sent),
        (*grad_blocks, *expert_weight, slope),
        work=6 * micro,
    )
    sources = (*grad_blocks, hidden, grad_before)
    expert_result, grad_sent, (up_send, down_send) = give_back(
        reduce_shard(*forward, backward[1]),
        reduce_shard(*backward),
        row_blocks,
        lambda rows_late: call(
            weights_to_send,
            (shape(expert_in.shape), shape(expert_out.shape)),
            (*rows_late, *sources),
            work=4 * micro,
        ),
    )

    layer_out = (hidden_one + gate[:, None] * expert_result).astype(bf16)
    grad_gate = jnp.sum(upstream * expert_result, axis=1)
    grad_logits = (grad_gate * gate)[:, None] * (chosen - probs)
    grad_router = lax.dot_general(
        grad_logits,
        normed_two,
        (((0,), (0,)), ((), ())),
        precision=lax.Precision.HIGHEST,
        preferred_element_type=f32,
    )
    grad_normed_two = grad_sent + lax.dot_general(
        grad_logits,
        router,
        (((1,), (1,)), ((), ())),
        precision=lax.Precision.HIGHEST,
        preferred_element_type=f32,
    )
    grad_middle, grad_gain_two = rms_backward(hidden_one, factor_two, gain_two, grad_normed_two)
    grad_hidden = upstream + grad_middle
    branch = grad_hidden.astype(bf16)
    far_branch, pair_branch = swap(branch, "shard", 2 * pair), swap(branch, "shard", pair)
    far_branch, grad_router, gain_two_row = lax.optimization_barrier(
        (far_branch, grad_router, grad_gain_two)
    )
    branch_blocks = [branch, pair_branch, far_branch, swap(far_branch, "shard", pair)]
    branch_blocks, up_send, down_send = lax.optimization_barrier(
        (branch_blocks, up_send, down_send)
    )
    up_came, down_came = swap(up_send, "shard", pair), swap(down_send, "shard", pair)
    holders = m if direct else 1
    piece = part // m
    if direct:
        share_shapes = [
            shape((held, n + 1, piece, full)) for held in (m // 4, m // 4, m // 4, m // 4 - 1, 1)
        ]
    else:
        share_shapes = [shape((n, part, wide)), shape((part, width))]
    answers = call(
        lambda *refs: attention_backward(n, holders, rows, width, heads, buckets, experts, *refs),
        (
            *share_shapes,
            *[shape((n // 2, rows, width))] * 2,
            shape((row_tile, width), f32),
            shape((row_tile, 128), f32),
        ),
        (
            projected,
            tokens_all,
            gain_one,
            weight,
            weights,
            mixed,
            own_out,
            gain_two_row,
            grad_router,
            *branch_blocks,
        ),
        "",
        [
            pltpu.VMEM((n, rows, width), bf16),
            pltpu.VMEM((group, group), bf16),
            pltpu.VMEM((group, wide), bf16),
            pltpu.VMEM((width, full), f32),
            pltpu.VMEM((part, width), f32),
            pltpu.VMEM((group, width), bf16),
            pltpu.VMEM((n, rows, width), bf16),
            pltpu.VMEM((group, group), f32),
        ],
        work=8 * micro,
    )
    shares = answers[: len(share_shapes)]
    normed_keep, normed_send, gain_row, table = answers[len(share_shapes) :]

    def kept_weights(late_rows):
        return call(
            weights_to_keep,
            (shape(expert_in.shape, f32), shape(expert_out.shape, f32)),
            (*late_rows, *sources, up_came, down_came),
            work=4 * micro,
        )

    per_line = buckets // row_tile

    def biases(block):
        return block.reshape(row_tile, heads, per_line).swapaxes(0, 1).reshape(heads, buckets)

    def far_normed(pair_came):
        normed_sum = normed_keep.astype(f32) + pair_came.astype(f32)
        return normed_sum[0], swap(normed_sum[1].astype(bf16), "shard", 2 * pair)

    def finish_tokens(own_sum, far_sum):
        late, far_sum = lax.optimization_barrier((tokens, far_sum))
        late = late.astype(f32)
        grad_input_norm, _ = rms_backward(
            late, rms_factor(late), gain_one, own_sum + far_sum.astype(f32)
        )
        return (grad_hidden + grad_input_norm).astype(bf16)

    normed_came = swap(normed_send, "shard", pair)
    if direct:
        near_keep, far_keep, near_send, far_send, last_send = shares
        last_came = swap(last_send, "expert", 1)[0]
        far_came = swap(far_send, "expert", 1)
        last_came, near_send, up_came, down_came = lax.optimization_barrier(
            (last_came, near_send, up_came, down_came)
        )
        came = [swap((far_keep[-1].astype(f32) + last_came.astype(f32)).astype(bf16), "expert", m - 2)]
        far = far_keep[:-1].astype(f32) + far_came.astype(f32)
        near_came, late_rows, normed_came = lax.optimization_barrier(
            (swap(near_send, "expert", 1), row_blocks, normed_came)
        )
        own_sum, far_sum = far_normed(normed_came)
        near = near_keep.astype(f32) + near_came.astype(f32)
        came += [swap(far[d].astype(bf16), "expert", m // 2 + 2 * d) for d in range(m // 4 - 1)]
        came += [swap(near[d].astype(bf16), "expert", 2 * d) for d in range(1, m // 4)]
        came, (grad_up, grad_down) = lax.optimization_barrier((came, kept_weights(late_rows)))
        came, far_sum = lax.optimization_barrier((came, far_sum))
        grad_tokens = finish_tokens(own_sum, far_sum)
        summed = near[0] + sum(x.astype(f32) for x in came)
        at = wide + 2 + experts
        rest = (width - full) // n
        table_total = biases(
            summed[0, :row_tile, at + rest : at + rest + heads * per_line]
        )
        low = summed.astype(bf16)
        mine = exchange_relative(
            [lax.dynamic_index_in_dim(low, s ^ p, 0, keepdims=False) for p in range(n)], "shard"
        )
        lane = lax.iota(jnp.int32, full)[None, :]
        own_lane = (lane >= at) & (lane < at + rest)
        mine = jnp.stack(
            [jnp.where(own_lane, low[p], mine[p]) for p in range(n)] + [low[n]], axis=0
        )
        blocks = {0: mine, 1: swap(mine, "expert", 1), 4: swap(mine, "expert", 4)}
        blocks[2] = swap(mine, "expert", 2)
        blocks[2], blocks[1] = lax.optimization_barrier((blocks[2], blocks[1]))
        blocks[3] = swap(blocks[2], "expert", 1)
        blocks[4], blocks[3] = lax.optimization_barrier((blocks[4], blocks[3]))
        blocks[6] = swap(blocks[4], "expert", 2)
        blocks[5] = swap(blocks[4], "expert", 1)
        blocks[6], grad_tokens = lax.optimization_barrier((blocks[6], grad_tokens))
        blocks[7] = swap(blocks[6], "expert", 1)
        blocks = [blocks[d] for d in range(m)]
        grad_attention_in, grad_attention_out, total_one, total_two, total_router = call(
            lambda *refs: assemble(n, m, part, piece, experts, *refs),
            (
                shape((part, 3 * width), f32),
                shape((part, width), f32),
                shape((1, part), f32),
                shape((1, part), f32),
                shape((experts, part), f32),
            ),
            (*blocks,),
            "",
            [pltpu.VMEM((part, 128), f32)],
        )
    else:
        grad_up, grad_down = kept_weights(row_blocks)
        grad_tokens = finish_tokens(*far_normed(normed_came))
        came = lax.all_to_all(
            shares[0].reshape(n, m, piece, wide).swapaxes(0, 1), "expert", 0, 0, tiled=True
        )
        summed = sum(x.astype(f32) for x in came).astype(bf16)
        mine = lax.all_to_all(summed, "shard", 0, 0, tiled=True)
        mine = mine.reshape(n, piece, 3, part).transpose(1, 2, 0, 3).reshape(piece, 3 * width)
        came = lax.all_to_all(shares[1].reshape(m, piece, width), "expert", 0, 0, tiled=True)
        out_mine = sum(x.astype(f32) for x in came).astype(bf16)
        grad_attention_in = lax.all_gather(mine, "expert", axis=0, tiled=True).astype(f32)
        grad_attention_out = lax.all_gather(out_mine, "expert", axis=0, tiled=True).astype(f32)
        small = jnp.concatenate([gain_row[0:1], grad_gain_two[None], grad_router], axis=0)
        small_total = lax.psum_scatter(small, "shard", scatter_dimension=1, tiled=True)
        small_total, table_total = lax.psum(
            (small_total, biases(table[:, : heads * per_line])), "expert"
        )
        total_one, total_two, total_router = small_total[0:1], small_total[1:2], small_total[2:]
    return (
        layer_out,
        grad_tokens,
        grad_attention_in,
        grad_attention_out,
        table_total,
        total_one[0],
        total_two[0],
        total_router.T,
        grad_up,
        grad_down,
    )


def solution(mesh):
    in_specs = (
        P(("expert", "shard"), None),
        P("expert", None),
        P(("expert", "shard"), None),
        P("shard", None),
        P("shard", None),
        P("shard", None),
        P("shard"),
        P("shard"),
        P(),
        P("expert", None, "shard"),
        P("expert", "shard", None),
        P(("expert", "shard"), None),
    )
    out_specs = (
        P(("expert", "shard"), None),
        P(("expert", "shard"), None),
        P("shard", None),
        P("shard", None),
        P("shard", None),
        P("shard"),
        P("shard"),
        P("shard", None),
        P("expert", None, "shard"),
        P("expert", "shard", None),
    )
    return jax.shard_map(local, mesh=mesh, in_specs=in_specs, out_specs=out_specs, check_vma=False)
```

```python
import jax
import jax.numpy as jnp
from jax import lax
from jax.experimental import pallas as pl
from jax.experimental.pallas import tpu as pltpu
from jax.sharding import PartitionSpec as P

norm_eps = 1e-06
gelu_scale = 0.7978845608028654
gelu_cubic = 0.044715
big_negative = -1e30
near_steps = 8
far_steps = (12, 16, 23, 32, 46, 64, 91)
bf16 = jnp.bfloat16
f32 = jnp.float32
row_tile = 8
pair = 1
slot_tile = 4


def bucket_index(offset):
    distance = jnp.abs(offset)
    far_level = jnp.full_like(distance, near_steps)
    for step_edge in far_steps:
        far_level = far_level + (distance >= step_edge).astype(jnp.int32)
    near = jnp.where(distance < near_steps, distance, far_level)
    return near + 16 * (offset > 0).astype(jnp.int32)


def dot(left, right):
    return jnp.dot(left, right, preferred_element_type=f32)


def dot_nt(left, right):
    return lax.dot_general(left, right, (((1,), (1,)), ((), ())), preferred_element_type=f32)


def dot_tn(left, right):
    return lax.dot_general(left, right, (((0,), (0,)), ((), ())), preferred_element_type=f32)


def swap(value, axis, bit):
    size = lax.axis_size(axis)
    return lax.ppermute(value, axis, [(i, i ^ bit) for i in range(size)])


def gather_relative(value, axis):
    blocks = [value]
    bit = lax.axis_size(axis) // 2
    parts = {0: value}
    while bit:
        for p in list(parts):
            parts[p ^ bit] = swap(parts[p], axis, bit)
        bit //= 2
    return [parts[p] for p in range(lax.axis_size(axis))]


def exchange_relative(blocks, axis):
    return [blocks[0]] + [swap(block, axis, p) for p, block in enumerate(blocks) if p]


def call(kernel, out_shape, operands, spaces="", scratch=(), work=0):
    vmem = pl.BlockSpec(memory_space=pltpu.VMEM)
    smem = pl.BlockSpec(memory_space=pltpu.SMEM)
    in_specs = [smem if spaces[i : i + 1] == "s" else vmem for i in range(len(operands))]
    return pl.pallas_call(
        kernel,
        out_shape=out_shape,
        in_specs=in_specs,
        out_specs=jax.tree.map(lambda _: vmem, out_shape),
        scratch_shapes=list(scratch),
        compiler_params=pltpu.CompilerParams(vmem_limit_bytes=28 * 2**20),
        cost_estimate=pl.CostEstimate(flops=work, bytes_accessed=0, transcendentals=0),
    )(*operands)


def shape(dims, dtype=bf16):
    return jax.ShapeDtypeStruct(tuple(dims), dtype)


def diagonal(size):
    return lax.broadcasted_iota(jnp.int32, (size, size), 0) == lax.broadcasted_iota(
        jnp.int32, (size, size), 1
    )


def to_column(row, size):
    return jnp.sum(jnp.where(diagonal(size), row, 0.0), axis=1, keepdims=True)


def to_row(column, size):
    return jnp.sum(jnp.where(diagonal(size), column, 0.0), axis=0, keepdims=True)


def prepare_weight(n, part, weight, gain_one, gain_two, *outs):
    wide = 3 * part
    s = lax.axis_index("shard")
    extra = outs[0].shape[1] - wide
    one, two = (
        to_column(gain[...].astype(f32).reshape(1, part), part) for gain in (gain_one, gain_two)
    )
    lane = lax.broadcasted_iota(jnp.int32, (part, extra), 1)
    beside = jnp.where(lane == 0, one, jnp.where(lane == 1, two, 0.0)).astype(bf16)
    for p in range(n):
        outs[p][:, wide:] = beside
    for k in range(n):

        @pl.when(s == k)
        def _():
            for p in range(n):
                for kind in range(3):
                    at = (kind * n + (k ^ p)) * part
                    outs[p][:, kind * part : (kind + 1) * part] = weight[:, at : at + part]


def offsets(rows):
    return lax.broadcasted_iota(jnp.int32, (rows, rows), 1) - lax.broadcasted_iota(
        jnp.int32, (rows, rows), 0
    )


def near_buckets(diff, buckets):
    if diff == 0:
        return range(buckets)
    return range(buckets // 2, buckets) if diff > 0 else range(buckets // 2)


def attention_forward(n, rows, width, heads, seqs, buckets, *refs):
    lengths, table = refs[:2]
    token_refs = refs[2 : 2 + n]
    weight_refs = refs[2 + n : 2 + 2 * n]
    tokens_out, weight_out, projected_out, weights_out, *gains_out, mixed_all = refs[
        2 + 2 * n : 9 + 2 * n
    ]
    mixed_out = refs[9 + 2 * n : 9 + 3 * n]
    normed_scr, scores_scr = refs[9 + 3 * n :]
    s = lax.axis_index("shard")
    part = width // n
    wide = 3 * part
    head_dim = part // heads
    for p in range(n):
        tokens_out[s ^ p] = token_refs[p][...]
        weight_out[pl.ds(pl.multiple_of((s ^ p) * part, part & -part), part), :] = weight_refs[p][...]
    size = 128
    for c in range(width // size):
        beside = weight_out[c * size : (c + 1) * size, wide:].astype(f32)
        for i in range(2):
            row = to_row(beside[:, i : i + 1], size)
            gains_out[i][:, c * size : (c + 1) * size] = jnp.broadcast_to(
                row, (gains_out[i].shape[0], size)
            )
    gain = gains_out[0][...]
    for j in range(n):
        value = tokens_out[j].astype(f32)
        factor = lax.rsqrt(jnp.mean(value * value, axis=-1, keepdims=True) + norm_eps)
        normed_scr[j * rows : (j + 1) * rows, :] = (value * factor * gain).astype(bf16)
    projected_out[...] = dot(normed_scr[...], weight_out[:, :wide]).astype(bf16)
    total_rows = n * rows
    key_place = lax.broadcasted_iota(jnp.int32, (1, total_rows), 1)
    key_segment = jnp.zeros((1, total_rows), jnp.int32)
    end = jnp.int32(0)
    ends = []
    for j in range(seqs):
        end = end + lengths[0, j]
        ends.append(end)
        key_segment = key_segment + (key_place >= end).astype(jnp.int32)
    base = offsets(rows)
    steps = {diff: bucket_index(base + diff * rows) for diff in (-1, 0, 1)}
    for h in range(heads):
        query = projected_out[:, h * head_dim : (h + 1) * head_dim]
        key = projected_out[:, part + h * head_dim : part + (h + 1) * head_dim]
        value = projected_out[:, 2 * part + h * head_dim : 2 * part + (h + 1) * head_dim]
        bias = {}
        for diff in (-1, 0, 1):
            block = jnp.zeros((rows, rows), f32)
            for b in near_buckets(diff, buckets):
                block = jnp.where(steps[diff] == b, table[h, b], block)
            bias[diff] = block
        low_side = jnp.full((rows, rows), table[h, buckets // 2 - 1], f32)
        high_side = jnp.full((rows, rows), table[h, buckets - 1], f32)
        scores_scr[...] = dot_nt(query, key)
        for i in range(n):
            scores = scores_scr[i * rows : (i + 1) * rows, :]
            side = [
                bias[j - i] if abs(j - i) <= 1 else (high_side if j > i else low_side)
                for j in range(n)
            ]
            scores = scores + jnp.concatenate(side, axis=1)
            query_place = i * rows + lax.broadcasted_iota(jnp.int32, (rows, 1), 0)
            query_segment = jnp.zeros((rows, 1), jnp.int32)
            for j in range(seqs):
                query_segment = query_segment + (query_place >= ends[j]).astype(jnp.int32)
            scores = jnp.where(query_segment == key_segment, scores, big_negative)
            top = jnp.max(scores, axis=-1, keepdims=True)
            raised = jnp.exp(scores - top)
            total = jnp.sum(raised, axis=-1, keepdims=True)
            weights = (raised * (1.0 / total)).astype(bf16)
            weights_out[h, i * rows : (i + 1) * rows, :] = weights
        mixed_all[:, :, h * head_dim : (h + 1) * head_dim] = (
            dot(weights_out[h], value).astype(bf16).reshape(n, rows, head_dim)
        )
    for p in range(n):
        mixed_out[p][...] = mixed_all[s ^ p]


def attention_backward(n, m, rows, width, heads, buckets, experts, *refs):
    projected, tokens, gains, weight, weights, mixed, weight_out, gain_two, router = refs[:9]
    branch_refs = refs[9 : 9 + n]
    at = 9 + n
    shares = 4 if m > 1 else 2
    share_out = refs[at : at + shares]
    normed_grad_out = refs[at + shares : at + shares + 2]
    gain_out, table_out = refs[at + shares + 2 : at + shares + 4]
    branch_scr, scores_scr, projected_scr, total_scr, out_scr, normed_scr, send_scr, weights_scr = (
        refs[at + shares + 4 :]
    )
    s = lax.axis_index("shard")
    e = lax.axis_index("expert")
    part = width // n
    wide = 3 * part
    group = n * rows
    head_dim = part // heads
    for p in range(n):
        branch_scr[s ^ p] = branch_refs[p][...]
    branch = branch_scr[...].reshape(group, width)
    grad_mixed = dot_nt(branch, weight_out[...]).astype(bf16)
    out_scr[...] = dot_tn(mixed[...].reshape(group, part), branch)
    base = offsets(rows)
    steps = {diff: bucket_index(base + diff * rows) for diff in (-1, 0, 1)}
    lane = lax.broadcasted_iota(jnp.int32, (row_tile, 128), 1)
    line = lax.broadcasted_iota(jnp.int32, (row_tile, 128), 0)
    table_total = jnp.zeros((row_tile, 128), f32)
    per_line = buckets // row_tile
    for h in range(heads):
        query = projected[:, h * head_dim : (h + 1) * head_dim]
        key = projected[:, part + h * head_dim : part + (h + 1) * head_dim]
        value = projected[:, 2 * part + h * head_dim : 2 * part + (h + 1) * head_dim]
        near = {diff: jnp.zeros((rows, rows), f32) for diff in (-1, 0, 1)}
        low_side = jnp.zeros((1, rows), f32)
        high_side = jnp.zeros((1, rows), f32)
        upstream = grad_mixed[:, h * head_dim : (h + 1) * head_dim]
        weights_scr[...] = dot_nt(upstream, value)
        for i in range(n):
            weights_i = weights[h, i * rows : (i + 1) * rows, :].astype(f32)
            grad_weights = weights_scr[i * rows : (i + 1) * rows, :]
            inner = jnp.sum(weights_i * grad_weights, axis=-1, keepdims=True)
            grad_scores = weights_i * (grad_weights - inner)
            scores_scr[i * rows : (i + 1) * rows, :] = grad_scores.astype(bf16)
            for j in range(n):
                block = grad_scores[:, j * rows : (j + 1) * rows]
                if abs(j - i) <= 1:
                    near[j - i] = near[j - i] + block
                elif j > i:
                    high_side = high_side + jnp.sum(block, axis=0, keepdims=True)
                else:
                    low_side = low_side + jnp.sum(block, axis=0, keepdims=True)
        for b in range(buckets):
            amount = jnp.zeros((1, rows), f32)
            for diff in (-1, 0, 1):
                if b in near_buckets(diff, buckets):
                    amount = amount + jnp.sum(
                        jnp.where(steps[diff] == b, near[diff], 0.0), axis=0, keepdims=True
                    )
            if b == buckets - 1:
                amount = amount + high_side
            if b == buckets // 2 - 1:
                amount = amount + low_side
            amount = jnp.sum(amount, axis=1, keepdims=True)
            spot = (line == b // per_line) & (lane == h * per_line + b % per_line)
            table_total = jnp.where(spot, amount, table_total)
        grad_scores_all = scores_scr[...]
        projected_scr[:, h * head_dim : (h + 1) * head_dim] = dot(grad_scores_all, key).astype(bf16)
        projected_scr[:, part + h * head_dim : part + (h + 1) * head_dim] = (
            dot_tn(query, grad_scores_all).T.astype(bf16)
        )
        projected_scr[:, 2 * part + h * head_dim : 2 * part + (h + 1) * head_dim] = (
            dot_tn(upstream, weights[h]).T.astype(bf16)
        )
    table_out[...] = table_total
    grad_projected = projected_scr[...]
    normed_grad = dot_nt(grad_projected, weight[:, :wide])
    send_scr[...] = normed_grad.astype(bf16).reshape(n, rows, width)
    for p in range(n):
        normed_grad_out[p & 1][p >> 1] = send_scr[s ^ p]
    gain = gains[...]
    grad_gain = jnp.zeros((1, width), f32)
    for j in range(n):
        value = tokens[j].astype(f32)
        unit = value * lax.rsqrt(jnp.mean(value * value, axis=-1, keepdims=True) + norm_eps)
        normed_scr[j * rows : (j + 1) * rows, :] = (unit * gain).astype(bf16)
        grad_gain = grad_gain + jnp.sum(
            normed_grad[j * rows : (j + 1) * rows, :] * unit, axis=0, keepdims=True
        )
    gain_out[...] = jnp.broadcast_to(grad_gain, gain_out.shape)
    total_scr[:, :wide] = dot_tn(normed_scr[...], grad_projected)
    full = total_scr.shape[1]
    if m == 1:
        for t in range(n):
            share_out[0][t] = total_scr[t * part : (t + 1) * part, :wide].astype(bf16)
        share_out[1][...] = out_scr[...].astype(bf16)
        return
    piece = part // m
    total_scr[:, wide:] = jnp.zeros((width, full - wide), f32)
    grad_two = gain_two[...].reshape(1, width)
    size = 128
    for c in range(width // size):
        here = slice(c * size, (c + 1) * size)
        total_scr[here, wide : wide + 1] = to_column(grad_gain[:, here], size)
        total_scr[here, wide + 1 : wide + 2] = to_column(grad_two[:, here], size)
        total_scr[here, wide + 2 : wide + 2 + experts] = router[:, here].T
    at = wide + 2 + experts
    rest = (width - full) // n
    for t in range(n):
        total_scr[t * part : (t + 1) * part, at : at + rest] = out_scr[
            :, full + t * rest : full + (t + 1) * rest
        ]
    at = at + rest
    for d in range(m):
        total_scr[d * piece : d * piece + row_tile, at : at + heads * per_line] = table_total[
            :, : heads * per_line
        ]
    for d in range(m):
        target = share_out[(d & 1) + 2 * (d < m // 2)]
        place = (d >> 1) % (m // 4)
        start = (e ^ d) * piece
        for t in range(n):
            rows_at = pl.multiple_of(t * part + start, row_tile)
            target[place, t] = total_scr[pl.ds(rows_at, piece), :].astype(bf16)
        rows_at = pl.multiple_of(start, row_tile)
        target[place, n] = out_scr[pl.ds(rows_at, piece), :full].astype(bf16)


def beside_columns(ref, p, wide):
    last = ref[p, :, ref.shape[2] - 128 :]
    skip = wide - (ref.shape[2] - 128)
    return jnp.concatenate([last[:, skip:], last[:, :skip]], axis=1)


def assemble(n, m, part, piece, experts, *refs):
    total_out, out_out, one_out, two_out, router_out, small_scr = refs[m:]
    s = lax.axis_index("shard")
    e = lax.axis_index("expert")
    wide = 3 * part
    full = refs[0].shape[2]
    at = wide + 2 + experts
    rest = (n * part - full) // n
    for d in range(m):
        start = pl.multiple_of((e ^ d) * piece, row_tile)
        own = pl.ds(start, piece)
        small = jnp.zeros((piece, 128), f32)
        for p in range(n):
            small = small + beside_columns(refs[d], p, wide).astype(f32)
            out_out[own, full + p * rest : full + (p + 1) * rest] = refs[d][p, :, at : at + rest].astype(
                f32
            )
        out_out[own, :full] = refs[d][n].astype(f32)
        small_scr[own, :] = small
    small = small_scr[...].T
    one_out[...] = small[0:1, :]
    two_out[...] = small[1:2, :]
    router_out[...] = small[2 : 2 + experts, :]
    for k in range(n):

        @pl.when(s == k)
        def _():
            for d in range(m):
                own = pl.ds(pl.multiple_of((e ^ d) * piece, row_tile), piece)
                for p in range(n):
                    for kind in range(3):
                        to = (kind * n + (k ^ p)) * part
                        total_out[own, to : to + part] = refs[d][
                            p, :, kind * part : (kind + 1) * part
                        ].astype(f32)


def expert_forward(rows, own, came, up_own, up_pair, down_own, down_pair, *outs):
    hidden_out, slope_out, keep_out, send_out = outs
    source = jnp.concatenate([own[...], came[...]], axis=0)
    result = 0.0
    for k, (up, down) in enumerate(((up_own, down_own), (up_pair, down_pair))):
        before = dot(source, up[0])
        square = before * before
        tanh_value = jnp.tanh(gelu_scale * before * (1.0 + gelu_cubic * square))
        half = 0.5 * (1.0 + tanh_value)
        hidden = (before * half).astype(bf16)
        slope = half + 0.5 * before * (1.0 - tanh_value * tanh_value) * gelu_scale * (
            1.0 + 3.0 * gelu_cubic * square
        )
        hidden_out[k] = hidden
        slope_out[k] = slope.astype(bf16)
        result = result + dot(hidden, down[0])
    keep_out[...] = result[:rows]
    send_out[...] = result[rows:].astype(bf16)


def expert_backward(rows, own, came, up_own, up_pair, down_own, down_pair, slope, *outs):
    before_out, keep_out, send_out = outs
    grads = jnp.concatenate([own[...], came[...]], axis=0)
    result = 0.0
    for k, (up, down) in enumerate(((up_own, down_own), (up_pair, down_pair))):
        grad_before = (dot_nt(grads, down[0]) * slope[k].astype(f32)).astype(bf16)
        before_out[k] = grad_before
        result = result + dot_nt(grad_before, up[0])
    keep_out[...] = result[:rows]
    send_out[...] = result[rows:].astype(bf16)


def weights_to_send(own, came, own_grad, came_grad, hidden, grad_before, up_send, down_send):
    grads = jnp.concatenate([own_grad[...], came_grad[...]], axis=0)
    rows = jnp.concatenate([own[...], came[...]], axis=0)
    up_send[0] = dot_tn(rows, grad_before[1]).astype(bf16)
    down_send[0] = dot_tn(hidden[1], grads).astype(bf16)


def weights_to_keep(
    own, came, own_grad, came_grad, hidden, grad_before, up_came, down_came, up_out, down_out
):
    grads = jnp.concatenate([own_grad[...], came_grad[...]], axis=0)
    rows = jnp.concatenate([own[...], came[...]], axis=0)
    up_out[0] = dot_tn(rows, grad_before[0]) + up_came[0].astype(f32)
    down_out[0] = dot_tn(hidden[0], grads) + down_came[0].astype(f32)


def rms_factor(value):
    return lax.rsqrt(jnp.mean(value * value, axis=-1, keepdims=True) + norm_eps)


def rms_backward(value, factor, gain, upstream):
    scaled = upstream * gain
    grad_value = factor * scaled - value * factor * factor * factor * jnp.mean(
        scaled * value, axis=-1, keepdims=True
    )
    grad_gain = jnp.sum(upstream * value * factor, axis=0)
    return (grad_value, grad_gain)


def local(
    tokens,
    lengths,
    routes,
    attention_in,
    attention_out,
    position_bias,
    first_gain,
    second_gain,
    router,
    expert_in,
    expert_out,
    cotangent,
):
    n = lax.axis_size("shard")
    m = lax.axis_size("expert")
    s = lax.axis_index("shard")
    e = lax.axis_index("expert")
    rows, width = tokens.shape
    heads, buckets = position_bias.shape
    part = width // n
    wide = 3 * part
    group = n * rows
    seqs = lengths.shape[1]
    experts = router.shape[1]
    direct = m == 8
    full = wide + -wide % 128
    micro = 10**9

    far_tokens, pair_tokens = swap(tokens, "shard", 2 * pair), swap(tokens, "shard", pair)
    weight_blocks = exchange_relative(
        call(
            lambda *refs: prepare_weight(n, part, *refs),
            [shape((part, full))] * n,
            (attention_in, first_gain, second_gain),
        ),
        "shard",
    )
    far_tokens, own_up, own_down, table_scalars = lax.optimization_barrier(
        (far_tokens, expert_in, expert_out, position_bias.astype(f32))
    )
    token_blocks = [tokens, pair_tokens, far_tokens, swap(far_tokens, "shard", pair)]
    pair_up = swap(own_up, "shard", pair)
    pair_down = swap(own_down, "shard", pair)
    own_out, token_blocks, weight_blocks = lax.optimization_barrier(
        (attention_out, token_blocks, weight_blocks)
    )
    far_out, pair_out = swap(own_out, "shard", 2 * pair), swap(own_out, "shard", pair)

    answers = call(
        lambda *refs: attention_forward(n, rows, width, heads, seqs, buckets, *refs),
        (
            shape((n, rows, width)),
            shape((width, full)),
            shape((group, wide)),
            shape((heads, group, group)),
            shape((1, width), f32),
            shape((rows, width), f32),
            shape((n, rows, part)),
            *[shape((rows, part))] * n,
        ),
        (lengths, table_scalars, *token_blocks, *weight_blocks),
        "ss",
        [pltpu.VMEM((group, width), bf16), pltpu.VMEM((group, group), f32)],
        work=10 * micro,
    )
    tokens_all, weight, projected, weights, gain_one, gain_two, mixed = answers[:7]
    mixed_mine, pair_up, pair_down, pair_out = lax.optimization_barrier(
        (list(answers[7:]), pair_up, pair_down, pair_out)
    )
    mixed_blocks = exchange_relative(mixed_mine, "shard")
    out_blocks = [own_out, pair_out, far_out, swap(far_out, "shard", pair)]

    inputs = tokens.astype(f32)
    hidden_one = inputs + sum(dot(mixed_blocks[p], out_blocks[p]) for p in range(n))
    factor_two = rms_factor(hidden_one)
    normed_two = hidden_one * factor_two * gain_two
    logits = jnp.dot(
        normed_two, router, precision=lax.Precision.HIGHEST, preferred_element_type=f32
    )
    shifted = jnp.exp(logits - jnp.max(logits, axis=-1, keepdims=True))
    probs = shifted / jnp.sum(shifted, axis=-1, keepdims=True)
    route = routes[:, 0]
    chosen = (route[:, None] == lax.iota(jnp.int32, experts)[None, :]).astype(f32)
    gate = jnp.sum(probs * chosen, axis=1)
    lower = (lax.iota(jnp.int32, rows)[:, None] >= lax.iota(jnp.int32, rows)[None, :]).astype(bf16)
    running = dot(lower, chosen.astype(bf16))
    slot = jnp.sum((running - 1.0) * chosen, axis=1).astype(jnp.int32)
    capacity = max(2, 9 * rows // (8 * experts) + 1)
    capacity = -(-capacity // slot_tile) * slot_tile
    places = experts * capacity
    half = places // 2
    if direct:
        holder = route ^ e
        target = (holder & 1) * half + (holder >> 1) * capacity + slot
    else:
        target = route * capacity + slot
    collect = (target[:, None] == lax.iota(jnp.int32, places)[None, :]).astype(bf16)
    upstream = cotangent.astype(f32)
    grad_result = (gate[:, None] * upstream).astype(bf16)

    def plain(value):
        return lax.all_to_all(
            value.reshape(experts, capacity, width), "expert", 0, 0, tiled=True
        ).reshape(places, width)

    def dispatch(forward, backward):
        if not direct:
            return [plain(dot_tn(collect, x).astype(bf16)) for x in (forward, backward)]
        came = swap(dot_tn(collect[:, half:], forward).astype(bf16), "expert", 1)
        came, other = lax.optimization_barrier(
            (came, dot_tn(collect[:, half:], backward).astype(bf16))
        )

        def both(own, came):
            own = dot_tn(collect[:, :half], own).astype(bf16).reshape(m // 2, capacity, width)
            return jnp.concatenate([own, came.reshape(m // 2, capacity, width)], axis=1)

        first = among_pairs(both(forward, came))
        second, first[1] = lax.optimization_barrier(
            (both(backward, swap(other, "expert", 1)), first[1])
        )
        return [jnp.concatenate(x, axis=0) for x in (first, among_pairs(second))]

    def among_pairs(both):
        return [both[d] if d == 0 else swap(both[d], "expert", 2 * d) for d in range(m // 2)]

    def give_back(forward, backward, late, work):
        if not direct:
            return [dot(collect, plain(x)) for x in (forward, backward)] + [work(late)]
        forward, backward = (
            x.reshape(m // 2, 2 * capacity, width) for x in (forward, backward)
        )
        blocks = [among_pairs(forward)]
        backward, blocks[0][1] = lax.optimization_barrier((backward, blocks[0][1]))
        blocks.append(among_pairs(backward))
        late, blocks = lax.optimization_barrier((late, blocks))
        own, other = (
            jnp.concatenate(
                [jnp.concatenate([x[at : at + capacity] for x in side]) for side in blocks], axis=1
            )
            for at in (0, capacity)
        )
        beside = work(late)
        other, beside = lax.optimization_barrier((swap(other, "expert", 1), beside))
        total = dot(collect[:, :half], own) + dot(collect[:, half:], other)
        return total[:, :width], total[:, width:], beside

    def reduce_shard(keep, out, after=None):
        came = swap(out, "shard", 2 * pair)
        if after is not None:
            came, _ = lax.optimization_barrier((came, after))
        return (keep + came.astype(f32)).astype(bf16)

    arrived, arrived_grad = dispatch(normed_two.astype(bf16), grad_result)
    came = swap(arrived, "shard", 2 * pair)
    row_blocks = (arrived, came)
    grad_blocks = (arrived_grad, swap(arrived_grad, "shard", 2 * pair))

    units = expert_in.shape[2]
    expert_weight = (own_up, pair_up, own_down, pair_down)
    middle = shape((2, 2 * places, units))
    kept, sent = shape((places, width), f32), shape((places, width))
    hidden, slope, *forward = call(
        lambda *refs: expert_forward(places, *refs),
        (middle, middle, kept, sent),
        (*row_blocks, *expert_weight),
        work=6 * micro,
    )
    grad_before, *backward = call(
        lambda *refs: expert_backward(places, *refs),
        (middle, kept, sent),
        (*grad_blocks, *expert_weight, slope),
        work=6 * micro,
    )
    sources = (*grad_blocks, hidden, grad_before)
    expert_result, grad_sent, (up_send, down_send) = give_back(
        reduce_shard(*forward, backward[1]),
        reduce_shard(*backward),
        row_blocks,
        lambda rows_late: call(
            weights_to_send,
            (shape(expert_in.shape), shape(expert_out.shape)),
            (*rows_late, *sources),
            work=4 * micro,
        ),
    )

    layer_out = (hidden_one + gate[:, None] * expert_result).astype(bf16)
    grad_gate = jnp.sum(upstream * expert_result, axis=1)
    grad_logits = (grad_gate * gate)[:, None] * (chosen - probs)
    grad_router = lax.dot_general(
        grad_logits,
        normed_two,
        (((0,), (0,)), ((), ())),
        precision=lax.Precision.HIGHEST,
        preferred_element_type=f32,
    )
    grad_normed_two = grad_sent + lax.dot_general(
        grad_logits,
        router,
        (((1,), (1,)), ((), ())),
        precision=lax.Precision.HIGHEST,
        preferred_element_type=f32,
    )
    grad_middle, grad_gain_two = rms_backward(hidden_one, factor_two, gain_two, grad_normed_two)
    grad_hidden = upstream + grad_middle
    branch = grad_hidden.astype(bf16)
    far_branch, pair_branch = swap(branch, "shard", 2 * pair), swap(branch, "shard", pair)
    far_branch, grad_router, gain_two_row = lax.optimization_barrier(
        (far_branch, grad_router, grad_gain_two)
    )
    branch_blocks = [branch, pair_branch, far_branch, swap(far_branch, "shard", pair)]
    branch_blocks, up_send, down_send = lax.optimization_barrier(
        (branch_blocks, up_send, down_send)
    )
    up_came, down_came = swap(up_send, "shard", pair), swap(down_send, "shard", pair)
    holders = m if direct else 1
    piece = part // m
    if direct:
        share_shapes = [shape((m // 4, n + 1, piece, full))] * 4
    else:
        share_shapes = [shape((n, part, wide)), shape((part, width))]
    answers = call(
        lambda *refs: attention_backward(n, holders, rows, width, heads, buckets, experts, *refs),
        (
            *share_shapes,
            *[shape((n // 2, rows, width))] * 2,
            shape((row_tile, width), f32),
            shape((row_tile, 128), f32),
        ),
        (
            projected,
            tokens_all,
            gain_one,
            weight,
            weights,
            mixed,
            own_out,
            gain_two_row,
            grad_router,
            *branch_blocks,
        ),
        "",
        [
            pltpu.VMEM((n, rows, width), bf16),
            pltpu.VMEM((group, group), bf16),
            pltpu.VMEM((group, wide), bf16),
            pltpu.VMEM((width, full), f32),
            pltpu.VMEM((part, width), f32),
            pltpu.VMEM((group, width), bf16),
            pltpu.VMEM((n, rows, width), bf16),
            pltpu.VMEM((group, group), f32),
        ],
        work=8 * micro,
    )
    shares = answers[: len(share_shapes)]
    normed_keep, normed_send, gain_row, table = answers[len(share_shapes) :]

    def kept_weights(late_rows):
        return call(
            weights_to_keep,
            (shape(expert_in.shape, f32), shape(expert_out.shape, f32)),
            (*late_rows, *sources, up_came, down_came),
            work=4 * micro,
        )

    per_line = buckets // row_tile

    def biases(block):
        return block.reshape(row_tile, heads, per_line).swapaxes(0, 1).reshape(heads, buckets)

    normed_sum = normed_keep.astype(f32) + swap(normed_send, "shard", pair).astype(f32)
    far_sum = swap(normed_sum[1].astype(bf16), "shard", 2 * pair)
    late, far_sum = lax.optimization_barrier((tokens, far_sum))
    late = late.astype(f32)
    grad_input_norm, _ = rms_backward(
        late, rms_factor(late), gain_one, normed_sum[0] + far_sum.astype(f32)
    )
    grad_tokens = (grad_hidden + grad_input_norm).astype(bf16)
    if direct:
        far_keep, far_send, near_keep, near_send = shares
        far_came = swap(far_send, "expert", 1)
        far_came, near_send, up_came, down_came = lax.optimization_barrier(
            (far_came, near_send, up_came, down_came)
        )
        far = far_keep.astype(f32) + far_came.astype(f32)
        near_came, late_rows = lax.optimization_barrier((swap(near_send, "expert", 1), row_blocks))
        near = near_keep.astype(f32) + near_came.astype(f32)
        came = [swap(far[d].astype(bf16), "expert", m // 2 + 2 * d) for d in range(m // 4)]
        came += [swap(near[d].astype(bf16), "expert", 2 * d) for d in range(1, m // 4)]
        came, (grad_up, grad_down) = lax.optimization_barrier((came, kept_weights(late_rows)))
        summed = near[0] + sum(x.astype(f32) for x in came)
        at = wide + 2 + experts
        rest = (width - full) // n
        table_total = biases(
            summed[0, :row_tile, at + rest : at + rest + heads * per_line]
        )
        low = summed.astype(bf16)
        mine = exchange_relative(
            [lax.dynamic_index_in_dim(low, s ^ p, 0, keepdims=False) for p in range(n)], "shard"
        )
        lane = lax.iota(jnp.int32, full)[None, :]
        own_lane = (lane >= at) & (lane < at + rest)
        mine = jnp.stack(
            [jnp.where(own_lane, low[p], mine[p]) for p in range(n)] + [low[n]], axis=0
        )
        blocks = {0: mine, 1: swap(mine, "expert", 1), 4: swap(mine, "expert", 4)}
        blocks[2] = swap(mine, "expert", 2)
        blocks[2], blocks[1] = lax.optimization_barrier((blocks[2], blocks[1]))
        blocks[3] = swap(blocks[2], "expert", 1)
        blocks[4], blocks[3] = lax.optimization_barrier((blocks[4], blocks[3]))
        blocks[6] = swap(blocks[4], "expert", 2)
        blocks[5] = swap(blocks[4], "expert", 1)
        blocks[6], grad_tokens = lax.optimization_barrier((blocks[6], grad_tokens))
        blocks[7] = swap(blocks[6], "expert", 1)
        blocks = [blocks[d] for d in range(m)]
        grad_attention_in, grad_attention_out, total_one, total_two, total_router = call(
            lambda *refs: assemble(n, m, part, piece, experts, *refs),
            (
                shape((part, 3 * width), f32),
                shape((part, width), f32),
                shape((1, part), f32),
                shape((1, part), f32),
                shape((experts, part), f32),
            ),
            (*blocks,),
            "",
            [pltpu.VMEM((part, 128), f32)],
        )
    else:
        grad_up, grad_down = kept_weights(row_blocks)
        came = lax.all_to_all(
            shares[0].reshape(n, m, piece, wide).swapaxes(0, 1), "expert", 0, 0, tiled=True
        )
        summed = sum(x.astype(f32) for x in came).astype(bf16)
        mine = lax.all_to_all(summed, "shard", 0, 0, tiled=True)
        mine = mine.reshape(n, piece, 3, part).transpose(1, 2, 0, 3).reshape(piece, 3 * width)
        came = lax.all_to_all(shares[1].reshape(m, piece, width), "expert", 0, 0, tiled=True)
        out_mine = sum(x.astype(f32) for x in came).astype(bf16)
        grad_attention_in = lax.all_gather(mine, "expert", axis=0, tiled=True).astype(f32)
        grad_attention_out = lax.all_gather(out_mine, "expert", axis=0, tiled=True).astype(f32)
        small = jnp.concatenate([gain_row[0:1], grad_gain_two[None], grad_router], axis=0)
        small_total = lax.psum_scatter(small, "shard", scatter_dimension=1, tiled=True)
        small_total, table_total = lax.psum(
            (small_total, biases(table[:, : heads * per_line])), "expert"
        )
        total_one, total_two, total_router = small_total[0:1], small_total[1:2], small_total[2:]
    return (
        layer_out,
        grad_tokens,
        grad_attention_in,
        grad_attention_out,
        table_total,
        total_one[0],
        total_two[0],
        total_router.T,
        grad_up,
        grad_down,
    )


def solution(mesh):
    in_specs = (
        P(("expert", "shard"), None),
        P("expert", None),
        P(("expert", "shard"), None),
        P("shard", None),
        P("shard", None),
        P("shard", None),
        P("shard"),
        P("shard"),
        P(),
        P("expert", None, "shard"),
        P("expert", "shard", None),
        P(("expert", "shard"), None),
    )
    out_specs = (
        P(("expert", "shard"), None),
        P(("expert", "shard"), None),
        P("shard", None),
        P("shard", None),
        P("shard", None),
        P("shard"),
        P("shard"),
        P("shard", None),
        P("expert", None, "shard"),
        P("expert", "shard", None),
    )
    return jax.shard_map(local, mesh=mesh, in_specs=in_specs, out_specs=out_specs, check_vma=False)
```

```python
import jax
import jax.numpy as jnp
from jax import lax
from jax.experimental import pallas as pl
from jax.experimental.pallas import tpu as pltpu
from jax.sharding import PartitionSpec as P

norm_eps = 1e-06
gelu_scale = 0.7978845608028654
gelu_cubic = 0.044715
big_negative = -1e30
near_steps = 8
far_steps = (12, 16, 23, 32, 46, 64, 91)
bf16 = jnp.bfloat16
f32 = jnp.float32
row_tile = 8
pair = 1
slot_tile = 4


def bucket_index(offset):
    distance = jnp.abs(offset)
    far_level = jnp.full_like(distance, near_steps)
    for step_edge in far_steps:
        far_level = far_level + (distance >= step_edge).astype(jnp.int32)
    near = jnp.where(distance < near_steps, distance, far_level)
    return near + 16 * (offset > 0).astype(jnp.int32)


def dot(left, right):
    return jnp.dot(left, right, preferred_element_type=f32)


def dot_nt(left, right):
    return lax.dot_general(left, right, (((1,), (1,)), ((), ())), preferred_element_type=f32)


def dot_tn(left, right):
    return lax.dot_general(left, right, (((0,), (0,)), ((), ())), preferred_element_type=f32)


def swap(value, axis, bit):
    size = lax.axis_size(axis)
    return lax.ppermute(value, axis, [(i, i ^ bit) for i in range(size)])


def gather_relative(value, axis):
    blocks = [value]
    bit = lax.axis_size(axis) // 2
    parts = {0: value}
    while bit:
        for p in list(parts):
            parts[p ^ bit] = swap(parts[p], axis, bit)
        bit //= 2
    return [parts[p] for p in range(lax.axis_size(axis))]


def exchange_relative(blocks, axis):
    return [blocks[0]] + [swap(block, axis, p) for p, block in enumerate(blocks) if p]


def call(kernel, out_shape, operands, spaces="", scratch=(), work=0, room=24):
    vmem = pl.BlockSpec(memory_space=pltpu.VMEM)
    smem = pl.BlockSpec(memory_space=pltpu.SMEM)
    in_specs = [smem if spaces[i : i + 1] == "s" else vmem for i in range(len(operands))]
    return pl.pallas_call(
        kernel,
        out_shape=out_shape,
        in_specs=in_specs,
        out_specs=jax.tree.map(lambda _: vmem, out_shape),
        scratch_shapes=list(scratch),
        compiler_params=pltpu.CompilerParams(vmem_limit_bytes=room * 2**20),
        cost_estimate=pl.CostEstimate(flops=work, bytes_accessed=0, transcendentals=0),
    )(*operands)


def shape(dims, dtype=bf16):
    return jax.ShapeDtypeStruct(tuple(dims), dtype)


def diagonal(size):
    return lax.broadcasted_iota(jnp.int32, (size, size), 0) == lax.broadcasted_iota(
        jnp.int32, (size, size), 1
    )


def to_column(row, size):
    return jnp.sum(jnp.where(diagonal(size), row, 0.0), axis=1, keepdims=True)


def to_row(column, size):
    return jnp.sum(jnp.where(diagonal(size), column, 0.0), axis=0, keepdims=True)


def prepare_weight(n, part, weight, gain_one, gain_two, *outs):
    wide = 3 * part
    s = lax.axis_index("shard")
    extra = outs[0].shape[1] - wide
    one, two = (
        to_column(gain[...].astype(f32).reshape(1, part), part) for gain in (gain_one, gain_two)
    )
    lane = lax.broadcasted_iota(jnp.int32, (part, extra), 1)
    beside = jnp.where(lane == 0, one, jnp.where(lane == 1, two, 0.0)).astype(bf16)
    for p in range(n):
        outs[p][:, wide:] = beside
    for k in range(n):

        @pl.when(s == k)
        def _():
            for p in range(n):
                for kind in range(3):
                    at = (kind * n + (k ^ p)) * part
                    outs[p][:, kind * part : (kind + 1) * part] = weight[:, at : at + part]


def offsets(rows):
    return lax.broadcasted_iota(jnp.int32, (rows, rows), 1) - lax.broadcasted_iota(
        jnp.int32, (rows, rows), 0
    )


def near_buckets(diff, buckets):
    if diff == 0:
        return range(buckets)
    return range(buckets // 2, buckets) if diff > 0 else range(buckets // 2)


def attention_forward(n, rows, width, heads, seqs, buckets, *refs):
    lengths, table = refs[:2]
    token_refs = refs[2 : 2 + n]
    weight_refs = refs[2 + n : 2 + 2 * n]
    tokens_out, weight_out, projected_out, weights_out, *gains_out, mixed_all = refs[
        2 + 2 * n : 9 + 2 * n
    ]
    mixed_out = refs[9 + 2 * n : 9 + 3 * n]
    normed_scr, scores_scr = refs[9 + 3 * n :]
    s = lax.axis_index("shard")
    part = width // n
    wide = 3 * part
    head_dim = part // heads
    for p in range(n):
        tokens_out[s ^ p] = token_refs[p][...]
        weight_out[pl.ds(pl.multiple_of((s ^ p) * part, part & -part), part), :] = weight_refs[p][...]
    size = 128
    for c in range(width // size):
        beside = weight_out[c * size : (c + 1) * size, wide:].astype(f32)
        for i in range(2):
            row = to_row(beside[:, i : i + 1], size)
            gains_out[i][:, c * size : (c + 1) * size] = jnp.broadcast_to(
                row, (gains_out[i].shape[0], size)
            )
    gain = gains_out[0][...]
    for j in range(n):
        value = tokens_out[j].astype(f32)
        factor = lax.rsqrt(jnp.mean(value * value, axis=-1, keepdims=True) + norm_eps)
        normed_scr[j * rows : (j + 1) * rows, :] = (value * factor * gain).astype(bf16)
    projected_out[...] = dot(normed_scr[...], weight_out[:, :wide]).astype(bf16)
    total_rows = n * rows
    key_place = lax.broadcasted_iota(jnp.int32, (1, total_rows), 1)
    key_segment = jnp.zeros((1, total_rows), jnp.int32)
    end = jnp.int32(0)
    ends = []
    for j in range(seqs):
        end = end + lengths[0, j]
        ends.append(end)
        key_segment = key_segment + (key_place >= end).astype(jnp.int32)
    base = offsets(rows)
    steps = {diff: bucket_index(base + diff * rows) for diff in (-1, 0, 1)}
    for h in range(heads):
        query = projected_out[:, h * head_dim : (h + 1) * head_dim]
        key = projected_out[:, part + h * head_dim : part + (h + 1) * head_dim]
        value = projected_out[:, 2 * part + h * head_dim : 2 * part + (h + 1) * head_dim]
        bias = {}
        for diff in (-1, 0, 1):
            block = jnp.zeros((rows, rows), f32)
            for b in near_buckets(diff, buckets):
                block = jnp.where(steps[diff] == b, table[h, b], block)
            bias[diff] = block
        low_side = jnp.full((rows, rows), table[h, buckets // 2 - 1], f32)
        high_side = jnp.full((rows, rows), table[h, buckets - 1], f32)
        scores_scr[...] = dot_nt(query, key)
        for i in range(n):
            scores = scores_scr[i * rows : (i + 1) * rows, :]
            side = [
                bias[j - i] if abs(j - i) <= 1 else (high_side if j > i else low_side)
                for j in range(n)
            ]
            scores = scores + jnp.concatenate(side, axis=1)
            query_place = i * rows + lax.broadcasted_iota(jnp.int32, (rows, 1), 0)
            query_segment = jnp.zeros((rows, 1), jnp.int32)
            for j in range(seqs):
                query_segment = query_segment + (query_place >= ends[j]).astype(jnp.int32)
            scores = jnp.where(query_segment == key_segment, scores, big_negative)
            top = jnp.max(scores, axis=-1, keepdims=True)
            raised = jnp.exp(scores - top)
            total = jnp.sum(raised, axis=-1, keepdims=True)
            weights = (raised * (1.0 / total)).astype(bf16)
            weights_out[h, i * rows : (i + 1) * rows, :] = weights
        mixed_all[:, :, h * head_dim : (h + 1) * head_dim] = (
            dot(weights_out[h], value).astype(bf16).reshape(n, rows, head_dim)
        )
    for p in range(n):
        mixed_out[p][...] = mixed_all[s ^ p]


def attention_backward(n, m, rows, width, heads, buckets, experts, *refs):
    projected, tokens, gains, weight, weights, mixed, weight_out, gain_two, router = refs[:9]
    branch_refs = refs[9 : 9 + n]
    at = 9 + n
    shares = 4 if m > 1 else 2
    share_out = refs[at : at + shares]
    normed_grad_out = refs[at + shares : at + shares + 2]
    gain_out, table_out = refs[at + shares + 2 : at + shares + 4]
    branch_scr, scores_scr, projected_scr, total_scr, out_scr, normed_scr, send_scr, weights_scr = (
        refs[at + shares + 4 :]
    )
    s = lax.axis_index("shard")
    e = lax.axis_index("expert")
    part = width // n
    wide = 3 * part
    group = n * rows
    head_dim = part // heads
    for p in range(n):
        branch_scr[s ^ p] = branch_refs[p][...]
    branch = branch_scr[...].reshape(group, width)
    grad_mixed = dot_nt(branch, weight_out[...]).astype(bf16)
    out_scr[...] = dot_tn(mixed[...].reshape(group, part), branch)
    base = offsets(rows)
    steps = {diff: bucket_index(base + diff * rows) for diff in (-1, 0, 1)}
    lane = lax.broadcasted_iota(jnp.int32, (row_tile, 128), 1)
    line = lax.broadcasted_iota(jnp.int32, (row_tile, 128), 0)
    table_total = jnp.zeros((row_tile, 128), f32)
    per_line = buckets // row_tile
    for h in range(heads):
        query = projected[:, h * head_dim : (h + 1) * head_dim]
        key = projected[:, part + h * head_dim : part + (h + 1) * head_dim]
        value = projected[:, 2 * part + h * head_dim : 2 * part + (h + 1) * head_dim]
        near = {diff: jnp.zeros((rows, rows), f32) for diff in (-1, 0, 1)}
        low_side = jnp.zeros((1, rows), f32)
        high_side = jnp.zeros((1, rows), f32)
        upstream = grad_mixed[:, h * head_dim : (h + 1) * head_dim]
        weights_scr[...] = dot_nt(upstream, value)
        for i in range(n):
            weights_i = weights[h, i * rows : (i + 1) * rows, :].astype(f32)
            grad_weights = weights_scr[i * rows : (i + 1) * rows, :]
            inner = jnp.sum(weights_i * grad_weights, axis=-1, keepdims=True)
            grad_scores = weights_i * (grad_weights - inner)
            scores_scr[i * rows : (i + 1) * rows, :] = grad_scores.astype(bf16)
            for j in range(n):
                block = grad_scores[:, j * rows : (j + 1) * rows]
                if abs(j - i) <= 1:
                    near[j - i] = near[j - i] + block
                elif j > i:
                    high_side = high_side + jnp.sum(block, axis=0, keepdims=True)
                else:
                    low_side = low_side + jnp.sum(block, axis=0, keepdims=True)
        for b in range(buckets):
            amount = jnp.zeros((1, rows), f32)
            for diff in (-1, 0, 1):
                if b in near_buckets(diff, buckets):
                    amount = amount + jnp.sum(
                        jnp.where(steps[diff] == b, near[diff], 0.0), axis=0, keepdims=True
                    )
            if b == buckets - 1:
                amount = amount + high_side
            if b == buckets // 2 - 1:
                amount = amount + low_side
            amount = jnp.sum(amount, axis=1, keepdims=True)
            spot = (line == b // per_line) & (lane == h * per_line + b % per_line)
            table_total = jnp.where(spot, amount, table_total)
        grad_scores_all = scores_scr[...]
        projected_scr[:, h * head_dim : (h + 1) * head_dim] = dot(grad_scores_all, key).astype(bf16)
        projected_scr[:, part + h * head_dim : part + (h + 1) * head_dim] = (
            dot_tn(query, grad_scores_all).T.astype(bf16)
        )
        projected_scr[:, 2 * part + h * head_dim : 2 * part + (h + 1) * head_dim] = (
            dot_tn(upstream, weights[h]).T.astype(bf16)
        )
    table_out[...] = table_total
    grad_projected = projected_scr[...]
    normed_grad = dot_nt(grad_projected, weight[:, :wide])
    send_scr[...] = normed_grad.astype(bf16).reshape(n, rows, width)
    for p in range(n):
        normed_grad_out[p & 1][p >> 1] = send_scr[s ^ p]
    gain = gains[...]
    grad_gain = jnp.zeros((1, width), f32)
    for j in range(n):
        value = tokens[j].astype(f32)
        unit = value * lax.rsqrt(jnp.mean(value * value, axis=-1, keepdims=True) + norm_eps)
        normed_scr[j * rows : (j + 1) * rows, :] = (unit * gain).astype(bf16)
        grad_gain = grad_gain + jnp.sum(
            normed_grad[j * rows : (j + 1) * rows, :] * unit, axis=0, keepdims=True
        )
    gain_out[...] = jnp.broadcast_to(grad_gain, gain_out.shape)
    total_scr[:, :wide] = dot_tn(normed_scr[...], grad_projected)
    full = total_scr.shape[1]
    if m == 1:
        for t in range(n):
            share_out[0][t] = total_scr[t * part : (t + 1) * part, :wide].astype(bf16)
        share_out[1][...] = out_scr[...].astype(bf16)
        return
    piece = part // m
    total_scr[:, wide:] = jnp.zeros((width, full - wide), f32)
    grad_two = gain_two[...].reshape(1, width)
    size = 128
    for c in range(width // size):
        here = slice(c * size, (c + 1) * size)
        total_scr[here, wide : wide + 1] = to_column(grad_gain[:, here], size)
        total_scr[here, wide + 1 : wide + 2] = to_column(grad_two[:, here], size)
        total_scr[here, wide + 2 : wide + 2 + experts] = router[:, here].T
    at = wide + 2 + experts
    rest = (width - full) // n
    for t in range(n):
        total_scr[t * part : (t + 1) * part, at : at + rest] = out_scr[
            :, full + t * rest : full + (t + 1) * rest
        ]
    at = at + rest
    for d in range(m):
        total_scr[d * piece : d * piece + row_tile, at : at + heads * per_line] = table_total[
            :, : heads * per_line
        ]
    for d in range(m):
        target = share_out[(d & 1) + 2 * (d < m // 2)]
        place = (d >> 1) % (m // 4)
        start = (e ^ d) * piece
        for t in range(n):
            rows_at = pl.multiple_of(t * part + start, row_tile)
            target[place, t] = total_scr[pl.ds(rows_at, piece), :].astype(bf16)
        rows_at = pl.multiple_of(start, row_tile)
        target[place, n] = out_scr[pl.ds(rows_at, piece), :full].astype(bf16)


def beside_columns(ref, p, wide):
    last = ref[p, :, ref.shape[2] - 128 :]
    skip = wide - (ref.shape[2] - 128)
    return jnp.concatenate([last[:, skip:], last[:, :skip]], axis=1)


def assemble(n, m, part, piece, experts, *refs):
    total_out, out_out, one_out, two_out, router_out, small_scr = refs[m:]
    s = lax.axis_index("shard")
    e = lax.axis_index("expert")
    wide = 3 * part
    full = refs[0].shape[2]
    at = wide + 2 + experts
    rest = (n * part - full) // n
    for d in range(m):
        start = pl.multiple_of((e ^ d) * piece, row_tile)
        own = pl.ds(start, piece)
        small = jnp.zeros((piece, 128), f32)
        for p in range(n):
            small = small + beside_columns(refs[d], p, wide).astype(f32)
            out_out[own, full + p * rest : full + (p + 1) * rest] = refs[d][p, :, at : at + rest].astype(
                f32
            )
        out_out[own, :full] = refs[d][n].astype(f32)
        small_scr[own, :] = small
    small = small_scr[...].T
    one_out[...] = small[0:1, :]
    two_out[...] = small[1:2, :]
    router_out[...] = small[2 : 2 + experts, :]
    for k in range(n):

        @pl.when(s == k)
        def _():
            for d in range(m):
                own = pl.ds(pl.multiple_of((e ^ d) * piece, row_tile), piece)
                for p in range(n):
                    for kind in range(3):
                        to = (kind * n + (k ^ p)) * part
                        total_out[own, to : to + part] = refs[d][
                            p, :, kind * part : (kind + 1) * part
                        ].astype(f32)


def expert_forward(rows, own, came, up_own, up_pair, down_own, down_pair, *outs):
    hidden_out, slope_out, keep_out, send_out = outs
    source = jnp.concatenate([own[...], came[...]], axis=0)
    result = 0.0
    for k, (up, down) in enumerate(((up_own, down_own), (up_pair, down_pair))):
        before = dot(source, up[0])
        square = before * before
        tanh_value = jnp.tanh(gelu_scale * before * (1.0 + gelu_cubic * square))
        half = 0.5 * (1.0 + tanh_value)
        hidden = (before * half).astype(bf16)
        slope = half + 0.5 * before * (1.0 - tanh_value * tanh_value) * gelu_scale * (
            1.0 + 3.0 * gelu_cubic * square
        )
        hidden_out[k] = hidden
        slope_out[k] = slope.astype(bf16)
        result = result + dot(hidden, down[0])
    keep_out[...] = result[:rows]
    send_out[...] = result[rows:].astype(bf16)


def expert_backward(rows, own, came, up_own, up_pair, down_own, down_pair, slope, *outs):
    before_out, keep_out, send_out = outs
    grads = jnp.concatenate([own[...], came[...]], axis=0)
    result = 0.0
    for k, (up, down) in enumerate(((up_own, down_own), (up_pair, down_pair))):
        grad_before = (dot_nt(grads, down[0]) * slope[k].astype(f32)).astype(bf16)
        before_out[k] = grad_before
        result = result + dot_nt(grad_before, up[0])
    keep_out[...] = result[:rows]
    send_out[...] = result[rows:].astype(bf16)


def weights_to_send(own, came, own_grad, came_grad, hidden, grad_before, up_send, down_send):
    grads = jnp.concatenate([own_grad[...], came_grad[...]], axis=0)
    rows = jnp.concatenate([own[...], came[...]], axis=0)
    up_send[0] = dot_tn(rows, grad_before[1]).astype(bf16)
    down_send[0] = dot_tn(hidden[1], grads).astype(bf16)


def weights_to_keep(
    own, came, own_grad, came_grad, hidden, grad_before, up_came, down_came, up_out, down_out
):
    grads = jnp.concatenate([own_grad[...], came_grad[...]], axis=0)
    rows = jnp.concatenate([own[...], came[...]], axis=0)
    up_out[0] = dot_tn(rows, grad_before[0]) + up_came[0].astype(f32)
    down_out[0] = dot_tn(hidden[0], grads) + down_came[0].astype(f32)


def rms_factor(value):
    return lax.rsqrt(jnp.mean(value * value, axis=-1, keepdims=True) + norm_eps)


def rms_backward(value, factor, gain, upstream):
    scaled = upstream * gain
    grad_value = factor * scaled - value * factor * factor * factor * jnp.mean(
        scaled * value, axis=-1, keepdims=True
    )
    grad_gain = jnp.sum(upstream * value * factor, axis=0)
    return (grad_value, grad_gain)


def local(
    tokens,
    lengths,
    routes,
    attention_in,
    attention_out,
    position_bias,
    first_gain,
    second_gain,
    router,
    expert_in,
    expert_out,
    cotangent,
):
    n = lax.axis_size("shard")
    m = lax.axis_size("expert")
    s = lax.axis_index("shard")
    e = lax.axis_index("expert")
    rows, width = tokens.shape
    heads, buckets = position_bias.shape
    part = width // n
    wide = 3 * part
    group = n * rows
    seqs = lengths.shape[1]
    experts = router.shape[1]
    direct = m == 8
    full = wide + -wide % 128
    micro = 10**9

    far_tokens, pair_tokens = swap(tokens, "shard", 2 * pair), swap(tokens, "shard", pair)
    weight_blocks = exchange_relative(
        call(
            lambda *refs: prepare_weight(n, part, *refs),
            [shape((part, full))] * n,
            (attention_in, first_gain, second_gain),
            room=56,
        ),
        "shard",
    )
    far_tokens, own_up, own_down, table_scalars = lax.optimization_barrier(
        (far_tokens, expert_in, expert_out, position_bias.astype(f32))
    )
    token_blocks = [tokens, pair_tokens, far_tokens, swap(far_tokens, "shard", pair)]
    pair_up = swap(own_up, "shard", pair)
    pair_down = swap(own_down, "shard", pair)
    own_out, token_blocks, weight_blocks = lax.optimization_barrier(
        (attention_out, token_blocks, weight_blocks)
    )
    far_out, pair_out = swap(own_out, "shard", 2 * pair), swap(own_out, "shard", pair)

    answers = call(
        lambda *refs: attention_forward(n, rows, width, heads, seqs, buckets, *refs),
        (
            shape((n, rows, width)),
            shape((width, full)),
            shape((group, wide)),
            shape((heads, group, group)),
            shape((1, width), f32),
            shape((rows, width), f32),
            shape((n, rows, part)),
            *[shape((rows, part))] * n,
        ),
        (lengths, table_scalars, *token_blocks, *weight_blocks),
        "ss",
        [pltpu.VMEM((group, width), bf16), pltpu.VMEM((group, group), f32)],
        work=10 * micro,
        room=56,
    )
    tokens_all, weight, projected, weights, gain_one, gain_two, mixed = answers[:7]
    mixed_mine, pair_up, pair_down, pair_out = lax.optimization_barrier(
        (list(answers[7:]), pair_up, pair_down, pair_out)
    )
    mixed_blocks = exchange_relative(mixed_mine, "shard")
    out_blocks = [own_out, pair_out, far_out, swap(far_out, "shard", pair)]

    inputs = tokens.astype(f32)
    hidden_one = inputs + sum(dot(mixed_blocks[p], out_blocks[p]) for p in range(n))
    factor_two = rms_factor(hidden_one)
    normed_two = hidden_one * factor_two * gain_two
    logits = jnp.dot(
        normed_two, router, precision=lax.Precision.HIGHEST, preferred_element_type=f32
    )
    shifted = jnp.exp(logits - jnp.max(logits, axis=-1, keepdims=True))
    probs = shifted / jnp.sum(shifted, axis=-1, keepdims=True)
    route = routes[:, 0]
    chosen = (route[:, None] == lax.iota(jnp.int32, experts)[None, :]).astype(f32)
    gate = jnp.sum(probs * chosen, axis=1)
    lower = (lax.iota(jnp.int32, rows)[:, None] >= lax.iota(jnp.int32, rows)[None, :]).astype(bf16)
    running = dot(lower, chosen.astype(bf16))
    slot = jnp.sum((running - 1.0) * chosen, axis=1).astype(jnp.int32)
    capacity = max(2, 9 * rows // (8 * experts) + 1)
    capacity = -(-capacity // slot_tile) * slot_tile
    places = experts * capacity
    half = places // 2
    if direct:
        holder = route ^ e
        target = (holder & 1) * half + (holder >> 1) * capacity + slot
    else:
        target = route * capacity + slot
    collect = (target[:, None] == lax.iota(jnp.int32, places)[None, :]).astype(bf16)
    upstream = cotangent.astype(f32)
    grad_result = (gate[:, None] * upstream).astype(bf16)

    def plain(value):
        return lax.all_to_all(
            value.reshape(experts, capacity, width), "expert", 0, 0, tiled=True
        ).reshape(places, width)

    def dispatch(forward, backward):
        if not direct:
            return [plain(dot_tn(collect, x).astype(bf16)) for x in (forward, backward)]
        came = swap(dot_tn(collect[:, half:], forward).astype(bf16), "expert", 1)
        came, other = lax.optimization_barrier(
            (came, dot_tn(collect[:, half:], backward).astype(bf16))
        )

        def both(own, came):
            own = dot_tn(collect[:, :half], own).astype(bf16).reshape(m // 2, capacity, width)
            return jnp.concatenate([own, came.reshape(m // 2, capacity, width)], axis=1)

        first = among_pairs(both(forward, came))
        second, first[1] = lax.optimization_barrier(
            (both(backward, swap(other, "expert", 1)), first[1])
        )
        return [jnp.concatenate(x, axis=0) for x in (first, among_pairs(second))]

    def among_pairs(both):
        return [both[d] if d == 0 else swap(both[d], "expert", 2 * d) for d in range(m // 2)]

    def give_back(forward, backward, late, work):
        if not direct:
            return [dot(collect, plain(x)) for x in (forward, backward)] + [work(late)]
        forward, backward = (
            x.reshape(m // 2, 2 * capacity, width) for x in (forward, backward)
        )
        blocks = [among_pairs(forward)]
        backward, blocks[0][1] = lax.optimization_barrier((backward, blocks[0][1]))
        blocks.append(among_pairs(backward))
        late, blocks = lax.optimization_barrier((late, blocks))
        own, other = (
            jnp.concatenate(
                [jnp.concatenate([x[at : at + capacity] for x in side]) for side in blocks], axis=1
            )
            for at in (0, capacity)
        )
        beside = work(late)
        other, beside = lax.optimization_barrier((swap(other, "expert", 1), beside))
        total = dot(collect[:, :half], own) + dot(collect[:, half:], other)
        return total[:, :width], total[:, width:], beside

    def reduce_shard(keep, out, after=None):
        came = swap(out, "shard", 2 * pair)
        if after is not None:
            came, _ = lax.optimization_barrier((came, after))
        return (keep + came.astype(f32)).astype(bf16)

    arrived, arrived_grad = dispatch(normed_two.astype(bf16), grad_result)
    came = swap(arrived, "shard", 2 * pair)
    row_blocks = (arrived, came)
    grad_blocks = (arrived_grad, swap(arrived_grad, "shard", 2 * pair))

    units = expert_in.shape[2]
    expert_weight = (own_up, pair_up, own_down, pair_down)
    middle = shape((2, 2 * places, units))
    kept, sent = shape((places, width), f32), shape((places, width))
    hidden, slope, *forward = call(
        lambda *refs: expert_forward(places, *refs),
        (middle, middle, kept, sent),
        (*row_blocks, *expert_weight),
        work=6 * micro,
    )
    grad_before, *backward = call(
        lambda *refs: expert_backward(places, *refs),
        (middle, kept, sent),
        (*grad_blocks, *expert_weight, slope),
        work=6 * micro,
    )
    sources = (*grad_blocks, hidden, grad_before)
    expert_result, grad_sent, (up_send, down_send) = give_back(
        reduce_shard(*forward, backward[1]),
        reduce_shard(*backward),
        row_blocks,
        lambda rows_late: call(
            weights_to_send,
            (shape(expert_in.shape), shape(expert_out.shape)),
            (*rows_late, *sources),
            work=4 * micro,
        ),
    )

    layer_out = (hidden_one + gate[:, None] * expert_result).astype(bf16)
    grad_gate = jnp.sum(upstream * expert_result, axis=1)
    grad_logits = (grad_gate * gate)[:, None] * (chosen - probs)
    grad_router = lax.dot_general(
        grad_logits,
        normed_two,
        (((0,), (0,)), ((), ())),
        precision=lax.Precision.HIGHEST,
        preferred_element_type=f32,
    )
    grad_normed_two = grad_sent + lax.dot_general(
        grad_logits,
        router,
        (((1,), (1,)), ((), ())),
        precision=lax.Precision.HIGHEST,
        preferred_element_type=f32,
    )
    grad_middle, grad_gain_two = rms_backward(hidden_one, factor_two, gain_two, grad_normed_two)
    grad_hidden = upstream + grad_middle
    branch = grad_hidden.astype(bf16)
    far_branch, pair_branch = swap(branch, "shard", 2 * pair), swap(branch, "shard", pair)
    far_branch, grad_router, gain_two_row = lax.optimization_barrier(
        (far_branch, grad_router, grad_gain_two)
    )
    branch_blocks = [branch, pair_branch, far_branch, swap(far_branch, "shard", pair)]
    branch_blocks, up_send, down_send = lax.optimization_barrier(
        (branch_blocks, up_send, down_send)
    )
    up_came, down_came = swap(up_send, "shard", pair), swap(down_send, "shard", pair)
    holders = m if direct else 1
    piece = part // m
    if direct:
        share_shapes = [shape((m // 4, n + 1, piece, full))] * 4
    else:
        share_shapes = [shape((n, part, wide)), shape((part, width))]
    answers = call(
        lambda *refs: attention_backward(n, holders, rows, width, heads, buckets, experts, *refs),
        (
            *share_shapes,
            *[shape((n // 2, rows, width))] * 2,
            shape((row_tile, width), f32),
            shape((row_tile, 128), f32),
        ),
        (
            projected,
            tokens_all,
            gain_one,
            weight,
            weights,
            mixed,
            own_out,
            gain_two_row,
            grad_router,
            *branch_blocks,
        ),
        "",
        [
            pltpu.VMEM((n, rows, width), bf16),
            pltpu.VMEM((group, group), bf16),
            pltpu.VMEM((group, wide), bf16),
            pltpu.VMEM((width, full), f32),
            pltpu.VMEM((part, width), f32),
            pltpu.VMEM((group, width), bf16),
            pltpu.VMEM((n, rows, width), bf16),
            pltpu.VMEM((group, group), f32),
        ],
        work=8 * micro,
    )
    shares = answers[: len(share_shapes)]
    normed_keep, normed_send, gain_row, table = answers[len(share_shapes) :]

    def kept_weights(late_rows):
        return call(
            weights_to_keep,
            (shape(expert_in.shape, f32), shape(expert_out.shape, f32)),
            (*late_rows, *sources, up_came, down_came),
            work=4 * micro,
        )

    per_line = buckets // row_tile

    def biases(block):
        return block.reshape(row_tile, heads, per_line).swapaxes(0, 1).reshape(heads, buckets)

    normed_sum = normed_keep.astype(f32) + swap(normed_send, "shard", pair).astype(f32)
    far_sum = swap(normed_sum[1].astype(bf16), "shard", 2 * pair)
    late, far_sum = lax.optimization_barrier((tokens, far_sum))
    late = late.astype(f32)
    grad_input_norm, _ = rms_backward(
        late, rms_factor(late), gain_one, normed_sum[0] + far_sum.astype(f32)
    )
    grad_tokens = (grad_hidden + grad_input_norm).astype(bf16)
    if direct:
        far_keep, far_send, near_keep, near_send = shares
        far_came = swap(far_send, "expert", 1)
        far_came, near_send, up_came, down_came = lax.optimization_barrier(
            (far_came, near_send, up_came, down_came)
        )
        far = far_keep.astype(f32) + far_came.astype(f32)
        near_came, late_rows = lax.optimization_barrier((swap(near_send, "expert", 1), row_blocks))
        near = near_keep.astype(f32) + near_came.astype(f32)
        came = [swap(far[d].astype(bf16), "expert", m // 2 + 2 * d) for d in range(m // 4)]
        came += [swap(near[d].astype(bf16), "expert", 2 * d) for d in range(1, m // 4)]
        came, (grad_up, grad_down) = lax.optimization_barrier((came, kept_weights(late_rows)))
        summed = near[0] + sum(x.astype(f32) for x in came)
        at = wide + 2 + experts
        rest = (width - full) // n
        table_total = biases(
            summed[0, :row_tile, at + rest : at + rest + heads * per_line]
        )
        low = summed.astype(bf16)
        mine = exchange_relative(
            [lax.dynamic_index_in_dim(low, s ^ p, 0, keepdims=False) for p in range(n)], "shard"
        )
        lane = lax.iota(jnp.int32, full)[None, :]
        own_lane = (lane >= at) & (lane < at + rest)
        mine = jnp.stack(
            [jnp.where(own_lane, low[p], mine[p]) for p in range(n)] + [low[n]], axis=0
        )
        blocks = {0: mine, 1: swap(mine, "expert", 1), 4: swap(mine, "expert", 4)}
        blocks[2] = swap(mine, "expert", 2)
        blocks[2], blocks[1] = lax.optimization_barrier((blocks[2], blocks[1]))
        blocks[3] = swap(blocks[2], "expert", 1)
        blocks[4], blocks[3] = lax.optimization_barrier((blocks[4], blocks[3]))
        blocks[6] = swap(blocks[4], "expert", 2)
        blocks[5] = swap(blocks[4], "expert", 1)
        blocks[6], grad_tokens = lax.optimization_barrier((blocks[6], grad_tokens))
        blocks[7] = swap(blocks[6], "expert", 1)
        blocks = [blocks[d] for d in range(m)]
        grad_attention_in, grad_attention_out, total_one, total_two, total_router = call(
            lambda *refs: assemble(n, m, part, piece, experts, *refs),
            (
                shape((part, 3 * width), f32),
                shape((part, width), f32),
                shape((1, part), f32),
                shape((1, part), f32),
                shape((experts, part), f32),
            ),
            (*blocks,),
            "",
            [pltpu.VMEM((part, 128), f32)],
        )
    else:
        grad_up, grad_down = kept_weights(row_blocks)
        came = lax.all_to_all(
            shares[0].reshape(n, m, piece, wide).swapaxes(0, 1), "expert", 0, 0, tiled=True
        )
        summed = sum(x.astype(f32) for x in came).astype(bf16)
        mine = lax.all_to_all(summed, "shard", 0, 0, tiled=True)
        mine = mine.reshape(n, piece, 3, part).transpose(1, 2, 0, 3).reshape(piece, 3 * width)
        came = lax.all_to_all(shares[1].reshape(m, piece, width), "expert", 0, 0, tiled=True)
        out_mine = sum(x.astype(f32) for x in came).astype(bf16)
        grad_attention_in = lax.all_gather(mine, "expert", axis=0, tiled=True).astype(f32)
        grad_attention_out = lax.all_gather(out_mine, "expert", axis=0, tiled=True).astype(f32)
        small = jnp.concatenate([gain_row[0:1], grad_gain_two[None], grad_router], axis=0)
        small_total = lax.psum_scatter(small, "shard", scatter_dimension=1, tiled=True)
        small_total, table_total = lax.psum(
            (small_total, biases(table[:, : heads * per_line])), "expert"
        )
        total_one, total_two, total_router = small_total[0:1], small_total[1:2], small_total[2:]
    return (
        layer_out,
        grad_tokens,
        grad_attention_in,
        grad_attention_out,
        table_total,
        total_one[0],
        total_two[0],
        total_router.T,
        grad_up,
        grad_down,
    )


def solution(mesh):
    in_specs = (
        P(("expert", "shard"), None),
        P("expert", None),
        P(("expert", "shard"), None),
        P("shard", None),
        P("shard", None),
        P("shard", None),
        P("shard"),
        P("shard"),
        P(),
        P("expert", None, "shard"),
        P("expert", "shard", None),
        P(("expert", "shard"), None),
    )
    out_specs = (
        P(("expert", "shard"), None),
        P(("expert", "shard"), None),
        P("shard", None),
        P("shard", None),
        P("shard", None),
        P("shard"),
        P("shard"),
        P("shard", None),
        P("expert", None, "shard"),
        P("expert", "shard", None),
    )
    return jax.shard_map(local, mesh=mesh, in_specs=in_specs, out_specs=out_specs, check_vma=False)
```
